32 devices in a mesh: expert: 4 (over y, x), context: 4 (over z), dp: 2 (over core).
Axes of the slice: x: 2, y: 2, z: 4, core: 2. Of those that a mesh axis runs over, the one named last changes fastest.
Arguments:
- tokens: bfloat16 [8, 1024, 2048], P('expert', ('context', 'dp')), may hold values from -6 to 6
- block_ids: int32 [8, 1024], P('expert', ('context', 'dp')), may hold values from 0 to 7, never falling along the last dimension, each value on 1 to 256 neighbouring positions
- routes: int32 [8, 1024, 8], P('expert', ('context', 'dp')), may hold values from 0 to 15, all different within a row
- norm_gains: bfloat16 [2048, 4], P(('expert', 'context', 'dp')), may hold values from 0.099609375 to 1.8984375
- w_query: bfloat16 [2048, 2048], P(('expert', 'context', 'dp')), may hold values from -0.125 to 0.125
- w_key: bfloat16 [2048, 2048], P(('expert', 'context', 'dp')), may hold values from -0.125 to 0.125
- w_value: bfloat16 [2048, 2048], P(('expert', 'context', 'dp')), may hold values from -0.125 to 0.125
- w_output: bfloat16 [2048, 2048], P(('expert', 'context', 'dp')), may hold values from -3 to 3
- router: bfloat16 [2048, 16], P(('expert', 'context', 'dp')), may hold values from -0.0625 to 0.0625
- expert_gate: bfloat16 [16, 2048, 1024], P(('expert', 'context')), may hold values from -0.125 to 0.125
- expert_up: bfloat16 [16, 2048, 1024], P(('expert', 'context')), may hold values from -0.125 to 0.125
- expert_down: bfloat16 [16, 1024, 2048], P(('expert', 'context')), may hold values from -1 to 1
- cotangent: bfloat16 [8, 1024, 2048], P('expert', ('context', 'dp')), may hold values from -6 to 6
Outputs:
- activations: bfloat16 [8, 1024, 2048], P('expert', ('context', 'dp'))
- input_grad: float32 [8, 1024, 2048], P('expert', ('context', 'dp'))
- grad_gains: float32 [2048, 4], P(('expert', 'context', 'dp'))
- grad_query: float32 [2048, 2048], P(('expert', 'context', 'dp'))
- grad_key: float32 [2048, 2048], P(('expert', 'context', 'dp'))
- grad_value: float32 [2048, 2048], P(('expert', 'context', 'dp'))
- grad_output: float32 [2048, 2048], P(('expert', 'context', 'dp'))
- grad_router: float32 [2048, 16], P(('expert', 'context', 'dp'))
- grad_gate: float32 [16, 2048, 1024], P(('expert', 'context'), None, 'dp')
- grad_up: float32 [16, 2048, 1024], P(('expert', 'context'), None, 'dp')
- grad_down: float32 [16, 1024, 2048], P(('expert', 'context'), 'dp')
The draws below stay inside these ranges and needn't reach their ends.
Inputs may be any that keep to these rules, and one draw needn't show every extreme that they name: `block_ids`: block ids never fall along a sequence; one block holds at most 256 tokens. `routes`: each token names 8 different experts; a smaller position is a higher priority for slots.
All inputs are finite; a program needn't handle non-finite values.
Results may differ from the reference program's by a relative error of at most 0.017.
Values may be sent and summed in bfloat16 or wider, within the bound.
A program may use at most 200 MiB of HBM per device.

```python
import math
import jax
import jax.numpy as jnp
import numpy as np
from jax import lax

D = 2048
HEADS = 16
HEAD = 128
FF = 1024
TOPK = 8
BLOCK = 256
SEQ_DEV = 128
LEN = 1024
SEQS = 8
EXPERTS = 16
CAP = 64


def block_levels(rng, shape, cuts, least, high):
    def one(dim, parts):
        heights = jax.random.uniform(jax.random.fold_in(jax.random.fold_in(rng, 6), dim), (parts,), jnp.float32, least / len(cuts), high / len(cuts))
        return jnp.repeat(jnp.exp(heights), shape[dim] // parts).reshape((-1,) + (1,) * (len(shape) - dim - 1))

    loudness = one(*cuts[0])
    for cut in cuts[1:]:
        loudness = loudness * one(*cut)
    return loudness


def picks_of(rng, rows, count, top, lift):
    sequence = jax.random.permutation(jax.random.fold_in(rng, 1), count)
    favour = sequence
    for power in range(3):
        favour = favour * favour // count
    favour = favour * lift // count
    tickets = jax.random.randint(jax.random.fold_in(rng, 2), (rows, count), 0, 4096) + favour
    fixed_rows = jax.random.permutation(jax.random.fold_in(rng, 3), rows)[jnp.arange(count) % rows]
    tickets = jnp.where(jnp.arange(rows)[:, None] == fixed_rows[None, :], 1 << 14, tickets)
    score = tickets * count + jnp.arange(count)
    return lax.top_k(score.astype(jnp.int32), top)[1].astype(jnp.int32)


def profile(number_of, total, limit, skew):
    weights = [(1 << 20) // math.isqrt(grade ** skew) + 1 for grade in range(2, number_of + 1)]
    surplus, holding = total - limit - (number_of - 1), [1] * (number_of - 1)
    while surplus > 0:
        movable = [i for i in range(number_of - 1) if holding[i] < limit]
        pool, remaining = sum([weights[i] for i in movable]), surplus
        for i in movable:
            addition = min(limit - holding[i], max(1, remaining * weights[i] // pool), surplus)
            holding[i] = holding[i] + addition
            surplus = surplus - addition
    return np.array([limit] + holding)


def uneven_parts(stream_key, count, total, limit, slope):
    if count == 2:
        one = jax.random.randint(stream_key, (), max(1, total - limit), min(limit, total - 1) + 1)
        return jnp.stack([one, total - one])
    sizes = jnp.asarray(profile(count, total, limit, slope), jnp.int32)
    couples = (count - 1) // 2
    giver, taker = sizes[1:1 + 2 * couples:2], sizes[2:2 + 2 * couples:2]
    slack = jnp.minimum(giver - 1, limit - taker)
    shifted = jax.random.randint(jax.random.fold_in(stream_key, 1), (couples,), 0, 1 << 20) % (slack + 1)
    sizes = sizes.at[1:1 + 2 * couples:2].set(giver - shifted).at[2:2 + 2 * couples:2].set(taker + shifted)
    return sizes[jax.random.permutation(jax.random.fold_in(stream_key, 2), count)]


def normal_values(key, extent, spread, reach, split=(), kind=jnp.bfloat16):
    values = jax.random.normal(key, extent, jnp.float32) * spread
    if len(split) > 0:
        values = block_levels(key, extent, split, -0.22, 0.18) * values
    return jnp.clip(values, min=-reach, max=reach).astype(kind)


def setup_inputs(seed: int = 0) -> dict:
    arg_keys = jax.random.split(jax.random.key(seed), 14)
    tokens = normal_values(arg_keys[0], (SEQS, LEN, D), 1.0, 6.0, ((0, 4), (1, 8)))
    block_ids = jax.vmap(lambda own: jnp.searchsorted(jnp.cumsum(uneven_parts(own, 2 * LEN // BLOCK, LEN, BLOCK, 1)), jnp.arange(LEN), side="right"))(jax.random.split(arg_keys[1], SEQS)).reshape((SEQS, LEN)).astype(jnp.int32)
    routes = picks_of(arg_keys[2], SEQS * LEN, EXPERTS, TOPK, 4096).reshape((SEQS, LEN, TOPK))
    norm_gains = jnp.clip(1.0 + 0.18 * jax.random.normal(arg_keys[3], (D, 4), jnp.float32), 0.099609375, 1.8984375).astype(jnp.bfloat16)
    w_query = normal_values(arg_keys[4], (D, D), D ** -0.5, 0.125, ((0, 32),))
    w_key = normal_values(arg_keys[5], (D, D), D ** -0.5, 0.125, ((0, 32),))
    w_value = normal_values(arg_keys[6], (D, D), D ** -0.5, 0.125, ((0, 32),))
    w_output = normal_values(arg_keys[7], (D, D), (max(1, 2 * D // LEN)) ** -0.5, 3.0, ((0, 32),))
    router = normal_values(arg_keys[8], (D, EXPERTS), (4 * D) ** -0.5, 0.0625, ((0, 32),))
    expert_gate = normal_values(arg_keys[9], (EXPERTS, D, FF), D ** -0.5, 0.125, ((0, 16),))
    expert_up = normal_values(arg_keys[10], (EXPERTS, D, FF), D ** -0.5, 0.125, ((0, 16),))
    expert_down = normal_values(arg_keys[11], (EXPERTS, FF, D), (max(1, FF * TOPK // (EXPERTS * EXPERTS))) ** -0.5, 1.0, ((0, 16),))
    cotangent = normal_values(arg_keys[12], (SEQS, LEN, D), 1.0, 6.0, ((0, 4), (1, 8)))
    return {"tokens": tokens, "block_ids": block_ids, "routes": routes, "norm_gains": norm_gains, "w_query": w_query, "w_key": w_key, "w_value": w_value, "w_output": w_output, "router": router, "expert_gate": expert_gate, "expert_up": expert_up, "expert_down": expert_down, "cotangent": cotangent}


epsilon = 1e-05
masked_value = -1e+30
highest = lax.Precision.HIGHEST

@jax.custom_vjp
def low(v):
    return lax.optimization_barrier(v.astype(jnp.bfloat16)).astype(jnp.float32)

@jax.custom_vjp
def low_back(v):
    return v

def low_keep(v):
    return (low(v), None)

def low_pass(kept, grad):
    return (grad,)

def back_keep(v):
    return (v, None)

def back_low(kept, grad):
    return (low(grad),)
low.defvjp(low_keep, low_pass)
low_back.defvjp(back_keep, back_low)

def rms_factor(values):
    return lax.rsqrt(lax.optimization_barrier(jnp.mean(values * values, axis=-1, keepdims=True)) + epsilon)

def matmul_high(first_array, second_array):
    return jnp.dot(first_array, second_array, precision=highest)

def block_slots(route_block):
    pair_expert = route_block.T.reshape(-1)
    pair_count = pair_expert.shape[0]
    onehot = (pair_expert[:, None] == jnp.arange(EXPERTS, dtype=jnp.int32)[None, :]).astype(jnp.int32)
    earlier = jnp.cumsum(onehot, axis=0) - onehot
    slot_index = lax.optimization_barrier(jnp.sum(earlier * onehot, axis=1))
    kept_pair = slot_index < CAP
    target = jnp.where(kept_pair, pair_expert * CAP + slot_index, 0).astype(jnp.int32)
    cell_index = jnp.arange(EXPERTS * CAP, dtype=jnp.int32)
    matches = jnp.logical_and(target[None, :] == cell_index[:, None], kept_pair[None, :])
    filled = jnp.any(matches, axis=1)
    source = lax.optimization_barrier(jnp.sum(jnp.where(matches, jnp.arange(pair_count, dtype=jnp.int32)[None, :], 0), axis=1)).astype(jnp.int32)
    return (kept_pair, target, filled, source)

def attend(sequence_items):
    queries, keys, values, block_row = sequence_items
    query_heads = queries.reshape(LEN, HEADS, HEAD)
    key_heads = keys.reshape(LEN, HEADS, HEAD)
    value_heads = values.reshape(LEN, HEADS, HEAD)
    scores = low_back(jnp.einsum('qhd,khd->hqk', query_heads, key_heads, precision=highest) * HEAD ** (-0.5))
    allowed = block_row[None, :] <= block_row[:, None]
    scores = jnp.where(allowed[None], scores, masked_value)
    weights = low(jax.nn.softmax(scores, axis=-1))
    return jnp.einsum('hqk,khd->qhd', weights, value_heads, precision=highest).reshape(LEN, D)

def forward(tokens, norm_gains, w_query, w_key, w_value, w_output, router, expert_gate, expert_up, expert_down, block_ids, routes):
    flat_tokens = tokens.reshape(-1, D)
    normed = low(flat_tokens * rms_factor(flat_tokens) * norm_gains[:, 0])
    query_raw = low_back(matmul_high(normed, w_query))
    key_raw = low_back(matmul_high(normed, w_key))
    value_low = low(low_back(matmul_high(normed, w_value)))
    queries = low(query_raw * rms_factor(query_raw) * norm_gains[:, 1])
    keys = low(key_raw * rms_factor(key_raw) * norm_gains[:, 2])
    mixed = lax.map(jax.checkpoint(attend), (queries.reshape(SEQS, LEN, D), keys.reshape(SEQS, LEN, D), value_low.reshape(SEQS, LEN, D), block_ids))
    mixed_low = low(low_back(mixed.reshape(-1, D)))
    resid = flat_tokens + low_back(matmul_high(mixed_low, w_output))
    second_low = low(resid * rms_factor(resid) * norm_gains[:, 3])
    logits = low_back(matmul_high(second_low, router))
    router_probs = jax.nn.softmax(logits, axis=-1)
    flat_routes = routes.reshape(-1, TOPK)
    gate_vals = jnp.take_along_axis(router_probs, flat_routes, axis=1)
    block_count = flat_routes.shape[0] // SEQ_DEV
    kept_pair, target, filled, source = jax.vmap(block_slots)(flat_routes.reshape(block_count, SEQ_DEV, TOPK))
    token_index = (jnp.arange(block_count, dtype=jnp.int32)[:, None] * SEQ_DEV + source % SEQ_DEV).astype(jnp.int32)
    expert_in = low_back(second_low[token_index] * filled[..., None].astype(second_low.dtype))
    expert_in = expert_in.reshape(block_count, EXPERTS, CAP, D)
    gate_pre = low_back(jnp.einsum('becd,edf->becf', expert_in, expert_gate, precision=highest))
    up_pre = low_back(jnp.einsum('becd,edf->becf', expert_in, expert_up, precision=highest))
    act = low(jax.nn.silu(gate_pre) * up_pre)
    expert_out = low(low_back(jnp.einsum('becf,efd->becd', act, expert_down, precision=highest)))
    expert_out = expert_out.reshape(block_count, EXPERTS * CAP, D)
    pair_out = jax.vmap(lambda rows, where_to: jnp.take(rows, where_to, axis=0))(expert_out, target)
    pair_out = pair_out.reshape(block_count, TOPK, SEQ_DEV, D)
    pair_weight = jnp.transpose(gate_vals.reshape(block_count, SEQ_DEV, TOPK), (0, 2, 1))
    pair_weight = pair_weight * kept_pair.reshape(block_count, TOPK, SEQ_DEV).astype(pair_weight.dtype)
    mixture = lax.optimization_barrier(jnp.sum(pair_weight[..., None] * pair_out, axis=1)).reshape(-1, D)
    return (resid + mixture).reshape(SEQS, LEN, D)

def reference(tokens, block_ids, routes, norm_gains, w_query, w_key, w_value, w_output, router, expert_gate, expert_up, expert_down, cotangent):
    floats = tuple((array.astype(jnp.float32) for array in (tokens, norm_gains, w_query, w_key, w_value, w_output, router, expert_gate, expert_up, expert_down)))

    def closed(*arrays):
        return forward(*arrays, block_ids, routes)
    result, pullback = jax.vjp(closed, *floats)
    grads = pullback(cotangent.astype(jnp.float32))
    return (result.astype(jnp.bfloat16), grads[0], grads[1], grads[2], grads[3], grads[4], grads[5], grads[6], grads[7], grads[8], grads[9])
```

```python
import functools

import jax
import jax.numpy as jnp
from jax import lax
from jax.experimental import pallas as pl
from jax.experimental.pallas import tpu as pltpu
from jax.sharding import PartitionSpec as P

HEAD = 128
EPSILON = 1e-05
MASKED = -1e30
UNUSED_SLOT = 4096.0
ALL_AXES = ("expert", "context", "dp")
MESH = pl.DeviceIdType.MESH
ANY = pl.BlockSpec(memory_space=pl.ANY)
VMEM = pl.BlockSpec(memory_space=pltpu.VMEM)
DMA = pltpu.SemaphoreType.DMA
MIB = 1 << 20
f32 = jnp.float32
bf16 = jnp.bfloat16


def call(kernel, operands, out_shapes, in_specs, out_specs, scratch, collective, name, vmem=32):
    return pl.pallas_call(
        kernel,
        out_shape=out_shapes,
        in_specs=in_specs,
        out_specs=out_specs,
        scratch_shapes=scratch,
        compiler_params=pltpu.CompilerParams(
            collective_id=collective, has_side_effects=True, vmem_limit_bytes=vmem * MIB
        ),
        name=name,
    )(*operands)


def position():
    return lax.axis_index("expert"), lax.axis_index("context"), lax.axis_index("dp")


def meet(devices):
    barrier = pltpu.get_barrier_semaphore()
    for device in devices:
        pl.semaphore_signal(barrier, inc=1, device_id=device, device_id_type=MESH)
    pl.semaphore_wait(barrier, len(devices))


def remote(source, target, send_sem, recv_sem, device):
    return pltpu.make_async_remote_copy(
        src_ref=source,
        dst_ref=target,
        send_sem=send_sem,
        recv_sem=recv_sem,
        device_id=device,
        device_id_type=MESH,
    )


def column_peers(E, C, G):
    e, c, d = position()
    me = c * G + d
    peers = []
    for offset in range(1, C * G):
        index = lax.rem(me + offset, C * G)
        peers.append((offset, index, (e, index // G, lax.rem(index, G))))
    return me, peers


def plane_peers(E):
    e, c, d = position()
    return [(i, lax.rem(e + i, E), (lax.rem(e + i, E), c, d)) for i in range(1, E)]


def level_peers(C):
    e, c, d = position()
    return [(i, lax.rem(c + i, C), (e, lax.rem(c + i, C), d)) for i in range(1, C)]


def start_kernel(E, C, G, tokens, weights, column, gathered, ws, wr, bs, br, hs, hr, ts, tr, ls):
    e, c, d = position()
    me, peers = column_peers(E, C, G)
    planes = plane_peers(E)
    batches = tokens.shape[0]
    rows = weights.shape[1]
    per_plane = C * G * rows
    meet([device for _, _, device in peers] + [device for _, _, device in planes])
    mine = gathered.at[pl.ds(pl.multiple_of(e * per_plane + me * rows, rows), rows)]
    weight_copies = []
    for offset, index, device in peers:
        copy = remote(weights.at[index], mine, ws.at[offset], wr.at[offset], device)
        copy.start()
        weight_copies.append(copy)
    local = [pltpu.make_async_copy(weights.at[me], mine, ls.at[batches])]
    for b in range(batches):
        local.append(pltpu.make_async_copy(tokens.at[b], column.at[b, me], ls.at[b]))
    for copy in local:
        copy.start()

    sibling = (e, c, 1 - d)

    def to_sibling(source, b, index, level):
        return remote(source, column.at[b, index], ts.at[b, level], tr.at[b, level], sibling)

    def step(hop, source, b, index, up):
        to = (e, c + 1, d) if up else (e, c - 1, d)
        way = 0 if up else 1
        return remote(source, column.at[b, index], hs.at[way, b, hop], hr.at[way, b, hop], to)

    for b in range(batches):

        @pl.when(c < C - 1)
        def _():
            step(0, tokens.at[b], b, me, True).start()

        @pl.when(c > 0)
        def _():
            step(0, tokens.at[b], b, me, False).start()

        if G > 1:
            to_sibling(tokens.at[b], b, me, 0).start()
    for copy in weight_copies:
        copy.wait_recv()
    local[0].wait()
    block = gathered.at[pl.ds(pl.multiple_of(e * per_plane, per_plane), per_plane)]
    block_copies = []
    for i, _, device in planes:
        copy = remote(block, block, bs.at[i], br.at[i], device)
        copy.start()
        block_copies.append(copy)
    for hop in range(1, C):
        for b in range(batches):
            for up in (True, False):
                origin = c - hop if up else c + hop
                index = origin * G + d
                level = hop if up else C - 1 + hop
                here = (c >= hop) if up else (c + hop < C)
                onward = (c < C - 1) if up else (c > 0)

                @pl.when(here)
                def _():
                    landed = column.at[b, index]
                    step(hop - 1, landed, b, index, up).wait_recv()
                    if hop < C - 1:

                        @pl.when(onward)
                        def _():
                            step(hop, landed, b, index, up).start()

                    if G > 1:
                        to_sibling(landed, b, index, level).start()

    for b in range(batches):
        if G > 1:
            to_sibling(tokens.at[b], b, me, 0).wait()
        for hop in range(C - 1):
            for up in (True, False):
                level = hop + 1 if up else C + hop
                origin = c - hop if up else c + hop
                sends = jnp.logical_and(origin >= 0, c < C - 1) if up else jnp.logical_and(origin < C, c > 0)
                arrives = (c >= hop + 1) if up else (c + hop + 1 < C)

                @pl.when(sends)
                def _():
                    step(hop, tokens.at[b], b, me, up).wait_send()

                if G > 1:

                    @pl.when(arrives)
                    def _():
                        to_sibling(tokens.at[b], b, me, level).wait()

    for copy in weight_copies:
        copy.wait_send()
    for copy in block_copies:
        copy.wait()
    for copy in local[1:]:
        copy.wait()


def start(E, C, G, tokens, weights):
    batches, run, width = tokens.shape
    rows, columns = weights.shape[1:]
    return call(
        functools.partial(start_kernel, E, C, G),
        (tokens, weights),
        (
            jax.ShapeDtypeStruct((batches, C * G, run, width), tokens.dtype),
            jax.ShapeDtypeStruct((E * C * G * rows, columns), weights.dtype),
        ),
        [ANY, ANY],
        (ANY, ANY),
        [
            DMA((C * G,)),
            DMA((C * G,)),
            DMA((E,)),
            DMA((E,)),
            DMA((2, batches, C)),
            DMA((2, batches, C)),
            DMA((batches, 2 * C)),
            DMA((batches, 2 * C)),
            DMA((batches + 1,)),
        ],
        1,
        "start",
    )


def share_kernel(E, C, G, part, parts, ss, rs):
    me, peers = column_peers(E, C, G)
    meet([device for _, _, device in peers])
    copies = []
    for offset, _, device in peers:
        copy = remote(part, parts.at[me], ss.at[offset], rs.at[offset], device)
        copy.start()
        copies.append(copy)
    parts[me] = part[...]
    for copy in copies:
        copy.wait()


def column_sum(E, C, G, part, collective, name):
    parts = call(
        functools.partial(share_kernel, E, C, G),
        (part,),
        jax.ShapeDtypeStruct((C * G,) + part.shape, part.dtype),
        [VMEM],
        VMEM,
        [DMA((C * G,)), DMA((C * G,))],
        collective,
        name,
    )
    return jnp.sum(parts, axis=0)


def to_tokens_kernel(E, C, G, heads, rows, ss, rs, ls):
    me, peers = column_peers(E, C, G)
    batches = rows.shape[0]
    size = heads.shape[3]
    meet([device for _, _, device in peers])
    mine = pl.ds(pl.multiple_of(me * size, size), size)
    copies = []
    for b in range(batches):
        for offset, index, device in peers:
            copies.append(
                remote(
                    heads.at[b, index], rows.at[b, :, mine], ss.at[b, offset], rs.at[b, offset], device
                )
            )
        copies.append(pltpu.make_async_copy(heads.at[b, me], rows.at[b, :, mine], ls.at[b]))
    for copy in copies:
        copy.start()
    for copy in copies:
        copy.wait()


def to_tokens(E, C, G, heads, collective, name):
    batches, count, run, size = heads.shape
    return call(
        functools.partial(to_tokens_kernel, E, C, G),
        (heads,),
        jax.ShapeDtypeStruct((batches, run, count * size), heads.dtype),
        [ANY],
        ANY,
        [DMA((batches, C * G)), DMA((batches, C * G)), DMA((batches,))],
        collective,
        name,
    )


def to_heads_kernel(E, C, G, rows, heads, ss, rs, ls):
    me, peers = column_peers(E, C, G)
    batches = rows.shape[0]
    size = heads.shape[3]
    meet([device for _, _, device in peers])

    def part(b, index):
        return rows.at[b, :, pl.ds(pl.multiple_of(index * size, size), size)]

    copies = []
    for b in range(batches):
        for offset, index, device in peers:
            copies.append(
                remote(part(b, index), heads.at[b, me], ss.at[b, offset], rs.at[b, offset], device)
            )
        copies.append(pltpu.make_async_copy(part(b, me), heads.at[b, me], ls.at[b]))
    for copy in copies:
        copy.start()
    for copy in copies:
        copy.wait()


def to_heads(E, C, G, rows, collective, name):
    batches, run, width = rows.shape
    count = C * G
    return call(
        functools.partial(to_heads_kernel, E, C, G),
        (rows,),
        jax.ShapeDtypeStruct((batches, count, run, width // count), rows.dtype),
        [ANY],
        ANY,
        [DMA((batches, C * G)), DMA((batches, C * G)), DMA((batches,))],
        collective,
        name,
    )


def choose(slots, count):
    cells = lax.broadcasted_iota(jnp.int32, (count, slots.shape[1]), 0).astype(f32)
    return jnp.concatenate(
        [(cells == slots[i : i + 1, :]).astype(bf16) for i in range(slots.shape[0])], axis=0
    )


def dispatch_kernel(
    E, C, A, first, second, slots, gates, out_first, out_second, slots_out, gates_out, landed, packed, ss, sr, gs, gr, zs, zr, xs, xr, ls
):
    e, c, d = position()
    batches, run, width = first.shape
    cap = out_first.shape[3]
    levels, planes = level_peers(C), plane_peers(E)
    everyone = [
        (i, j, lax.rem(e + i, E), lax.rem(c + j, C)) for i in range(E) for j in range(C) if i + j > 0
    ]
    meet([(x, y, d) for _, _, x, y in everyone])
    small = []
    for i, level, device in levels:
        small.append(remote(slots.at[level], slots_out.at[c], ss.at[i], sr.at[i], device))
    for i, j, x, y in everyone:
        small.append(
            remote(gates.at[x, y], gates_out.at[e, c], gs.at[i, j], gr.at[i, j], (x, y, d))
        )
    for copy in small:
        copy.start()
    rows = (first, second)[:A]
    outs = (out_first, out_second)[:A]

    def down(a, b, i, device):
        return remote(rows[a].at[b], landed.at[a, i, b], zs.at[a, i, b], zr.at[a, i, b], device)

    for a in range(A):
        for b in range(batches):
            for i, _, device in levels:
                down(a, b, i, device).start()
    slots_out[c] = slots[c]
    gates_out[e, c] = gates[e, c]

    def across(a, b, i, k, plane, level, device):
        return remote(
            packed.at[a, i, b, plane],
            outs[a].at[e, level, b],
            xs.at[a, i, b, k],
            xr.at[a, i, b, k],
            device,
        )

    def stay(a, b, i, level):
        return pltpu.make_async_copy(packed.at[a, i, b, e], outs[a].at[e, level, b], ls.at[a, i, b])

    def compact(a, b, i, source):
        level = lax.rem(c + C - i, C)
        picks = choose(slots_out[level, b], cap)
        for piece in range(0, width, 512):
            part = jnp.dot(
                picks, source[:, piece : piece + 512], preferred_element_type=f32
            ).astype(bf16)
            packed[a, i, b, :, :, piece : piece + 512] = part.reshape(E, cap, 512)
        for k, plane, device in planes:
            across(a, b, i, k, plane, level, device).start()
        stay(a, b, i, level).start()

    for a in range(A):

        def own(b, carry, a=a):
            compact(a, b, 0, rows[a].at[b])
            return carry

        lax.fori_loop(0, batches, own, 0)
    for copy in small:
        copy.wait_recv()
    for a in range(A):

        def arrived(n, carry, a=a):
            b, i = n // (C - 1), lax.rem(n, C - 1) + 1
            down(a, b, i, (e, c, d)).wait_recv()
            compact(a, b, i, landed.at[a, i, b])
            return carry

        lax.fori_loop(0, batches * (C - 1), arrived, 0)
    for copy in small:
        copy.wait_send()
    for a in range(A):

        def finish(n, carry, a=a):
            b, i = n // C, lax.rem(n, C)
            level = lax.rem(c + C - i, C)
            for k, plane, device in planes:
                across(a, b, i, k, plane, level, device).wait()
            stay(a, b, i, level).wait()

            @pl.when(i > 0)
            def _():
                down(a, b, i, (e, c, d)).wait_send()

            return carry

        lax.fori_loop(0, batches * C, finish, 0)


def dispatch(E, C, first, second, slots, gates, cap, collective, name):
    batches, run, width = first.shape
    A = 2
    rows = jax.ShapeDtypeStruct((E, C, batches, cap, width), bf16)
    return call(
        functools.partial(dispatch_kernel, E, C, A),
        (first, second, slots, gates),
        (
            rows,
            rows,
            jax.ShapeDtypeStruct(slots.shape, f32),
            jax.ShapeDtypeStruct(gates.shape, f32),
        ),
        [VMEM] * 4,
        (ANY, ANY, VMEM, VMEM),
        [
            pltpu.VMEM((A, C, batches, run, width), bf16),
            pltpu.VMEM((A, C, batches, E, cap, width), bf16),
            DMA((C,)),
            DMA((C,)),
            DMA((E, C)),
            DMA((E, C)),
            DMA((A, C, batches)),
            DMA((A, C, batches)),
            DMA((A, C, batches, E)),
            DMA((A, C, batches, E)),
            DMA((A, C, batches)),
        ],
        collective,
        name,
        vmem=56,
    )


def combine_kernel(
    E, C, A, first, second, slots, scalars, out_first, out_second, scalars_out, packed, sums, gs, gr, xs, xr, ls, zs, zr, os
):
    e, c, d = position()
    cap, width = first.shape[3:]
    batches, run = out_first.shape[1:3]
    levels, planes = level_peers(C), plane_peers(E)
    everyone = [
        (i, j, lax.rem(e + i, E), lax.rem(c + j, C)) for i in range(E) for j in range(C) if i + j > 0
    ]
    meet([(x, y, d) for _, _, x, y in everyone])
    small = []
    for i, j, x, y in everyone:
        small.append(
            remote(scalars.at[x, y], scalars_out.at[e, c], gs.at[i, j], gr.at[i, j], (x, y, d))
        )
    for copy in small:
        copy.start()
    scalars_out[e, c] = scalars[e, c]
    rows = (first, second)[:A]
    outs = (out_first, out_second)[:A]

    def across(a, b, i, k, plane, device):
        level = lax.rem(c + i, C)
        return remote(
            rows[a].at[plane, level, b],
            packed.at[a, i, b, e],
            xs.at[a, i, b, k],
            xr.at[a, i, b, k],
            device,
        )

    def stay(a, b, i):
        level = lax.rem(c + i, C)
        return pltpu.make_async_copy(
            rows[a].at[e, level, b], packed.at[a, i, b, e], ls.at[a, i, b]
        )

    def up(a, b, i):
        level = lax.rem(c + i, C)
        return remote(
            sums.at[a, i, b], outs[a].at[c, b], zs.at[a, i, b], zr.at[a, i, b], (e, level, d)
        )

    def keep(a, b):
        return pltpu.make_async_copy(sums.at[a, 0, b], outs[a].at[c, b], os.at[a, b])

    def turn(n):
        return lax.rem(n, batches), lax.rem(n // batches + 1, C)

    for a in range(A):

        def send(n, carry, a=a):
            b, i = turn(n)
            for k, plane, device in planes:
                across(a, b, i, k, plane, device).start()
            stay(a, b, i).start()
            return carry

        lax.fori_loop(0, batches * C, send, 0)
    for a in range(A):

        def add(n, carry, a=a):
            b, i = turn(n)
            for k, plane, device in planes:
                across(a, b, i, k, plane, device).wait_recv()
            stay(a, b, i).wait()
            picks = choose(slots[lax.rem(c + i, C), b], cap)
            for piece in range(0, width, 512):
                part = packed[a, i, b, :, :, piece : piece + 512].reshape(E * cap, 512)
                sums[a, i, b, :, piece : piece + 512] = lax.dot_general(
                    picks, part, (((0,), (0,)), ((), ())), preferred_element_type=f32
                ).astype(bf16)

            @pl.when(i > 0)
            def _():
                up(a, b, i).start()

            @pl.when(i == 0)
            def _():
                keep(a, b).start()

            return carry

        lax.fori_loop(0, batches * C, add, 0)
    for copy in small:
        copy.wait()
    for a in range(A):

        def finish(n, carry, a=a):
            b, i = turn(n)
            for k, plane, device in planes:
                across(a, b, i, k, plane, device).wait_send()

            @pl.when(i > 0)
            def _():
                up(a, b, i).wait()

            @pl.when(i == 0)
            def _():
                keep(a, b).wait()

            return carry

        lax.fori_loop(0, batches * C, finish, 0)


def combine(E, C, first, second, slots, scalars, collective, name):
    batches, cap, width = first.shape[2:]
    run = slots.shape[3]
    A = 2
    rows = jax.ShapeDtypeStruct((C, batches, run, width), bf16)
    return call(
        functools.partial(combine_kernel, E, C, A),
        (first, second, slots, scalars),
        (rows, rows, jax.ShapeDtypeStruct(scalars.shape, f32)),
        [ANY, ANY, VMEM, VMEM],
        (ANY, ANY, VMEM),
        [
            pltpu.VMEM((A, C, batches, E, cap, width), bf16),
            pltpu.VMEM((A, C, batches, run, width), bf16),
            DMA((E, C)),
            DMA((E, C)),
            DMA((A, C, batches, E)),
            DMA((A, C, batches, E)),
            DMA((A, C, batches)),
            DMA((A, C, batches)),
            DMA((A, C, batches)),
            DMA((A, batches)),
        ],
        collective,
        name,
        vmem=56,
    )


def scatter_kernel(E, C, G, rows, out, other, sums, cs, cr, zs, zr, ls):
    e, c, d = position()
    batches = rows.shape[0]
    run, width = rows.shape[3:]
    levels = level_peers(C)
    sibling = (e, c, 1 - d)
    meet([device for _, _, device in levels] + ([sibling] if G > 1 else []))

    def swap(b, level):
        return remote(
            rows.at[b, level, 1 - d], other.at[b, level], cs.at[b, level], cr.at[b, level], sibling
        )

    def send(b, i, level):
        return remote(
            sums.at[b, level], out.at[c, b], zs.at[b, i], zr.at[b, i], (e, level, d)
        )

    def keep(b):
        return pltpu.make_async_copy(sums.at[b, c], out.at[c, b], ls.at[b])

    order = [(i, lax.rem(c + i, C)) for i in range(1, C)] + [(0, c)]
    if G > 1:
        for i, level in order:
            for b in range(batches):
                swap(b, level).start()
    for i, level in order:
        for b in range(batches):
            if G > 1:
                swap(b, level).wait_recv()
                sums[b, level] = (
                    rows[b, level, d].astype(f32) + other[b, level].astype(f32)
                ).astype(bf16)
            else:
                sums[b, level] = rows[b, level, d]
            if i > 0:
                send(b, i, level).start()
            else:
                keep(b).start()
    for i, level in order:
        for b in range(batches):
            if G > 1:
                swap(b, level).wait_send()
            if i > 0:
                send(b, i, level).wait()
            else:
                keep(b).wait()


def column_scatter(E, C, G, rows, collective, name):
    batches, _, _, run, width = rows.shape
    return call(
        functools.partial(scatter_kernel, E, C, G),
        (rows,),
        jax.ShapeDtypeStruct((C, batches, run, width), bf16),
        [VMEM],
        ANY,
        [
            pltpu.VMEM((batches, C, run, width), bf16),
            pltpu.VMEM((batches, C, run, width), bf16),
            DMA((batches, C)),
            DMA((batches, C)),
            DMA((batches, C)),
            DMA((batches, C)),
            DMA((batches,)),
        ],
        collective,
        name,
        vmem=48,
    )


def weights_kernel(
    E, C, G, qkv, proj, out_qkv, out_proj, plane_qkv, sum_qkv, other, pair, plane_proj, sum_proj, as_, ar, bs, br, cs, cr, ds, dr, es, er, ls
):
    e, c, d = position()
    me, peers = column_peers(E, C, G)
    planes, levels = plane_peers(E), level_peers(C)
    sibling = (e, c, 1 - d)
    meet([device for _, _, device in peers] + [device for _, _, device in planes])
    swaps = []
    if G > 1:
        for level in range(C):
            swaps.append(
                remote(proj.at[level, 1 - d], other.at[level], cs.at[level], cr.at[level], sibling)
            )
    for copy in swaps:
        copy.start()
    first = []
    for k, plane, device in planes:
        first.append(remote(qkv.at[plane], plane_qkv.at[k], as_.at[k], ar.at[k], device))
    for copy in first:
        copy.start()
    middle = []
    for level in range(C):
        if G > 1:
            swaps[level].wait_recv()
            pair[level] = (proj[level, d].astype(f32) + other[level].astype(f32)).astype(bf16)
        else:
            pair[level] = proj[level, d]
        for k, plane, device in planes:
            copy = remote(
                pair.at[level, plane], plane_proj.at[level, k], ds.at[level, k], dr.at[level, k], device
            )
            copy.start()
            middle.append(copy)
    for copy in first:
        copy.wait_recv()
    total = qkv[e].astype(f32)
    for k in range(1, E):
        total = total + plane_qkv[k].astype(f32)
    sum_qkv[...] = total.astype(bf16)
    second = []
    for offset, index, device in peers:
        copy = remote(sum_qkv.at[index], out_qkv.at[me], bs.at[offset], br.at[offset], device)
        copy.start()
        second.append(copy)
    out_qkv[me] = sum_qkv[me]
    for copy in middle:
        copy.wait_recv()
    for level in range(C):
        total = pair[level, e].astype(f32)
        for k in range(1, E):
            total = total + plane_proj[level, k].astype(f32)
        sum_proj[level] = total.astype(bf16)
    last = []
    for i, level, device in levels:
        copy = remote(sum_proj.at[level], out_proj.at[c], es.at[i], er.at[i], device)
        copy.start()
        last.append(copy)
    out_proj[c] = sum_proj[c]
    for copy in swaps + first + middle:
        copy.wait_send()
    for copy in second + last:
        copy.wait()


def weight_scatter(E, C, G, qkv, proj, collective, name):
    count, rows, columns = qkv.shape[1:]
    width = proj.shape[4]
    return call(
        functools.partial(weights_kernel, E, C, G),
        (qkv, proj),
        (
            jax.ShapeDtypeStruct((count, rows, columns), bf16),
            jax.ShapeDtypeStruct((C, rows, width), bf16),
        ),
        [VMEM, VMEM],
        (VMEM, VMEM),
        [
            pltpu.VMEM((E, count, rows, columns), bf16),
            pltpu.VMEM((count, rows, columns), bf16),
            pltpu.VMEM((C, E, rows, width), bf16),
            pltpu.VMEM((C, E, rows, width), bf16),
            pltpu.VMEM((C, E, rows, width), bf16),
            pltpu.VMEM((C, rows, width), bf16),
            DMA((E,)),
            DMA((E,)),
            DMA((count,)),
            DMA((count,)),
            DMA((C,)),
            DMA((C,)),
            DMA((C, E)),
            DMA((C, E)),
            DMA((C,)),
            DMA((C,)),
            DMA((1,)),
        ],
        collective,
        name,
        vmem=56,
    )


def contract(left, right, axes):
    return lax.dot_general(left, right, ((axes[:1], axes[1:]), ((), ())), preferred_element_type=f32)


def query_blocks(length):
    size = min(256, length)
    return [(i, size, min(length, i + 2 * size)) for i in range(0, length, size)]


def attend_kernel(scale, queries, keys, values, row_ids, key_ids, mixed, log_total):
    length = queries.shape[1]
    for first, size, seen in query_blocks(length):
        rows = pl.ds(first, size)
        scores = contract(queries[0, rows], keys[0, :seen], (1, 1)) * scale
        scores = jnp.where(key_ids[0, :, :seen] <= row_ids[0, rows], scores, MASKED)
        peak = jnp.max(scores, axis=1, keepdims=True)
        grown = jnp.exp(scores - peak)
        total = jnp.sum(grown, axis=1, keepdims=True)
        probs = (grown * (1.0 / total)).astype(bf16)
        mixed[0, rows] = jnp.dot(probs, values[0, :seen], preferred_element_type=f32).astype(bf16)
        log_total[0, 0, rows] = peak + jnp.log(total)


def attend_back_kernel(
    scale, queries, keys, values, grads, row_ids, key_ids, log_total, query_grad, key_grad, value_grad
):
    length = queries.shape[1]
    key_grad[...] = jnp.zeros_like(key_grad)
    value_grad[...] = jnp.zeros_like(value_grad)
    for first, size, seen in query_blocks(length):
        rows = pl.ds(first, size)
        query, grad = queries[0, rows], grads[0, rows]
        scores = contract(query, keys[0, :seen], (1, 1)) * scale
        scores = jnp.where(key_ids[0, :, :seen] <= row_ids[0, rows], scores, MASKED)
        probs = jnp.exp(scores - log_total[0, 0, rows])
        prod = contract(grad, values[0, :seen], (1, 1))
        delta = jnp.sum(probs * prod, axis=1, keepdims=True)
        score_grad = (probs * (prod - delta)).astype(bf16)
        query_grad[0, rows] = jnp.dot(score_grad, keys[0, :seen], preferred_element_type=f32) * scale
        key_grad[0, :seen] += contract(score_grad, query, (0, 0)) * scale
        value_grad[0, :seen] += contract(probs.astype(bf16), grad, (0, 0))


def attention_specs(length):
    head = pl.BlockSpec((1, length, HEAD), lambda b, h: (b, 0, h))
    row_ids = pl.BlockSpec((1, length, 1), lambda b, h: (b, 0, 0))
    key_ids = pl.BlockSpec((1, 1, length), lambda b, h: (b, 0, 0))
    log_total = pl.BlockSpec((1, 1, length, 1), lambda b, h: (b, h, 0, 0))
    return head, row_ids, key_ids, log_total


def attend(queries, keys, values, ids):
    batches, length, size = queries.shape
    heads = size // HEAD
    head, row_ids, key_ids, log_total = attention_specs(length)
    return pl.pallas_call(
        functools.partial(attend_kernel, HEAD**-0.5),
        grid=(batches, heads),
        out_shape=(
            jax.ShapeDtypeStruct(queries.shape, bf16),
            jax.ShapeDtypeStruct((batches, heads, length, 1), f32),
        ),
        in_specs=[head, head, head, row_ids, key_ids],
        out_specs=(head, log_total),
        compiler_params=pltpu.CompilerParams(vmem_limit_bytes=48 * MIB),
        name="attend",
    )(queries, keys, values, ids[:, :, None], ids[:, None, :])


def attend_back(queries, keys, values, grads, ids, totals):
    batches, length, size = queries.shape
    heads = size // HEAD
    head, row_ids, key_ids, log_total = attention_specs(length)
    grad = jax.ShapeDtypeStruct(queries.shape, f32)
    return pl.pallas_call(
        functools.partial(attend_back_kernel, HEAD**-0.5),
        grid=(batches, heads),
        out_shape=(grad, grad, grad),
        in_specs=[head, head, head, head, row_ids, key_ids, log_total],
        out_specs=(head, head, head),
        compiler_params=pltpu.CompilerParams(vmem_limit_bytes=48 * MIB),
        name="attend_back",
    )(queries, keys, values, grads, ids[:, :, None], ids[:, None, :], totals)


def rms_factor(values):
    return lax.rsqrt(jnp.mean(values * values, axis=-1, keepdims=True) + EPSILON)


def norm_back(grad_hat, hatted, factor):
    return factor * (grad_hat - hatted * jnp.mean(grad_hat * hatted, axis=-1, keepdims=True))


def slot_table(routes, experts):
    batches, run, top = routes.shape
    hits = jnp.swapaxes(routes, 1, 2)[:, :, :, None] == jnp.arange(experts, dtype=jnp.int32)
    ones = hits.astype(bf16)
    tokens, ranks = jnp.arange(run), jnp.arange(top)
    before = (tokens[None, :] < tokens[:, None]).astype(bf16)
    above = (ranks[None, :] < ranks[:, None]).astype(bf16)
    within = jnp.einsum("ts,bksx->bktx", before, ones, preferred_element_type=f32)
    totals = jnp.sum(hits.astype(f32), axis=2)
    earlier = jnp.einsum(
        "kj,bjx->bkx", above, totals.astype(bf16), preferred_element_type=f32
    )
    places = jnp.sum(jnp.where(hits, within + earlier[:, :, None, :], 0.0), axis=1)
    places = jnp.where(jnp.any(hits, axis=1), places, UNUSED_SLOT)
    return jnp.swapaxes(places, 1, 2)


def body(
    tokens,
    block_ids,
    routes,
    norm_gains,
    w_query,
    w_key,
    w_value,
    w_output,
    router,
    expert_gate,
    expert_up,
    expert_down,
    cotangent,
):
    E, C, G = lax.axis_size("expert"), lax.axis_size("context"), lax.axis_size("dp")
    batches, run, width = tokens.shape
    top = routes.shape[2]
    experts = E * C * expert_gate.shape[0]
    capacity = max(2, run * top // experts)
    count = C * G
    size = width // count
    length = count * run
    every = batches * length
    own = batches * run
    me = lax.axis_index("context") * G + lax.axis_index("dp")

    rows = w_query.shape[0]
    small_width = -(-(norm_gains.shape[1] + experts) // 128) * 128
    small = jnp.concatenate([norm_gains, router], axis=1)
    small = jnp.pad(small, ((0, 0), (0, small_width - small.shape[1])))
    pieces = [w.reshape(rows, count, size) for w in (w_query, w_key, w_value)]
    pieces.append(jnp.broadcast_to(small[:, None, :], (rows, count, small_width)))
    weights = jnp.swapaxes(jnp.concatenate(pieces, axis=2), 0, 1)
    full_output = lax.all_gather(w_output, ALL_AXES, axis=0, tiled=True)
    ids = lax.all_gather(block_ids, ("context", "dp"), axis=1, tiled=True)
    column, gathered = start(E, C, G, tokens, weights)
    w_qkv = gathered[:, : 3 * size]
    gains = gathered[:, 3 * size : 3 * size + 4].astype(f32)
    full_router = gathered[:, 3 * size + 4 : 3 * size + 4 + experts]
    head_gains = lax.dynamic_slice(gains, (me * size, 0), (size, 4))

    column = column.reshape(every, width).astype(f32)
    normed = (column * rms_factor(column) * gains[:, 0]).astype(bf16)
    qkv = jnp.dot(normed, w_qkv, preferred_element_type=f32)
    query_raw, key_raw = qkv[:, :size], qkv[:, size : 2 * size]
    value_low = qkv[:, 2 * size :].astype(bf16)
    squares = jnp.stack([jnp.sum(query_raw * query_raw, axis=1), jnp.sum(key_raw * key_raw, axis=1)])
    factors = lax.rsqrt(column_sum(E, C, G, squares, 2, "squares") / width + EPSILON)
    query_factor, key_factor = factors[0][:, None], factors[1][:, None]
    query_hat, key_hat = query_raw * query_factor, key_raw * key_factor
    by_sequence = (batches, length, size)
    query_low = (query_hat * head_gains[:, 1]).astype(bf16).reshape(by_sequence)
    key_low = (key_hat * head_gains[:, 2]).astype(bf16).reshape(by_sequence)
    value_low = value_low.reshape(by_sequence)
    mixed_heads, log_total = attend(query_low, key_low, value_low, ids)
    mixed_low = to_tokens(
        E, C, G, mixed_heads.reshape(batches, count, run, size), 3, "mixed_rows"
    ).reshape(own, width)

    inputs = tokens.reshape(own, width).astype(f32)
    resid = inputs + jnp.dot(mixed_low, full_output, preferred_element_type=f32)
    second_factor = rms_factor(resid)
    second_hat = resid * second_factor
    second_low = (second_hat * gains[:, 3]).astype(bf16)
    logits = jnp.dot(second_low, full_router, preferred_element_type=f32)
    router_probs = jax.nn.softmax(logits, axis=-1)
    places = slot_table(routes, experts).reshape(batches, E, C, run)
    by_level = jnp.transpose(places, (2, 0, 1, 3))
    by_expert = jnp.transpose(places, (1, 2, 0, 3))
    gate_table = jnp.transpose(router_probs.reshape(batches, run, E, C), (2, 3, 0, 1))
    table = jnp.concatenate([by_expert, gate_table], axis=2)

    expert_in, expert_up_in, slots, table = dispatch(
        E,
        C,
        second_low.reshape(batches, run, width),
        cotangent,
        by_level,
        table,
        capacity,
        4,
        "dispatch",
    )
    slot_count = E * C * batches * capacity
    x = expert_in.reshape(slot_count, width)
    upstream_rows = expert_up_in.reshape(slot_count, width)
    cells = jnp.arange(capacity, dtype=jnp.int32).astype(f32)
    holds = table[:, :, :batches, None, :] == cells[:, None]
    gate = jnp.sum(jnp.where(holds, table[:, :, batches:, None, :], 0.0), axis=-1)
    gate = gate.reshape(slot_count, 1)
    w_gate, w_up, w_down = expert_gate[0], expert_up[0], expert_down[0]
    gate_pre = jnp.dot(x, w_gate, preferred_element_type=f32)
    up_pre = jnp.dot(x, w_up, preferred_element_type=f32)
    sigmoid_gate = jax.nn.sigmoid(gate_pre)
    silu_gate = gate_pre * sigmoid_gate
    act = (silu_gate * up_pre).astype(bf16)
    expert_out = jnp.dot(act, w_down, preferred_element_type=f32).astype(bf16).astype(f32)
    upstream_wide = upstream_rows.astype(f32)
    gate_grad = jnp.sum(expert_out * upstream_wide, axis=1)
    out_rows = (gate * expert_out).astype(bf16)
    pair_grad = (gate * upstream_wide).astype(bf16)
    act_grad = contract(pair_grad, w_down, (1, 1))
    gate_pre_grad = (
        act_grad * up_pre * sigmoid_gate * (1.0 + gate_pre * (1.0 - sigmoid_gate))
    ).astype(bf16)
    up_pre_grad = (act_grad * silu_gate).astype(bf16)
    input_back = contract(gate_pre_grad, w_gate, (1, 1)) + contract(up_pre_grad, w_up, (1, 1))
    gate_grad = gate_grad.reshape(E, C, batches, capacity, 1)
    gate_grad = jnp.sum(jnp.where(holds, gate_grad, 0.0), axis=3)
    by_slot = (E, C, batches, capacity, width)
    mixture, second_grad, gate_grad = combine(
        E,
        C,
        out_rows.reshape(by_slot),
        input_back.astype(bf16).reshape(by_slot),
        slots,
        gate_grad,
        5,
        "combine",
    )
    share = functools.partial(lax.psum_scatter, axis_name="dp", tiled=True)
    grad_gate = share(contract(x, gate_pre_grad, (0, 0)).astype(bf16), scatter_dimension=1)
    grad_up = share(contract(x, up_pre_grad, (0, 0)).astype(bf16), scatter_dimension=1)
    grad_down = share(contract(act, pair_grad, (0, 0)).astype(bf16), scatter_dimension=0)

    upstream = cotangent.reshape(own, width).astype(f32)
    mixture = jnp.sum(mixture.astype(f32), axis=0).reshape(own, width)
    activations = (resid + mixture).astype(bf16).reshape(tokens.shape)
    prob_grad = jnp.transpose(gate_grad, (2, 3, 0, 1)).reshape(own, experts)
    logit_grad = router_probs * (
        prob_grad - jnp.sum(router_probs * prob_grad, axis=-1, keepdims=True)
    )
    logit_grad = logit_grad.astype(bf16)
    second_grad = jnp.sum(second_grad.astype(f32), axis=0).reshape(own, width)
    second_grad = second_grad + contract(logit_grad, full_router, (1, 1))
    gain_second = jnp.sum(second_grad * second_hat, axis=0)
    resid_grad = upstream + norm_back(second_grad * gains[:, 3], second_hat, second_factor)
    attn_grad = resid_grad.astype(bf16)
    mixed_grad = contract(attn_grad, full_output, (1, 1)).astype(bf16)

    mixed_grad = to_heads(E, C, G, mixed_grad.reshape(batches, run, width), 6, "mixed_grad_heads")
    query_grad, key_grad, value_grad = (
        grad.reshape(every, size)
        for grad in attend_back(
            query_low, key_low, value_low, mixed_grad.reshape(by_sequence), ids, log_total
        )
    )
    query_back, key_back = query_grad * head_gains[:, 1], key_grad * head_gains[:, 2]
    means = jnp.stack([jnp.sum(query_back * query_hat, axis=1), jnp.sum(key_back * key_hat, axis=1)])
    means = column_sum(E, C, G, means, 7, "norm_means") / width
    raw_grads = jnp.concatenate(
        [
            (query_factor * (query_back - query_hat * means[0][:, None])).astype(bf16),
            (key_factor * (key_back - key_hat * means[1][:, None])).astype(bf16),
            value_grad.astype(bf16),
        ],
        axis=1,
    )
    first_part = contract(raw_grads, w_qkv, (1, 1)).astype(bf16)
    first_grad = column_scatter(
        E, C, G, first_part.reshape(batches, C, G, run, width), 8, "first_grad"
    )
    first_grad = jnp.sum(first_grad.astype(f32), axis=0).reshape(own, width)
    first_factor = rms_factor(inputs)
    first_hat = inputs * first_factor
    gain_first = jnp.sum(first_grad * first_hat, axis=0)
    input_grad = resid_grad + norm_back(first_grad * gains[:, 0], first_hat, first_factor)

    grad_qkv = contract(normed, raw_grads, (0, 0)).astype(bf16)
    grad_proj = contract(mixed_low, attn_grad, (0, 0)).astype(bf16)
    grad_proj = jnp.transpose(grad_proj.reshape(E, C, G, rows, width), (1, 2, 0, 3, 4))
    grad_qkv, grad_proj = weight_scatter(
        E, C, G, grad_qkv.reshape(E, count, rows, 3 * size), grad_proj, 9, "weight_grads"
    )
    grad_qkv = jnp.swapaxes(grad_qkv.astype(f32), 0, 1)
    grad_query, grad_key, grad_value = (
        grad_qkv[:, :, i * size : (i + 1) * size].reshape(rows, width) for i in range(3)
    )
    grad_proj = jnp.sum(grad_proj.astype(f32), axis=0)
    gain_heads = jnp.stack(
        [jnp.sum(query_grad * query_hat, axis=0), jnp.sum(key_grad * key_hat, axis=0)], axis=1
    )
    gain_heads = lax.dynamic_update_slice(
        jnp.zeros((width, 2), f32), gain_heads, (me * size, 0)
    )
    sums = jnp.concatenate(
        [
            gain_first[:, None],
            gain_heads,
            gain_second[:, None],
            contract(second_low, logit_grad, (0, 0)),
        ],
        axis=1,
    )
    sums = lax.psum_scatter(sums, ALL_AXES, scatter_dimension=0, tiled=True)
    return (
        activations,
        input_grad.reshape(tokens.shape),
        sums[:, :4],
        grad_query,
        grad_key,
        grad_value,
        grad_proj,
        sums[:, 4:],
        grad_gate.astype(f32)[None],
        grad_up.astype(f32)[None],
        grad_down.astype(f32)[None],
    )


def solution(mesh):
    by_token = ("context", "dp")
    by_expert = P(("expert", "context"), None, None)
    by_row = P(ALL_AXES, None)
    rows = P("expert", by_token, None)
    return jax.shard_map(
        body,
        mesh=mesh,
        in_specs=(
            rows,
            P("expert", by_token),
            rows,
            by_row,
            by_row,
            by_row,
            by_row,
            by_row,
            by_row,
            by_expert,
            by_expert,
            by_expert,
            rows,
        ),
        out_specs=(
            rows,
            rows,
            by_row,
            by_row,
            by_row,
            by_row,
            by_row,
            by_row,
            P(("expert", "context"), None, "dp"),
            P(("expert", "context"), None, "dp"),
            P(("expert", "context"), "dp", None),
        ),
        check_vma=False,
    )
```

```python
import functools

import jax
import jax.numpy as jnp
from jax import lax
from jax.experimental import pallas as pl
from jax.experimental.pallas import tpu as pltpu
from jax.sharding import PartitionSpec as P

HEAD = 128
EPSILON = 1e-05
MASKED = -1e30
UNUSED_SLOT = 4096.0
ALL_AXES = ("expert", "context", "dp")
MESH = pl.DeviceIdType.MESH
ANY = pl.BlockSpec(memory_space=pl.ANY)
VMEM = pl.BlockSpec(memory_space=pltpu.VMEM)
DMA = pltpu.SemaphoreType.DMA
MIB = 1 << 20
f32 = jnp.float32
bf16 = jnp.bfloat16


def call(kernel, operands, out_shapes, in_specs, out_specs, scratch, collective, name, vmem=32):
    return pl.pallas_call(
        kernel,
        out_shape=out_shapes,
        in_specs=in_specs,
        out_specs=out_specs,
        scratch_shapes=scratch,
        compiler_params=pltpu.CompilerParams(
            collective_id=collective, has_side_effects=True, vmem_limit_bytes=vmem * MIB
        ),
        name=name,
    )(*operands)


def position():
    return lax.axis_index("expert"), lax.axis_index("context"), lax.axis_index("dp")


def meet(devices):
    barrier = pltpu.get_barrier_semaphore()
    for device in devices:
        pl.semaphore_signal(barrier, inc=1, device_id=device, device_id_type=MESH)
    pl.semaphore_wait(barrier, len(devices))


def remote(source, target, send_sem, recv_sem, device):
    return pltpu.make_async_remote_copy(
        src_ref=source,
        dst_ref=target,
        send_sem=send_sem,
        recv_sem=recv_sem,
        device_id=device,
        device_id_type=MESH,
    )


def column_peers(E, C, G):
    e, c, d = position()
    me = c * G + d
    peers = []
    for offset in range(1, C * G):
        index = lax.rem(me + offset, C * G)
        peers.append((offset, index, (e, index // G, lax.rem(index, G))))
    return me, peers


def plane_peers(E):
    e, c, d = position()
    return [(i, lax.rem(e + i, E), (lax.rem(e + i, E), c, d)) for i in range(1, E)]


def level_peers(C):
    e, c, d = position()
    return [(i, lax.rem(c + i, C), (e, lax.rem(c + i, C), d)) for i in range(1, C)]


def start_kernel(
    E, C, G, tokens, weights, ids, slots, column, gathered, ids_out, slots_out, ws, wr, bs, br, hs, hr, ts, tr, ls, ms, mr, ps, pr
):
    e, c, d = position()
    me, peers = column_peers(E, C, G)
    planes = plane_peers(E)
    batches = tokens.shape[0]
    rows = weights.shape[1]
    per_plane = C * G * rows
    meet([device for _, _, device in peers] + [device for _, _, device in planes])
    mine = gathered.at[pl.ds(pl.multiple_of(e * per_plane + me * rows, rows), rows)]
    weight_copies = []
    for offset, index, device in peers:
        copy = remote(weights.at[index], mine, ws.at[offset], wr.at[offset], device)
        copy.start()
        weight_copies.append(copy)
    small = []
    for offset, _, device in peers:
        small.append(remote(ids, ids_out.at[me], ms.at[offset], mr.at[offset], device))
    for i, level, device in level_peers(C):
        small.append(remote(slots.at[level], slots_out.at[i], ps.at[i], pr.at[i], device))
    for copy in small:
        copy.start()
    ids_out[me] = ids[...]
    slots_out[0] = slots[c]
    local = [pltpu.make_async_copy(weights.at[me], mine, ls.at[batches])]
    for b in range(batches):
        local.append(pltpu.make_async_copy(tokens.at[b], column.at[b, me], ls.at[b]))
    for copy in local:
        copy.start()

    sibling = (e, c, 1 - d)

    def to_sibling(source, b, index, level):
        return remote(source, column.at[b, index], ts.at[b, level], tr.at[b, level], sibling)

    def step(hop, source, b, index, up):
        to = (e, c + 1, d) if up else (e, c - 1, d)
        way = 0 if up else 1
        return remote(source, column.at[b, index], hs.at[way, b, hop], hr.at[way, b, hop], to)

    for b in range(batches):

        @pl.when(c < C - 1)
        def _():
            step(0, tokens.at[b], b, me, True).start()

        @pl.when(c > 0)
        def _():
            step(0, tokens.at[b], b, me, False).start()

        if G > 1:
            to_sibling(tokens.at[b], b, me, 0).start()
    for copy in weight_copies:
        copy.wait_recv()
    local[0].wait()
    block = gathered.at[pl.ds(pl.multiple_of(e * per_plane, per_plane), per_plane)]
    block_copies = []
    for i, _, device in planes:
        copy = remote(block, block, bs.at[i], br.at[i], device)
        copy.start()
        block_copies.append(copy)
    for hop in range(1, C):
        for b in range(batches):
            for up in (True, False):
                origin = c - hop if up else c + hop
                index = origin * G + d
                level = hop if up else C - 1 + hop
                here = (c >= hop) if up else (c + hop < C)
                onward = (c < C - 1) if up else (c > 0)

                @pl.when(here)
                def _():
                    landed = column.at[b, index]
                    step(hop - 1, landed, b, index, up).wait_recv()
                    if hop < C - 1:

                        @pl.when(onward)
                        def _():
                            step(hop, landed, b, index, up).start()

                    if G > 1:
                        to_sibling(landed, b, index, level).start()

    for b in range(batches):
        if G > 1:
            to_sibling(tokens.at[b], b, me, 0).wait()
        for hop in range(C - 1):
            for up in (True, False):
                level = hop + 1 if up else C + hop
                origin = c - hop if up else c + hop
                sends = jnp.logical_and(origin >= 0, c < C - 1) if up else jnp.logical_and(origin < C, c > 0)
                arrives = (c >= hop + 1) if up else (c + hop + 1 < C)

                @pl.when(sends)
                def _():
                    step(hop, tokens.at[b], b, me, up).wait_send()

                if G > 1:

                    @pl.when(arrives)
                    def _():
                        to_sibling(tokens.at[b], b, me, level).wait()

    for copy in weight_copies:
        copy.wait_send()
    for copy in block_copies + small:
        copy.wait()
    for copy in local[1:]:
        copy.wait()


def start(E, C, G, tokens, weights, ids, slots):
    batches, run, width = tokens.shape
    rows, columns = weights.shape[1:]
    return call(
        functools.partial(start_kernel, E, C, G),
        (tokens, weights, ids, slots),
        (
            jax.ShapeDtypeStruct((batches, C * G, run, width), tokens.dtype),
            jax.ShapeDtypeStruct((E * C * G * rows, columns), weights.dtype),
            jax.ShapeDtypeStruct((C * G,) + ids.shape, ids.dtype),
            jax.ShapeDtypeStruct(slots.shape, slots.dtype),
        ),
        [ANY, ANY, VMEM, VMEM],
        (ANY, ANY, VMEM, VMEM),
        [
            DMA((C * G,)),
            DMA((C * G,)),
            DMA((E,)),
            DMA((E,)),
            DMA((2, batches, C)),
            DMA((2, batches, C)),
            DMA((batches, 2 * C)),
            DMA((batches, 2 * C)),
            DMA((batches + 1,)),
            DMA((C * G,)),
            DMA((C * G,)),
            DMA((C,)),
            DMA((C,)),
        ],
        1,
        "start",
    )


def share_kernel(E, C, G, part, parts, ss, rs):
    me, peers = column_peers(E, C, G)
    meet([device for _, _, device in peers])
    copies = []
    for offset, _, device in peers:
        copy = remote(part, parts.at[me], ss.at[offset], rs.at[offset], device)
        copy.start()
        copies.append(copy)
    parts[me] = part[...]
    for copy in copies:
        copy.wait()


def column_sum(E, C, G, part, collective, name):
    parts = call(
        functools.partial(share_kernel, E, C, G),
        (part,),
        jax.ShapeDtypeStruct((C * G,) + part.shape, part.dtype),
        [VMEM],
        VMEM,
        [DMA((C * G,)), DMA((C * G,))],
        collective,
        name,
    )
    return jnp.sum(parts, axis=0)


def to_tokens_kernel(E, C, G, heads, rows, ss, rs, ls):
    me, peers = column_peers(E, C, G)
    batches = rows.shape[0]
    size = heads.shape[3]
    meet([device for _, _, device in peers])
    mine = pl.ds(pl.multiple_of(me * size, size), size)
    copies = []
    for b in range(batches):
        for offset, index, device in peers:
            copies.append(
                remote(
                    heads.at[b, index], rows.at[b, :, mine], ss.at[b, offset], rs.at[b, offset], device
                )
            )
        copies.append(pltpu.make_async_copy(heads.at[b, me], rows.at[b, :, mine], ls.at[b]))
    for copy in copies:
        copy.start()
    for copy in copies:
        copy.wait()


def to_tokens(E, C, G, heads, collective, name):
    batches, count, run, size = heads.shape
    return call(
        functools.partial(to_tokens_kernel, E, C, G),
        (heads,),
        jax.ShapeDtypeStruct((batches, run, count * size), heads.dtype),
        [ANY],
        ANY,
        [DMA((batches, C * G)), DMA((batches, C * G)), DMA((batches,))],
        collective,
        name,
    )


def to_heads_kernel(E, C, G, rows, heads, ss, rs, ls):
    me, peers = column_peers(E, C, G)
    batches = rows.shape[0]
    size = heads.shape[3]
    meet([device for _, _, device in peers])

    def part(b, index):
        return rows.at[b, :, pl.ds(pl.multiple_of(index * size, size), size)]

    copies = []
    for b in range(batches):
        for offset, index, device in peers:
            copies.append(
                remote(part(b, index), heads.at[b, me], ss.at[b, offset], rs.at[b, offset], device)
            )
        copies.append(pltpu.make_async_copy(part(b, me), heads.at[b, me], ls.at[b]))
    for copy in copies:
        copy.start()
    for copy in copies:
        copy.wait()


def to_heads(E, C, G, rows, collective, name):
    batches, run, width = rows.shape
    count = C * G
    return call(
        functools.partial(to_heads_kernel, E, C, G),
        (rows,),
        jax.ShapeDtypeStruct((batches, count, run, width // count), rows.dtype),
        [ANY],
        ANY,
        [DMA((batches, C * G)), DMA((batches, C * G)), DMA((batches,))],
        collective,
        name,
    )


def choose(slots, count):
    cells = lax.broadcasted_iota(jnp.int32, (count, slots.shape[1]), 0).astype(f32)
    return jnp.concatenate(
        [(cells == slots[i : i + 1, :]).astype(bf16) for i in range(slots.shape[0])], axis=0
    )


def experts_kernel(
    E,
    C,
    rows_x,
    rows_u,
    slots,
    gates,
    w_gate,
    w_up,
    w_down,
    out_y,
    out_b,
    x_out,
    u_out,
    pair_out,
    act_out,
    gate_back_out,
    up_back_out,
    scalars_out,
    table,
    scalars,
    landed,
    packed,
    returned,
    x,
    u,
    pair,
    act,
    gate_back,
    up_back,
    sent,
    gs,
    gr,
    ss,
    sr,
    os,
    zs,
    zr,
    xs,
    xr,
    ls,
    ys,
    yr,
    bs,
    us,
    ur,
    ks,
    loads,
    stores,
):
    e, c, d = position()
    batches, run, width = rows_x.shape
    cap = x_out.shape[3]
    units = w_gate.shape[1]
    chunks = batches * C
    total = E * cap
    slots_kept, kept = packed.shape[1], sent.shape[1]
    lead, lag = 1, 2
    everyone = [(k, i) for k in range(E) for i in range(C) if k + i > 0]
    ahead = [(k, i, (lax.rem(e + k, E), lax.rem(c + i, C), d)) for k, i in everyone]
    behind = [(k, i, (lax.rem(e + E - k, E), lax.rem(c + C - i, C), d)) for k, i in everyone]
    meet([device for _, _, device in ahead])
    sources, arrivals, outs = (rows_x, rows_u), (x_out, u_out), (out_y, out_b)

    high = 2 * c // C

    def far_of(n):
        return lax.rem((n + batches - 1) // batches, C), lax.rem(n + batches - 1, batches)

    def chunk_of(n):
        m, b = far_of(n)
        return b, high * m + (1 - high) * lax.rem(C - m, C)

    def hop(a, b, i, way):
        there = i + 1 if way == 0 else lax.rem(i + C - 1, C)
        level = lax.rem(c + 1, C) if way == 0 else lax.rem(c + C - 1, C)
        return remote(
            landed.at[a, i, b],
            landed.at[a, there, b],
            zs.at[way, a, i, b],
            zr.at[a, there, b],
            (e, level, d),
        )

    def arrival(a, b, i):
        return remote(
            landed.at[a, i, b], landed.at[a, i, b], zs.at[0, a, i, b], zr.at[a, i, b], (e, c, 1 - d)
        )

    def onward(i, way):
        if way == 0:
            return jnp.logical_and(i <= c, c < C - 1)
        return jnp.logical_and(lax.rem(C - i, C) + c < C, c > 0)

    def own(a, b):
        return pltpu.make_async_copy(sources[a].at[b], landed.at[a, 0, b], os.at[a, b])

    def across(a, n, k):
        plane = lax.rem(e + k, E)
        b, i = chunk_of(n)
        return remote(
            packed.at[a, lax.rem(n, slots_kept), plane],
            arrivals[a].at[i, b, k],
            xs.at[a, i, b, k],
            xr.at[a, i, b, k],
            (plane, c, d),
        )

    def stay(a, n):
        b, i = chunk_of(n)
        return pltpu.make_async_copy(
            packed.at[a, lax.rem(n, slots_kept), e], arrivals[a].at[i, b, 0], ls.at[a, i, b]
        )

    def back(a, n, b, i, k):
        return remote(
            sent.at[a, lax.rem(n, kept), k],
            returned.at[a, i, b, e],
            ys.at[a, i, b, k],
            yr.at[a, i, b, k],
            (lax.rem(e + E - k, E), c, d),
        )

    def back_own(a, n, b, i):
        return pltpu.make_async_copy(
            sent.at[a, lax.rem(n, kept), 0], returned.at[a, i, b, e], bs.at[a, i, b]
        )

    def up(a, b, i):
        return remote(
            landed.at[a, i, b],
            outs[a].at[c, b],
            us.at[a, i, b],
            ur.at[a, i, b],
            (e, lax.rem(c + C - i, C), d),
        )

    def keep(a, b):
        return pltpu.make_async_copy(landed.at[a, 0, b], outs[a].at[c, b], ks.at[a, b])

    def load(a, b, i):
        target = (x, u)[a]
        return pltpu.make_async_copy(arrivals[a].at[i, b], target, loads.at[a])

    def store(j, b, i):
        source = (pair, act, gate_back, up_back)[j]
        target = (pair_out, act_out, gate_back_out, up_back_out)[j]
        return pltpu.make_async_copy(source, target.at[i, b], stores.at[j])

    for b in range(batches):
        for a in range(2):
            own(a, b).start()
    for b in range(batches):
        for a in range(2):
            own(a, b).wait()
            for way in range(2):

                @pl.when(onward(0, way))
                def _():
                    hop(a, b, 0, way).start()

    small = [
        remote(gates.at[device[0], device[1]], table.at[k, i], gs.at[k, i], gr.at[k, i], device)
        for k, i, device in ahead
    ]
    for copy in small:
        copy.start()
    table[0, 0] = gates[e, c]

    def relay(n):
        far, b = far_of(n)
        for a in range(2):
            for way in range(2):
                i = far if way == 0 else C - far

                @pl.when((far <= c) if way == 0 else (far + c < C))
                def _():
                    arrival(a, b, i).wait_recv()

                    @pl.when(onward(i, way))
                    def _():
                        hop(a, b, i, way).start()

    def compact(n):
        b, i = chunk_of(n)
        picks = choose(slots[i, b], cap)
        place = lax.rem(n, slots_kept)

        @pl.when(n >= slots_kept)
        def _():
            for a in range(2):
                for k in range(1, E):
                    across(a, n - slots_kept, k).wait_send()

        for a in range(2):
            for at in range(0, width, 512):
                part = jnp.dot(
                    picks, landed[a, i, b, :, at : at + 512], preferred_element_type=f32
                ).astype(bf16)
                packed[a, place, :, :, at : at + 512] = part.reshape(E, cap, 512)
            for k in range(1, E):
                across(a, n, k).start()
            stay(a, n).start()

    def expert(n):
        b, i = chunk_of(n)
        for a in range(2):
            for k in range(1, E):
                across(a, n, k).wait_recv()
            stay(a, n).wait()
            load(a, b, i).start()

        @pl.when(n > 0)
        def _():
            before = chunk_of(n - 1)
            for j in range(4):
                store(j, *before).wait()

        @pl.when(n >= kept)
        def _():
            before = chunk_of(n - kept)
            for a in range(2):
                for k in range(1, E):
                    back(a, n - kept, *before, k).wait_send()

        holds, gate = [], []
        cells = lax.broadcasted_iota(jnp.int32, (cap, run), 0).astype(f32)
        for k in range(E):
            hold = cells == table[k, i, b]
            holds.append(hold)
            gate.append(
                jnp.sum(jnp.where(hold, table[k, i, batches + b], 0.0), axis=1, keepdims=True)
            )
        gate = jnp.concatenate(gate, axis=0)
        for a in range(2):
            load(a, b, i).wait()
        for at in range(0, width, 512):
            part = u[:, :, at : at + 512].reshape(total, 512).astype(f32)
            pair[:, :, at : at + 512] = (gate * part).astype(bf16).reshape(E, cap, 512)
        store(0, b, i).start()
        inputs = x[...].reshape(total, width)
        grads = pair[...].reshape(total, width)
        for at in range(0, units, 256):
            gate_pre = jnp.dot(inputs, w_gate[:, at : at + 256], preferred_element_type=f32)
            up_pre = jnp.dot(inputs, w_up[:, at : at + 256], preferred_element_type=f32)
            act_grad = contract(grads, w_down[at : at + 256, :], (1, 1))
            sigmoid = jax.nn.sigmoid(gate_pre)
            silu = gate_pre * sigmoid
            act[:, at : at + 256] = (silu * up_pre).astype(bf16)
            gate_back[:, at : at + 256] = (
                act_grad * up_pre * sigmoid * (1.0 + gate_pre * (1.0 - sigmoid))
            ).astype(bf16)
            up_back[:, at : at + 256] = (act_grad * silu).astype(bf16)
        for j in range(1, 4):
            store(j, b, i).start()
        place = lax.rem(n, kept)
        gate_grad = jnp.zeros((total, 1), f32)
        for at in range(0, width, 512):
            out = jnp.dot(act[...], w_down[:, at : at + 512], preferred_element_type=f32)
            out = out.astype(bf16).astype(f32)
            gate_grad += jnp.sum(
                out * u[:, :, at : at + 512].reshape(total, 512).astype(f32), axis=1, keepdims=True
            )
            sent[0, place, :, :, at : at + 512] = (gate * out).astype(bf16).reshape(E, cap, 512)
            back_rows = contract(gate_back[...], w_gate[at : at + 512, :], (1, 1))
            back_rows += contract(up_back[...], w_up[at : at + 512, :], (1, 1))
            sent[1, place, :, :, at : at + 512] = back_rows.astype(bf16).reshape(E, cap, 512)
        for a in (1, 0):
            for k in range(1, E):
                back(a, n, b, i, k).start()
            back_own(a, n, b, i).start()
        for k in range(E):
            scalars[k, i, b] = jnp.sum(
                jnp.where(holds[k], gate_grad[k * cap : (k + 1) * cap], 0.0), axis=0, keepdims=True
            )

    def combine(n):
        b, i = chunk_of(n)
        picks = choose(slots[i, b], cap)
        for a in (1, 0):
            for k in range(1, E):
                back(a, n, b, i, k).wait_recv()
            back_own(a, n, b, i).wait()
            for way in range(2):

                @pl.when(onward(i, way))
                def _():
                    hop(a, b, i, way).wait_send()

            for at in range(0, width, 512):
                part = returned[a, i, b, :, :, at : at + 512].reshape(total, 512)
                landed[a, i, b, :, at : at + 512] = contract(picks, part, (0, 0)).astype(bf16)

            @pl.when(i > 0)
            def _():
                up(a, b, i).start()

            @pl.when(i == 0)
            def _():
                keep(a, b).start()

    def step(s, carry):
        @pl.when(jnp.logical_and(s > 0, s <= batches * (C - 1)))
        def _():
            relay(s)

        @pl.when(s < chunks)
        def _():
            compact(s)

        @pl.when(jnp.logical_and(s >= lead, s < chunks + lead))
        def _():
            expert(s - lead)

        @pl.when(s >= lag)
        def _():
            combine(s - lag)

        return carry

    for copy in small:
        copy.wait_recv()
    lax.fori_loop(0, chunks + lag, step, 0)
    scalars_out[e, c] = scalars[0, 0]
    last = [
        remote(scalars.at[k, i], scalars_out.at[e, c], ss.at[k, i], sr.at[k, i], device)
        for k, i, device in behind
    ]
    for copy in last:
        copy.start()
    for copy in small:
        copy.wait_send()
    for j in range(4):
        store(j, *chunk_of(chunks - 1)).wait()

    def finish(n, carry):
        b, i = chunk_of(n)
        for a in range(2):

            @pl.when(n >= chunks - slots_kept)
            def _():
                for k in range(1, E):
                    across(a, n, k).wait_send()

            @pl.when(n >= chunks - kept)
            def _():
                for k in range(1, E):
                    back(a, n, b, i, k).wait_send()

            @pl.when(i > 0)
            def _():
                up(a, b, i).wait()

            @pl.when(i == 0)
            def _():
                keep(a, b).wait()

        return carry

    lax.fori_loop(0, chunks, finish, 0)
    for copy in last:
        copy.wait()


def run_experts(E, C, rows_x, rows_u, slots, gates, w_gate, w_up, w_down, cap, collective, name):
    batches, run, width = rows_x.shape
    units = w_gate.shape[1]
    total = E * cap
    kept = 3
    by_slot = jax.ShapeDtypeStruct((C, batches, E, cap, width), bf16)
    by_token = jax.ShapeDtypeStruct((C, batches, run, width), bf16)
    hidden = jax.ShapeDtypeStruct((C, batches, total, units), bf16)
    return call(
        functools.partial(experts_kernel, E, C),
        (rows_x, rows_u, slots, gates, w_gate, w_up, w_down),
        (
            by_token,
            by_token,
            by_slot,
            by_slot,
            by_slot,
            hidden,
            hidden,
            hidden,
            jax.ShapeDtypeStruct((E, C, batches, 1, run), f32),
        ),
        [ANY, ANY, VMEM, VMEM, VMEM, VMEM, VMEM],
        (ANY,) * 8 + (VMEM,),
        [
            pltpu.VMEM(gates.shape, f32),
            pltpu.VMEM((E, C, batches, 1, run), f32),
            pltpu.VMEM((2, C, batches, run, width), bf16),
            pltpu.VMEM((2, kept, E, cap, width), bf16),
            pltpu.VMEM((2, C, batches, E, cap, width), bf16),
            pltpu.VMEM((E, cap, width), bf16),
            pltpu.VMEM((E, cap, width), bf16),
            pltpu.VMEM((E, cap, width), bf16),
            pltpu.VMEM((total, units), bf16),
            pltpu.VMEM((total, units), bf16),
            pltpu.VMEM((total, units), bf16),
            pltpu.VMEM((2, kept, E, cap, width), bf16),
            DMA((E, C)),
            DMA((E, C)),
            DMA((E, C)),
            DMA((E, C)),
            DMA((2, batches)),
            DMA((2, 2, C, batches)),
            DMA((2, C, batches)),
            DMA((2, C, batches, E)),
            DMA((2, C, batches, E)),
            DMA((2, C, batches)),
            DMA((2, C, batches, E)),
            DMA((2, C, batches, E)),
            DMA((2, C, batches)),
            DMA((2, C, batches)),
            DMA((2, C, batches)),
            DMA((2, batches)),
            DMA((2,)),
            DMA((4,)),
        ],
        collective,
        name,
        vmem=60,
    )


def scatter_kernel(E, C, G, rows, out, other, sums, cs, cr, zs, zr, ls):
    e, c, d = position()
    batches = rows.shape[0]
    run, width = rows.shape[3:]
    levels = level_peers(C)
    sibling = (e, c, 1 - d)
    meet([device for _, _, device in levels] + ([sibling] if G > 1 else []))

    def swap(b, level):
        return remote(
            rows.at[b, level, 1 - d], other.at[b, level], cs.at[b, level], cr.at[b, level], sibling
        )

    def send(b, i, level):
        return remote(
            sums.at[b, level], out.at[c, b], zs.at[b, i], zr.at[b, i], (e, level, d)
        )

    def keep(b):
        return pltpu.make_async_copy(sums.at[b, c], out.at[c, b], ls.at[b])

    order = [(i, lax.rem(c + i, C)) for i in range(1, C)] + [(0, c)]
    if G > 1:
        for i, level in order:
            for b in range(batches):
                swap(b, level).start()
    for i, level in order:
        for b in range(batches):
            if G > 1:
                swap(b, level).wait_recv()
                sums[b, level] = (
                    rows[b, level, d].astype(f32) + other[b, level].astype(f32)
                ).astype(bf16)
            else:
                sums[b, level] = rows[b, level, d]
            if i > 0:
                send(b, i, level).start()
            else:
                keep(b).start()
    for i, level in order:
        for b in range(batches):
            if G > 1:
                swap(b, level).wait_send()
            if i > 0:
                send(b, i, level).wait()
            else:
                keep(b).wait()


def column_scatter(E, C, G, rows, collective, name):
    batches, _, _, run, width = rows.shape
    return call(
        functools.partial(scatter_kernel, E, C, G),
        (rows,),
        jax.ShapeDtypeStruct((C, batches, run, width), bf16),
        [VMEM],
        ANY,
        [
            pltpu.VMEM((batches, C, run, width), bf16),
            pltpu.VMEM((batches, C, run, width), bf16),
            DMA((batches, C)),
            DMA((batches, C)),
            DMA((batches, C)),
            DMA((batches, C)),
            DMA((batches,)),
        ],
        collective,
        name,
        vmem=48,
    )


def weights_kernel(
    E, C, G, qkv, proj, out_qkv, out_proj, plane_qkv, sum_qkv, other, pair, plane_proj, sum_proj, as_, ar, bs, br, cs, cr, ds, dr, es, er, ls
):
    e, c, d = position()
    me, peers = column_peers(E, C, G)
    planes, levels = plane_peers(E), level_peers(C)
    sibling = (e, c, 1 - d)
    meet([device for _, _, device in peers] + [device for _, _, device in planes])
    swaps = []
    if G > 1:
        for level in range(C):
            swaps.append(
                remote(proj.at[level, 1 - d], other.at[level], cs.at[level], cr.at[level], sibling)
            )
    for copy in swaps:
        copy.start()
    first = []
    for k, plane, device in planes:
        first.append(remote(qkv.at[plane], plane_qkv.at[k], as_.at[k], ar.at[k], device))
    for copy in first:
        copy.start()
    middle = []
    for level in range(C):
        if G > 1:
            swaps[level].wait_recv()
            pair[level] = (proj[level, d].astype(f32) + other[level].astype(f32)).astype(bf16)
        else:
            pair[level] = proj[level, d]
        for k, plane, device in planes:
            copy = remote(
                pair.at[level, plane], plane_proj.at[level, k], ds.at[level, k], dr.at[level, k], device
            )
            copy.start()
            middle.append(copy)
    for copy in first:
        copy.wait_recv()
    total = qkv[e].astype(f32)
    for k in range(1, E):
        total = total + plane_qkv[k].astype(f32)
    sum_qkv[...] = total.astype(bf16)
    second = []
    for offset, index, device in peers:
        copy = remote(sum_qkv.at[index], out_qkv.at[me], bs.at[offset], br.at[offset], device)
        copy.start()
        second.append(copy)
    out_qkv[me] = sum_qkv[me]
    for copy in middle:
        copy.wait_recv()
    for level in range(C):
        total = pair[level, e].astype(f32)
        for k in range(1, E):
            total = total + plane_proj[level, k].astype(f32)
        sum_proj[level] = total.astype(bf16)
    last = []
    for i, level, device in levels:
        copy = remote(sum_proj.at[level], out_proj.at[c], es.at[i], er.at[i], device)
        copy.start()
        last.append(copy)
    out_proj[c] = sum_proj[c]
    for copy in swaps + first + middle:
        copy.wait_send()
    for copy in second + last:
        copy.wait()


def weight_scatter(E, C, G, qkv, proj, collective, name):
    count, rows, columns = qkv.shape[1:]
    width = proj.shape[4]
    return call(
        functools.partial(weights_kernel, E, C, G),
        (qkv, proj),
        (
            jax.ShapeDtypeStruct((count, rows, columns), bf16),
            jax.ShapeDtypeStruct((C, rows, width), bf16),
        ),
        [VMEM, VMEM],
        (VMEM, VMEM),
        [
            pltpu.VMEM((E, count, rows, columns), bf16),
            pltpu.VMEM((count, rows, columns), bf16),
            pltpu.VMEM((C, E, rows, width), bf16),
            pltpu.VMEM((C, E, rows, width), bf16),
            pltpu.VMEM((C, E, rows, width), bf16),
            pltpu.VMEM((C, rows, width), bf16),
            DMA((E,)),
            DMA((E,)),
            DMA((count,)),
            DMA((count,)),
            DMA((C,)),
            DMA((C,)),
            DMA((C, E)),
            DMA((C, E)),
            DMA((C,)),
            DMA((C,)),
            DMA((1,)),
        ],
        collective,
        name,
        vmem=56,
    )


def contract(left, right, axes):
    return lax.dot_general(left, right, ((axes[:1], axes[1:]), ((), ())), preferred_element_type=f32)


def query_blocks(length):
    size = min(256, length)
    return [(i, size, min(length, i + 2 * size)) for i in range(0, length, size)]


def attend_kernel(scale, queries, keys, values, row_ids, key_ids, mixed, log_total):
    length = queries.shape[1]
    for first, size, seen in query_blocks(length):
        rows = pl.ds(first, size)
        scores = contract(queries[0, rows], keys[0, :seen], (1, 1)) * scale
        scores = jnp.where(key_ids[0, :, :seen] <= row_ids[0, rows], scores, MASKED)
        peak = jnp.max(scores, axis=1, keepdims=True)
        grown = jnp.exp(scores - peak)
        total = jnp.sum(grown, axis=1, keepdims=True)
        probs = (grown * (1.0 / total)).astype(bf16)
        mixed[0, rows] = jnp.dot(probs, values[0, :seen], preferred_element_type=f32).astype(bf16)
        log_total[0, 0, rows] = peak + jnp.log(total)


def attend_back_kernel(
    scale, queries, keys, values, grads, row_ids, key_ids, log_total, query_grad, key_grad, value_grad
):
    length = queries.shape[1]
    key_grad[...] = jnp.zeros_like(key_grad)
    value_grad[...] = jnp.zeros_like(value_grad)
    for first, size, seen in query_blocks(length):
        rows = pl.ds(first, size)
        query, grad = queries[0, rows], grads[0, rows]
        scores = contract(query, keys[0, :seen], (1, 1)) * scale
        scores = jnp.where(key_ids[0, :, :seen] <= row_ids[0, rows], scores, MASKED)
        probs = jnp.exp(scores - log_total[0, 0, rows])
        prod = contract(grad, values[0, :seen], (1, 1))
        delta = jnp.sum(probs * prod, axis=1, keepdims=True)
        score_grad = (probs * (prod - delta)).astype(bf16)
        query_grad[0, rows] = jnp.dot(score_grad, keys[0, :seen], preferred_element_type=f32) * scale
        key_grad[0, :seen] += contract(score_grad, query, (0, 0)) * scale
        value_grad[0, :seen] += contract(probs.astype(bf16), grad, (0, 0))


def attention_specs(length):
    head = pl.BlockSpec((1, length, HEAD), lambda b, h: (b, 0, h))
    row_ids = pl.BlockSpec((1, length, 1), lambda b, h: (b, 0, 0))
    key_ids = pl.BlockSpec((1, 1, length), lambda b, h: (b, 0, 0))
    log_total = pl.BlockSpec((1, 1, length, 1), lambda b, h: (b, h, 0, 0))
    return head, row_ids, key_ids, log_total


def attend(queries, keys, values, ids):
    batches, length, size = queries.shape
    heads = size // HEAD
    head, row_ids, key_ids, log_total = attention_specs(length)
    return pl.pallas_call(
        functools.partial(attend_kernel, HEAD**-0.5),
        grid=(batches, heads),
        out_shape=(
            jax.ShapeDtypeStruct(queries.shape, bf16),
            jax.ShapeDtypeStruct((batches, heads, length, 1), f32),
        ),
        in_specs=[head, head, head, row_ids, key_ids],
        out_specs=(head, log_total),
        compiler_params=pltpu.CompilerParams(vmem_limit_bytes=48 * MIB),
        name="attend",
    )(queries, keys, values, ids[:, :, None], ids[:, None, :])


def attend_back(queries, keys, values, grads, ids, totals):
    batches, length, size = queries.shape
    heads = size // HEAD
    head, row_ids, key_ids, log_total = attention_specs(length)
    grad = jax.ShapeDtypeStruct(queries.shape, f32)
    return pl.pallas_call(
        functools.partial(attend_back_kernel, HEAD**-0.5),
        grid=(batches, heads),
        out_shape=(grad, grad, grad),
        in_specs=[head, head, head, head, row_ids, key_ids, log_total],
        out_specs=(head, head, head),
        compiler_params=pltpu.CompilerParams(vmem_limit_bytes=48 * MIB),
        name="attend_back",
    )(queries, keys, values, grads, ids[:, :, None], ids[:, None, :], totals)


def rms_factor(values):
    return lax.rsqrt(jnp.mean(values * values, axis=-1, keepdims=True) + EPSILON)


def norm_back(grad_hat, hatted, factor):
    return factor * (grad_hat - hatted * jnp.mean(grad_hat * hatted, axis=-1, keepdims=True))


def slot_table(routes, experts):
    batches, run, top = routes.shape
    hits = jnp.swapaxes(routes, 1, 2)[:, :, :, None] == jnp.arange(experts, dtype=jnp.int32)
    ones = hits.astype(bf16)
    tokens, ranks = jnp.arange(run), jnp.arange(top)
    before = (tokens[None, :] < tokens[:, None]).astype(bf16)
    above = (ranks[None, :] < ranks[:, None]).astype(bf16)
    within = jnp.einsum("ts,bksx->bktx", before, ones, preferred_element_type=f32)
    totals = jnp.sum(hits.astype(f32), axis=2)
    earlier = jnp.einsum(
        "kj,bjx->bkx", above, totals.astype(bf16), preferred_element_type=f32
    )
    places = jnp.sum(jnp.where(hits, within + earlier[:, :, None, :], 0.0), axis=1)
    places = jnp.where(jnp.any(hits, axis=1), places, UNUSED_SLOT)
    return jnp.swapaxes(places, 1, 2)


def body(
    tokens,
    block_ids,
    routes,
    norm_gains,
    w_query,
    w_key,
    w_value,
    w_output,
    router,
    expert_gate,
    expert_up,
    expert_down,
    cotangent,
):
    E, C, G = lax.axis_size("expert"), lax.axis_size("context"), lax.axis_size("dp")
    batches, run, width = tokens.shape
    top = routes.shape[2]
    experts = E * C * expert_gate.shape[0]
    capacity = max(2, run * top // experts)
    count = C * G
    size = width // count
    length = count * run
    every = batches * length
    own = batches * run
    me = lax.axis_index("context") * G + lax.axis_index("dp")

    rows = w_query.shape[0]
    small_width = -(-(norm_gains.shape[1] + experts) // 128) * 128
    small = jnp.concatenate([norm_gains, router], axis=1)
    small = jnp.pad(small, ((0, 0), (0, small_width - small.shape[1])))
    pieces = [w.reshape(rows, count, size) for w in (w_query, w_key, w_value)]
    pieces.append(jnp.broadcast_to(small[:, None, :], (rows, count, small_width)))
    weights = jnp.swapaxes(jnp.concatenate(pieces, axis=2), 0, 1)
    full_output = lax.all_gather(w_output, ALL_AXES, axis=0, tiled=True)
    places = slot_table(routes, experts).reshape(batches, E, C, run)
    by_level = jnp.transpose(places, (2, 0, 1, 3))
    by_expert = jnp.transpose(places, (1, 2, 0, 3))
    column, gathered, ids, slots = start(E, C, G, tokens, weights, block_ids, by_level)
    ids = jnp.swapaxes(ids, 0, 1).reshape(batches, length)
    w_qkv = gathered[:, : 3 * size]
    gains = gathered[:, 3 * size : 3 * size + 4].astype(f32)
    full_router = gathered[:, 3 * size + 4 : 3 * size + 4 + experts]
    head_gains = lax.dynamic_slice(gains, (me * size, 0), (size, 4))

    column = column.reshape(every, width).astype(f32)
    normed = (column * rms_factor(column) * gains[:, 0]).astype(bf16)
    qkv = jnp.dot(normed, w_qkv, preferred_element_type=f32)
    query_raw, key_raw = qkv[:, :size], qkv[:, size : 2 * size]
    value_low = qkv[:, 2 * size :].astype(bf16)
    squares = jnp.stack([jnp.sum(query_raw * query_raw, axis=1), jnp.sum(key_raw * key_raw, axis=1)])
    factors = lax.rsqrt(column_sum(E, C, G, squares, 2, "squares") / width + EPSILON)
    query_factor, key_factor = factors[0][:, None], factors[1][:, None]
    query_hat, key_hat = query_raw * query_factor, key_raw * key_factor
    by_sequence = (batches, length, size)
    query_low = (query_hat * head_gains[:, 1]).astype(bf16).reshape(by_sequence)
    key_low = (key_hat * head_gains[:, 2]).astype(bf16).reshape(by_sequence)
    value_low = value_low.reshape(by_sequence)
    mixed_heads, log_total = attend(query_low, key_low, value_low, ids)
    mixed_low = to_tokens(
        E, C, G, mixed_heads.reshape(batches, count, run, size), 3, "mixed_rows"
    ).reshape(own, width)

    inputs = tokens.reshape(own, width).astype(f32)
    resid = inputs + jnp.dot(mixed_low, full_output, preferred_element_type=f32)
    second_factor = rms_factor(resid)
    second_hat = resid * second_factor
    second_low = (second_hat * gains[:, 3]).astype(bf16)
    logits = jnp.dot(second_low, full_router, preferred_element_type=f32)
    router_probs = jax.nn.softmax(logits, axis=-1)
    gate_table = jnp.transpose(router_probs.reshape(batches, run, E, C), (2, 3, 0, 1))
    table = jnp.concatenate([by_expert, gate_table], axis=2)[:, :, :, None, :]

    mixture, second_grad, x, _, pair_grad, act, gate_pre_grad, up_pre_grad, gate_grad = run_experts(
        E,
        C,
        second_low.reshape(batches, run, width),
        cotangent,
        slots,
        table,
        expert_gate[0],
        expert_up[0],
        expert_down[0],
        capacity,
        4,
        "experts",
    )
    slot_count = E * C * batches * capacity
    x, pair_grad, act, gate_pre_grad, up_pre_grad = (
        rows.reshape(slot_count, -1) for rows in (x, pair_grad, act, gate_pre_grad, up_pre_grad)
    )
    share = functools.partial(lax.psum_scatter, axis_name="dp", tiled=True)
    grad_gate = share(contract(x, gate_pre_grad, (0, 0)).astype(bf16), scatter_dimension=1)
    grad_up = share(contract(x, up_pre_grad, (0, 0)).astype(bf16), scatter_dimension=1)
    grad_down = share(contract(act, pair_grad, (0, 0)).astype(bf16), scatter_dimension=0)

    upstream = cotangent.reshape(own, width).astype(f32)
    mixture = jnp.sum(mixture.astype(f32), axis=0).reshape(own, width)
    activations = (resid + mixture).astype(bf16).reshape(tokens.shape)
    prob_grad = jnp.transpose(gate_grad[:, :, :, 0, :], (2, 3, 0, 1)).reshape(own, experts)
    logit_grad = router_probs * (
        prob_grad - jnp.sum(router_probs * prob_grad, axis=-1, keepdims=True)
    )
    logit_grad = logit_grad.astype(bf16)
    second_grad = jnp.sum(second_grad.astype(f32), axis=0).reshape(own, width)
    second_grad = second_grad + contract(logit_grad, full_router, (1, 1))
    gain_second = jnp.sum(second_grad * second_hat, axis=0)
    resid_grad = upstream + norm_back(second_grad * gains[:, 3], second_hat, second_factor)
    attn_grad = resid_grad.astype(bf16)
    mixed_grad = contract(attn_grad, full_output, (1, 1)).astype(bf16)

    mixed_grad = to_heads(E, C, G, mixed_grad.reshape(batches, run, width), 6, "mixed_grad_heads")
    query_grad, key_grad, value_grad = (
        grad.reshape(every, size)
        for grad in attend_back(
            query_low, key_low, value_low, mixed_grad.reshape(by_sequence), ids, log_total
        )
    )
    query_back, key_back = query_grad * head_gains[:, 1], key_grad * head_gains[:, 2]
    means = jnp.stack([jnp.sum(query_back * query_hat, axis=1), jnp.sum(key_back * key_hat, axis=1)])
    means = column_sum(E, C, G, means, 7, "norm_means") / width
    raw_grads = jnp.concatenate(
        [
            (query_factor * (query_back - query_hat * means[0][:, None])).astype(bf16),
            (key_factor * (key_back - key_hat * means[1][:, None])).astype(bf16),
            value_grad.astype(bf16),
        ],
        axis=1,
    )
    first_part = contract(raw_grads, w_qkv, (1, 1)).astype(bf16)
    first_grad = column_scatter(
        E, C, G, first_part.reshape(batches, C, G, run, width), 8, "first_grad"
    )
    first_grad = jnp.sum(first_grad.astype(f32), axis=0).reshape(own, width)
    first_factor = rms_factor(inputs)
    first_hat = inputs * first_factor
    gain_first = jnp.sum(first_grad * first_hat, axis=0)
    input_grad = resid_grad + norm_back(first_grad * gains[:, 0], first_hat, first_factor)

    grad_qkv = contract(normed, raw_grads, (0, 0)).astype(bf16)
    grad_proj = contract(mixed_low, attn_grad, (0, 0)).astype(bf16)
    grad_proj = jnp.transpose(grad_proj.reshape(E, C, G, rows, width), (1, 2, 0, 3, 4))
    grad_qkv, grad_proj = weight_scatter(
        E, C, G, grad_qkv.reshape(E, count, rows, 3 * size), grad_proj, 9, "weight_grads"
    )
    grad_qkv = jnp.swapaxes(grad_qkv.astype(f32), 0, 1)
    grad_query, grad_key, grad_value = (
        grad_qkv[:, :, i * size : (i + 1) * size].reshape(rows, width) for i in range(3)
    )
    grad_proj = jnp.sum(grad_proj.astype(f32), axis=0)
    gain_heads = jnp.stack(
        [jnp.sum(query_grad * query_hat, axis=0), jnp.sum(key_grad * key_hat, axis=0)], axis=1
    )
    gain_heads = lax.dynamic_update_slice(
        jnp.zeros((width, 2), f32), gain_heads, (me * size, 0)
    )
    sums = jnp.concatenate(
        [
            gain_first[:, None],
            gain_heads,
            gain_second[:, None],
            contract(second_low, logit_grad, (0, 0)),
        ],
        axis=1,
    )
    sums = lax.psum_scatter(sums, ALL_AXES, scatter_dimension=0, tiled=True)
    return (
        activations,
        input_grad.reshape(tokens.shape),
        sums[:, :4],
        grad_query,
        grad_key,
        grad_value,
        grad_proj,
        sums[:, 4:],
        grad_gate.astype(f32)[None],
        grad_up.astype(f32)[None],
        grad_down.astype(f32)[None],
    )


def solution(mesh):
    by_token = ("context", "dp")
    by_expert = P(("expert", "context"), None, None)
    by_row = P(ALL_AXES, None)
    rows = P("expert", by_token, None)
    return jax.shard_map(
        body,
        mesh=mesh,
        in_specs=(
            rows,
            P("expert", by_token),
            rows,
            by_row,
            by_row,
            by_row,
            by_row,
            by_row,
            by_row,
            by_expert,
            by_expert,
            by_expert,
            rows,
        ),
        out_specs=(
            rows,
            rows,
            by_row,
            by_row,
            by_row,
            by_row,
            by_row,
            by_row,
            P(("expert", "context"), None, "dp"),
            P(("expert", "context"), None, "dp"),
            P(("expert", "context"), "dp", None),
        ),
        check_vma=False,
    )
```

```python
import functools

import jax
import jax.numpy as jnp
from jax import lax
from jax.experimental import pallas as pl
from jax.experimental.pallas import tpu as pltpu
from jax.sharding import PartitionSpec as P

HEAD = 128
EPSILON = 1e-05
MASKED = -1e30
UNUSED_SLOT = 4096.0
ALL_AXES = ("expert", "context", "dp")
MESH = pl.DeviceIdType.MESH
ANY = pl.BlockSpec(memory_space=pl.ANY)
VMEM = pl.BlockSpec(memory_space=pltpu.VMEM)
DMA = pltpu.SemaphoreType.DMA
MIB = 1 << 20
f32 = jnp.float32
bf16 = jnp.bfloat16


def call(kernel, operands, out_shapes, in_specs, out_specs, scratch, collective, name, vmem=32):
    return pl.pallas_call(
        kernel,
        out_shape=out_shapes,
        in_specs=in_specs,
        out_specs=out_specs,
        scratch_shapes=scratch,
        compiler_params=pltpu.CompilerParams(
            collective_id=collective, has_side_effects=True, vmem_limit_bytes=vmem * MIB
        ),
        name=name,
    )(*operands)


def position():
    return lax.axis_index("expert"), lax.axis_index("context"), lax.axis_index("dp")


def meet(devices):
    barrier = pltpu.get_barrier_semaphore()
    for device in devices:
        pl.semaphore_signal(barrier, inc=1, device_id=device, device_id_type=MESH)
    pl.semaphore_wait(barrier, len(devices))


def remote(source, target, send_sem, recv_sem, device):
    return pltpu.make_async_remote_copy(
        src_ref=source,
        dst_ref=target,
        send_sem=send_sem,
        recv_sem=recv_sem,
        device_id=device,
        device_id_type=MESH,
    )


def column_peers(E, C, G):
    e, c, d = position()
    me = c * G + d
    peers = []
    for offset in range(1, C * G):
        index = lax.rem(me + offset, C * G)
        peers.append((offset, index, (e, index // G, lax.rem(index, G))))
    return me, peers


def plane_peers(E):
    e, c, d = position()
    return [(i, lax.rem(e + i, E), (lax.rem(e + i, E), c, d)) for i in range(1, E)]


def level_peers(C):
    e, c, d = position()
    return [(i, lax.rem(c + i, C), (e, lax.rem(c + i, C), d)) for i in range(1, C)]


def start_kernel(
    E,
    C,
    G,
    tokens,
    weights,
    small_weights,
    output,
    ids,
    slots,
    column,
    gathered,
    small_gathered,
    full_output,
    ids_out,
    slots_out,
    ws,
    wr,
    bs,
    br,
    hs,
    hr,
    ts,
    tr,
    ls,
    ms,
    mr,
    ps,
    pr,
    fs,
    fr,
    gs,
    gr,
):
    e, c, d = position()
    me, peers = column_peers(E, C, G)
    planes = plane_peers(E)
    batches = tokens.shape[0]
    sibling = (e, c, 1 - d)
    meet([device for _, _, device in peers] + [device for _, _, device in planes])
    kinds = ((weights, gathered), (small_weights, small_gathered))
    weight_copies = []
    for j, (source, target) in enumerate(kinds):
        for offset, index, device in peers:
            part = source.at[index] if j == 0 else source
            weight_copies.append(
                remote(part, target.at[e, me], ws.at[j, offset], wr.at[j, offset], device)
            )
    for copy in weight_copies:
        copy.start()
    local = [
        pltpu.make_async_copy(weights.at[me], gathered.at[e, me], ls.at[0]),
        pltpu.make_async_copy(small_weights, small_gathered.at[e, me], ls.at[1]),
        pltpu.make_async_copy(output, full_output.at[e, c, d], ls.at[2]),
    ]
    for b in range(batches):
        local.append(pltpu.make_async_copy(tokens.at[b], column.at[b, me], ls.at[3 + b]))
    for copy in local:
        copy.start()

    def source_of(item):
        return output if item == 0 else tokens.at[item - 1]

    def place(item, level):
        return full_output.at[e, level, d] if item == 0 else column.at[item - 1, level * G + d]

    def to_sibling(source, item, level, arrival):
        return remote(
            source, place(item, level), ts.at[item, arrival], tr.at[item, arrival], sibling
        )

    def step(hop, source, item, level, up):
        to = (e, c + 1, d) if up else (e, c - 1, d)
        way = 0 if up else 1
        return remote(
            source, place(item, level), hs.at[way, item, hop], hr.at[way, item, hop], to
        )

    def relay(item, hop):
        for up in (True, False):
            level = c - hop if up else c + hop
            here = (c >= hop) if up else (c + hop < C)
            onward = (c < C - 1) if up else (c > 0)

            @pl.when(here)
            def _():
                landed = place(item, level)
                step(hop - 1, landed, item, level, up).wait_recv()
                if hop < C - 1:

                    @pl.when(onward)
                    def _():
                        step(hop, landed, item, level, up).start()

                if G > 1:
                    to_sibling(landed, item, level, hop if up else C - 1 + hop).start()

    for item in range(batches + 1):

        @pl.when(c < C - 1)
        def _():
            step(0, source_of(item), item, c, True).start()

        @pl.when(c > 0)
        def _():
            step(0, source_of(item), item, c, False).start()

        if G > 1:
            to_sibling(source_of(item), item, c, 0).start()
    small = []
    for offset, _, device in peers:
        small.append(remote(ids, ids_out.at[me], ms.at[offset], mr.at[offset], device))
    for i, level, device in level_peers(C):
        small.append(remote(slots.at[level], slots_out.at[i], ps.at[i], pr.at[i], device))
    for copy in small:
        copy.start()
    ids_out[me] = ids[...]
    slots_out[0] = slots[c]
    for copy in weight_copies:
        copy.wait_recv()
    for copy in local[:3]:
        copy.wait()
    plane_copies = []
    for j, (_, target) in enumerate(kinds):
        for i, _, device in planes:
            copy = remote(target.at[e], target.at[e], bs.at[j, i], br.at[j, i], device)
            copy.start()
            plane_copies.append(copy)
    for hop in range(1, C):
        relay(0, hop)

    def output_copy(i, plane, device):
        mine = full_output.at[e, :, d]
        return remote(mine, mine, fs.at[i], fr.at[i], device)

    def output_sibling(i):
        part = full_output.at[lax.rem(e + E - i, E), :, d]
        return remote(part, part, gs.at[i], gr.at[i], sibling)

    for i, plane, device in planes:
        output_copy(i, plane, device).start()
    for hop in range(1, C):
        for item in range(1, batches + 1):
            relay(item, hop)
    for i, plane, device in planes:
        output_copy(i, plane, device).wait_recv()
        if G > 1:
            output_sibling(i).start()

    for item in range(batches + 1):
        if G > 1:
            to_sibling(source_of(item), item, c, 0).wait()
        for hop in range(C - 1):
            for up in (True, False):
                arrival = hop + 1 if up else C + hop
                origin = c - hop if up else c + hop
                if up:
                    sends = jnp.logical_and(origin >= 0, c < C - 1)
                    arrives = c >= hop + 1
                else:
                    sends = jnp.logical_and(origin < C, c > 0)
                    arrives = c + hop + 1 < C

                @pl.when(sends)
                def _():
                    step(hop, source_of(item), item, c, up).wait_send()

                if G > 1:

                    @pl.when(arrives)
                    def _():
                        to_sibling(source_of(item), item, c, arrival).wait()

    for i, plane, device in planes:
        output_copy(i, plane, device).wait_send()
        if G > 1:
            output_sibling(i).wait()
    for copy in weight_copies:
        copy.wait_send()
    for copy in plane_copies + small + local[3:]:
        copy.wait()


def start(E, C, G, tokens, weights, small_weights, output, ids, slots):
    batches, run, width = tokens.shape
    count = C * G
    rows, columns = weights.shape[1:]
    items = batches + 1
    return call(
        functools.partial(start_kernel, E, C, G),
        (tokens, weights, small_weights, output, ids, slots),
        (
            jax.ShapeDtypeStruct((batches, count, run, width), tokens.dtype),
            jax.ShapeDtypeStruct((E, count, rows, columns), weights.dtype),
            jax.ShapeDtypeStruct((E, count) + small_weights.shape, weights.dtype),
            jax.ShapeDtypeStruct((E, C, G, rows, width), weights.dtype),
            jax.ShapeDtypeStruct((count,) + ids.shape, ids.dtype),
            jax.ShapeDtypeStruct(slots.shape, slots.dtype),
        ),
        [ANY, ANY, ANY, ANY, VMEM, VMEM],
        (ANY, ANY, ANY, ANY, VMEM, VMEM),
        [
            DMA((2, count)),
            DMA((2, count)),
            DMA((2, E)),
            DMA((2, E)),
            DMA((2, items, C)),
            DMA((2, items, C)),
            DMA((items, 2 * C)),
            DMA((items, 2 * C)),
            DMA((items + 2,)),
            DMA((count,)),
            DMA((count,)),
            DMA((C,)),
            DMA((C,)),
            DMA((E,)),
            DMA((E,)),
            DMA((E,)),
            DMA((E,)),
        ],
        1,
        "start",
    )


def share_kernel(E, C, G, part, parts, ss, rs):
    me, peers = column_peers(E, C, G)
    meet([device for _, _, device in peers])
    copies = []
    for offset, _, device in peers:
        copy = remote(part, parts.at[me], ss.at[offset], rs.at[offset], device)
        copy.start()
        copies.append(copy)
    parts[me] = part[...]
    for copy in copies:
        copy.wait()


def column_sum(E, C, G, part, collective, name):
    parts = call(
        functools.partial(share_kernel, E, C, G),
        (part,),
        jax.ShapeDtypeStruct((C * G,) + part.shape, part.dtype),
        [VMEM],
        VMEM,
        [DMA((C * G,)), DMA((C * G,))],
        collective,
        name,
    )
    return jnp.sum(parts, axis=0)


def to_tokens_kernel(E, C, G, heads, rows, ss, rs, ls):
    me, peers = column_peers(E, C, G)
    batches = rows.shape[0]
    size = heads.shape[3]
    meet([device for _, _, device in peers])
    mine = pl.ds(pl.multiple_of(me * size, size), size)
    copies = []
    for b in range(batches):
        for offset, index, device in peers:
            copies.append(
                remote(
                    heads.at[b, index], rows.at[b, :, mine], ss.at[b, offset], rs.at[b, offset], device
                )
            )
        copies.append(pltpu.make_async_copy(heads.at[b, me], rows.at[b, :, mine], ls.at[b]))
    for copy in copies:
        copy.start()
    for copy in copies:
        copy.wait()


def to_tokens(E, C, G, heads, collective, name):
    batches, count, run, size = heads.shape
    return call(
        functools.partial(to_tokens_kernel, E, C, G),
        (heads,),
        jax.ShapeDtypeStruct((batches, run, count * size), heads.dtype),
        [ANY],
        ANY,
        [DMA((batches, C * G)), DMA((batches, C * G)), DMA((batches,))],
        collective,
        name,
    )


def choose(slots, count):
    cells = lax.broadcasted_iota(jnp.int32, (count, slots.shape[1]), 0).astype(f32)
    return jnp.concatenate(
        [(cells == slots[i : i + 1, :]).astype(bf16) for i in range(slots.shape[0])], axis=0
    )


def experts_kernel(
    E,
    C,
    rows_x,
    rows_u,
    slots,
    gates,
    w_gate,
    w_up,
    w_down,
    out_y,
    out_b,
    x_out,
    u_out,
    pair_out,
    act_out,
    gate_back_out,
    up_back_out,
    scalars_out,
    table,
    scalars,
    landed,
    packed,
    returned,
    x,
    u,
    pair,
    act,
    gate_back,
    up_back,
    sent,
    gs,
    gr,
    ss,
    sr,
    os,
    zs,
    zr,
    xs,
    xr,
    ls,
    ys,
    yr,
    bs,
    us,
    ur,
    ks,
    loads,
    stores,
):
    e, c, d = position()
    batches, run, width = rows_x.shape
    cap = x_out.shape[3]
    units = w_gate.shape[1]
    chunks = batches * C
    total = E * cap
    slots_kept, kept = packed.shape[1], sent.shape[1]
    lead, lag = 1, 2
    everyone = [(k, i) for k in range(E) for i in range(C) if k + i > 0]
    ahead = [(k, i, (lax.rem(e + k, E), lax.rem(c + i, C), d)) for k, i in everyone]
    behind = [(k, i, (lax.rem(e + E - k, E), lax.rem(c + C - i, C), d)) for k, i in everyone]
    meet([device for _, _, device in ahead])
    sources, arrivals, outs = (rows_x, rows_u), (x_out, u_out), (out_y, out_b)

    high = 2 * c // C

    def far_of(n):
        return lax.rem((n + batches - 1) // batches, C), lax.rem(n + batches - 1, batches)

    def chunk_of(n):
        m, b = far_of(n)
        return b, high * m + (1 - high) * lax.rem(C - m, C)

    def hop(a, b, i, way):
        there = i + 1 if way == 0 else lax.rem(i + C - 1, C)
        level = lax.rem(c + 1, C) if way == 0 else lax.rem(c + C - 1, C)
        return remote(
            landed.at[a, i, b],
            landed.at[a, there, b],
            zs.at[way, a, i, b],
            zr.at[a, there, b],
            (e, level, d),
        )

    def arrival(a, b, i):
        return remote(
            landed.at[a, i, b], landed.at[a, i, b], zs.at[0, a, i, b], zr.at[a, i, b], (e, c, 1 - d)
        )

    def onward(i, way):
        if way == 0:
            return jnp.logical_and(i <= c, c < C - 1)
        return jnp.logical_and(lax.rem(C - i, C) + c < C, c > 0)

    def own(a, b):
        return pltpu.make_async_copy(sources[a].at[b], landed.at[a, 0, b], os.at[a, b])

    def across(a, n, k):
        plane = lax.rem(e + k, E)
        b, i = chunk_of(n)
        return remote(
            packed.at[a, lax.rem(n, slots_kept), plane],
            arrivals[a].at[i, b, k],
            xs.at[a, i, b, k],
            xr.at[a, i, b, k],
            (plane, c, d),
        )

    def stay(a, n):
        b, i = chunk_of(n)
        return pltpu.make_async_copy(
            packed.at[a, lax.rem(n, slots_kept), e], arrivals[a].at[i, b, 0], ls.at[a, i, b]
        )

    def back(a, n, b, i, k):
        return remote(
            sent.at[a, lax.rem(n, kept), k],
            returned.at[a, i, b, e],
            ys.at[a, i, b, k],
            yr.at[a, i, b, k],
            (lax.rem(e + E - k, E), c, d),
        )

    def back_own(a, n, b, i):
        return pltpu.make_async_copy(
            sent.at[a, lax.rem(n, kept), 0], returned.at[a, i, b, e], bs.at[a, i, b]
        )

    def up(a, b, i):
        return remote(
            landed.at[a, i, b],
            outs[a].at[c, b],
            us.at[a, i, b],
            ur.at[a, i, b],
            (e, lax.rem(c + C - i, C), d),
        )

    def keep(a, b):
        return pltpu.make_async_copy(landed.at[a, 0, b], outs[a].at[c, b], ks.at[a, b])

    def load(a, b, i):
        target = (x, u)[a]
        return pltpu.make_async_copy(arrivals[a].at[i, b], target, loads.at[a])

    def store(j, b, i):
        source = (pair, act, gate_back, up_back)[j]
        target = (pair_out, act_out, gate_back_out, up_back_out)[j]
        return pltpu.make_async_copy(source, target.at[i, b], stores.at[j])

    for b in range(batches):
        for a in range(2):
            own(a, b).start()
    for b in range(batches):
        for a in range(2):
            own(a, b).wait()
            for way in range(2):

                @pl.when(onward(0, way))
                def _():
                    hop(a, b, 0, way).start()

    small = [
        remote(gates.at[device[0], device[1]], table.at[k, i], gs.at[k, i], gr.at[k, i], device)
        for k, i, device in ahead
    ]
    for copy in small:
        copy.start()
    table[0, 0] = gates[e, c]

    def relay(n):
        far, b = far_of(n)
        for a in range(2):
            for way in range(2):
                i = far if way == 0 else C - far

                @pl.when((far <= c) if way == 0 else (far + c < C))
                def _():
                    arrival(a, b, i).wait_recv()

                    @pl.when(onward(i, way))
                    def _():
                        hop(a, b, i, way).start()

    def compact(n):
        b, i = chunk_of(n)
        picks = choose(slots[i, b], cap)
        place = lax.rem(n, slots_kept)

        @pl.when(n >= slots_kept)
        def _():
            for a in range(2):
                for k in range(1, E):
                    across(a, n - slots_kept, k).wait_send()

        for a in range(2):
            for at in range(0, width, 512):
                part = jnp.dot(
                    picks, landed[a, i, b, :, at : at + 512], preferred_element_type=f32
                ).astype(bf16)
                packed[a, place, :, :, at : at + 512] = part.reshape(E, cap, 512)
            for k in range(1, E):
                across(a, n, k).start()
            stay(a, n).start()

    def expert(n):
        b, i = chunk_of(n)
        for a in range(2):
            for k in range(1, E):
                across(a, n, k).wait_recv()
            stay(a, n).wait()
            load(a, b, i).start()

        @pl.when(n > 0)
        def _():
            before = chunk_of(n - 1)
            for j in range(4):
                store(j, *before).wait()

        @pl.when(n >= kept)
        def _():
            before = chunk_of(n - kept)
            for a in range(2):
                for k in range(1, E):
                    back(a, n - kept, *before, k).wait_send()

        holds, gate = [], []
        cells = lax.broadcasted_iota(jnp.int32, (cap, run), 0).astype(f32)
        for k in range(E):
            hold = cells == table[k, i, b]
            holds.append(hold)
            gate.append(
                jnp.sum(jnp.where(hold, table[k, i, batches + b], 0.0), axis=1, keepdims=True)
            )
        gate = jnp.concatenate(gate, axis=0)
        for a in range(2):
            load(a, b, i).wait()
        for at in range(0, width, 512):
            part = u[:, :, at : at + 512].reshape(total, 512).astype(f32)
            pair[:, :, at : at + 512] = (gate * part).astype(bf16).reshape(E, cap, 512)
        store(0, b, i).start()
        inputs = x[...].reshape(total, width)
        grads = pair[...].reshape(total, width)
        for at in range(0, units, 256):
            gate_pre = jnp.dot(inputs, w_gate[:, at : at + 256], preferred_element_type=f32)
            up_pre = jnp.dot(inputs, w_up[:, at : at + 256], preferred_element_type=f32)
            act_grad = contract(grads, w_down[at : at + 256, :], (1, 1))
            sigmoid = jax.nn.sigmoid(gate_pre)
            silu = gate_pre * sigmoid
            act[:, at : at + 256] = (silu * up_pre).astype(bf16)
            gate_back[:, at : at + 256] = (
                act_grad * up_pre * sigmoid * (1.0 + gate_pre * (1.0 - sigmoid))
            ).astype(bf16)
            up_back[:, at : at + 256] = (act_grad * silu).astype(bf16)
        for j in range(1, 4):
            store(j, b, i).start()
        place = lax.rem(n, kept)
        gate_grad = jnp.zeros((total, 1), f32)
        for at in range(0, width, 512):
            out = jnp.dot(act[...], w_down[:, at : at + 512], preferred_element_type=f32)
            out = out.astype(bf16).astype(f32)
            gate_grad += jnp.sum(
                out * u[:, :, at : at + 512].reshape(total, 512).astype(f32), axis=1, keepdims=True
            )
            sent[0, place, :, :, at : at + 512] = (gate * out).astype(bf16).reshape(E, cap, 512)
            back_rows = contract(gate_back[...], w_gate[at : at + 512, :], (1, 1))
            back_rows += contract(up_back[...], w_up[at : at + 512, :], (1, 1))
            sent[1, place, :, :, at : at + 512] = back_rows.astype(bf16).reshape(E, cap, 512)
        for a in (1, 0):
            for k in range(1, E):
                back(a, n, b, i, k).start()
            back_own(a, n, b, i).start()
        for k in range(E):
            scalars[k, i, b] = jnp.sum(
                jnp.where(holds[k], gate_grad[k * cap : (k + 1) * cap], 0.0), axis=0, keepdims=True
            )

    def combine(n):
        b, i = chunk_of(n)
        picks = choose(slots[i, b], cap)
        for a in (1, 0):
            for k in range(1, E):
                back(a, n, b, i, k).wait_recv()
            back_own(a, n, b, i).wait()
            for way in range(2):

                @pl.when(onward(i, way))
                def _():
                    hop(a, b, i, way).wait_send()

            for at in range(0, width, 512):
                part = returned[a, i, b, :, :, at : at + 512].reshape(total, 512)
                landed[a, i, b, :, at : at + 512] = contract(picks, part, (0, 0)).astype(bf16)

            @pl.when(i > 0)
            def _():
                up(a, b, i).start()

            @pl.when(i == 0)
            def _():
                keep(a, b).start()

    def step(s, carry):
        @pl.when(jnp.logical_and(s > 0, s <= batches * (C - 1)))
        def _():
            relay(s)

        @pl.when(s < chunks)
        def _():
            compact(s)

        @pl.when(jnp.logical_and(s >= lead, s < chunks + lead))
        def _():
            expert(s - lead)

        @pl.when(s >= lag)
        def _():
            combine(s - lag)

        return carry

    for copy in small:
        copy.wait_recv()
    lax.fori_loop(0, chunks + lag, step, 0)
    scalars_out[e, c] = scalars[0, 0]
    last = [
        remote(scalars.at[k, i], scalars_out.at[e, c], ss.at[k, i], sr.at[k, i], device)
        for k, i, device in behind
    ]
    for copy in last:
        copy.start()
    for copy in small:
        copy.wait_send()
    for j in range(4):
        store(j, *chunk_of(chunks - 1)).wait()

    def finish(n, carry):
        b, i = chunk_of(n)
        for a in range(2):

            @pl.when(n >= chunks - slots_kept)
            def _():
                for k in range(1, E):
                    across(a, n, k).wait_send()

            @pl.when(n >= chunks - kept)
            def _():
                for k in range(1, E):
                    back(a, n, b, i, k).wait_send()

            @pl.when(i > 0)
            def _():
                up(a, b, i).wait()

            @pl.when(i == 0)
            def _():
                keep(a, b).wait()

        return carry

    lax.fori_loop(0, chunks, finish, 0)
    for copy in last:
        copy.wait()


def run_experts(E, C, rows_x, rows_u, slots, gates, w_gate, w_up, w_down, cap, collective, name):
    batches, run, width = rows_x.shape
    units = w_gate.shape[1]
    total = E * cap
    kept = 3
    by_slot = jax.ShapeDtypeStruct((C, batches, E, cap, width), bf16)
    by_token = jax.ShapeDtypeStruct((C, batches, run, width), bf16)
    hidden = jax.ShapeDtypeStruct((C, batches, total, units), bf16)
    return call(
        functools.partial(experts_kernel, E, C),
        (rows_x, rows_u, slots, gates, w_gate, w_up, w_down),
        (
            by_token,
            by_token,
            by_slot,
            by_slot,
            by_slot,
            hidden,
            hidden,
            hidden,
            jax.ShapeDtypeStruct((E, C, batches, 1, run), f32),
        ),
        [ANY, ANY, VMEM, VMEM, VMEM, VMEM, VMEM],
        (ANY,) * 8 + (VMEM,),
        [
            pltpu.VMEM(gates.shape, f32),
            pltpu.VMEM((E, C, batches, 1, run), f32),
            pltpu.VMEM((2, C, batches, run, width), bf16),
            pltpu.VMEM((2, kept, E, cap, width), bf16),
            pltpu.VMEM((2, C, batches, E, cap, width), bf16),
            pltpu.VMEM((E, cap, width), bf16),
            pltpu.VMEM((E, cap, width), bf16),
            pltpu.VMEM((E, cap, width), bf16),
            pltpu.VMEM((total, units), bf16),
            pltpu.VMEM((total, units), bf16),
            pltpu.VMEM((total, units), bf16),
            pltpu.VMEM((2, kept, E, cap, width), bf16),
            DMA((E, C)),
            DMA((E, C)),
            DMA((E, C)),
            DMA((E, C)),
            DMA((2, batches)),
            DMA((2, 2, C, batches)),
            DMA((2, C, batches)),
            DMA((2, C, batches, E)),
            DMA((2, C, batches, E)),
            DMA((2, C, batches)),
            DMA((2, C, batches, E)),
            DMA((2, C, batches, E)),
            DMA((2, C, batches)),
            DMA((2, C, batches)),
            DMA((2, C, batches)),
            DMA((2, batches)),
            DMA((2,)),
            DMA((4,)),
        ],
        collective,
        name,
        vmem=60,
    )


def middle_kernel(
    E,
    C,
    G,
    rows,
    mixed,
    grads,
    x,
    pair,
    gate_back,
    up_back,
    act,
    heads,
    proj,
    own_gate,
    own_up,
    own_down,
    other_gate,
    other_up,
    other_down,
    hidden,
    wide,
    kept,
    sent,
    swap,
    swapped,
    chip,
    plane_parts,
    level_part,
    hs,
    hr,
    hl,
    cs,
    cr,
    ps,
    pr,
    zs,
    zr,
    rs,
    wide_sem,
    ks,
    xs,
    xr,
):
    e, c, d = position()
    me, peers = column_peers(E, C, G)
    planes, levels = plane_peers(E), level_peers(C)
    batches = rows.shape[0]
    size = heads.shape[3]
    block, width = swap.shape[1:]
    step = wide.shape[2]
    half = own_gate.shape[1]
    sibling = (e, c, 1 - d)
    meet([device for _, _, device in peers] + [device for _, _, device in planes])

    def head_part(b, index):
        return rows.at[b, :, pl.ds(pl.multiple_of(index * size, size), size)]

    head_copies = []
    for b in range(batches):
        for offset, index, device in peers:
            head_copies.append(
                remote(head_part(b, index), heads.at[b, me], hs.at[b, offset], hr.at[b, offset], device)
            )
        head_copies.append(pltpu.make_async_copy(head_part(b, me), heads.at[b, me], hl.at[b]))
    for copy in head_copies:
        copy.start()

    hidden_copies = [
        pltpu.make_async_copy(source, hidden.at[j], rs.at[j])
        for j, source in enumerate((gate_back, up_back, act))
    ]
    for copy in hidden_copies:
        copy.start()
    count = width // step
    sources = [x] * count + [pair] * count

    def wide_copy(item):
        at = (item % count) * step
        return pltpu.make_async_copy(
            sources[item].at[:, pl.ds(at, step)], wide.at[item % 2], wide_sem.at[item % 2]
        )

    wide_copy(0).start()
    wide_copy(1).start()

    def chip_copy(level):
        return remote(swap.at[level], swapped.at[level], cs.at[level], cr.at[level], sibling)

    def proj_part(core, level):
        part = mixed[:, level, core].reshape(block, mixed.shape[4])
        return jnp.dot(part, grads[...], preferred_element_type=f32)

    def plane_copy(level, k, device):
        return remote(
            chip.at[level, lax.rem(e + k, E)],
            plane_parts.at[level, k],
            ps.at[level, k],
            pr.at[level, k],
            device,
        )

    def give(level, carry):
        swap[level] = proj_part(1 - d, level).astype(bf16)
        chip_copy(level).start()
        return carry

    def take(level, carry):
        part = proj_part(d, level)
        chip_copy(level).wait_recv()
        part = (part + swapped[level].astype(f32)).astype(bf16)
        chip[level] = part.reshape(chip.shape[1:])
        for k, _, device in planes:
            plane_copy(level, k, device).start()
        return carry

    lax.fori_loop(0, C, give, 0)
    lax.fori_loop(0, C, take, 0)

    def plane_sum(level, carry):
        total = chip[level, e].astype(f32)
        for k, _, device in planes:
            plane_copy(level, k, device).wait_recv()
            total = total + plane_parts[level, k].astype(f32)
        level_part[level] = total.astype(bf16)
        return carry

    def keep_copy(j, at, place):
        target = (own_gate, own_up, own_down)[j]
        where = target.at[:, pl.ds(at, step)] if j == 2 else target.at[pl.ds(at, step)]
        return pltpu.make_async_copy(kept.at[place], where, ks.at[place])

    def send_copy(j, at, place):
        target = (other_gate, other_up, other_down)[j]
        where = target.at[:, pl.ds(at, step)] if j == 2 else target.at[pl.ds(at, step)]
        return remote(sent.at[place], where, xs.at[place], xr.at[place], sibling)

    kept_copies, sent_copies = [], []
    for copy in hidden_copies:
        copy.wait()
    for item in range(2 * count):
        wide_copy(item).wait()
        at = (item % count) * step
        left = wide[item % 2]
        for j in (0, 1) if item < count else (2,):
            place = len(sent_copies)

            def product(core):
                part = hidden[j, :, pl.ds(pl.multiple_of(core * half, half), half)]
                return contract(part, left, (0, 0)) if j == 2 else contract(left, part, (0, 0))

            sent[place] = product(1 - d).astype(bf16)
            copy = send_copy(j, at, place)
            copy.start()
            sent_copies.append(copy)
            if place >= 2:
                kept_copies[place - 2].wait()
            kept[place % 2] = product(d)
            copy = keep_copy(j, at, place % 2)
            copy.start()
            kept_copies.append(copy)
        if item + 2 < 2 * count:
            wide_copy(item + 2).start()
        if item == count - 1:
            lax.fori_loop(0, C, plane_sum, 0)
            level_copies = []
            for i, level, device in levels:
                copy = remote(level_part.at[level], proj.at[c], zs.at[i], zr.at[i], device)
                copy.start()
                level_copies.append(copy)
            proj[c] = level_part[c]

    for copy in kept_copies[-2:]:
        copy.wait()
    for copy in sent_copies + level_copies + head_copies:
        copy.wait()

    def done(level, carry):
        chip_copy(level).wait_send()
        for k, _, device in planes:
            plane_copy(level, k, device).wait_send()
        return carry

    lax.fori_loop(0, C, done, 0)


def middle(E, C, G, rows, mixed, grads, x, pair, gate_back, up_back, act, collective, name):
    batches, run, width = rows.shape
    count = C * G
    part = mixed.shape[3]
    block = E * part
    total, units = act.shape
    half = units // G
    step = min(512, width)
    items = 3 * (width // step)
    tall = (width, half)
    flat = (half, width)
    return call(
        functools.partial(middle_kernel, E, C, G),
        (rows, mixed, grads, x, pair, gate_back, up_back, act),
        (
            jax.ShapeDtypeStruct((batches, count, run, width // count), bf16),
            jax.ShapeDtypeStruct((C, part, width), bf16),
            jax.ShapeDtypeStruct(tall, f32),
            jax.ShapeDtypeStruct(tall, f32),
            jax.ShapeDtypeStruct(flat, f32),
            jax.ShapeDtypeStruct(tall, bf16),
            jax.ShapeDtypeStruct(tall, bf16),
            jax.ShapeDtypeStruct(flat, bf16),
        ),
        [ANY, VMEM, VMEM] + [ANY] * 5,
        (ANY, VMEM) + (ANY,) * 6,
        [
            pltpu.VMEM((3, total, units), bf16),
            pltpu.VMEM((2, total, step), bf16),
            pltpu.VMEM((2, step, half), f32),
            pltpu.VMEM((items, step, half), bf16),
            pltpu.VMEM((C, block, width), bf16),
            pltpu.VMEM((C, block, width), bf16),
            pltpu.VMEM((C, E, part, width), bf16),
            pltpu.VMEM((C, E, part, width), bf16),
            pltpu.VMEM((C, part, width), bf16),
            DMA((batches, count)),
            DMA((batches, count)),
            DMA((batches,)),
            DMA((C,)),
            DMA((C,)),
            DMA((C, E)),
            DMA((C, E)),
            DMA((C,)),
            DMA((C,)),
            DMA((3,)),
            DMA((2,)),
            DMA((2,)),
            DMA((items,)),
            DMA((items,)),
        ],
        collective,
        name,
        vmem=60,
    )


def finish_kernel(
    E,
    C,
    G,
    raw,
    w_qkv,
    normed,
    small,
    first,
    out_qkv,
    out_small,
    small_parts,
    small_sum,
    swap,
    swapped,
    own,
    passed,
    tokens,
    parts,
    plane_parts,
    sum_qkv,
    cs,
    cr,
    zs,
    zr,
    ts,
    qs,
    qr,
    os,
    orr,
    ss,
    sr,
    fs,
    fr,
):
    e, c, d = position()
    me, peers = column_peers(E, C, G)
    planes = plane_peers(E)
    batches, _, run, columns = raw.shape
    width = w_qkv.shape[0]
    rows = batches * run
    sibling = (e, c, 1 - d)
    meet([device for _, _, device in peers] + [device for _, _, device in planes])
    block = tokens.shape[2]

    def token_copy(item):
        plane = lax.rem(e + 1 + item, E)
        return pltpu.make_async_copy(
            normed.at[:, pl.ds(pl.multiple_of(plane * block, block), block)],
            tokens.at[item % 2],
            ts.at[item % 2],
        )

    token_copy(0).start()
    token_copy(1).start()
    small_copies = [
        remote(small.at[plane], small_parts.at[i], ss.at[i], sr.at[i], device)
        for i, plane, device in planes
    ]
    for copy in small_copies:
        copy.start()

    def product(level, core, at, size):
        left = jnp.concatenate([raw[b, level * G + core] for b in range(batches)], axis=0)
        return contract(left, w_qkv[at : at + size, :], (1, 1))

    def chip_copy(level):
        return remote(swap.at[level], swapped.at[level], cs.at[level], cr.at[level], sibling)

    def give(level):
        for at in range(0, width, 512):
            swap[level, :, at : at + 512] = product(level, 1 - d, at, 512).astype(bf16)
        chip_copy(level).start()

    def take(level):
        chip_copy(level).wait_recv()
        for at in range(0, width, 512):
            part = product(level, d, at, 512) + swapped[level, :, at : at + 512].astype(f32)
            own[level, :, at : at + 512] = part.astype(bf16)

    def hop(way, level, b):
        there = c + 1 if way == 0 else c - 1
        to = level if way == 0 else level + (C - level) * ((C - 1 - (there - level)) // (C - 1))
        return remote(
            own.at[level, pl.ds(b * run, run)],
            passed.at[to, pl.ds(b * run, run)],
            zs.at[way, level, b],
            zr.at[to, b],
            (e, there, d),
        )

    def arrival(entry, b):
        part = passed.at[entry, pl.ds(b * run, run)]
        return remote(part, part, zs.at[0, 0, b], zr.at[entry, b], sibling)

    def send(way, level, last):
        for b in range(batches):

            @pl.when(last)
            def _():
                arrival(level, b).wait_recv()
                piece = pl.ds(b * run, run)
                own[level, piece] = (
                    own[level, piece].astype(f32) + passed[level, piece].astype(f32)
                ).astype(bf16)

            hop(way, level, b).start()

    order = [C - 1, 0] + list(range(C - 2, 0, -1))
    for level in order:
        give(level)

    def plane_copy(item):
        plane = lax.rem(e + 1 + item, E)
        return remote(
            parts.at[item],
            plane_parts.at[item],
            qs.at[item],
            qr.at[item],
            (plane, c, d),
        )

    raw_flat = raw[...].reshape(-1, columns)

    def weights(item):
        token_copy(item).wait()
        for at in range(0, columns, 256):
            size = min(256, columns - at)
            parts[item, :, at : at + size] = contract(
                tokens[item % 2], raw_flat[:, at : at + size], (0, 0)
            ).astype(bf16)
        if item + 2 < E:
            token_copy(item + 2).start()
        if item < E - 1:
            plane_copy(item).start()

    mirror = C - 1 - c
    items = list(range(E))
    for level in order:
        take(level)
        if level == 0:
            @pl.when(c == 0)
            def _():
                send(0, C - 1, False)

            @pl.when(c == C - 1)
            def _():
                send(1, 0, False)

            weights(items.pop(0))
    weights(items.pop(0))
    for turn in range(1, C - 1):

        @pl.when(c <= turn)
        def _():
            send(0, C - 1 - (turn - c), c > 0)

        @pl.when(mirror <= turn)
        def _():
            send(1, turn - mirror, mirror > 0)

        if items:
            weights(items.pop(0))
    while items:
        weights(items.pop(0))
    for item in range(E - 1):
        plane_copy(item).wait_recv()
    for at in range(0, block, 128):
        piece = pl.ds(at, min(128, block - at))
        total = parts[E - 1, piece].astype(f32)
        for item in range(E - 1):
            total = total + plane_parts[item, piece].astype(f32)
        sum_qkv[piece] = total.astype(bf16)
    share = block // (C * G)

    def row_copy(offset, index, device):
        return remote(
            sum_qkv.at[pl.ds(pl.multiple_of(index * share, share), share)],
            out_qkv.at[me],
            os.at[offset],
            orr.at[offset],
            device,
        )

    def small_copy(offset, index, device):
        return remote(
            small_sum.at[pl.ds(pl.multiple_of(index * share, share), share)],
            out_small.at[me],
            fs.at[offset],
            fr.at[offset],
            device,
        )

    for copy in small_copies:
        copy.wait_recv()
    total = small[e]
    for i in range(1, E):
        total = total + small_parts[i]
    small_sum[...] = total
    for offset, index, device in peers:
        small_copy(offset, index, device).start()
        row_copy(offset, index, device).start()
    out_small[me] = small_sum[pl.ds(pl.multiple_of(me * share, share), share)]
    out_qkv[me] = sum_qkv[pl.ds(pl.multiple_of(me * share, share), share)]

    def arrived(entry):
        for b in range(batches):
            arrival(entry, b).wait_recv()

    @pl.when(c > 0)
    def _():
        arrived(c)

    @pl.when(c < C - 1)
    def _():
        arrived(C)

    for at in range(0, width, 512):
        first[:, at : at + 512] = own[c, :, at : at + 512].astype(f32)

    @pl.when(c > 0)
    def _():
        for at in range(0, width, 512):
            first[:, at : at + 512] += passed[c, :, at : at + 512].astype(f32)

    @pl.when(c < C - 1)
    def _():
        for at in range(0, width, 512):
            first[:, at : at + 512] += passed[C, :, at : at + 512].astype(f32)

    for level in range(C):
        chip_copy(level).wait_send()
        for b in range(batches):

            @pl.when(level > c)
            def _():
                hop(0, level, b).wait_send()

            @pl.when(level < c)
            def _():
                hop(1, level, b).wait_send()

    for item in range(E - 1):
        plane_copy(item).wait_send()
    for copy in small_copies:
        copy.wait_send()
    for offset, index, device in peers:
        row_copy(offset, index, device).wait()
        small_copy(offset, index, device).wait()


def finish(E, C, G, raw, w_qkv, normed, small, collective, name):
    batches, count, run, columns = raw.shape
    width = w_qkv.shape[0]
    every = normed.shape[0]
    rows = batches * run
    block = width // E
    share = block // count
    lanes = small.shape[2]
    by_level = pltpu.VMEM((C, rows, width), bf16)
    return call(
        functools.partial(finish_kernel, E, C, G),
        (raw, w_qkv, normed, small),
        (
            jax.ShapeDtypeStruct((rows, width), f32),
            jax.ShapeDtypeStruct((count, share, columns), bf16),
            jax.ShapeDtypeStruct((count, share, lanes), f32),
        ),
        [VMEM, VMEM, ANY, VMEM],
        (VMEM, VMEM, VMEM),
        [
            pltpu.VMEM((E, block, lanes), f32),
            pltpu.VMEM((block, lanes), f32),
            by_level,
            by_level,
            by_level,
            pltpu.VMEM((C + 1, rows, width), bf16),
            pltpu.VMEM((2, every, block), bf16),
            pltpu.VMEM((E, block, columns), bf16),
            pltpu.VMEM((E, block, columns), bf16),
            pltpu.VMEM((block, columns), bf16),
            DMA((C,)),
            DMA((C,)),
            DMA((2, C, batches)),
            DMA((C + 1, batches)),
            DMA((2,)),
            DMA((E,)),
            DMA((E,)),
            DMA((count,)),
            DMA((count,)),
            DMA((E,)),
            DMA((E,)),
            DMA((count,)),
            DMA((count,)),
        ],
        collective,
        name,
        vmem=60,
    )


def contract(left, right, axes):
    return lax.dot_general(left, right, ((axes[:1], axes[1:]), ((), ())), preferred_element_type=f32)


def query_blocks(length):
    size = min(256, length)
    return [(i, size, min(length, i + 2 * size)) for i in range(0, length, size)]


def attend_kernel(scale, queries, keys, values, row_ids, key_ids, mixed, log_total):
    length = queries.shape[1]
    for first, size, seen in query_blocks(length):
        rows = pl.ds(first, size)
        scores = contract(queries[0, rows], keys[0, :seen], (1, 1)) * scale
        scores = jnp.where(key_ids[0, :, :seen] <= row_ids[0, rows], scores, MASKED)
        peak = jnp.max(scores, axis=1, keepdims=True)
        grown = jnp.exp(scores - peak)
        total = jnp.sum(grown, axis=1, keepdims=True)
        probs = (grown * (1.0 / total)).astype(bf16)
        mixed[0, rows] = jnp.dot(probs, values[0, :seen], preferred_element_type=f32).astype(bf16)
        log_total[0, 0, rows] = peak + jnp.log(total)


def attend_back_kernel(
    scale, queries, keys, values, grads, row_ids, key_ids, log_total, query_grad, key_grad, value_grad
):
    length = queries.shape[1]
    key_grad[...] = jnp.zeros_like(key_grad)
    value_grad[...] = jnp.zeros_like(value_grad)
    for first, size, seen in query_blocks(length):
        rows = pl.ds(first, size)
        query, grad = queries[0, rows], grads[0, rows]
        scores = contract(query, keys[0, :seen], (1, 1)) * scale
        scores = jnp.where(key_ids[0, :, :seen] <= row_ids[0, rows], scores, MASKED)
        probs = jnp.exp(scores - log_total[0, 0, rows])
        prod = contract(grad, values[0, :seen], (1, 1))
        delta = jnp.sum(probs * prod, axis=1, keepdims=True)
        score_grad = (probs * (prod - delta)).astype(bf16)
        query_grad[0, rows] = jnp.dot(score_grad, keys[0, :seen], preferred_element_type=f32) * scale
        key_grad[0, :seen] += contract(score_grad, query, (0, 0)) * scale
        value_grad[0, :seen] += contract(probs.astype(bf16), grad, (0, 0))


def attention_specs(length):
    head = pl.BlockSpec((1, length, HEAD), lambda b, h: (b, 0, h))
    row_ids = pl.BlockSpec((1, length, 1), lambda b, h: (b, 0, 0))
    key_ids = pl.BlockSpec((1, 1, length), lambda b, h: (b, 0, 0))
    log_total = pl.BlockSpec((1, 1, length, 1), lambda b, h: (b, h, 0, 0))
    return head, row_ids, key_ids, log_total


def attend(queries, keys, values, ids):
    batches, length, size = queries.shape
    heads = size // HEAD
    head, row_ids, key_ids, log_total = attention_specs(length)
    return pl.pallas_call(
        functools.partial(attend_kernel, HEAD**-0.5),
        grid=(batches, heads),
        out_shape=(
            jax.ShapeDtypeStruct(queries.shape, bf16),
            jax.ShapeDtypeStruct((batches, heads, length, 1), f32),
        ),
        in_specs=[head, head, head, row_ids, key_ids],
        out_specs=(head, log_total),
        compiler_params=pltpu.CompilerParams(vmem_limit_bytes=48 * MIB),
        name="attend",
    )(queries, keys, values, ids[:, :, None], ids[:, None, :])


def attend_back(queries, keys, values, grads, ids, totals):
    batches, length, size = queries.shape
    heads = size // HEAD
    head, row_ids, key_ids, log_total = attention_specs(length)
    grad = jax.ShapeDtypeStruct(queries.shape, f32)
    return pl.pallas_call(
        functools.partial(attend_back_kernel, HEAD**-0.5),
        grid=(batches, heads),
        out_shape=(grad, grad, grad),
        in_specs=[head, head, head, head, row_ids, key_ids, log_total],
        out_specs=(head, head, head),
        compiler_params=pltpu.CompilerParams(vmem_limit_bytes=48 * MIB),
        name="attend_back",
    )(queries, keys, values, grads, ids[:, :, None], ids[:, None, :], totals)


def rms_factor(values):
    return lax.rsqrt(jnp.mean(values * values, axis=-1, keepdims=True) + EPSILON)


def norm_back(grad_hat, hatted, factor):
    return factor * (grad_hat - hatted * jnp.mean(grad_hat * hatted, axis=-1, keepdims=True))


def slot_table(routes, experts):
    batches, run, top = routes.shape
    hits = jnp.swapaxes(routes, 1, 2)[:, :, :, None] == jnp.arange(experts, dtype=jnp.int32)
    ones = hits.astype(bf16)
    tokens, ranks = jnp.arange(run), jnp.arange(top)
    before = (tokens[None, :] < tokens[:, None]).astype(bf16)
    above = (ranks[None, :] < ranks[:, None]).astype(bf16)
    within = jnp.einsum("ts,bksx->bktx", before, ones, preferred_element_type=f32)
    totals = jnp.sum(hits.astype(f32), axis=2)
    earlier = jnp.einsum(
        "kj,bjx->bkx", above, totals.astype(bf16), preferred_element_type=f32
    )
    places = jnp.sum(jnp.where(hits, within + earlier[:, :, None, :], 0.0), axis=1)
    places = jnp.where(jnp.any(hits, axis=1), places, UNUSED_SLOT)
    return jnp.swapaxes(places, 1, 2)


def body(
    tokens,
    block_ids,
    routes,
    norm_gains,
    w_query,
    w_key,
    w_value,
    w_output,
    router,
    expert_gate,
    expert_up,
    expert_down,
    cotangent,
):
    E, C, G = lax.axis_size("expert"), lax.axis_size("context"), lax.axis_size("dp")
    batches, run, width = tokens.shape
    top = routes.shape[2]
    experts = E * C * expert_gate.shape[0]
    capacity = max(2, run * top // experts)
    count = C * G
    size = width // count
    length = count * run
    every = batches * length
    own = batches * run
    me = lax.axis_index("context") * G + lax.axis_index("dp")

    rows = w_query.shape[0]
    small_width = -(-(norm_gains.shape[1] + experts) // 128) * 128
    small = jnp.concatenate([norm_gains, router], axis=1)
    small = jnp.pad(small, ((0, 0), (0, small_width - small.shape[1])))
    pieces = [w.reshape(rows, count, size) for w in (w_query, w_key, w_value)]
    weights = jnp.swapaxes(jnp.concatenate(pieces, axis=2), 0, 1)
    places = slot_table(routes, experts).reshape(batches, E, C, run)
    by_level = jnp.transpose(places, (2, 0, 1, 3))
    by_expert = jnp.transpose(places, (1, 2, 0, 3))
    column, w_qkv, small, full_output, ids, slots = start(
        E, C, G, tokens, weights, small, w_output, block_ids, by_level
    )
    ids = jnp.swapaxes(ids, 0, 1).reshape(batches, length)
    w_qkv = w_qkv.reshape(width, 3 * size)
    small = small.reshape(width, small_width)
    full_output = full_output.reshape(width, width)
    gains = small[:, :4].astype(f32)
    full_router = small[:, 4 : 4 + experts]
    head_gains = lax.dynamic_slice(gains, (me * size, 0), (size, 4))

    column = column.reshape(every, width).astype(f32)
    normed = (column * rms_factor(column) * gains[:, 0]).astype(bf16)
    qkv = jnp.dot(normed, w_qkv, preferred_element_type=f32)
    query_raw, key_raw = qkv[:, :size], qkv[:, size : 2 * size]
    value_low = qkv[:, 2 * size :].astype(bf16)
    squares = jnp.stack([jnp.sum(query_raw * query_raw, axis=1), jnp.sum(key_raw * key_raw, axis=1)])
    factors = lax.rsqrt(column_sum(E, C, G, squares, 2, "squares") / width + EPSILON)
    query_factor, key_factor = factors[0][:, None], factors[1][:, None]
    query_hat, key_hat = query_raw * query_factor, key_raw * key_factor
    by_sequence = (batches, length, size)
    query_low = (query_hat * head_gains[:, 1]).astype(bf16).reshape(by_sequence)
    key_low = (key_hat * head_gains[:, 2]).astype(bf16).reshape(by_sequence)
    value_low = value_low.reshape(by_sequence)
    mixed_heads, log_total = attend(query_low, key_low, value_low, ids)
    mixed_low = to_tokens(
        E, C, G, mixed_heads.reshape(batches, count, run, size), 3, "mixed_rows"
    ).reshape(own, width)

    inputs = tokens.reshape(own, width).astype(f32)
    resid = inputs + jnp.dot(mixed_low, full_output, preferred_element_type=f32)
    second_factor = rms_factor(resid)
    second_hat = resid * second_factor
    second_low = (second_hat * gains[:, 3]).astype(bf16)
    logits = jnp.dot(second_low, full_router, preferred_element_type=f32)
    router_probs = jax.nn.softmax(logits, axis=-1)
    gate_table = jnp.transpose(router_probs.reshape(batches, run, E, C), (2, 3, 0, 1))
    table = jnp.concatenate([by_expert, gate_table], axis=2)[:, :, :, None, :]

    mixture, second_grad, x, _, pair_grad, act, gate_pre_grad, up_pre_grad, gate_grad = run_experts(
        E,
        C,
        second_low.reshape(batches, run, width),
        cotangent,
        slots,
        table,
        expert_gate[0],
        expert_up[0],
        expert_down[0],
        capacity,
        4,
        "experts",
    )
    slot_count = E * C * batches * capacity
    x, pair_grad, act, gate_pre_grad, up_pre_grad = (
        rows.reshape(slot_count, -1) for rows in (x, pair_grad, act, gate_pre_grad, up_pre_grad)
    )
    upstream = cotangent.reshape(own, width).astype(f32)
    mixture = jnp.sum(mixture.astype(f32), axis=0).reshape(own, width)
    activations = (resid + mixture).astype(bf16).reshape(tokens.shape)
    prob_grad = jnp.transpose(gate_grad[:, :, :, 0, :], (2, 3, 0, 1)).reshape(own, experts)
    logit_grad = router_probs * (
        prob_grad - jnp.sum(router_probs * prob_grad, axis=-1, keepdims=True)
    )
    logit_grad = logit_grad.astype(bf16)
    second_grad = jnp.sum(second_grad.astype(f32), axis=0).reshape(own, width)
    second_grad = second_grad + contract(logit_grad, full_router, (1, 1))
    gain_second = jnp.sum(second_grad * second_hat, axis=0)
    resid_grad = upstream + norm_back(second_grad * gains[:, 3], second_hat, second_factor)
    attn_grad = resid_grad.astype(bf16)
    mixed_grad = contract(attn_grad, full_output, (1, 1)).astype(bf16)

    mixed_grad, grad_proj, *expert_grads = middle(
        E,
        C,
        G,
        mixed_grad.reshape(batches, run, width),
        jnp.swapaxes(mixed_low, 0, 1).reshape(E, C, G, rows, own),
        attn_grad,
        x,
        pair_grad,
        gate_pre_grad,
        up_pre_grad,
        act,
        6,
        "middle",
    )
    grad_gate, grad_up, grad_down = (
        (mine + other.astype(f32))[None] for mine, other in zip(expert_grads[:3], expert_grads[3:])
    )
    grad_proj = jnp.sum(grad_proj.astype(f32), axis=0)
    query_grad, key_grad, value_grad = (
        grad.reshape(every, size)
        for grad in attend_back(
            query_low, key_low, value_low, mixed_grad.reshape(by_sequence), ids, log_total
        )
    )
    query_back, key_back = query_grad * head_gains[:, 1], key_grad * head_gains[:, 2]
    means = jnp.stack([jnp.sum(query_back * query_hat, axis=1), jnp.sum(key_back * key_hat, axis=1)])
    means = column_sum(E, C, G, means, 7, "norm_means") / width
    raw_grads = jnp.concatenate(
        [
            (query_factor * (query_back - query_hat * means[0][:, None])).astype(bf16),
            (key_factor * (key_back - key_hat * means[1][:, None])).astype(bf16),
            value_grad.astype(bf16),
        ],
        axis=1,
    )
    gain_heads = jnp.stack(
        [jnp.sum(query_grad * query_hat, axis=0), jnp.sum(key_grad * key_hat, axis=0)], axis=1
    )
    gain_heads = lax.dynamic_update_slice(
        jnp.zeros((width, 2), f32), gain_heads, (me * size, 0)
    )
    sums = jnp.concatenate(
        [gain_heads, gain_second[:, None], contract(second_low, logit_grad, (0, 0))], axis=1
    )
    sums = jnp.pad(sums, ((0, 0), (0, small_width - sums.shape[1])))
    first_grad, grad_qkv, sums = finish(
        E,
        C,
        G,
        raw_grads.reshape(batches, count, run, 3 * size),
        w_qkv,
        normed,
        sums.reshape(E, width // E, small_width),
        8,
        "finish",
    )
    sums = jnp.sum(sums, axis=0)
    first_factor = rms_factor(inputs)
    first_hat = inputs * first_factor
    input_grad = resid_grad + norm_back(first_grad * gains[:, 0], first_hat, first_factor)

    grad_qkv = jnp.swapaxes(grad_qkv.astype(f32), 0, 1)
    grad_query, grad_key, grad_value = (
        grad_qkv[:, :, i * size : (i + 1) * size].reshape(rows, width) for i in range(3)
    )
    gain_first = sum(
        jnp.sum(w.astype(f32) * grad, axis=1)
        for w, grad in ((w_query, grad_query), (w_key, grad_key), (w_value, grad_value))
    )
    gain_first = gain_first / norm_gains[:, 0].astype(f32)
    grad_gains = jnp.concatenate([gain_first[:, None], sums[:, :3]], axis=1)
    return (
        activations,
        input_grad.reshape(tokens.shape),
        grad_gains,
        grad_query,
        grad_key,
        grad_value,
        grad_proj,
        sums[:, 3 : 3 + experts],
        grad_gate,
        grad_up,
        grad_down,
    )


def solution(mesh):
    by_token = ("context", "dp")
    by_expert = P(("expert", "context"), None, None)
    by_row = P(ALL_AXES, None)
    rows = P("expert", by_token, None)
    return jax.shard_map(
        body,
        mesh=mesh,
        in_specs=(
            rows,
            P("expert", by_token),
            rows,
            by_row,
            by_row,
            by_row,
            by_row,
            by_row,
            by_row,
            by_expert,
            by_expert,
            by_expert,
            rows,
        ),
        out_specs=(
            rows,
            rows,
            by_row,
            by_row,
            by_row,
            by_row,
            by_row,
            by_row,
            P(("expert", "context"), None, "dp"),
            P(("expert", "context"), None, "dp"),
            P(("expert", "context"), "dp", None),
        ),
        check_vma=False,
    )
```

```python
import functools

import jax
import jax.numpy as jnp
from jax import lax
from jax.experimental import pallas as pl
from jax.experimental.pallas import tpu as pltpu
from jax.sharding import PartitionSpec as P

HEAD = 128
EPSILON = 1e-05
MASKED = -1e30
UNUSED_SLOT = 4096.0
ALL_AXES = ("expert", "context", "dp")
MESH = pl.DeviceIdType.MESH
ANY = pl.BlockSpec(memory_space=pl.ANY)
VMEM = pl.BlockSpec(memory_space=pltpu.VMEM)
DMA = pltpu.SemaphoreType.DMA
MIB = 1 << 20
f32 = jnp.float32
bf16 = jnp.bfloat16


def call(kernel, operands, out_shapes, in_specs, out_specs, scratch, collective, name, vmem=32):
    return pl.pallas_call(
        kernel,
        out_shape=out_shapes,
        in_specs=in_specs,
        out_specs=out_specs,
        scratch_shapes=scratch,
        compiler_params=pltpu.CompilerParams(
            collective_id=collective, has_side_effects=True, vmem_limit_bytes=vmem * MIB
        ),
        name=name,
    )(*operands)


def position():
    return lax.axis_index("expert"), lax.axis_index("context"), lax.axis_index("dp")


def meet(devices):
    barrier = pltpu.get_barrier_semaphore()
    for device in devices:
        pl.semaphore_signal(barrier, inc=1, device_id=device, device_id_type=MESH)
    pl.semaphore_wait(barrier, len(devices))


def remote(source, target, send_sem, recv_sem, device):
    return pltpu.make_async_remote_copy(
        src_ref=source,
        dst_ref=target,
        send_sem=send_sem,
        recv_sem=recv_sem,
        device_id=device,
        device_id_type=MESH,
    )


def column_peers(E, C, G):
    e, c, d = position()
    me = c * G + d
    peers = []
    for offset in range(1, C * G):
        index = lax.rem(me + offset, C * G)
        peers.append((offset, index, (e, index // G, lax.rem(index, G))))
    return me, peers


def plane_peers(E):
    e, c, d = position()
    return [(i, lax.rem(e + i, E), (lax.rem(e + i, E), c, d)) for i in range(1, E)]


def level_peers(C):
    e, c, d = position()
    return [(i, lax.rem(c + i, C), (e, lax.rem(c + i, C), d)) for i in range(1, C)]


def start_kernel(
    E,
    C,
    G,
    tokens,
    weights,
    small_weights,
    output,
    ids,
    slots,
    column,
    gathered,
    small_gathered,
    full_output,
    ids_out,
    slots_out,
    ws,
    wr,
    bs,
    br,
    hs,
    hr,
    ts,
    tr,
    ls,
    ms,
    mr,
    ps,
    pr,
    fs,
    fr,
    gs,
    gr,
):
    e, c, d = position()
    me, peers = column_peers(E, C, G)
    planes = plane_peers(E)
    batches = tokens.shape[0]
    sibling = (e, c, 1 - d)
    meet([device for _, _, device in peers] + [device for _, _, device in planes])
    kinds = ((weights, gathered), (small_weights, small_gathered))
    weight_copies = []
    for j, (source, target) in enumerate(kinds):
        for offset, index, device in peers:
            part = source.at[index] if j == 0 else source
            weight_copies.append(
                remote(part, target.at[e, me], ws.at[j, offset], wr.at[j, offset], device)
            )
    for copy in weight_copies:
        copy.start()
    local = [
        pltpu.make_async_copy(weights.at[me], gathered.at[e, me], ls.at[0]),
        pltpu.make_async_copy(small_weights, small_gathered.at[e, me], ls.at[1]),
        pltpu.make_async_copy(output, full_output.at[e, c, d], ls.at[2]),
    ]
    for b in range(batches):
        local.append(pltpu.make_async_copy(tokens.at[b], column.at[b, me], ls.at[3 + b]))
    for copy in local:
        copy.start()

    def source_of(item):
        return output if item == 0 else tokens.at[item - 1]

    def place(item, level):
        return full_output.at[e, level, d] if item == 0 else column.at[item - 1, level * G + d]

    def to_sibling(source, item, level, arrival):
        return remote(
            source, place(item, level), ts.at[item, arrival], tr.at[item, arrival], sibling
        )

    def step(hop, source, item, level, up):
        to = (e, c + 1, d) if up else (e, c - 1, d)
        way = 0 if up else 1
        return remote(
            source, place(item, level), hs.at[way, item, hop], hr.at[way, item, hop], to
        )

    def relay(item, hop):
        for up in (True, False):
            level = c - hop if up else c + hop
            here = (c >= hop) if up else (c + hop < C)
            onward = (c < C - 1) if up else (c > 0)

            @pl.when(here)
            def _():
                landed = place(item, level)
                step(hop - 1, landed, item, level, up).wait_recv()
                if hop < C - 1:

                    @pl.when(onward)
                    def _():
                        step(hop, landed, item, level, up).start()

                if G > 1:
                    to_sibling(landed, item, level, hop if up else C - 1 + hop).start()

    for item in range(batches + 1):

        @pl.when(c < C - 1)
        def _():
            step(0, source_of(item), item, c, True).start()

        @pl.when(c > 0)
        def _():
            step(0, source_of(item), item, c, False).start()

        if G > 1:
            to_sibling(source_of(item), item, c, 0).start()
    small = []
    for offset, _, device in peers:
        small.append(remote(ids, ids_out.at[me], ms.at[offset], mr.at[offset], device))
    for i, level, device in level_peers(C):
        small.append(remote(slots.at[level], slots_out.at[i], ps.at[i], pr.at[i], device))
    for copy in small:
        copy.start()
    ids_out[me] = ids[...]
    slots_out[0] = slots[c]
    for copy in weight_copies:
        copy.wait_recv()
    for copy in local[:3]:
        copy.wait()
    plane_copies = []
    for j, (_, target) in enumerate(kinds):
        for i, _, device in planes:
            copy = remote(target.at[e], target.at[e], bs.at[j, i], br.at[j, i], device)
            copy.start()
            plane_copies.append(copy)
    for hop in range(1, C):
        relay(0, hop)

    def output_copy(i, plane, device):
        mine = full_output.at[e, :, d]
        return remote(mine, mine, fs.at[i], fr.at[i], device)

    def output_sibling(i):
        part = full_output.at[lax.rem(e + E - i, E), :, d]
        return remote(part, part, gs.at[i], gr.at[i], sibling)

    for i, plane, device in planes:
        output_copy(i, plane, device).start()
    for hop in range(1, C):
        for item in range(1, batches + 1):
            relay(item, hop)
    for i, plane, device in planes:
        output_copy(i, plane, device).wait_recv()
        if G > 1:
            output_sibling(i).start()

    for item in range(batches + 1):
        if G > 1:
            to_sibling(source_of(item), item, c, 0).wait()
        for hop in range(C - 1):
            for up in (True, False):
                arrival = hop + 1 if up else C + hop
                origin = c - hop if up else c + hop
                if up:
                    sends = jnp.logical_and(origin >= 0, c < C - 1)
                    arrives = c >= hop + 1
                else:
                    sends = jnp.logical_and(origin < C, c > 0)
                    arrives = c + hop + 1 < C

                @pl.when(sends)
                def _():
                    step(hop, source_of(item), item, c, up).wait_send()

                if G > 1:

                    @pl.when(arrives)
                    def _():
                        to_sibling(source_of(item), item, c, arrival).wait()

    for i, plane, device in planes:
        output_copy(i, plane, device).wait_send()
        if G > 1:
            output_sibling(i).wait()
    for copy in weight_copies:
        copy.wait_send()
    for copy in plane_copies + small + local[3:]:
        copy.wait()


def start(E, C, G, tokens, weights, small_weights, output, ids, slots):
    batches, run, width = tokens.shape
    count = C * G
    rows, columns = weights.shape[1:]
    items = batches + 1
    return call(
        functools.partial(start_kernel, E, C, G),
        (tokens, weights, small_weights, output, ids, slots),
        (
            jax.ShapeDtypeStruct((batches, count, run, width), tokens.dtype),
            jax.ShapeDtypeStruct((E, count, rows, columns), weights.dtype),
            jax.ShapeDtypeStruct((E, count) + small_weights.shape, weights.dtype),
            jax.ShapeDtypeStruct((E, C, G, rows, width), weights.dtype),
            jax.ShapeDtypeStruct((count,) + ids.shape, ids.dtype),
            jax.ShapeDtypeStruct(slots.shape, slots.dtype),
        ),
        [ANY, ANY, ANY, ANY, VMEM, VMEM],
        (ANY, ANY, ANY, ANY, VMEM, VMEM),
        [
            DMA((2, count)),
            DMA((2, count)),
            DMA((2, E)),
            DMA((2, E)),
            DMA((2, items, C)),
            DMA((2, items, C)),
            DMA((items, 2 * C)),
            DMA((items, 2 * C)),
            DMA((items + 2,)),
            DMA((count,)),
            DMA((count,)),
            DMA((C,)),
            DMA((C,)),
            DMA((E,)),
            DMA((E,)),
            DMA((E,)),
            DMA((E,)),
        ],
        1,
        "start",
    )


def share_kernel(E, C, G, part, parts, ss, rs):
    me, peers = column_peers(E, C, G)
    meet([device for _, _, device in peers])
    copies = []
    for offset, _, device in peers:
        copy = remote(part, parts.at[me], ss.at[offset], rs.at[offset], device)
        copy.start()
        copies.append(copy)
    parts[me] = part[...]
    for copy in copies:
        copy.wait()


def column_sum(E, C, G, part, collective, name):
    parts = call(
        functools.partial(share_kernel, E, C, G),
        (part,),
        jax.ShapeDtypeStruct((C * G,) + part.shape, part.dtype),
        [VMEM],
        VMEM,
        [DMA((C * G,)), DMA((C * G,))],
        collective,
        name,
    )
    return jnp.sum(parts, axis=0)


def choose(slots, count):
    cells = lax.broadcasted_iota(jnp.int32, (count, slots.shape[1]), 0).astype(f32)
    return jnp.concatenate(
        [(cells == slots[i : i + 1, :]).astype(bf16) for i in range(slots.shape[0])], axis=0
    )


class Flow:
    def __init__(self, E, C, rows, slots, landed, packed, target, own, zs, zr, xs, xr, stay):
        self.E, self.C, self.rows, self.slots = E, C, rows, slots
        self.landed, self.packed, self.target = landed, packed, target
        self.sems = own, zs, zr, xs, xr, stay
        self.e, self.c, self.d = position()
        self.batches = rows.shape[0]
        self.cap, self.width = target.shape[3:]
        self.kept = packed.shape[0]
        self.chunks = self.batches * C

    def level_entry(self, far):
        high = 2 * self.c // self.C
        return high * far + (1 - high) * lax.rem(self.C - far, self.C)

    def own(self, b):
        return pltpu.make_async_copy(self.rows.at[b], self.landed.at[0, b], self.sems[0].at[b])

    def hop(self, b, i, way):
        there = i + 1 if way == 0 else lax.rem(i + self.C - 1, self.C)
        level = lax.rem(self.c + (1 if way == 0 else self.C - 1), self.C)
        return remote(
            self.landed.at[i, b],
            self.landed.at[there, b],
            self.sems[1].at[way, i, b],
            self.sems[2].at[there, b],
            (self.e, level, self.d),
        )

    def arrival(self, b, i):
        entry = self.landed.at[i, b]
        return remote(
            entry,
            entry,
            self.sems[1].at[0, i, b],
            self.sems[2].at[i, b],
            (self.e, self.c, 1 - self.d),
        )

    def onward(self, i, way):
        if way == 0:
            return jnp.logical_and(i <= self.c, self.c < self.C - 1)
        return jnp.logical_and(lax.rem(self.C - i, self.C) + self.c < self.C, self.c > 0)

    def begin(self):
        for b in range(self.batches):
            self.own(b).start()
        for b in range(self.batches):
            self.own(b).wait()
            for way in range(2):

                @pl.when(self.onward(0, way))
                def _():
                    self.hop(b, 0, way).start()

    def relay(self, far, b):
        for way in range(2):
            i = far if way == 0 else self.C - far

            @pl.when((far <= self.c) if way == 0 else (far + self.c < self.C))
            def _():
                self.arrival(b, i).wait_recv()

                @pl.when(self.onward(i, way))
                def _():
                    self.hop(b, i, way).start()

    def hops_sent(self, b, i):
        for way in range(2):

            @pl.when(self.onward(i, way))
            def _():
                self.hop(b, i, way).wait_send()

    def across(self, n, b, i, k):
        plane = lax.rem(self.e + k, self.E)
        return remote(
            self.packed.at[lax.rem(n, self.kept), plane],
            self.target.at[i, b, k],
            self.sems[3].at[i, b, k],
            self.sems[4].at[i, b, k],
            (plane, self.c, self.d),
        )

    def stay(self, n, b, i):
        return pltpu.make_async_copy(
            self.packed.at[lax.rem(n, self.kept), self.e],
            self.target.at[i, b, 0],
            self.sems[5].at[i, b],
        )

    def compact(self, n, b, i):
        place = lax.rem(n, self.kept)
        picks = choose(self.slots[i, b], self.cap)
        for at in range(0, self.width, 512):
            part = jnp.dot(
                picks, self.landed[i, b, :, at : at + 512], preferred_element_type=f32
            ).astype(bf16)
            self.packed[place, :, :, at : at + 512] = part.reshape(self.E, self.cap, 512)
        for k in range(1, self.E):
            self.across(n, b, i, k).start()
        self.stay(n, b, i).start()

    def crossed(self, n, b, i):
        for k in range(1, self.E):
            self.across(n, b, i, k).wait_send()

    def arrived(self, n, b, i):
        for k in range(1, self.E):
            self.across(n, b, i, k).wait_recv()

    @staticmethod
    def scratch(E, C, batches, run, width, cap, kept):
        return [
            pltpu.VMEM((C, batches, run, width), bf16),
            pltpu.VMEM((kept, E, cap, width), bf16),
            DMA((batches,)),
            DMA((2, C, batches)),
            DMA((C, batches)),
            DMA((C, batches, E)),
            DMA((C, batches, E)),
            DMA((C, batches)),
        ]


def forward_kernel(
    E,
    C,
    G,
    column,
    gain,
    head_gains,
    w_qkv,
    row_ids,
    key_ids,
    slots,
    upstream,
    normed,
    queries,
    keys,
    values,
    query_hat,
    key_hat,
    log_total,
    factors,
    mixed,
    u_out,
    raw,
    low,
    squares,
    parts,
    heads,
    landed,
    packed,
    own,
    zs,
    zr,
    xs,
    xr,
    stay,
    raw_sem,
    low_sem,
    ss,
    sr,
    ms,
    mr,
    ml,
):
    me, peers = column_peers(E, C, G)
    planes = plane_peers(E)
    every, width = column.shape
    batches, length, size = heads.shape
    run = length // (C * G)
    block = raw.shape[1]
    blocks = every // block
    scale = HEAD**-0.5
    meet([device for _, _, device in peers] + [device for _, _, device in planes])
    flow = Flow(E, C, upstream, slots, landed, packed, u_out, own, zs, zr, xs, xr, stay)

    def load(j):
        at = pl.multiple_of(j * block, block)
        place = lax.rem(j, 2)
        return pltpu.make_async_copy(column.at[pl.ds(at, block)], raw.at[place], raw_sem.at[place])

    def store(j):
        at = pl.multiple_of(j * block, block)
        place = lax.rem(j, 2)
        return pltpu.make_async_copy(low.at[place], normed.at[pl.ds(at, block)], low_sem.at[place])

    def chunk_of(n):
        return n % batches, flow.level_entry(n // batches)

    chunk = iter(range(flow.chunks))

    def carry_on(count):
        for _ in range(count):
            n = next(chunk, None)
            if n is None:
                return
            if n >= flow.kept:
                before = n - flow.kept, *chunk_of(n - flow.kept)
                flow.crossed(*before)
                flow.stay(*before).wait()
            if n >= batches:
                flow.relay(n // batches, n % batches)
            flow.compact(n, *chunk_of(n))

    load(0).start()
    load(1).start()
    flow.begin()
    carry_on(batches)
    ones = jnp.ones((8, size), f32)

    def project(j, carry):
        place = lax.rem(j, 2)
        rows = pl.ds(pl.multiple_of(j * block, block), block)
        load(j).wait()

        @pl.when(j >= 2)
        def _():
            store(j - 2).wait()

        total = jnp.zeros((block, 1), f32)
        for at in range(0, width, 512):
            part = raw[place, :, at : at + 512].astype(f32)
            total += jnp.sum(part * part, axis=1, keepdims=True)
        factor = lax.rsqrt(total / width + EPSILON)
        for at in range(0, width, 512):
            part = raw[place, :, at : at + 512].astype(f32) * factor
            low[place, :, at : at + 512] = (part * gain[:, at : at + 512]).astype(bf16)
        store(j).start()

        @pl.when(j + 2 < blocks)
        def _():
            load(j + 2).start()

        for kind in range(3):
            part = jnp.dot(
                low[place],
                w_qkv[:, kind * size : (kind + 1) * size],
                preferred_element_type=f32,
            )
            if kind == 2:
                values[rows] = part.astype(bf16)
            else:
                (query_hat, key_hat)[kind][rows] = part
                sums = lax.dot_general(
                    ones,
                    part * part,
                    (((1,), (1,)), ((), ())),
                    precision=lax.Precision.HIGHEST,
                    preferred_element_type=f32,
                )
                squares[kind, :, rows] = sums[:1]
        return carry

    half = blocks // 2
    lax.fori_loop(0, half, project, 0)
    carry_on(1)
    lax.fori_loop(half, blocks, project, 0)
    shares = [
        remote(squares, parts.at[me], ss.at[offset], sr.at[offset], device)
        for offset, _, device in peers
    ]
    for copy in shares:
        copy.start()
    parts[me] = squares[...]
    carry_on(1)
    for copy in shares:
        copy.wait_recv()
    total = parts[0]
    for index in range(1, C * G):
        total = total + parts[index]
    factors[...] = lax.rsqrt(total / width + EPSILON)
    rows_at = lax.broadcasted_iota(jnp.int32, (block, block), 0)
    same = rows_at == lax.broadcasted_iota(jnp.int32, (block, block), 1)

    def scaled(j, carry):
        rows = pl.ds(pl.multiple_of(j * block, block), block)
        for kind, (hat, out) in enumerate(((query_hat, queries), (key_hat, keys))):
            factor = jnp.sum(jnp.where(same, factors[kind, :, rows], 0.0), axis=1, keepdims=True)
            part = hat[rows] * factor
            hat[rows] = part
            out[rows] = (part * head_gains[kind : kind + 1]).astype(bf16)
        return carry

    lax.fori_loop(0, blocks, scaled, 0)
    carry_on(1)

    def mixed_copy(b, offset, index, device):
        where = pl.ds(pl.multiple_of(me * size, size), size)
        part = heads.at[b, pl.ds(pl.multiple_of(index * run, run), run)]
        return remote(part, mixed.at[b, :, where], ms.at[b, offset], mr.at[b, offset], device)

    def mixed_own(b):
        where = pl.ds(pl.multiple_of(me * size, size), size)
        part = heads.at[b, pl.ds(pl.multiple_of(me * run, run), run)]
        return pltpu.make_async_copy(part, mixed.at[b, :, where], ml.at[b])

    for b in range(batches):

        def head(h, carry, b=b):
            lanes = pl.ds(pl.multiple_of(h * HEAD, HEAD), HEAD)
            for first, count, seen in query_blocks(length):
                rows = pl.ds(b * length + first, count)
                seen_rows = pl.ds(b * length, seen)
                scores = contract(queries[rows, lanes], keys[seen_rows, lanes], (1, 1)) * scale
                allowed = key_ids[b, :, :seen] <= row_ids[b, first : first + count]
                scores = jnp.where(allowed, scores, MASKED)
                peak = jnp.max(scores, axis=1, keepdims=True)
                grown = jnp.exp(scores - peak)
                total = jnp.sum(grown, axis=1, keepdims=True)
                probs = (grown * (1.0 / total)).astype(bf16)
                heads[b, first : first + count, lanes] = jnp.dot(
                    probs, values[seen_rows, lanes], preferred_element_type=f32
                ).astype(bf16)
                log_total[b, h, first : first + count] = peak + jnp.log(total)
            return carry

        lax.fori_loop(0, size // HEAD, head, 0)
        for offset, index, device in peers:
            mixed_copy(b, offset, index, device).start()
        mixed_own(b).start()
        carry_on(1)
    carry_on(flow.chunks)

    for copy in shares:
        copy.wait_send()
    for j in (blocks - 2, blocks - 1):
        store(j).wait()
    for b in range(batches):
        for offset, index, device in peers:
            mixed_copy(b, offset, index, device).wait()
        mixed_own(b).wait()

    for n in range(flow.chunks):
        b, i = chunk_of(n)
        flow.hops_sent(b, i)
        flow.arrived(n, b, i)
        if n >= flow.chunks - flow.kept:
            flow.crossed(n, b, i)
            flow.stay(n, b, i).wait()


def run_forward(E, C, G, column, gain, head_gains, w_qkv, ids, slots, upstream, cap, collective, name):
    every, width = column.shape
    batches, run = upstream.shape[:2]
    count = C * G
    length = count * run
    size = width // count
    block = min(256, every)
    low = jax.ShapeDtypeStruct((every, size), bf16)
    wide = jax.ShapeDtypeStruct((every, size), f32)
    return call(
        functools.partial(forward_kernel, E, C, G),
        (column, gain, head_gains, w_qkv, ids[:, :, None], ids[:, None, :], slots, upstream),
        (
            jax.ShapeDtypeStruct((every, width), bf16),
            low,
            low,
            low,
            wide,
            wide,
            jax.ShapeDtypeStruct((batches, size // HEAD, length, 1), f32),
            jax.ShapeDtypeStruct((2, 1, every), f32),
            jax.ShapeDtypeStruct(upstream.shape, bf16),
            jax.ShapeDtypeStruct((C, batches, E, cap, width), bf16),
        ),
        [ANY] + [VMEM] * 6 + [ANY],
        (ANY,) + (VMEM,) * 7 + (ANY, ANY),
        [
            pltpu.VMEM((2, block, width), bf16),
            pltpu.VMEM((2, block, width), bf16),
            pltpu.VMEM((2, 1, every), f32),
            pltpu.VMEM((count, 2, 1, every), f32),
            pltpu.VMEM((batches, length, size), bf16),
        ]
        + Flow.scratch(E, C, batches, run, width, cap, 3)
        + [
            DMA((2,)),
            DMA((2,)),
            DMA((count,)),
            DMA((count,)),
            DMA((batches, count)),
            DMA((batches, count)),
            DMA((batches,)),
        ],
        collective,
        name,
        vmem=56,
    )


def experts_kernel(
    E,
    C,
    rows_x,
    u_in,
    slots,
    gates,
    w_gate,
    w_up,
    w_down,
    out_y,
    out_b,
    x_out,
    pair_out,
    act_out,
    gate_back_out,
    up_back_out,
    scalars_out,
    table,
    scalars,
    landed,
    packed,
    own,
    zs,
    zr,
    xs,
    xr,
    stay,
    sums,
    returned,
    x,
    u,
    pair,
    act,
    gate_back,
    up_back,
    sent,
    gs,
    gr,
    ss,
    sr,
    ys,
    yr,
    bs,
    us,
    ur,
    ks,
    loads,
    stores,
):
    e, c, d = position()
    batches, run, width = rows_x.shape
    cap = x_out.shape[3]
    units = w_gate.shape[1]
    chunks = batches * C
    total = E * cap
    kept = sent.shape[1]
    lead, lag = 1, 2
    everyone = [(k, i) for k in range(E) for i in range(C) if k + i > 0]
    ahead = [(k, i, (lax.rem(e + k, E), lax.rem(c + i, C), d)) for k, i in everyone]
    behind = [(k, i, (lax.rem(e + E - k, E), lax.rem(c + C - i, C), d)) for k, i in everyone]
    meet([device for _, _, device in ahead])
    outs = out_y, out_b
    flow = Flow(E, C, rows_x, slots, landed, packed, x_out, own, zs, zr, xs, xr, stay)

    def far_of(n):
        return lax.rem((n + batches - 1) // batches, C), lax.rem(n + batches - 1, batches)

    def chunk_of(n):
        far, b = far_of(n)
        return b, flow.level_entry(far)

    def back(a, n, b, i, k):
        return remote(
            sent.at[a, lax.rem(n, kept), k],
            returned.at[a, i, b, e],
            ys.at[a, i, b, k],
            yr.at[a, i, b, k],
            (lax.rem(e + E - k, E), c, d),
        )

    def back_own(a, n, b, i):
        return pltpu.make_async_copy(
            sent.at[a, lax.rem(n, kept), 0], returned.at[a, i, b, e], bs.at[a, i, b]
        )

    def up(a, b, i):
        return remote(
            sums.at[a, i, b],
            outs[a].at[c, b],
            us.at[a, i, b],
            ur.at[a, i, b],
            (e, lax.rem(c + C - i, C), d),
        )

    def keep(a, b):
        return pltpu.make_async_copy(sums.at[a, 0, b], outs[a].at[c, b], ks.at[a, b])

    def load(a, b, i):
        source, target = ((x_out, x), (u_in, u))[a]
        return pltpu.make_async_copy(source.at[i, b], target, loads.at[a])

    def store(j, b, i):
        source = (pair, act, gate_back, up_back)[j]
        target = (pair_out, act_out, gate_back_out, up_back_out)[j]
        return pltpu.make_async_copy(source, target.at[i, b], stores.at[j])

    flow.begin()
    small = [
        remote(gates.at[device[0], device[1]], table.at[k, i], gs.at[k, i], gr.at[k, i], device)
        for k, i, device in ahead
    ]
    for copy in small:
        copy.start()
    table[0, 0] = gates[e, c]

    def compact(n):
        @pl.when(n >= flow.kept)
        def _():
            flow.crossed(n - flow.kept, *chunk_of(n - flow.kept))

        flow.compact(n, *chunk_of(n))

    def expert(n):
        b, i = chunk_of(n)
        load(1, b, i).start()
        flow.arrived(n, b, i)
        flow.stay(n, b, i).wait()
        load(0, b, i).start()

        @pl.when(n > 0)
        def _():
            before = chunk_of(n - 1)
            for j in range(4):
                store(j, *before).wait()

        @pl.when(n >= kept)
        def _():
            before = chunk_of(n - kept)
            for a in range(2):
                for k in range(1, E):
                    back(a, n - kept, *before, k).wait_send()

        holds, gate = [], []
        cells = lax.broadcasted_iota(jnp.int32, (cap, run), 0).astype(f32)
        for k in range(E):
            hold = cells == table[k, i, b]
            holds.append(hold)
            gate.append(
                jnp.sum(jnp.where(hold, table[k, i, batches + b], 0.0), axis=1, keepdims=True)
            )
        gate = jnp.concatenate(gate, axis=0)
        for a in range(2):
            load(a, b, i).wait()
        for at in range(0, width, 512):
            part = u[:, :, at : at + 512].reshape(total, 512).astype(f32)
            pair[:, :, at : at + 512] = (gate * part).astype(bf16).reshape(E, cap, 512)
        store(0, b, i).start()
        inputs = x[...].reshape(total, width)
        grads = pair[...].reshape(total, width)
        for at in range(0, units, 256):
            gate_pre = jnp.dot(inputs, w_gate[:, at : at + 256], preferred_element_type=f32)
            up_pre = jnp.dot(inputs, w_up[:, at : at + 256], preferred_element_type=f32)
            act_grad = contract(grads, w_down[at : at + 256, :], (1, 1))
            sigmoid = jax.nn.sigmoid(gate_pre)
            silu = gate_pre * sigmoid
            act[:, at : at + 256] = (silu * up_pre).astype(bf16)
            gate_back[:, at : at + 256] = (
                act_grad * up_pre * sigmoid * (1.0 + gate_pre * (1.0 - sigmoid))
            ).astype(bf16)
            up_back[:, at : at + 256] = (act_grad * silu).astype(bf16)
        for j in range(1, 4):
            store(j, b, i).start()
        place = lax.rem(n, kept)
        gate_grad = jnp.zeros((total, 1), f32)
        for at in range(0, width, 512):
            out = jnp.dot(act[...], w_down[:, at : at + 512], preferred_element_type=f32)
            out = out.astype(bf16).astype(f32)
            gate_grad += jnp.sum(
                out * u[:, :, at : at + 512].reshape(total, 512).astype(f32), axis=1, keepdims=True
            )
            sent[0, place, :, :, at : at + 512] = (gate * out).astype(bf16).reshape(E, cap, 512)
            back_rows = contract(gate_back[...], w_gate[at : at + 512, :], (1, 1))
            back_rows += contract(up_back[...], w_up[at : at + 512, :], (1, 1))
            sent[1, place, :, :, at : at + 512] = back_rows.astype(bf16).reshape(E, cap, 512)
        for a in (1, 0):
            for k in range(1, E):
                back(a, n, b, i, k).start()
            back_own(a, n, b, i).start()
        for k in range(E):
            scalars[k, i, b] = jnp.sum(
                jnp.where(holds[k], gate_grad[k * cap : (k + 1) * cap], 0.0), axis=0, keepdims=True
            )

    def combine(n):
        b, i = chunk_of(n)
        picks = choose(slots[i, b], cap)
        for a in (1, 0):
            for k in range(1, E):
                back(a, n, b, i, k).wait_recv()
            back_own(a, n, b, i).wait()
            for at in range(0, width, 512):
                part = returned[a, i, b, :, :, at : at + 512].reshape(total, 512)
                sums[a, i, b, :, at : at + 512] = contract(picks, part, (0, 0)).astype(bf16)

            @pl.when(i > 0)
            def _():
                up(a, b, i).start()

            @pl.when(i == 0)
            def _():
                keep(a, b).start()

    def step(s, carry):
        @pl.when(jnp.logical_and(s > 0, s <= batches * (C - 1)))
        def _():
            flow.relay(*far_of(s))

        @pl.when(s < chunks)
        def _():
            compact(s)

        @pl.when(jnp.logical_and(s >= lead, s < chunks + lead))
        def _():
            expert(s - lead)

        @pl.when(s >= lag)
        def _():
            combine(s - lag)

        return carry

    for copy in small:
        copy.wait_recv()
    lax.fori_loop(0, chunks + lag, step, 0)
    scalars_out[e, c] = scalars[0, 0]
    last = [
        remote(scalars.at[k, i], scalars_out.at[e, c], ss.at[k, i], sr.at[k, i], device)
        for k, i, device in behind
    ]
    for copy in last:
        copy.start()
    for copy in small:
        copy.wait_send()
    for j in range(4):
        store(j, *chunk_of(chunks - 1)).wait()

    def finish(n, carry):
        b, i = chunk_of(n)
        flow.hops_sent(b, i)

        @pl.when(n >= chunks - flow.kept)
        def _():
            flow.crossed(n, b, i)

        for a in range(2):

            @pl.when(n >= chunks - kept)
            def _():
                for k in range(1, E):
                    back(a, n, b, i, k).wait_send()

            @pl.when(i > 0)
            def _():
                up(a, b, i).wait()

            @pl.when(i == 0)
            def _():
                keep(a, b).wait()

        return carry

    lax.fori_loop(0, chunks, finish, 0)
    for copy in last:
        copy.wait()


def run_experts(E, C, rows_x, u_in, slots, gates, w_gate, w_up, w_down, cap, collective, name):
    batches, run, width = rows_x.shape
    units = w_gate.shape[1]
    total = E * cap
    kept = 3
    by_slot = jax.ShapeDtypeStruct((C, batches, E, cap, width), bf16)
    by_token = jax.ShapeDtypeStruct((C, batches, run, width), bf16)
    hidden = jax.ShapeDtypeStruct((C, batches, total, units), bf16)
    return call(
        functools.partial(experts_kernel, E, C),
        (rows_x, u_in, slots, gates, w_gate, w_up, w_down),
        (
            by_token,
            by_token,
            by_slot,
            by_slot,
            hidden,
            hidden,
            hidden,
            jax.ShapeDtypeStruct((E, C, batches, 1, run), f32),
        ),
        [ANY, ANY, VMEM, VMEM, VMEM, VMEM, VMEM],
        (ANY,) * 7 + (VMEM,),
        [
            pltpu.VMEM(gates.shape, f32),
            pltpu.VMEM((E, C, batches, 1, run), f32),
        ]
        + Flow.scratch(E, C, batches, run, width, cap, kept)
        + [
            pltpu.VMEM((2, C, batches, run, width), bf16),
            pltpu.VMEM((2, C, batches, E, cap, width), bf16),
            pltpu.VMEM((E, cap, width), bf16),
            pltpu.VMEM((E, cap, width), bf16),
            pltpu.VMEM((E, cap, width), bf16),
            pltpu.VMEM((total, units), bf16),
            pltpu.VMEM((total, units), bf16),
            pltpu.VMEM((total, units), bf16),
            pltpu.VMEM((2, kept, E, cap, width), bf16),
            DMA((E, C)),
            DMA((E, C)),
            DMA((E, C)),
            DMA((E, C)),
            DMA((2, C, batches, E)),
            DMA((2, C, batches, E)),
            DMA((2, C, batches)),
            DMA((2, C, batches)),
            DMA((2, C, batches)),
            DMA((2, batches)),
            DMA((2,)),
            DMA((4,)),
        ],
        collective,
        name,
        vmem=60,
    )


def middle_kernel(
    E,
    C,
    G,
    rows,
    mixed,
    grads,
    x,
    pair,
    gate_back,
    up_back,
    act,
    heads,
    proj,
    own_gate,
    own_up,
    own_down,
    other_gate,
    other_up,
    other_down,
    hidden,
    wide,
    kept,
    sent,
    swap,
    swapped,
    chip,
    plane_parts,
    level_part,
    hs,
    hr,
    hl,
    cs,
    cr,
    ps,
    pr,
    zs,
    zr,
    rs,
    wide_sem,
    ks,
    xs,
    xr,
):
    e, c, d = position()
    me, peers = column_peers(E, C, G)
    planes, levels = plane_peers(E), level_peers(C)
    batches = rows.shape[0]
    size = heads.shape[3]
    block, width = swap.shape[1:]
    step = wide.shape[2]
    half = own_gate.shape[1]
    sibling = (e, c, 1 - d)
    meet([device for _, _, device in peers] + [device for _, _, device in planes])

    def head_part(b, index):
        return rows.at[b, :, pl.ds(pl.multiple_of(index * size, size), size)]

    head_copies = []
    for b in range(batches):
        for offset, index, device in peers:
            head_copies.append(
                remote(head_part(b, index), heads.at[b, me], hs.at[b, offset], hr.at[b, offset], device)
            )
        head_copies.append(pltpu.make_async_copy(head_part(b, me), heads.at[b, me], hl.at[b]))
    for copy in head_copies:
        copy.start()

    hidden_copies = [
        pltpu.make_async_copy(source, hidden.at[j], rs.at[j])
        for j, source in enumerate((gate_back, up_back, act))
    ]
    for copy in hidden_copies:
        copy.start()
    count = width // step
    sources = [x] * count + [pair] * count

    def wide_copy(item):
        at = (item % count) * step
        return pltpu.make_async_copy(
            sources[item].at[:, pl.ds(at, step)], wide.at[item % 2], wide_sem.at[item % 2]
        )

    wide_copy(0).start()
    wide_copy(1).start()

    def chip_copy(level):
        return remote(swap.at[level], swapped.at[level], cs.at[level], cr.at[level], sibling)

    def proj_part(core, level):
        part = mixed[:, level, core].reshape(block, mixed.shape[4])
        return jnp.dot(part, grads[...], preferred_element_type=f32)

    def plane_copy(level, k, device):
        return remote(
            chip.at[level, lax.rem(e + k, E)],
            plane_parts.at[level, k],
            ps.at[level, k],
            pr.at[level, k],
            device,
        )

    def give(level, carry):
        swap[level] = proj_part(1 - d, level).astype(bf16)
        chip_copy(level).start()
        return carry

    def take(level, carry):
        part = proj_part(d, level)
        chip_copy(level).wait_recv()
        part = (part + swapped[level].astype(f32)).astype(bf16)
        chip[level] = part.reshape(chip.shape[1:])
        for k, _, device in planes:
            plane_copy(level, k, device).start()
        return carry

    lax.fori_loop(0, C, give, 0)
    lax.fori_loop(0, C, take, 0)

    def plane_sum(level, carry):
        total = chip[level, e].astype(f32)
        for k, _, device in planes:
            plane_copy(level, k, device).wait_recv()
            total = total + plane_parts[level, k].astype(f32)
        level_part[level] = total.astype(bf16)
        return carry

    def keep_copy(j, at, place):
        target = (own_gate, own_up, own_down)[j]
        where = target.at[:, pl.ds(at, step)] if j == 2 else target.at[pl.ds(at, step)]
        return pltpu.make_async_copy(kept.at[place], where, ks.at[place])

    def send_copy(j, at, place):
        target = (other_gate, other_up, other_down)[j]
        where = target.at[:, pl.ds(at, step)] if j == 2 else target.at[pl.ds(at, step)]
        return remote(sent.at[place], where, xs.at[place], xr.at[place], sibling)

    kept_copies, sent_copies = [], []
    for copy in hidden_copies:
        copy.wait()
    for item in range(2 * count):
        wide_copy(item).wait()
        at = (item % count) * step
        left = wide[item % 2]
        for j in (0, 1) if item < count else (2,):
            place = len(sent_copies)

            def product(core):
                part = hidden[j, :, pl.ds(pl.multiple_of(core * half, half), half)]
                return contract(part, left, (0, 0)) if j == 2 else contract(left, part, (0, 0))

            sent[place] = product(1 - d).astype(bf16)
            copy = send_copy(j, at, place)
            copy.start()
            sent_copies.append(copy)
            if place >= 2:
                kept_copies[place - 2].wait()
            kept[place % 2] = product(d)
            copy = keep_copy(j, at, place % 2)
            copy.start()
            kept_copies.append(copy)
        if item + 2 < 2 * count:
            wide_copy(item + 2).start()
        if item == count - 1:
            lax.fori_loop(0, C, plane_sum, 0)
            level_copies = []
            for i, level, device in levels:
                copy = remote(level_part.at[level], proj.at[c], zs.at[i], zr.at[i], device)
                copy.start()
                level_copies.append(copy)
            proj[c] = level_part[c]

    for copy in kept_copies[-2:]:
        copy.wait()
    for copy in sent_copies + level_copies + head_copies:
        copy.wait()

    def done(level, carry):
        chip_copy(level).wait_send()
        for k, _, device in planes:
            plane_copy(level, k, device).wait_send()
        return carry

    lax.fori_loop(0, C, done, 0)


def middle(E, C, G, rows, mixed, grads, x, pair, gate_back, up_back, act, collective, name):
    batches, run, width = rows.shape
    count = C * G
    part = mixed.shape[3]
    block = E * part
    total, units = act.shape
    half = units // G
    step = min(512, width)
    items = 3 * (width // step)
    tall = (width, half)
    flat = (half, width)
    return call(
        functools.partial(middle_kernel, E, C, G),
        (rows, mixed, grads, x, pair, gate_back, up_back, act),
        (
            jax.ShapeDtypeStruct((batches, count, run, width // count), bf16),
            jax.ShapeDtypeStruct((C, part, width), bf16),
            jax.ShapeDtypeStruct(tall, f32),
            jax.ShapeDtypeStruct(tall, f32),
            jax.ShapeDtypeStruct(flat, f32),
            jax.ShapeDtypeStruct(tall, bf16),
            jax.ShapeDtypeStruct(tall, bf16),
            jax.ShapeDtypeStruct(flat, bf16),
        ),
        [ANY, VMEM, VMEM] + [ANY] * 5,
        (ANY, VMEM) + (ANY,) * 6,
        [
            pltpu.VMEM((3, total, units), bf16),
            pltpu.VMEM((2, total, step), bf16),
            pltpu.VMEM((2, step, half), f32),
            pltpu.VMEM((items, step, half), bf16),
            pltpu.VMEM((C, block, width), bf16),
            pltpu.VMEM((C, block, width), bf16),
            pltpu.VMEM((C, E, part, width), bf16),
            pltpu.VMEM((C, E, part, width), bf16),
            pltpu.VMEM((C, part, width), bf16),
            DMA((batches, count)),
            DMA((batches, count)),
            DMA((batches,)),
            DMA((C,)),
            DMA((C,)),
            DMA((C, E)),
            DMA((C, E)),
            DMA((C,)),
            DMA((C,)),
            DMA((3,)),
            DMA((2,)),
            DMA((2,)),
            DMA((items,)),
            DMA((items,)),
        ],
        collective,
        name,
        vmem=60,
    )


def finish_kernel(
    E,
    C,
    G,
    raw,
    w_qkv,
    normed,
    small,
    first,
    out_qkv,
    out_small,
    small_parts,
    small_sum,
    swap,
    swapped,
    own,
    passed,
    tokens,
    parts,
    plane_parts,
    sum_qkv,
    cs,
    cr,
    zs,
    zr,
    ts,
    qs,
    qr,
    os,
    orr,
    ss,
    sr,
    fs,
    fr,
):
    e, c, d = position()
    me, peers = column_peers(E, C, G)
    planes = plane_peers(E)
    batches, _, run, columns = raw.shape
    width = w_qkv.shape[0]
    rows = batches * run
    sibling = (e, c, 1 - d)
    meet([device for _, _, device in peers] + [device for _, _, device in planes])
    block = tokens.shape[2]

    def token_copy(item):
        plane = lax.rem(e + 1 + item, E)
        return pltpu.make_async_copy(
            normed.at[:, pl.ds(pl.multiple_of(plane * block, block), block)],
            tokens.at[item % 2],
            ts.at[item % 2],
        )

    token_copy(0).start()
    token_copy(1).start()
    small_copies = [
        remote(small.at[plane], small_parts.at[i], ss.at[i], sr.at[i], device)
        for i, plane, device in planes
    ]
    for copy in small_copies:
        copy.start()

    def product(level, core, at, size):
        left = jnp.concatenate([raw[b, level * G + core] for b in range(batches)], axis=0)
        return contract(left, w_qkv[at : at + size, :], (1, 1))

    def chip_copy(level):
        return remote(swap.at[level], swapped.at[level], cs.at[level], cr.at[level], sibling)

    def give(level):
        for at in range(0, width, 512):
            swap[level, :, at : at + 512] = product(level, 1 - d, at, 512).astype(bf16)
        chip_copy(level).start()

    def take(level):
        chip_copy(level).wait_recv()
        for at in range(0, width, 512):
            part = product(level, d, at, 512) + swapped[level, :, at : at + 512].astype(f32)
            own[level, :, at : at + 512] = part.astype(bf16)

    def hop(way, level, b):
        there = c + 1 if way == 0 else c - 1
        to = level if way == 0 else level + (C - level) * ((C - 1 - (there - level)) // (C - 1))
        return remote(
            own.at[level, pl.ds(b * run, run)],
            passed.at[to, pl.ds(b * run, run)],
            zs.at[way, level, b],
            zr.at[to, b],
            (e, there, d),
        )

    def arrival(entry, b):
        part = passed.at[entry, pl.ds(b * run, run)]
        return remote(part, part, zs.at[0, 0, b], zr.at[entry, b], sibling)

    def send(way, level, last):
        for b in range(batches):

            @pl.when(last)
            def _():
                arrival(level, b).wait_recv()
                piece = pl.ds(b * run, run)
                own[level, piece] = (
                    own[level, piece].astype(f32) + passed[level, piece].astype(f32)
                ).astype(bf16)

            hop(way, level, b).start()

    order = [C - 1, 0] + list(range(C - 2, 0, -1))
    for level in order:
        give(level)

    def plane_copy(item):
        plane = lax.rem(e + 1 + item, E)
        return remote(
            parts.at[item],
            plane_parts.at[item],
            qs.at[item],
            qr.at[item],
            (plane, c, d),
        )

    raw_flat = raw[...].reshape(-1, columns)

    def weights(item):
        token_copy(item).wait()
        for at in range(0, columns, 256):
            size = min(256, columns - at)
            parts[item, :, at : at + size] = contract(
                tokens[item % 2], raw_flat[:, at : at + size], (0, 0)
            ).astype(bf16)
        if item + 2 < E:
            token_copy(item + 2).start()
        if item < E - 1:
            plane_copy(item).start()

    mirror = C - 1 - c
    items = list(range(E))
    for level in order:
        take(level)
        if level == 0:
            @pl.when(c == 0)
            def _():
                send(0, C - 1, False)

            @pl.when(c == C - 1)
            def _():
                send(1, 0, False)

            weights(items.pop(0))
    weights(items.pop(0))
    for turn in range(1, C - 1):

        @pl.when(c <= turn)
        def _():
            send(0, C - 1 - (turn - c), c > 0)

        @pl.when(mirror <= turn)
        def _():
            send(1, turn - mirror, mirror > 0)

        if items:
            weights(items.pop(0))
    while items:
        weights(items.pop(0))
    for item in range(E - 1):
        plane_copy(item).wait_recv()
    for at in range(0, block, 128):
        piece = pl.ds(at, min(128, block - at))
        total = parts[E - 1, piece].astype(f32)
        for item in range(E - 1):
            total = total + plane_parts[item, piece].astype(f32)
        sum_qkv[piece] = total.astype(bf16)
    share = block // (C * G)

    def row_copy(offset, index, device):
        return remote(
            sum_qkv.at[pl.ds(pl.multiple_of(index * share, share), share)],
            out_qkv.at[me],
            os.at[offset],
            orr.at[offset],
            device,
        )

    def small_copy(offset, index, device):
        return remote(
            small_sum.at[pl.ds(pl.multiple_of(index * share, share), share)],
            out_small.at[me],
            fs.at[offset],
            fr.at[offset],
            device,
        )

    for copy in small_copies:
        copy.wait_recv()
    total = small[e]
    for i in range(1, E):
        total = total + small_parts[i]
    small_sum[...] = total
    for offset, index, device in peers:
        small_copy(offset, index, device).start()
        row_copy(offset, index, device).start()
    out_small[me] = small_sum[pl.ds(pl.multiple_of(me * share, share), share)]
    out_qkv[me] = sum_qkv[pl.ds(pl.multiple_of(me * share, share), share)]

    def arrived(entry):
        for b in range(batches):
            arrival(entry, b).wait_recv()

    @pl.when(c > 0)
    def _():
        arrived(c)

    @pl.when(c < C - 1)
    def _():
        arrived(C)

    for at in range(0, width, 512):
        first[:, at : at + 512] = own[c, :, at : at + 512].astype(f32)

    @pl.when(c > 0)
    def _():
        for at in range(0, width, 512):
            first[:, at : at + 512] += passed[c, :, at : at + 512].astype(f32)

    @pl.when(c < C - 1)
    def _():
        for at in range(0, width, 512):
            first[:, at : at + 512] += passed[C, :, at : at + 512].astype(f32)

    for level in range(C):
        chip_copy(level).wait_send()
        for b in range(batches):

            @pl.when(level > c)
            def _():
                hop(0, level, b).wait_send()

            @pl.when(level < c)
            def _():
                hop(1, level, b).wait_send()

    for item in range(E - 1):
        plane_copy(item).wait_send()
    for copy in small_copies:
        copy.wait_send()
    for offset, index, device in peers:
        row_copy(offset, index, device).wait()
        small_copy(offset, index, device).wait()


def finish(E, C, G, raw, w_qkv, normed, small, collective, name):
    batches, count, run, columns = raw.shape
    width = w_qkv.shape[0]
    every = normed.shape[0]
    rows = batches * run
    block = width // E
    share = block // count
    lanes = small.shape[2]
    by_level = pltpu.VMEM((C, rows, width), bf16)
    return call(
        functools.partial(finish_kernel, E, C, G),
        (raw, w_qkv, normed, small),
        (
            jax.ShapeDtypeStruct((rows, width), f32),
            jax.ShapeDtypeStruct((count, share, columns), bf16),
            jax.ShapeDtypeStruct((count, share, lanes), f32),
        ),
        [VMEM, VMEM, ANY, VMEM],
        (VMEM, VMEM, VMEM),
        [
            pltpu.VMEM((E, block, lanes), f32),
            pltpu.VMEM((block, lanes), f32),
            by_level,
            by_level,
            by_level,
            pltpu.VMEM((C + 1, rows, width), bf16),
            pltpu.VMEM((2, every, block), bf16),
            pltpu.VMEM((E, block, columns), bf16),
            pltpu.VMEM((E, block, columns), bf16),
            pltpu.VMEM((block, columns), bf16),
            DMA((C,)),
            DMA((C,)),
            DMA((2, C, batches)),
            DMA((C + 1, batches)),
            DMA((2,)),
            DMA((E,)),
            DMA((E,)),
            DMA((count,)),
            DMA((count,)),
            DMA((E,)),
            DMA((E,)),
            DMA((count,)),
            DMA((count,)),
        ],
        collective,
        name,
        vmem=60,
    )


def contract(left, right, axes):
    return lax.dot_general(left, right, ((axes[:1], axes[1:]), ((), ())), preferred_element_type=f32)


def query_blocks(length):
    size = min(256, length)
    return [(i, size, min(length, i + 2 * size)) for i in range(0, length, size)]


def attend_back_kernel(
    scale, queries, keys, values, grads, row_ids, key_ids, log_total, query_grad, key_grad, value_grad
):
    length = queries.shape[1]
    key_grad[...] = jnp.zeros_like(key_grad)
    value_grad[...] = jnp.zeros_like(value_grad)
    for first, size, seen in query_blocks(length):
        rows = pl.ds(first, size)
        query, grad = queries[0, rows], grads[0, rows]
        scores = contract(query, keys[0, :seen], (1, 1)) * scale
        scores = jnp.where(key_ids[0, :, :seen] <= row_ids[0, rows], scores, MASKED)
        probs = jnp.exp(scores - log_total[0, 0, rows])
        prod = contract(grad, values[0, :seen], (1, 1))
        delta = jnp.sum(probs * prod, axis=1, keepdims=True)
        score_grad = (probs * (prod - delta)).astype(bf16)
        query_grad[0, rows] = jnp.dot(score_grad, keys[0, :seen], preferred_element_type=f32) * scale
        key_grad[0, :seen] += contract(score_grad, query, (0, 0)) * scale
        value_grad[0, :seen] += contract(probs.astype(bf16), grad, (0, 0))


def attention_specs(length):
    head = pl.BlockSpec((1, length, HEAD), lambda b, h: (b, 0, h))
    row_ids = pl.BlockSpec((1, length, 1), lambda b, h: (b, 0, 0))
    key_ids = pl.BlockSpec((1, 1, length), lambda b, h: (b, 0, 0))
    log_total = pl.BlockSpec((1, 1, length, 1), lambda b, h: (b, h, 0, 0))
    return head, row_ids, key_ids, log_total


def attend_back(queries, keys, values, grads, ids, totals):
    batches, length, size = queries.shape
    heads = size // HEAD
    head, row_ids, key_ids, log_total = attention_specs(length)
    grad = jax.ShapeDtypeStruct(queries.shape, f32)
    return pl.pallas_call(
        functools.partial(attend_back_kernel, HEAD**-0.5),
        grid=(batches, heads),
        out_shape=(grad, grad, grad),
        in_specs=[head, head, head, head, row_ids, key_ids, log_total],
        out_specs=(head, head, head),
        compiler_params=pltpu.CompilerParams(vmem_limit_bytes=48 * MIB),
        name="attend_back",
    )(queries, keys, values, grads, ids[:, :, None], ids[:, None, :], totals)


def rms_factor(values):
    return lax.rsqrt(jnp.mean(values * values, axis=-1, keepdims=True) + EPSILON)


def norm_back(grad_hat, hatted, factor):
    return factor * (grad_hat - hatted * jnp.mean(grad_hat * hatted, axis=-1, keepdims=True))


def slot_table(routes, experts):
    batches, run, top = routes.shape
    hits = jnp.swapaxes(routes, 1, 2)[:, :, :, None] == jnp.arange(experts, dtype=jnp.int32)
    ones = hits.astype(bf16)
    tokens, ranks = jnp.arange(run), jnp.arange(top)
    before = (tokens[None, :] < tokens[:, None]).astype(bf16)
    above = (ranks[None, :] < ranks[:, None]).astype(bf16)
    within = jnp.einsum("ts,bksx->bktx", before, ones, preferred_element_type=f32)
    totals = jnp.sum(hits.astype(f32), axis=2)
    earlier = jnp.einsum(
        "kj,bjx->bkx", above, totals.astype(bf16), preferred_element_type=f32
    )
    places = jnp.sum(jnp.where(hits, within + earlier[:, :, None, :], 0.0), axis=1)
    places = jnp.where(jnp.any(hits, axis=1), places, UNUSED_SLOT)
    return jnp.swapaxes(places, 1, 2)


def body(
    tokens,
    block_ids,
    routes,
    norm_gains,
    w_query,
    w_key,
    w_value,
    w_output,
    router,
    expert_gate,
    expert_up,
    expert_down,
    cotangent,
):
    E, C, G = lax.axis_size("expert"), lax.axis_size("context"), lax.axis_size("dp")
    batches, run, width = tokens.shape
    top = routes.shape[2]
    experts = E * C * expert_gate.shape[0]
    capacity = max(2, run * top // experts)
    count = C * G
    size = width // count
    length = count * run
    every = batches * length
    own = batches * run
    me = lax.axis_index("context") * G + lax.axis_index("dp")

    rows = w_query.shape[0]
    small_width = -(-(norm_gains.shape[1] + experts) // 128) * 128
    small = jnp.concatenate([norm_gains, router], axis=1)
    small = jnp.pad(small, ((0, 0), (0, small_width - small.shape[1])))
    pieces = [w.reshape(rows, count, size) for w in (w_query, w_key, w_value)]
    weights = jnp.swapaxes(jnp.concatenate(pieces, axis=2), 0, 1)
    places = slot_table(routes, experts).reshape(batches, E, C, run)
    by_level = jnp.transpose(places, (2, 0, 1, 3))
    by_expert = jnp.transpose(places, (1, 2, 0, 3))
    column, w_qkv, small, full_output, ids, slots = start(
        E, C, G, tokens, weights, small, w_output, block_ids, by_level
    )
    ids = jnp.swapaxes(ids, 0, 1).reshape(batches, length)
    w_qkv = w_qkv.reshape(width, 3 * size)
    small = small.reshape(width, small_width)
    full_output = full_output.reshape(width, width)
    gains = small[:, :4].astype(f32)
    full_router = small[:, 4 : 4 + experts]
    head_gains = lax.dynamic_slice(gains, (me * size, 0), (size, 4))

    (
        normed,
        query_low,
        key_low,
        value_low,
        query_hat,
        key_hat,
        log_total,
        factors,
        mixed_low,
        upstream_rows,
    ) = run_forward(
        E,
        C,
        G,
        column.reshape(every, width),
        jnp.swapaxes(gains[:, :1], 0, 1),
        jnp.swapaxes(head_gains[:, 1:3], 0, 1),
        w_qkv,
        ids,
        slots,
        cotangent,
        capacity,
        2,
        "forward",
    )
    mixed_low = mixed_low.reshape(own, width)
    query_factor, key_factor = factors[0, 0][:, None], factors[1, 0][:, None]
    by_sequence = (batches, length, size)
    query_low, key_low, value_low = (
        low.reshape(by_sequence) for low in (query_low, key_low, value_low)
    )

    inputs = tokens.reshape(own, width).astype(f32)
    resid = inputs + jnp.dot(mixed_low, full_output, preferred_element_type=f32)
    second_factor = rms_factor(resid)
    second_hat = resid * second_factor
    second_low = (second_hat * gains[:, 3]).astype(bf16)
    logits = jnp.dot(second_low, full_router, preferred_element_type=f32)
    router_probs = jax.nn.softmax(logits, axis=-1)
    gate_table = jnp.transpose(router_probs.reshape(batches, run, E, C), (2, 3, 0, 1))
    table = jnp.concatenate([by_expert, gate_table], axis=2)[:, :, :, None, :]

    mixture, second_grad, x, pair_grad, act, gate_pre_grad, up_pre_grad, gate_grad = run_experts(
        E,
        C,
        second_low.reshape(batches, run, width),
        upstream_rows,
        slots,
        table,
        expert_gate[0],
        expert_up[0],
        expert_down[0],
        capacity,
        4,
        "experts",
    )
    slot_count = E * C * batches * capacity
    x, pair_grad, act, gate_pre_grad, up_pre_grad = (
        rows.reshape(slot_count, -1) for rows in (x, pair_grad, act, gate_pre_grad, up_pre_grad)
    )
    upstream = cotangent.reshape(own, width).astype(f32)
    mixture = jnp.sum(mixture.astype(f32), axis=0).reshape(own, width)
    activations = (resid + mixture).astype(bf16).reshape(tokens.shape)
    prob_grad = jnp.transpose(gate_grad[:, :, :, 0, :], (2, 3, 0, 1)).reshape(own, experts)
    logit_grad = router_probs * (
        prob_grad - jnp.sum(router_probs * prob_grad, axis=-1, keepdims=True)
    )
    logit_grad = logit_grad.astype(bf16)
    second_grad = jnp.sum(second_grad.astype(f32), axis=0).reshape(own, width)
    second_grad = second_grad + contract(logit_grad, full_router, (1, 1))
    gain_second = jnp.sum(second_grad * second_hat, axis=0)
    resid_grad = upstream + norm_back(second_grad * gains[:, 3], second_hat, second_factor)
    attn_grad = resid_grad.astype(bf16)
    mixed_grad = contract(attn_grad, full_output, (1, 1)).astype(bf16)

    mixed_grad, grad_proj, *expert_grads = middle(
        E,
        C,
        G,
        mixed_grad.reshape(batches, run, width),
        jnp.swapaxes(mixed_low, 0, 1).reshape(E, C, G, rows, own),
        attn_grad,
        x,
        pair_grad,
        gate_pre_grad,
        up_pre_grad,
        act,
        6,
        "middle",
    )
    grad_gate, grad_up, grad_down = (
        (mine + other.astype(f32))[None] for mine, other in zip(expert_grads[:3], expert_grads[3:])
    )
    grad_proj = jnp.sum(grad_proj.astype(f32), axis=0)
    query_grad, key_grad, value_grad = (
        grad.reshape(every, size)
        for grad in attend_back(
            query_low, key_low, value_low, mixed_grad.reshape(by_sequence), ids, log_total
        )
    )
    query_back, key_back = query_grad * head_gains[:, 1], key_grad * head_gains[:, 2]
    means = jnp.stack([jnp.sum(query_back * query_hat, axis=1), jnp.sum(key_back * key_hat, axis=1)])
    means = column_sum(E, C, G, means, 7, "norm_means") / width
    raw_grads = jnp.concatenate(
        [
            (query_factor * (query_back - query_hat * means[0][:, None])).astype(bf16),
            (key_factor * (key_back - key_hat * means[1][:, None])).astype(bf16),
            value_grad.astype(bf16),
        ],
        axis=1,
    )
    gain_heads = jnp.stack(
        [jnp.sum(query_grad * query_hat, axis=0), jnp.sum(key_grad * key_hat, axis=0)], axis=1
    )
    gain_heads = lax.dynamic_update_slice(
        jnp.zeros((width, 2), f32), gain_heads, (me * size, 0)
    )
    sums = jnp.concatenate(
        [gain_heads, gain_second[:, None], contract(second_low, logit_grad, (0, 0))], axis=1
    )
    sums = jnp.pad(sums, ((0, 0), (0, small_width - sums.shape[1])))
    first_grad, grad_qkv, sums = finish(
        E,
        C,
        G,
        raw_grads.reshape(batches, count, run, 3 * size),
        w_qkv,
        normed,
        sums.reshape(E, width // E, small_width),
        8,
        "finish",
    )
    sums = jnp.sum(sums, axis=0)
    first_factor = rms_factor(inputs)
    first_hat = inputs * first_factor
    input_grad = resid_grad + norm_back(first_grad * gains[:, 0], first_hat, first_factor)

    grad_qkv = jnp.swapaxes(grad_qkv.astype(f32), 0, 1)
    grad_query, grad_key, grad_value = (
        grad_qkv[:, :, i * size : (i + 1) * size].reshape(rows, width) for i in range(3)
    )
    gain_first = sum(
        jnp.sum(w.astype(f32) * grad, axis=1)
        for w, grad in ((w_query, grad_query), (w_key, grad_key), (w_value, grad_value))
    )
    gain_first = gain_first / norm_gains[:, 0].astype(f32)
    grad_gains = jnp.concatenate([gain_first[:, None], sums[:, :3]], axis=1)
    return (
        activations,
        input_grad.reshape(tokens.shape),
        grad_gains,
        grad_query,
        grad_key,
        grad_value,
        grad_proj,
        sums[:, 3 : 3 + experts],
        grad_gate,
        grad_up,
        grad_down,
    )


def solution(mesh):
    by_token = ("context", "dp")
    by_expert = P(("expert", "context"), None, None)
    by_row = P(ALL_AXES, None)
    rows = P("expert", by_token, None)
    return jax.shard_map(
        body,
        mesh=mesh,
        in_specs=(
            rows,
            P("expert", by_token),
            rows,
            by_row,
            by_row,
            by_row,
            by_row,
            by_row,
            by_row,
            by_expert,
            by_expert,
            by_expert,
            rows,
        ),
        out_specs=(
            rows,
            rows,
            by_row,
            by_row,
            by_row,
            by_row,
            by_row,
            by_row,
            P(("expert", "context"), None, "dp"),
            P(("expert", "context"), None, "dp"),
            P(("expert", "context"), "dp", None),
        ),
        check_vma=False,
    )
```

```python
import functools

import jax
import jax.numpy as jnp
from jax import lax
from jax.experimental import pallas as pl
from jax.experimental.pallas import tpu as pltpu
from jax.sharding import PartitionSpec as P

HEAD = 128
EPSILON = 1e-05
MASKED = -1e30
UNUSED_SLOT = 4096.0
ALL_AXES = ("expert", "context", "dp")
MESH = pl.DeviceIdType.MESH
ANY = pl.BlockSpec(memory_space=pl.ANY)
VMEM = pl.BlockSpec(memory_space=pltpu.VMEM)
DMA = pltpu.SemaphoreType.DMA
MIB = 1 << 20
f32 = jnp.float32
bf16 = jnp.bfloat16


def call(kernel, operands, out_shapes, in_specs, out_specs, scratch, collective, name, vmem=32):
    return pl.pallas_call(
        kernel,
        out_shape=out_shapes,
        in_specs=in_specs,
        out_specs=out_specs,
        scratch_shapes=scratch,
        compiler_params=pltpu.CompilerParams(
            collective_id=collective, has_side_effects=True, vmem_limit_bytes=vmem * MIB
        ),
        name=name,
    )(*operands)


def position():
    return lax.axis_index("expert"), lax.axis_index("context"), lax.axis_index("dp")


def meet(devices):
    barrier = pltpu.get_barrier_semaphore()
    for device in devices:
        pl.semaphore_signal(barrier, inc=1, device_id=device, device_id_type=MESH)
    pl.semaphore_wait(barrier, len(devices))


def remote(source, target, send_sem, recv_sem, device):
    return pltpu.make_async_remote_copy(
        src_ref=source,
        dst_ref=target,
        send_sem=send_sem,
        recv_sem=recv_sem,
        device_id=device,
        device_id_type=MESH,
    )


def column_peers(E, C, G):
    e, c, d = position()
    me = c * G + d
    peers = []
    for offset in range(1, C * G):
        index = lax.rem(me + offset, C * G)
        peers.append((offset, index, (e, index // G, lax.rem(index, G))))
    return me, peers


def plane_peers(E):
    e, c, d = position()
    return [(i, lax.rem(e + i, E), (lax.rem(e + i, E), c, d)) for i in range(1, E)]


def level_peers(C):
    e, c, d = position()
    return [(i, lax.rem(c + i, C), (e, lax.rem(c + i, C), d)) for i in range(1, C)]


def start_kernel(
    E,
    C,
    G,
    tokens,
    weights,
    small_weights,
    output,
    ids,
    slots,
    column,
    gathered,
    small_gathered,
    full_output,
    ids_out,
    slots_out,
    ws,
    wr,
    bs,
    br,
    hs,
    hr,
    ts,
    tr,
    ls,
    ms,
    mr,
    ps,
    pr,
    fs,
    fr,
    gs,
    gr,
):
    e, c, d = position()
    me, peers = column_peers(E, C, G)
    planes = plane_peers(E)
    batches = tokens.shape[0]
    sibling = (e, c, 1 - d)
    meet([device for _, _, device in peers] + [device for _, _, device in planes])
    kinds = ((weights, gathered), (small_weights, small_gathered))
    weight_copies = []
    for j, (source, target) in enumerate(kinds):
        for offset, index, device in peers:
            part = source.at[index] if j == 0 else source
            weight_copies.append(
                remote(part, target.at[e, me], ws.at[j, offset], wr.at[j, offset], device)
            )
    for copy in weight_copies:
        copy.start()
    local = [
        pltpu.make_async_copy(weights.at[me], gathered.at[e, me], ls.at[0]),
        pltpu.make_async_copy(small_weights, small_gathered.at[e, me], ls.at[1]),
        pltpu.make_async_copy(output, full_output.at[e, c, d], ls.at[2]),
    ]
    for b in range(batches):
        local.append(pltpu.make_async_copy(tokens.at[b], column.at[b, me], ls.at[3 + b]))
    for copy in local:
        copy.start()

    def source_of(item):
        return output if item == 0 else tokens.at[item - 1]

    def place(item, level):
        return full_output.at[e, level, d] if item == 0 else column.at[item - 1, level * G + d]

    def to_sibling(source, item, level, arrival):
        return remote(
            source, place(item, level), ts.at[item, arrival], tr.at[item, arrival], sibling
        )

    def step(hop, source, item, level, up):
        to = (e, c + 1, d) if up else (e, c - 1, d)
        way = 0 if up else 1
        return remote(
            source, place(item, level), hs.at[way, item, hop], hr.at[way, item, hop], to
        )

    def relay(item, hop):
        for up in (True, False):
            level = c - hop if up else c + hop
            here = (c >= hop) if up else (c + hop < C)
            onward = (c < C - 1) if up else (c > 0)

            @pl.when(here)
            def _():
                landed = place(item, level)
                step(hop - 1, landed, item, level, up).wait_recv()
                if hop < C - 1:

                    @pl.when(onward)
                    def _():
                        step(hop, landed, item, level, up).start()

                if G > 1:
                    to_sibling(landed, item, level, hop if up else C - 1 + hop).start()

    for item in range(batches + 1):

        @pl.when(c < C - 1)
        def _():
            step(0, source_of(item), item, c, True).start()

        @pl.when(c > 0)
        def _():
            step(0, source_of(item), item, c, False).start()

        if G > 1:
            to_sibling(source_of(item), item, c, 0).start()
    small = []
    for offset, _, device in peers:
        small.append(remote(ids, ids_out.at[me], ms.at[offset], mr.at[offset], device))
    for i, level, device in level_peers(C):
        small.append(remote(slots.at[level], slots_out.at[i], ps.at[i], pr.at[i], device))
    for copy in small:
        copy.start()
    ids_out[me] = ids[...]
    slots_out[0] = slots[c]
    for copy in weight_copies:
        copy.wait_recv()
    for copy in local[:3]:
        copy.wait()
    plane_copies = []
    for j, (_, target) in enumerate(kinds):
        for i, _, device in planes:
            copy = remote(target.at[e], target.at[e], bs.at[j, i], br.at[j, i], device)
            copy.start()
            plane_copies.append(copy)
    for hop in range(1, C):
        relay(0, hop)

    def output_copy(i, plane, device):
        mine = full_output.at[e, :, d]
        return remote(mine, mine, fs.at[i], fr.at[i], device)

    def output_sibling(i):
        part = full_output.at[lax.rem(e + E - i, E), :, d]
        return remote(part, part, gs.at[i], gr.at[i], sibling)

    for i, plane, device in planes:
        output_copy(i, plane, device).start()
    for hop in range(1, C):
        for item in range(1, batches + 1):
            relay(item, hop)
    for i, plane, device in planes:
        output_copy(i, plane, device).wait_recv()
        if G > 1:
            output_sibling(i).start()

    for item in range(batches + 1):
        if G > 1:
            to_sibling(source_of(item), item, c, 0).wait()
        for hop in range(C - 1):
            for up in (True, False):
                arrival = hop + 1 if up else C + hop
                origin = c - hop if up else c + hop
                if up:
                    sends = jnp.logical_and(origin >= 0, c < C - 1)
                    arrives = c >= hop + 1
                else:
                    sends = jnp.logical_and(origin < C, c > 0)
                    arrives = c + hop + 1 < C

                @pl.when(sends)
                def _():
                    step(hop, source_of(item), item, c, up).wait_send()

                if G > 1:

                    @pl.when(arrives)
                    def _():
                        to_sibling(source_of(item), item, c, arrival).wait()

    for i, plane, device in planes:
        output_copy(i, plane, device).wait_send()
        if G > 1:
            output_sibling(i).wait()
    for copy in weight_copies:
        copy.wait_send()
    for copy in plane_copies + small + local[3:]:
        copy.wait()


def start(E, C, G, tokens, weights, small_weights, output, ids, slots):
    batches, run, width = tokens.shape
    count = C * G
    rows, columns = weights.shape[1:]
    items = batches + 1
    return call(
        functools.partial(start_kernel, E, C, G),
        (tokens, weights, small_weights, output, ids, slots),
        (
            jax.ShapeDtypeStruct((batches, count, run, width), tokens.dtype),
            jax.ShapeDtypeStruct((E, count, rows, columns), weights.dtype),
            jax.ShapeDtypeStruct((E, count) + small_weights.shape, weights.dtype),
            jax.ShapeDtypeStruct((E, C, G, rows, width), weights.dtype),
            jax.ShapeDtypeStruct((count,) + ids.shape, ids.dtype),
            jax.ShapeDtypeStruct(slots.shape, slots.dtype),
        ),
        [ANY, ANY, ANY, ANY, VMEM, VMEM],
        (ANY, ANY, ANY, ANY, VMEM, VMEM),
        [
            DMA((2, count)),
            DMA((2, count)),
            DMA((2, E)),
            DMA((2, E)),
            DMA((2, items, C)),
            DMA((2, items, C)),
            DMA((items, 2 * C)),
            DMA((items, 2 * C)),
            DMA((items + 2,)),
            DMA((count,)),
            DMA((count,)),
            DMA((C,)),
            DMA((C,)),
            DMA((E,)),
            DMA((E,)),
            DMA((E,)),
            DMA((E,)),
        ],
        1,
        "start",
    )


def choose(slots, count):
    cells = lax.broadcasted_iota(jnp.int32, (count, slots.shape[1]), 0).astype(f32)
    return jnp.concatenate(
        [(cells == slots[i : i + 1, :]).astype(bf16) for i in range(slots.shape[0])], axis=0
    )


class Flow:
    def __init__(self, E, C, rows, slots, landed, packed, target, own, zs, zr, xs, xr, stay):
        self.E, self.C, self.rows, self.slots = E, C, rows, slots
        self.landed, self.packed, self.target = landed, packed, target
        self.sems = own, zs, zr, xs, xr, stay
        self.e, self.c, self.d = position()
        self.batches = rows.shape[0]
        self.cap, self.width = target.shape[3:]
        self.kept = packed.shape[0]
        self.chunks = self.batches * C

    def level_entry(self, far):
        high = 2 * self.c // self.C
        return high * far + (1 - high) * lax.rem(self.C - far, self.C)

    def own(self, b):
        return pltpu.make_async_copy(self.rows.at[b], self.landed.at[0, b], self.sems[0].at[b])

    def hop(self, b, i, way):
        there = i + 1 if way == 0 else lax.rem(i + self.C - 1, self.C)
        level = lax.rem(self.c + (1 if way == 0 else self.C - 1), self.C)
        return remote(
            self.landed.at[i, b],
            self.landed.at[there, b],
            self.sems[1].at[way, i, b],
            self.sems[2].at[there, b],
            (self.e, level, self.d),
        )

    def arrival(self, b, i):
        entry = self.landed.at[i, b]
        return remote(
            entry,
            entry,
            self.sems[1].at[0, i, b],
            self.sems[2].at[i, b],
            (self.e, self.c, 1 - self.d),
        )

    def onward(self, i, way):
        if way == 0:
            return jnp.logical_and(i <= self.c, self.c < self.C - 1)
        return jnp.logical_and(lax.rem(self.C - i, self.C) + self.c < self.C, self.c > 0)

    def begin(self):
        for b in range(self.batches):
            self.own(b).start()
        for b in range(self.batches):
            self.own(b).wait()
            for way in range(2):

                @pl.when(self.onward(0, way))
                def _():
                    self.hop(b, 0, way).start()

    def relay(self, far, b):
        for way in range(2):
            i = far if way == 0 else self.C - far

            @pl.when((far <= self.c) if way == 0 else (far + self.c < self.C))
            def _():
                self.arrival(b, i).wait_recv()

                @pl.when(self.onward(i, way))
                def _():
                    self.hop(b, i, way).start()

    def hops_sent(self, b, i):
        for way in range(2):

            @pl.when(self.onward(i, way))
            def _():
                self.hop(b, i, way).wait_send()

    def across(self, n, b, i, k):
        plane = lax.rem(self.e + k, self.E)
        return remote(
            self.packed.at[lax.rem(n, self.kept), plane],
            self.target.at[i, b, k],
            self.sems[3].at[i, b, k],
            self.sems[4].at[i, b, k],
            (plane, self.c, self.d),
        )

    def stay(self, n, b, i):
        return pltpu.make_async_copy(
            self.packed.at[lax.rem(n, self.kept), self.e],
            self.target.at[i, b, 0],
            self.sems[5].at[i, b],
        )

    def compact(self, n, b, i):
        place = lax.rem(n, self.kept)
        picks = choose(self.slots[i, b], self.cap)
        for at in range(0, self.width, 512):
            part = jnp.dot(
                picks, self.landed[i, b, :, at : at + 512], preferred_element_type=f32
            ).astype(bf16)
            self.packed[place, :, :, at : at + 512] = part.reshape(self.E, self.cap, 512)
        for k in range(1, self.E):
            self.across(n, b, i, k).start()
        self.stay(n, b, i).start()

    def crossed(self, n, b, i):
        for k in range(1, self.E):
            self.across(n, b, i, k).wait_send()

    def arrived(self, n, b, i):
        for k in range(1, self.E):
            self.across(n, b, i, k).wait_recv()

    @staticmethod
    def scratch(E, C, batches, run, width, cap, kept):
        return [
            pltpu.VMEM((C, batches, run, width), bf16),
            pltpu.VMEM((kept, E, cap, width), bf16),
            DMA((batches,)),
            DMA((2, C, batches)),
            DMA((C, batches)),
            DMA((C, batches, E)),
            DMA((C, batches, E)),
            DMA((C, batches)),
        ]


class Return:
    def __init__(self, E, C, runs, rows, slots, out, returned, sums, ys, yr, bs, us, ur, ks):
        self.E, self.C, self.runs = E, C, runs
        self.rows, self.slots, self.out = rows, slots, out
        self.returned, self.sums = returned, sums
        self.sems = ys, yr, bs, us, ur, ks
        self.e, self.c, self.d = position()

    def back(self, n, k):
        b, i = self.runs[n]
        return remote(
            self.rows.at[i, b, k],
            self.returned.at[n, self.e],
            self.sems[0].at[n, k],
            self.sems[1].at[n, k],
            (lax.rem(self.e + self.E - k, self.E), self.c, self.d),
        )

    def own(self, n):
        b, i = self.runs[n]
        return pltpu.make_async_copy(
            self.rows.at[i, b, 0], self.returned.at[n, self.e], self.sems[2].at[n]
        )

    def along(self, n):
        i = self.runs[n][1]
        if i == 0:
            return pltpu.make_async_copy(self.sums.at[n], self.out.at[n], self.sems[5].at[n])
        to = (self.e, lax.rem(self.c + self.C - i, self.C), self.d)
        return remote(
            self.sums.at[n], self.out.at[n], self.sems[3].at[n], self.sems[4].at[n], to
        )

    def begin(self):
        for n in range(len(self.runs)):
            for k in range(1, self.E):
                self.back(n, k).start()
            self.own(n).start()

    def combine(self, n):
        b, i = self.runs[n]
        for k in range(1, self.E):
            self.back(n, k).wait_recv()
        self.own(n).wait()
        cap, width = self.rows.shape[3:]
        picks = choose(self.slots[i, b], cap)
        for at in range(0, width, 512):
            part = self.returned[n, :, :, at : at + 512].reshape(self.E * cap, 512)
            self.sums[n, :, at : at + 512] = contract(picks, part, (0, 0)).astype(bf16)
        self.along(n).start()

    def end(self):
        for n in range(len(self.runs)):
            for k in range(1, self.E):
                self.back(n, k).wait_send()
            self.along(n).wait()

    @staticmethod
    def scratch(E, C, count, run, width, cap):
        return [
            pltpu.VMEM((count, E, cap, width), bf16),
            pltpu.VMEM((count, run, width), bf16),
            DMA((count, E)),
            DMA((count, E)),
            DMA((count,)),
            DMA((count,)),
            DMA((count,)),
            DMA((count,)),
        ]


def forward_kernel(
    E,
    C,
    G,
    column,
    gain,
    head_gains,
    w_qkv,
    row_ids,
    key_ids,
    slots,
    upstream,
    normed,
    queries,
    keys,
    values,
    query_hat,
    key_hat,
    log_total,
    factors,
    mixed,
    u_out,
    raw,
    low,
    squares,
    parts,
    heads,
    landed,
    packed,
    own,
    zs,
    zr,
    xs,
    xr,
    stay,
    raw_sem,
    low_sem,
    ss,
    sr,
    ms,
    mr,
    ml,
):
    me, peers = column_peers(E, C, G)
    planes = plane_peers(E)
    every, width = column.shape
    batches, length, size = heads.shape
    run = length // (C * G)
    block = raw.shape[1]
    blocks = every // block
    scale = HEAD**-0.5
    meet([device for _, _, device in peers] + [device for _, _, device in planes])
    flow = Flow(E, C, upstream, slots, landed, packed, u_out, own, zs, zr, xs, xr, stay)

    def load(j):
        at = pl.multiple_of(j * block, block)
        place = lax.rem(j, 2)
        return pltpu.make_async_copy(column.at[pl.ds(at, block)], raw.at[place], raw_sem.at[place])

    def store(j):
        at = pl.multiple_of(j * block, block)
        place = lax.rem(j, 2)
        return pltpu.make_async_copy(low.at[place], normed.at[pl.ds(at, block)], low_sem.at[place])

    def chunk_of(n):
        return n % batches, flow.level_entry(n // batches)

    chunk = iter(range(flow.chunks))

    def carry_on(count):
        for _ in range(count):
            n = next(chunk, None)
            if n is None:
                return
            if n >= flow.kept:
                before = n - flow.kept, *chunk_of(n - flow.kept)
                flow.crossed(*before)
                flow.stay(*before).wait()
            if n >= batches:
                flow.relay(n // batches, n % batches)
            flow.compact(n, *chunk_of(n))

    load(0).start()
    load(1).start()
    flow.begin()
    carry_on(batches)
    ones = jnp.ones((8, size), f32)

    def project(j, carry):
        place = lax.rem(j, 2)
        rows = pl.ds(pl.multiple_of(j * block, block), block)
        load(j).wait()

        @pl.when(j >= 2)
        def _():
            store(j - 2).wait()

        total = jnp.zeros((block, 1), f32)
        for at in range(0, width, 512):
            part = raw[place, :, at : at + 512].astype(f32)
            total += jnp.sum(part * part, axis=1, keepdims=True)
        factor = lax.rsqrt(total / width + EPSILON)
        for at in range(0, width, 512):
            part = raw[place, :, at : at + 512].astype(f32) * factor
            low[place, :, at : at + 512] = (part * gain[:, at : at + 512]).astype(bf16)
        store(j).start()

        @pl.when(j + 2 < blocks)
        def _():
            load(j + 2).start()

        for kind in range(3):
            part = jnp.dot(
                low[place],
                w_qkv[:, kind * size : (kind + 1) * size],
                preferred_element_type=f32,
            )
            if kind == 2:
                values[rows] = part.astype(bf16)
            else:
                (query_hat, key_hat)[kind][rows] = part
                sums = lax.dot_general(
                    ones,
                    part * part,
                    (((1,), (1,)), ((), ())),
                    precision=lax.Precision.HIGHEST,
                    preferred_element_type=f32,
                )
                squares[kind, :, rows] = sums[:1]
        return carry

    half = blocks // 2
    lax.fori_loop(0, half, project, 0)
    carry_on(1)
    lax.fori_loop(half, blocks, project, 0)
    shares = [
        remote(squares, parts.at[me], ss.at[offset], sr.at[offset], device)
        for offset, _, device in peers
    ]
    for copy in shares:
        copy.start()
    parts[me] = squares[...]
    carry_on(1)
    for copy in shares:
        copy.wait_recv()
    total = parts[0]
    for index in range(1, C * G):
        total = total + parts[index]
    factors[...] = lax.rsqrt(total / width + EPSILON)
    rows_at = lax.broadcasted_iota(jnp.int32, (block, block), 0)
    same = rows_at == lax.broadcasted_iota(jnp.int32, (block, block), 1)

    def scaled(j, carry):
        rows = pl.ds(pl.multiple_of(j * block, block), block)
        for kind, (hat, out) in enumerate(((query_hat, queries), (key_hat, keys))):
            factor = jnp.sum(jnp.where(same, factors[kind, :, rows], 0.0), axis=1, keepdims=True)
            part = hat[rows] * factor
            hat[rows] = part
            out[rows] = (part * head_gains[kind : kind + 1]).astype(bf16)
        return carry

    lax.fori_loop(0, blocks, scaled, 0)
    carry_on(1)

    def mixed_copy(b, offset, index, device):
        where = pl.ds(pl.multiple_of(me * size, size), size)
        part = heads.at[b, pl.ds(pl.multiple_of(index * run, run), run)]
        return remote(part, mixed.at[b, :, where], ms.at[b, offset], mr.at[b, offset], device)

    def mixed_own(b):
        where = pl.ds(pl.multiple_of(me * size, size), size)
        part = heads.at[b, pl.ds(pl.multiple_of(me * run, run), run)]
        return pltpu.make_async_copy(part, mixed.at[b, :, where], ml.at[b])

    for b in range(batches):

        def head(h, carry, b=b):
            lanes = pl.ds(pl.multiple_of(h * HEAD, HEAD), HEAD)
            for first, count, seen in query_blocks(length):
                rows = pl.ds(b * length + first, count)
                seen_rows = pl.ds(b * length, seen)
                scores = contract(queries[rows, lanes], keys[seen_rows, lanes], (1, 1)) * scale
                allowed = key_ids[b, :, :seen] <= row_ids[b, first : first + count]
                scores = jnp.where(allowed, scores, MASKED)
                peak = jnp.max(scores, axis=1, keepdims=True)
                grown = jnp.exp(scores - peak)
                total = jnp.sum(grown, axis=1, keepdims=True)
                probs = (grown * (1.0 / total)).astype(bf16)
                heads[b, first : first + count, lanes] = jnp.dot(
                    probs, values[seen_rows, lanes], preferred_element_type=f32
                ).astype(bf16)
                log_total[b, h, first : first + count] = peak + jnp.log(total)
            return carry

        lax.fori_loop(0, size // HEAD, head, 0)
        for offset, index, device in peers:
            mixed_copy(b, offset, index, device).start()
        mixed_own(b).start()
        carry_on(1)
    carry_on(flow.chunks)

    for copy in shares:
        copy.wait_send()
    for j in (blocks - 2, blocks - 1):
        store(j).wait()
    for b in range(batches):
        for offset, index, device in peers:
            mixed_copy(b, offset, index, device).wait()
        mixed_own(b).wait()

    for n in range(flow.chunks):
        b, i = chunk_of(n)
        flow.hops_sent(b, i)
        flow.arrived(n, b, i)
        if n >= flow.chunks - flow.kept:
            flow.crossed(n, b, i)
            flow.stay(n, b, i).wait()


def run_forward(E, C, G, column, gain, head_gains, w_qkv, ids, slots, upstream, cap, collective, name):
    every, width = column.shape
    batches, run = upstream.shape[:2]
    count = C * G
    length = count * run
    size = width // count
    block = min(256, every)
    low = jax.ShapeDtypeStruct((every, size), bf16)
    wide = jax.ShapeDtypeStruct((every, size), f32)
    return call(
        functools.partial(forward_kernel, E, C, G),
        (column, gain, head_gains, w_qkv, ids[:, :, None], ids[:, None, :], slots, upstream),
        (
            jax.ShapeDtypeStruct((every, width), bf16),
            low,
            low,
            low,
            wide,
            wide,
            jax.ShapeDtypeStruct((batches, size // HEAD, length, 1), f32),
            jax.ShapeDtypeStruct((2, 1, every), f32),
            jax.ShapeDtypeStruct(upstream.shape, bf16),
            jax.ShapeDtypeStruct((C, batches, E, cap, width), bf16),
        ),
        [ANY] + [VMEM] * 6 + [ANY],
        (ANY,) + (VMEM,) * 7 + (ANY, ANY),
        [
            pltpu.VMEM((2, block, width), bf16),
            pltpu.VMEM((2, block, width), bf16),
            pltpu.VMEM((2, 1, every), f32),
            pltpu.VMEM((count, 2, 1, every), f32),
            pltpu.VMEM((batches, length, size), bf16),
        ]
        + Flow.scratch(E, C, batches, run, width, cap, 3)
        + [
            DMA((2,)),
            DMA((2,)),
            DMA((count,)),
            DMA((count,)),
            DMA((batches, count)),
            DMA((batches, count)),
            DMA((batches,)),
        ],
        collective,
        name,
        vmem=56,
    )


def experts_kernel(
    E,
    C,
    rows_x,
    u_in,
    slots,
    gates,
    w_gate,
    w_up,
    w_down,
    out,
    x_out,
    y_out,
    pair_out,
    act_out,
    gate_back_out,
    up_back_out,
    scalars_out,
    table,
    scalars,
    landed,
    packed,
    own,
    zs,
    zr,
    xs,
    xr,
    stay,
    sums,
    returned,
    x,
    u,
    pair,
    act,
    gate_back,
    up_back,
    gated,
    sent,
    gs,
    gr,
    ss,
    sr,
    ys,
    yr,
    bs,
    us,
    ur,
    ks,
    loads,
    stores,
):
    e, c, d = position()
    batches, run, width = rows_x.shape
    cap = x_out.shape[3]
    units = w_gate.shape[1]
    chunks = batches * C
    total = E * cap
    kept = sent.shape[0]
    lead, lag = 1, 2
    everyone = [(k, i) for k in range(E) for i in range(C) if k + i > 0]
    ahead = [(k, i, (lax.rem(e + k, E), lax.rem(c + i, C), d)) for k, i in everyone]
    behind = [(k, i, (lax.rem(e + E - k, E), lax.rem(c + C - i, C), d)) for k, i in everyone]
    meet([device for _, _, device in ahead])
    flow = Flow(E, C, rows_x, slots, landed, packed, x_out, own, zs, zr, xs, xr, stay)

    def far_of(n):
        return lax.rem((n + batches - 1) // batches, C), lax.rem(n + batches - 1, batches)

    def chunk_of(n):
        far, b = far_of(n)
        return b, flow.level_entry(far)

    def back(n, b, i, k):
        return remote(
            sent.at[lax.rem(n, kept), k],
            returned.at[i, b, e],
            ys.at[i, b, k],
            yr.at[i, b, k],
            (lax.rem(e + E - k, E), c, d),
        )

    def back_own(n, b, i):
        return pltpu.make_async_copy(
            sent.at[lax.rem(n, kept), 0], returned.at[i, b, e], bs.at[i, b]
        )

    def up(b, i):
        return remote(
            sums.at[i, b],
            out.at[c, b],
            us.at[i, b],
            ur.at[i, b],
            (e, lax.rem(c + C - i, C), d),
        )

    def keep(b):
        return pltpu.make_async_copy(sums.at[0, b], out.at[c, b], ks.at[b])

    def load(a, b, i):
        source, target = ((x_out, x), (u_in, u))[a]
        return pltpu.make_async_copy(source.at[i, b], target, loads.at[a])

    def store(j, b, i):
        source = (pair, act, gate_back, up_back, gated)[j]
        target = (pair_out, act_out, gate_back_out, up_back_out, y_out)[j]
        return pltpu.make_async_copy(source, target.at[i, b], stores.at[j])

    flow.begin()
    small = [
        remote(gates.at[device[0], device[1]], table.at[k, i], gs.at[k, i], gr.at[k, i], device)
        for k, i, device in ahead
    ]
    for copy in small:
        copy.start()
    table[0, 0] = gates[e, c]

    def compact(n):
        @pl.when(n >= flow.kept)
        def _():
            flow.crossed(n - flow.kept, *chunk_of(n - flow.kept))

        flow.compact(n, *chunk_of(n))

    def expert(n):
        b, i = chunk_of(n)
        load(1, b, i).start()
        flow.arrived(n, b, i)
        flow.stay(n, b, i).wait()
        load(0, b, i).start()

        @pl.when(n > 0)
        def _():
            before = chunk_of(n - 1)
            for j in range(5):
                store(j, *before).wait()

        @pl.when(n >= kept)
        def _():
            before = chunk_of(n - kept)
            for k in range(1, E):
                back(n - kept, *before, k).wait_send()

        holds, gate = [], []
        cells = lax.broadcasted_iota(jnp.int32, (cap, run), 0).astype(f32)
        for k in range(E):
            hold = cells == table[k, i, b]
            holds.append(hold)
            gate.append(
                jnp.sum(jnp.where(hold, table[k, i, batches + b], 0.0), axis=1, keepdims=True)
            )
        gate = jnp.concatenate(gate, axis=0)
        for a in range(2):
            load(a, b, i).wait()
        for at in range(0, width, 512):
            part = u[:, :, at : at + 512].reshape(total, 512).astype(f32)
            pair[:, :, at : at + 512] = (gate * part).astype(bf16).reshape(E, cap, 512)
        store(0, b, i).start()
        inputs = x[...].reshape(total, width)
        grads = pair[...].reshape(total, width)
        for at in range(0, units, 256):
            gate_pre = jnp.dot(inputs, w_gate[:, at : at + 256], preferred_element_type=f32)
            up_pre = jnp.dot(inputs, w_up[:, at : at + 256], preferred_element_type=f32)
            act_grad = contract(grads, w_down[at : at + 256, :], (1, 1))
            sigmoid = jax.nn.sigmoid(gate_pre)
            silu = gate_pre * sigmoid
            act[:, at : at + 256] = (silu * up_pre).astype(bf16)
            gate_back[:, at : at + 256] = (
                act_grad * up_pre * sigmoid * (1.0 + gate_pre * (1.0 - sigmoid))
            ).astype(bf16)
            up_back[:, at : at + 256] = (act_grad * silu).astype(bf16)
        for j in range(1, 4):
            store(j, b, i).start()
        place = lax.rem(n, kept)
        gate_grad = jnp.zeros((total, 1), f32)
        for at in range(0, width, 512):
            out = jnp.dot(act[...], w_down[:, at : at + 512], preferred_element_type=f32)
            out = out.astype(bf16).astype(f32)
            gate_grad += jnp.sum(
                out * u[:, :, at : at + 512].reshape(total, 512).astype(f32), axis=1, keepdims=True
            )
            gated[:, :, at : at + 512] = (gate * out).astype(bf16).reshape(E, cap, 512)
            back_rows = contract(gate_back[...], w_gate[at : at + 512, :], (1, 1))
            back_rows += contract(up_back[...], w_up[at : at + 512, :], (1, 1))
            sent[place, :, :, at : at + 512] = back_rows.astype(bf16).reshape(E, cap, 512)
        for k in range(1, E):
            back(n, b, i, k).start()
        back_own(n, b, i).start()
        store(4, b, i).start()
        for k in range(E):
            scalars[k, i, b] = jnp.sum(
                jnp.where(holds[k], gate_grad[k * cap : (k + 1) * cap], 0.0), axis=0, keepdims=True
            )

    def combine(n):
        b, i = chunk_of(n)
        picks = choose(slots[i, b], cap)
        for k in range(1, E):
            back(n, b, i, k).wait_recv()
        back_own(n, b, i).wait()
        for at in range(0, width, 512):
            part = returned[i, b, :, :, at : at + 512].reshape(total, 512)
            sums[i, b, :, at : at + 512] = contract(picks, part, (0, 0)).astype(bf16)

        @pl.when(i > 0)
        def _():
            up(b, i).start()

        @pl.when(i == 0)
        def _():
            keep(b).start()

    def step(s, carry):
        @pl.when(jnp.logical_and(s > 0, s <= batches * (C - 1)))
        def _():
            flow.relay(*far_of(s))

        @pl.when(s < chunks)
        def _():
            compact(s)

        @pl.when(jnp.logical_and(s >= lead, s < chunks + lead))
        def _():
            expert(s - lead)

        @pl.when(s >= lag)
        def _():
            combine(s - lag)

        return carry

    for copy in small:
        copy.wait_recv()
    lax.fori_loop(0, chunks + lag, step, 0)
    scalars_out[e, c] = scalars[0, 0]
    last = [
        remote(scalars.at[k, i], scalars_out.at[e, c], ss.at[k, i], sr.at[k, i], device)
        for k, i, device in behind
    ]
    for copy in last:
        copy.start()
    for copy in small:
        copy.wait_send()
    for j in range(5):
        store(j, *chunk_of(chunks - 1)).wait()

    def finish(n, carry):
        b, i = chunk_of(n)
        flow.hops_sent(b, i)

        @pl.when(n >= chunks - flow.kept)
        def _():
            flow.crossed(n, b, i)

        @pl.when(n >= chunks - kept)
        def _():
            for k in range(1, E):
                back(n, b, i, k).wait_send()

        @pl.when(i > 0)
        def _():
            up(b, i).wait()

        @pl.when(i == 0)
        def _():
            keep(b).wait()

        return carry

    lax.fori_loop(0, chunks, finish, 0)
    for copy in last:
        copy.wait()


def run_experts(E, C, rows_x, u_in, slots, gates, w_gate, w_up, w_down, cap, collective, name):
    batches, run, width = rows_x.shape
    units = w_gate.shape[1]
    total = E * cap
    kept = 3
    by_slot = jax.ShapeDtypeStruct((C, batches, E, cap, width), bf16)
    by_token = jax.ShapeDtypeStruct((C, batches, run, width), bf16)
    hidden = jax.ShapeDtypeStruct((C, batches, total, units), bf16)
    return call(
        functools.partial(experts_kernel, E, C),
        (rows_x, u_in, slots, gates, w_gate, w_up, w_down),
        (
            by_token,
            by_slot,
            by_slot,
            by_slot,
            hidden,
            hidden,
            hidden,
            jax.ShapeDtypeStruct((E, C, batches, 1, run), f32),
        ),
        [ANY, ANY, VMEM, VMEM, VMEM, VMEM, VMEM],
        (ANY,) * 7 + (VMEM,),
        [
            pltpu.VMEM(gates.shape, f32),
            pltpu.VMEM((E, C, batches, 1, run), f32),
        ]
        + Flow.scratch(E, C, batches, run, width, cap, kept)
        + [
            pltpu.VMEM((C, batches, run, width), bf16),
            pltpu.VMEM((C, batches, E, cap, width), bf16),
            pltpu.VMEM((E, cap, width), bf16),
            pltpu.VMEM((E, cap, width), bf16),
            pltpu.VMEM((E, cap, width), bf16),
            pltpu.VMEM((total, units), bf16),
            pltpu.VMEM((total, units), bf16),
            pltpu.VMEM((total, units), bf16),
            pltpu.VMEM((E, cap, width), bf16),
            pltpu.VMEM((kept, E, cap, width), bf16),
            DMA((E, C)),
            DMA((E, C)),
            DMA((E, C)),
            DMA((E, C)),
            DMA((C, batches, E)),
            DMA((C, batches, E)),
            DMA((C, batches)),
            DMA((C, batches)),
            DMA((C, batches)),
            DMA((batches,)),
            DMA((2,)),
            DMA((5,)),
        ],
        collective,
        name,
        vmem=60,
    )


def middle_kernel(
    E,
    C,
    G,
    runs,
    rows,
    mixed,
    grads,
    x,
    pair,
    gate_back,
    up_back,
    act,
    y_rows,
    slots,
    heads,
    proj,
    own_gate,
    own_up,
    own_down,
    other_gate,
    other_up,
    other_down,
    out,
    hidden,
    wide,
    kept,
    sent,
    swap,
    swapped,
    chip,
    plane_parts,
    level_part,
    hs,
    hr,
    hl,
    cs,
    cr,
    ps,
    pr,
    zs,
    zr,
    rs,
    wide_sem,
    ks,
    xs,
    xr,
    *return_scratch,
):
    e, c, d = position()
    me, peers = column_peers(E, C, G)
    planes, levels = plane_peers(E), level_peers(C)
    batches = rows.shape[0]
    size = heads.shape[3]
    block, width = swap.shape[1:]
    step = wide.shape[2]
    half = own_gate.shape[1]
    sibling = (e, c, 1 - d)
    meet([device for _, _, device in peers] + [device for _, _, device in planes])

    def head_part(b, index):
        return rows.at[b, :, pl.ds(pl.multiple_of(index * size, size), size)]

    head_copies = []
    for b in range(batches):
        for offset, index, device in peers:
            head_copies.append(
                remote(head_part(b, index), heads.at[b, me], hs.at[b, offset], hr.at[b, offset], device)
            )
        head_copies.append(pltpu.make_async_copy(head_part(b, me), heads.at[b, me], hl.at[b]))
    for copy in head_copies:
        copy.start()

    way_back = Return(E, C, runs, y_rows, slots, out, *return_scratch)
    way_back.begin()

    hidden_copies = [
        pltpu.make_async_copy(source, hidden.at[j], rs.at[j])
        for j, source in enumerate((gate_back, up_back, act))
    ]
    for copy in hidden_copies:
        copy.start()
    count = width // step
    sources = [x] * count + [pair] * count

    def wide_copy(item):
        at = (item % count) * step
        return pltpu.make_async_copy(
            sources[item].at[:, pl.ds(at, step)], wide.at[item % 2], wide_sem.at[item % 2]
        )

    wide_copy(0).start()
    wide_copy(1).start()

    def chip_copy(level):
        return remote(swap.at[level], swapped.at[level], cs.at[level], cr.at[level], sibling)

    def proj_part(core, level):
        part = mixed[:, level, core].reshape(block, mixed.shape[4])
        return jnp.dot(part, grads[...], preferred_element_type=f32)

    def plane_copy(level, k, device):
        return remote(
            chip.at[level, lax.rem(e + k, E)],
            plane_parts.at[level, k],
            ps.at[level, k],
            pr.at[level, k],
            device,
        )

    def give(i, carry):
        level = lax.rem(c + 1 + i, C)
        swap[level] = proj_part(1 - d, level).astype(bf16)
        chip_copy(level).start()
        return carry

    def take(i, carry):
        level = lax.rem(c + 1 + i, C)
        part = proj_part(d, level)
        chip_copy(level).wait_recv()
        part = (part + swapped[level].astype(f32)).astype(bf16)
        chip[level] = part.reshape(chip.shape[1:])
        for k, _, device in planes:
            plane_copy(level, k, device).start()
        return carry

    lax.fori_loop(0, C, give, 0)
    lax.fori_loop(0, C, take, 0)

    def level_copy(i, level):
        return remote(level_part.at[level], proj.at[c], zs.at[i], zr.at[i], (e, level, d))

    def plane_sum(i):
        level = lax.rem(c + i, C)
        total = chip[level, e].astype(f32)
        for k, _, device in planes:
            plane_copy(level, k, device).wait_recv()
            total = total + plane_parts[level, k].astype(f32)
        level_part[level] = total.astype(bf16)
        if i > 0:
            level_copy(i, level).start()
        else:
            proj[c] = level_part[c]

    def keep_copy(j, at, place):
        target = (own_gate, own_up, own_down)[j]
        where = target.at[:, pl.ds(at, step)] if j == 2 else target.at[pl.ds(at, step)]
        return pltpu.make_async_copy(kept.at[place], where, ks.at[place])

    def send_copy(j, at, place):
        target = (other_gate, other_up, other_down)[j]
        where = target.at[:, pl.ds(at, step)] if j == 2 else target.at[pl.ds(at, step)]
        return remote(sent.at[place], where, xs.at[place], xr.at[place], sibling)

    kept_copies, sent_copies, after = [], [], {}
    for n in range(len(runs)):
        after.setdefault(count + n * count // max(1, len(runs)), []).append(n)
    for copy in hidden_copies:
        copy.wait()
    for item in range(2 * count):
        wide_copy(item).wait()
        at = (item % count) * step
        left = wide[item % 2]
        for j in (0, 1) if item < count else (2,):
            place = len(sent_copies)

            def product(core):
                part = hidden[j, :, pl.ds(pl.multiple_of(core * half, half), half)]
                return contract(part, left, (0, 0)) if j == 2 else contract(left, part, (0, 0))

            sent[place] = product(1 - d).astype(bf16)
            copy = send_copy(j, at, place)
            copy.start()
            sent_copies.append(copy)
            if place >= 2:
                kept_copies[place - 2].wait()
            kept[place % 2] = product(d)
            copy = keep_copy(j, at, place % 2)
            copy.start()
            kept_copies.append(copy)
        if item + 2 < 2 * count:
            wide_copy(item + 2).start()
        for n in after.get(item, ()):
            way_back.combine(n)
    for i in list(range(1, C)) + [0]:
        plane_sum(i)

    for copy in kept_copies[-2:]:
        copy.wait()
    for copy in sent_copies + head_copies:
        copy.wait()
    for i, level, _ in levels:
        level_copy(i, level).wait()
    way_back.end()

    def done(level, carry):
        chip_copy(level).wait_send()
        for k, _, device in planes:
            plane_copy(level, k, device).wait_send()
        return carry

    lax.fori_loop(0, C, done, 0)


def middle(
    E, C, G, runs, rows, mixed, grads, x, pair, gate_back, up_back, act, y_rows, slots, collective, name
):
    batches, run, width = rows.shape
    count = C * G
    part = mixed.shape[3]
    block = E * part
    total, units = act.shape
    half = units // G
    step = min(512, width)
    items = 3 * (width // step)
    tall = (width, half)
    flat = (half, width)
    return call(
        functools.partial(middle_kernel, E, C, G, runs),
        (rows, mixed, grads, x, pair, gate_back, up_back, act, y_rows, slots),
        (
            jax.ShapeDtypeStruct((batches, count, run, width // count), bf16),
            jax.ShapeDtypeStruct((C, part, width), bf16),
            jax.ShapeDtypeStruct(tall, f32),
            jax.ShapeDtypeStruct(tall, f32),
            jax.ShapeDtypeStruct(flat, f32),
            jax.ShapeDtypeStruct(tall, bf16),
            jax.ShapeDtypeStruct(tall, bf16),
            jax.ShapeDtypeStruct(flat, bf16),
            jax.ShapeDtypeStruct((len(runs), run, width), bf16),
        ),
        [ANY, VMEM, VMEM] + [ANY] * 6 + [VMEM],
        (ANY, VMEM) + (ANY,) * 7,
        [
            pltpu.VMEM((3, total, units), bf16),
            pltpu.VMEM((2, total, step), bf16),
            pltpu.VMEM((2, step, half), f32),
            pltpu.VMEM((items, step, half), bf16),
            pltpu.VMEM((C, block, width), bf16),
            pltpu.VMEM((C, block, width), bf16),
            pltpu.VMEM((C, E, part, width), bf16),
            pltpu.VMEM((C, E, part, width), bf16),
            pltpu.VMEM((C, part, width), bf16),
            DMA((batches, count)),
            DMA((batches, count)),
            DMA((batches,)),
            DMA((C,)),
            DMA((C,)),
            DMA((C, E)),
            DMA((C, E)),
            DMA((C,)),
            DMA((C,)),
            DMA((3,)),
            DMA((2,)),
            DMA((2,)),
            DMA((items,)),
            DMA((items,)),
        ]
        + Return.scratch(E, C, len(runs), run, width, y_rows.shape[3]),
        collective,
        name,
        vmem=60,
    )


def backward_kernel(
    E,
    C,
    G,
    runs,
    queries,
    keys,
    values,
    grads,
    row_ids,
    key_ids,
    log_total,
    query_hat,
    key_hat,
    factors,
    head_gains,
    y_rows,
    slots,
    w_qkv,
    normed,
    small,
    first,
    out_qkv,
    out_small,
    out_gains,
    out,
    raw,
    query_grad,
    key_grad,
    key_sum,
    value_sum,
    sums,
    sum_parts,
    gain_sum,
    gain_parts,
    small_parts,
    small_sum,
    swap,
    swapped,
    own,
    passed,
    tokens,
    parts,
    plane_parts,
    sum_qkv,
    cs,
    cr,
    zs,
    zr,
    ts,
    qs,
    qr,
    os,
    orr,
    ss,
    sr,
    fs,
    fr,
    ms,
    mr,
    hs,
    hr,
    gs,
    gr,
    *return_scratch,
):
    e, c, d = position()
    me, peers = column_peers(E, C, G)
    planes = plane_peers(E)
    count = C * G
    _, run, columns = raw.shape
    every, size = queries.shape
    batches, length = row_ids.shape[:2]
    scale = HEAD**-0.5
    width = w_qkv.shape[0]
    rows = batches * run
    sibling = (e, c, 1 - d)
    meet([device for _, _, device in peers] + [device for _, _, device in planes])
    half = tokens.shape[2]
    block = parts.shape[1]
    cuts = block // half

    def token_copy(part):
        at = lax.rem(e + 1 + part // cuts, E) * block + part % cuts * half
        return pltpu.make_async_copy(
            normed.at[:, pl.ds(pl.multiple_of(at, half), half)],
            tokens.at[part % 2],
            ts.at[part % 2],
        )

    token_copy(0).start()
    token_copy(1).start()
    small_copies = [
        remote(small.at[plane], small_parts.at[i], ss.at[i], sr.at[i], device)
        for i, plane, device in planes
    ]
    for copy in small_copies:
        copy.start()

    way_back = Return(E, C, runs, y_rows, slots, out, *return_scratch)
    way_back.begin()
    heads = size // HEAD

    def head_back(n, carry):
        b, h = n // heads, lax.rem(n, heads)
        lanes = pl.ds(pl.multiple_of(h * HEAD, HEAD), HEAD)
        start = pl.multiple_of(b * length, length)
        key_sum[...] = jnp.zeros_like(key_sum)
        value_sum[...] = jnp.zeros_like(value_sum)
        for at, many, seen in query_blocks(length):
            rows_here = pl.ds(pl.multiple_of(start + at, many), many)
            rows_seen = pl.ds(start, seen)
            query, grad = queries[rows_here, lanes], grads[rows_here, lanes]
            scores = contract(query, keys[rows_seen, lanes], (1, 1)) * scale
            allowed = key_ids[b, :, :seen] <= row_ids[b, at : at + many]
            scores = jnp.where(allowed, scores, MASKED)
            probs = jnp.exp(scores - log_total[b, h, at : at + many])
            prod = contract(grad, values[rows_seen, lanes], (1, 1))
            delta = jnp.sum(probs * prod, axis=1, keepdims=True)
            score_grad = (probs * (prod - delta)).astype(bf16)
            query_grad[rows_here, lanes] = (
                jnp.dot(score_grad, keys[rows_seen, lanes], preferred_element_type=f32) * scale
            )
            key_sum[:seen] += contract(score_grad, query, (0, 0)) * scale
            value_sum[:seen] += contract(probs.astype(bf16), grad, (0, 0))
        key_grad[pl.ds(start, length), lanes] = key_sum[...]
        value_lanes = pl.ds(pl.multiple_of(2 * size + h * HEAD, HEAD), HEAD)
        raw[pl.ds(b * count, count), :, value_lanes] = (
            value_sum[...].astype(bf16).reshape(count, run, HEAD)
        )
        return carry

    pending = iter(range(len(runs)))

    def carry_on(many):
        for _ in range(many):
            n = next(pending, None)
            if n is not None:
                way_back.combine(n)

    lax.fori_loop(0, batches * heads, head_back, 0)

    chunk = min(2 * run, every)
    per_chunk = chunk // run
    ones = jnp.ones((8, size), f32)
    gain_sum[...] = jnp.zeros_like(gain_sum)
    pairs = ((query_grad, query_hat), (key_grad, key_hat))

    def dots(j, carry):
        rows_here = pl.ds(pl.multiple_of(j * chunk, chunk), chunk)
        for kind, (grad, hat) in enumerate(pairs):
            prod = grad[rows_here] * hat[rows_here]
            gain_sum[kind] += jnp.sum(prod, axis=0, keepdims=True)
            total = lax.dot_general(
                ones,
                prod * head_gains[kind : kind + 1],
                (((1,), (1,)), ((), ())),
                precision=lax.Precision.HIGHEST,
                preferred_element_type=f32,
            )
            sums[kind, :, rows_here] = total[:1]
        return carry

    lax.fori_loop(0, every // chunk, dots, 0)
    shares = [
        remote(sums, sum_parts.at[me], ms.at[offset], mr.at[offset], device)
        for offset, _, device in peers
    ]
    gain_copies = [
        remote(gain_sum, gain_parts.at[i], hs.at[i], hr.at[i], device) for i, _, device in planes
    ]
    for copy in shares + gain_copies:
        copy.start()
    sum_parts[me] = sums[...]
    carry_on(len(runs) // 2)
    for copy in shares:
        copy.wait()
    total = sum_parts[0]
    for index in range(1, count):
        total = total + sum_parts[index]
    sums[...] = total / width
    rows_at = lax.broadcasted_iota(jnp.int32, (chunk, chunk), 0)
    same = rows_at == lax.broadcasted_iota(jnp.int32, (chunk, chunk), 1)

    def column_of(row):
        return jnp.sum(jnp.where(same, row, 0.0), axis=1, keepdims=True)

    def through_norm(j, carry):
        rows_here = pl.ds(pl.multiple_of(j * chunk, chunk), chunk)
        for kind, (grad, hat) in enumerate(pairs):
            part = grad[rows_here] * head_gains[kind : kind + 1]
            part = part - hat[rows_here] * column_of(sums[kind, :, rows_here])
            part = (column_of(factors[kind, :, rows_here]) * part).astype(bf16)
            raw[pl.ds(j * per_chunk, per_chunk), :, kind * size : (kind + 1) * size] = part.reshape(
                per_chunk, run, size
            )
        return carry

    lax.fori_loop(0, every // chunk, through_norm, 0)

    def gain_copy(offset, device):
        return remote(gain_sum, out_gains.at[me], gs.at[offset], gr.at[offset], device)

    for copy in gain_copies:
        copy.wait()
    total = gain_sum[...]
    for i in range(1, E):
        total = total + gain_parts[i]
    gain_sum[...] = total
    out_gains[me] = total
    for offset, _, device in peers:
        gain_copy(offset, device).start()

    def product(level, core, at, many):
        left = jnp.concatenate(
            [raw[b * count + level * G + core] for b in range(batches)], axis=0
        )
        return contract(left, w_qkv[at : at + many, :], (1, 1))

    def chip_copy(level):
        return remote(swap.at[level], swapped.at[level], cs.at[level], cr.at[level], sibling)

    def give(level):
        for at in range(0, width, 512):
            swap[level, :, at : at + 512] = product(level, 1 - d, at, 512).astype(bf16)
        chip_copy(level).start()

    def take(level):
        chip_copy(level).wait_recv()
        for at in range(0, width, 512):
            part = product(level, d, at, 512) + swapped[level, :, at : at + 512].astype(f32)
            own[level, :, at : at + 512] = part.astype(bf16)

    def hop(way, level, b):
        there = c + 1 if way == 0 else c - 1
        to = level if way == 0 else level + (C - level) * ((C - 1 - (there - level)) // (C - 1))
        return remote(
            own.at[level, pl.ds(b * run, run)],
            passed.at[to, pl.ds(b * run, run)],
            zs.at[way, level, b],
            zr.at[to, b],
            (e, there, d),
        )

    def arrival(entry, b):
        part = passed.at[entry, pl.ds(b * run, run)]
        return remote(part, part, zs.at[0, 0, b], zr.at[entry, b], sibling)

    def send(way, level, last):
        for b in range(batches):

            @pl.when(last)
            def _():
                arrival(level, b).wait_recv()
                piece = pl.ds(b * run, run)
                own[level, piece] = (
                    own[level, piece].astype(f32) + passed[level, piece].astype(f32)
                ).astype(bf16)

            hop(way, level, b).start()

    order = [C - 1, 0] + list(range(C - 2, 0, -1))
    for level in order:
        give(level)

    def plane_copy(item):
        plane = lax.rem(e + 1 + item, E)
        return remote(
            parts.at[item],
            plane_parts.at[item],
            qs.at[item],
            qr.at[item],
            (plane, c, d),
        )

    def weights(item):
        for part in range(cuts * item, cuts * (item + 1)):
            token_copy(part).wait()
            for at in range(0, columns, 256):
                many = min(256, columns - at)
                piece = raw[:, :, at : at + many].reshape(every, many)
                rows_here = pl.ds(part % cuts * half, half)
                parts[item, rows_here, at : at + many] = contract(
                    tokens[part % 2], piece, (0, 0)
                ).astype(bf16)
            if part + 2 < cuts * E:
                token_copy(part + 2).start()
        if item < E - 1:
            plane_copy(item).start()

    mirror = C - 1 - c
    items = list(range(E))
    for level in order:
        take(level)
        if level == 0:
            @pl.when(c == 0)
            def _():
                send(0, C - 1, False)

            @pl.when(c == C - 1)
            def _():
                send(1, 0, False)

            weights(items.pop(0))
            carry_on(1)
    weights(items.pop(0))
    carry_on(len(runs))
    for turn in range(1, C - 1):

        @pl.when(c <= turn)
        def _():
            send(0, C - 1 - (turn - c), c > 0)

        @pl.when(mirror <= turn)
        def _():
            send(1, turn - mirror, mirror > 0)

        if items:
            weights(items.pop(0))
    while items:
        weights(items.pop(0))
    for item in range(E - 1):
        plane_copy(item).wait_recv()
    for at in range(0, block, 128):
        piece = pl.ds(at, min(128, block - at))
        total = parts[E - 1, piece].astype(f32)
        for item in range(E - 1):
            total = total + plane_parts[item, piece].astype(f32)
        sum_qkv[piece] = total.astype(bf16)
    share = block // (C * G)

    def row_copy(offset, index, device):
        return remote(
            sum_qkv.at[pl.ds(pl.multiple_of(index * share, share), share)],
            out_qkv.at[me],
            os.at[offset],
            orr.at[offset],
            device,
        )

    def small_copy(offset, index, device):
        return remote(
            small_sum.at[pl.ds(pl.multiple_of(index * share, share), share)],
            out_small.at[me],
            fs.at[offset],
            fr.at[offset],
            device,
        )

    for copy in small_copies:
        copy.wait_recv()
    total = small[e]
    for i in range(1, E):
        total = total + small_parts[i]
    small_sum[...] = total
    for offset, index, device in peers:
        small_copy(offset, index, device).start()
        row_copy(offset, index, device).start()
    out_small[me] = small_sum[pl.ds(pl.multiple_of(me * share, share), share)]
    out_qkv[me] = sum_qkv[pl.ds(pl.multiple_of(me * share, share), share)]

    def arrived(entry):
        for b in range(batches):
            arrival(entry, b).wait_recv()

    @pl.when(c > 0)
    def _():
        arrived(c)

    @pl.when(c < C - 1)
    def _():
        arrived(C)

    for at in range(0, width, 512):
        first[:, at : at + 512] = own[c, :, at : at + 512].astype(f32)

    @pl.when(c > 0)
    def _():
        for at in range(0, width, 512):
            first[:, at : at + 512] += passed[c, :, at : at + 512].astype(f32)

    @pl.when(c < C - 1)
    def _():
        for at in range(0, width, 512):
            first[:, at : at + 512] += passed[C, :, at : at + 512].astype(f32)

    for level in range(C):
        chip_copy(level).wait_send()
        for b in range(batches):

            @pl.when(level > c)
            def _():
                hop(0, level, b).wait_send()

            @pl.when(level < c)
            def _():
                hop(1, level, b).wait_send()

    for item in range(E - 1):
        plane_copy(item).wait_send()
    for copy in small_copies:
        copy.wait_send()
    for offset, _, device in peers:
        gain_copy(offset, device).wait()
    way_back.end()
    for offset, index, device in peers:
        row_copy(offset, index, device).wait()
        small_copy(offset, index, device).wait()


def run_backward(
    E,
    C,
    G,
    runs,
    queries,
    keys,
    values,
    grads,
    ids,
    log_total,
    query_hat,
    key_hat,
    factors,
    head_gains,
    y_rows,
    slots,
    w_qkv,
    normed,
    small,
    collective,
    name,
):
    every, size = queries.shape
    batches, length = ids.shape
    count = C * G
    run = length // count
    columns = 3 * size
    width = w_qkv.shape[0]
    rows = batches * run
    block = width // E
    share = block // count
    lanes = small.shape[2]
    by_level = pltpu.VMEM((C, rows, width), bf16)
    wide = pltpu.VMEM((every, size), f32)
    head = pltpu.VMEM((length, HEAD), f32)
    return call(
        functools.partial(backward_kernel, E, C, G, runs),
        (
            queries,
            keys,
            values,
            grads,
            ids[:, :, None],
            ids[:, None, :],
            log_total,
            query_hat,
            key_hat,
            factors,
            head_gains,
            y_rows,
            slots,
            w_qkv,
            normed,
            small,
        ),
        (
            jax.ShapeDtypeStruct((rows, width), f32),
            jax.ShapeDtypeStruct((count, share, columns), bf16),
            jax.ShapeDtypeStruct((count, share, lanes), f32),
            jax.ShapeDtypeStruct((count, 2, 1, size), f32),
            jax.ShapeDtypeStruct((len(runs), run, width), bf16),
        ),
        [VMEM] * 11 + [ANY, VMEM, VMEM, ANY, VMEM],
        (VMEM, VMEM, VMEM, VMEM, ANY),
        [
            pltpu.VMEM((batches * count, run, columns), bf16),
            wide,
            wide,
            head,
            head,
            pltpu.VMEM((2, 1, every), f32),
            pltpu.VMEM((count, 2, 1, every), f32),
            pltpu.VMEM((2, 1, size), f32),
            pltpu.VMEM((E, 2, 1, size), f32),
            pltpu.VMEM((E, block, lanes), f32),
            pltpu.VMEM((block, lanes), f32),
            by_level,
            by_level,
            by_level,
            pltpu.VMEM((C + 1, rows, width), bf16),
            pltpu.VMEM((2, every, min(block, 256)), bf16),
            pltpu.VMEM((E, block, columns), bf16),
            pltpu.VMEM((E, block, columns), bf16),
            pltpu.VMEM((block, columns), bf16),
            DMA((C,)),
            DMA((C,)),
            DMA((2, C, batches)),
            DMA((C + 1, batches)),
            DMA((2,)),
            DMA((E,)),
            DMA((E,)),
            DMA((count,)),
            DMA((count,)),
            DMA((E,)),
            DMA((E,)),
            DMA((count,)),
            DMA((count,)),
            DMA((count,)),
            DMA((count,)),
            DMA((E,)),
            DMA((E,)),
            DMA((count,)),
            DMA((count,)),
        ]
        + Return.scratch(E, C, len(runs), run, width, y_rows.shape[3]),
        collective,
        name,
        vmem=62,
    )


def contract(left, right, axes):
    return lax.dot_general(left, right, ((axes[:1], axes[1:]), ((), ())), preferred_element_type=f32)


def query_blocks(length):
    size = min(256, length)
    return [(i, size, min(length, i + 2 * size)) for i in range(0, length, size)]


def rms_factor(values):
    return lax.rsqrt(jnp.mean(values * values, axis=-1, keepdims=True) + EPSILON)


def norm_back(grad_hat, hatted, factor):
    return factor * (grad_hat - hatted * jnp.mean(grad_hat * hatted, axis=-1, keepdims=True))


def slot_table(routes, experts):
    batches, run, top = routes.shape
    hits = jnp.swapaxes(routes, 1, 2)[:, :, :, None] == jnp.arange(experts, dtype=jnp.int32)
    ones = hits.astype(bf16)
    tokens, ranks = jnp.arange(run), jnp.arange(top)
    before = (tokens[None, :] < tokens[:, None]).astype(bf16)
    above = (ranks[None, :] < ranks[:, None]).astype(bf16)
    within = jnp.einsum("ts,bksx->bktx", before, ones, preferred_element_type=f32)
    totals = jnp.sum(hits.astype(f32), axis=2)
    earlier = jnp.einsum(
        "kj,bjx->bkx", above, totals.astype(bf16), preferred_element_type=f32
    )
    places = jnp.sum(jnp.where(hits, within + earlier[:, :, None, :], 0.0), axis=1)
    places = jnp.where(jnp.any(hits, axis=1), places, UNUSED_SLOT)
    return jnp.swapaxes(places, 1, 2)


def body(
    tokens,
    block_ids,
    routes,
    norm_gains,
    w_query,
    w_key,
    w_value,
    w_output,
    router,
    expert_gate,
    expert_up,
    expert_down,
    cotangent,
):
    E, C, G = lax.axis_size("expert"), lax.axis_size("context"), lax.axis_size("dp")
    batches, run, width = tokens.shape
    top = routes.shape[2]
    experts = E * C * expert_gate.shape[0]
    capacity = max(2, run * top // experts)
    count = C * G
    size = width // count
    length = count * run
    every = batches * length
    own = batches * run
    me = lax.axis_index("context") * G + lax.axis_index("dp")

    rows = w_query.shape[0]
    small_width = -(-(norm_gains.shape[1] + experts) // 128) * 128
    small = jnp.concatenate([norm_gains, router], axis=1)
    small = jnp.pad(small, ((0, 0), (0, small_width - small.shape[1])))
    pieces = [w.reshape(rows, count, size) for w in (w_query, w_key, w_value)]
    weights = jnp.swapaxes(jnp.concatenate(pieces, axis=2), 0, 1)
    places = slot_table(routes, experts).reshape(batches, E, C, run)
    by_level = jnp.transpose(places, (2, 0, 1, 3))
    by_expert = jnp.transpose(places, (1, 2, 0, 3))
    column, w_qkv, small, full_output, ids, slots = start(
        E, C, G, tokens, weights, small, w_output, block_ids, by_level
    )
    ids = jnp.swapaxes(ids, 0, 1).reshape(batches, length)
    w_qkv = w_qkv.reshape(width, 3 * size)
    small = small.reshape(width, small_width)
    full_output = full_output.reshape(width, width)
    gains = small[:, :4].astype(f32)
    full_router = small[:, 4 : 4 + experts]
    head_gains = lax.dynamic_slice(gains, (me * size, 0), (size, 4))

    (
        normed,
        query_low,
        key_low,
        value_low,
        query_hat,
        key_hat,
        log_total,
        factors,
        mixed_low,
        upstream_rows,
    ) = run_forward(
        E,
        C,
        G,
        column.reshape(every, width),
        jnp.swapaxes(gains[:, :1], 0, 1),
        jnp.swapaxes(head_gains[:, 1:3], 0, 1),
        w_qkv,
        ids,
        slots,
        cotangent,
        capacity,
        2,
        "forward",
    )
    mixed_low = mixed_low.reshape(own, width)

    inputs = tokens.reshape(own, width).astype(f32)
    resid = inputs + jnp.dot(mixed_low, full_output, preferred_element_type=f32)
    second_factor = rms_factor(resid)
    second_hat = resid * second_factor
    second_low = (second_hat * gains[:, 3]).astype(bf16)
    logits = jnp.dot(second_low, full_router, preferred_element_type=f32)
    router_probs = jax.nn.softmax(logits, axis=-1)
    gate_table = jnp.transpose(router_probs.reshape(batches, run, E, C), (2, 3, 0, 1))
    table = jnp.concatenate([by_expert, gate_table], axis=2)[:, :, :, None, :]

    second_grad, x, y_rows, pair_grad, act, gate_pre_grad, up_pre_grad, gate_grad = run_experts(
        E,
        C,
        second_low.reshape(batches, run, width),
        upstream_rows,
        slots,
        table,
        expert_gate[0],
        expert_up[0],
        expert_down[0],
        capacity,
        4,
        "experts",
    )
    slot_count = E * C * batches * capacity
    x, pair_grad, act, gate_pre_grad, up_pre_grad = (
        rows.reshape(slot_count, -1) for rows in (x, pair_grad, act, gate_pre_grad, up_pre_grad)
    )
    upstream = cotangent.reshape(own, width).astype(f32)
    prob_grad = jnp.transpose(gate_grad[:, :, :, 0, :], (2, 3, 0, 1)).reshape(own, experts)
    logit_grad = router_probs * (
        prob_grad - jnp.sum(router_probs * prob_grad, axis=-1, keepdims=True)
    )
    logit_grad = logit_grad.astype(bf16)
    second_grad = jnp.sum(second_grad.astype(f32), axis=0).reshape(own, width)
    second_grad = second_grad + contract(logit_grad, full_router, (1, 1))
    gain_second = jnp.sum(second_grad * second_hat, axis=0)
    resid_grad = upstream + norm_back(second_grad * gains[:, 3], second_hat, second_factor)
    attn_grad = resid_grad.astype(bf16)
    mixed_grad = contract(attn_grad, full_output, (1, 1)).astype(bf16)

    early = [(b, i) for b in range(batches // 2) for i in list(range(1, C)) + [0]]
    late = [(b, i) for b in range(batches // 2, batches) for i in list(range(1, C)) + [0]]
    mixed_grad, grad_proj, *expert_grads, early_mixture = middle(
        E,
        C,
        G,
        early,
        mixed_grad.reshape(batches, run, width),
        jnp.swapaxes(mixed_low, 0, 1).reshape(E, C, G, rows, own),
        attn_grad,
        x,
        pair_grad,
        gate_pre_grad,
        up_pre_grad,
        act,
        y_rows,
        slots,
        6,
        "middle",
    )
    grad_gate, grad_up, grad_down = (
        (mine + other.astype(f32))[None] for mine, other in zip(expert_grads[:3], expert_grads[3:])
    )
    grad_proj = jnp.sum(grad_proj.astype(f32), axis=0)
    sums = jnp.concatenate(
        [gain_second[:, None], contract(second_low, logit_grad, (0, 0))], axis=1
    )
    sums = jnp.pad(sums, ((0, 0), (0, small_width - sums.shape[1])))
    first_grad, grad_qkv, sums, gain_heads, late_mixture = run_backward(
        E,
        C,
        G,
        late,
        query_low,
        key_low,
        value_low,
        mixed_grad.reshape(every, size),
        ids,
        log_total,
        query_hat,
        key_hat,
        factors,
        jnp.swapaxes(head_gains[:, 1:3], 0, 1),
        y_rows,
        slots,
        w_qkv,
        normed,
        sums.reshape(E, width // E, small_width),
        8,
        "backward",
    )
    gain_heads = jnp.swapaxes(gain_heads[:, :, 0], 0, 1).reshape(2, width)
    first_row = (lax.axis_index("expert") * count + me) * rows
    gain_heads = lax.dynamic_slice(gain_heads, (0, first_row), (2, rows))
    mixture = [0.0] * batches
    for runs, parts in ((early, early_mixture), (late, late_mixture)):
        for n, (b, _) in enumerate(runs):
            mixture[b] = mixture[b] + parts[n].astype(f32)
    mixture = jnp.stack(mixture)
    activations = (resid.reshape(tokens.shape) + mixture).astype(bf16)
    sums = jnp.sum(sums, axis=0)
    first_factor = rms_factor(inputs)
    first_hat = inputs * first_factor
    input_grad = resid_grad + norm_back(first_grad * gains[:, 0], first_hat, first_factor)

    grad_qkv = jnp.swapaxes(grad_qkv.astype(f32), 0, 1)
    grad_query, grad_key, grad_value = (
        grad_qkv[:, :, i * size : (i + 1) * size].reshape(rows, width) for i in range(3)
    )
    gain_first = sum(
        jnp.sum(w.astype(f32) * grad, axis=1)
        for w, grad in ((w_query, grad_query), (w_key, grad_key), (w_value, grad_value))
    )
    gain_first = gain_first / norm_gains[:, 0].astype(f32)
    grad_gains = jnp.stack([gain_first, gain_heads[0], gain_heads[1], sums[:, 0]], axis=1)
    return (
        activations,
        input_grad.reshape(tokens.shape),
        grad_gains,
        grad_query,
        grad_key,
        grad_value,
        grad_proj,
        sums[:, 1 : 1 + experts],
        grad_gate,
        grad_up,
        grad_down,
    )


def solution(mesh):
    by_token = ("context", "dp")
    by_expert = P(("expert", "context"), None, None)
    by_row = P(ALL_AXES, None)
    rows = P("expert", by_token, None)
    return jax.shard_map(
        body,
        mesh=mesh,
        in_specs=(
            rows,
            P("expert", by_token),
            rows,
            by_row,
            by_row,
            by_row,
            by_row,
            by_row,
            by_row,
            by_expert,
            by_expert,
            by_expert,
            rows,
        ),
        out_specs=(
            rows,
            rows,
            by_row,
            by_row,
            by_row,
            by_row,
            by_row,
            by_row,
            P(("expert", "context"), None, "dp"),
            P(("expert", "context"), None, "dp"),
            P(("expert", "context"), "dp", None),
        ),
        check_vma=False,
    )
```

```python
import functools

import jax
import jax.numpy as jnp
from jax import lax
from jax.experimental import pallas as pl
from jax.experimental.pallas import tpu as pltpu
from jax.sharding import PartitionSpec as P

HEAD = 128
EPSILON = 1e-05
MASKED = -1e30
UNUSED_SLOT = 4096.0
ALL_AXES = ("expert", "context", "dp")
MESH = pl.DeviceIdType.MESH
ANY = pl.BlockSpec(memory_space=pl.ANY)
VMEM = pl.BlockSpec(memory_space=pltpu.VMEM)
DMA = pltpu.SemaphoreType.DMA
MIB = 1 << 20
f32 = jnp.float32
bf16 = jnp.bfloat16


def call(kernel, operands, out_shapes, in_specs, out_specs, scratch, collective, name, vmem=32):
    return pl.pallas_call(
        kernel,
        out_shape=out_shapes,
        in_specs=in_specs,
        out_specs=out_specs,
        scratch_shapes=scratch,
        compiler_params=pltpu.CompilerParams(
            collective_id=collective, has_side_effects=True, vmem_limit_bytes=vmem * MIB
        ),
        name=name,
    )(*operands)


def position():
    return lax.axis_index("expert"), lax.axis_index("context"), lax.axis_index("dp")


def meet(devices):
    barrier = pltpu.get_barrier_semaphore()
    for device in devices:
        pl.semaphore_signal(barrier, inc=1, device_id=device, device_id_type=MESH)
    pl.semaphore_wait(barrier, len(devices))


def remote(source, target, send_sem, recv_sem, device):
    return pltpu.make_async_remote_copy(
        src_ref=source,
        dst_ref=target,
        send_sem=send_sem,
        recv_sem=recv_sem,
        device_id=device,
        device_id_type=MESH,
    )


def column_peers(E, C, G):
    e, c, d = position()
    me = c * G + d
    peers = []
    for offset in range(1, C * G):
        index = lax.rem(me + offset, C * G)
        peers.append((offset, index, (e, index // G, lax.rem(index, G))))
    return me, peers


def plane_peers(E):
    e, c, d = position()
    return [(i, lax.rem(e + i, E), (lax.rem(e + i, E), c, d)) for i in range(1, E)]


def level_peers(C):
    e, c, d = position()
    return [(i, lax.rem(c + i, C), (e, lax.rem(c + i, C), d)) for i in range(1, C)]


def start_kernel(
    E,
    C,
    G,
    tokens,
    weights,
    small_weights,
    output,
    ids,
    slots,
    column,
    gathered,
    small_gathered,
    full_output,
    ids_out,
    slots_out,
    ws,
    wr,
    bs,
    br,
    hs,
    hr,
    ts,
    tr,
    ls,
    ms,
    mr,
    ps,
    pr,
    fs,
    fr,
    gs,
    gr,
):
    e, c, d = position()
    me, peers = column_peers(E, C, G)
    planes = plane_peers(E)
    batches = tokens.shape[0]
    sibling = (e, c, 1 - d)
    meet([device for _, _, device in peers] + [device for _, _, device in planes])
    kinds = ((weights, gathered), (small_weights, small_gathered))
    weight_copies = []
    for j, (source, target) in enumerate(kinds):
        for offset, index, device in peers:
            part = source.at[index] if j == 0 else source
            weight_copies.append(
                remote(part, target.at[e, me], ws.at[j, offset], wr.at[j, offset], device)
            )
    for copy in weight_copies:
        copy.start()
    local = [
        pltpu.make_async_copy(weights.at[me], gathered.at[e, me], ls.at[0]),
        pltpu.make_async_copy(small_weights, small_gathered.at[e, me], ls.at[1]),
        pltpu.make_async_copy(output, full_output.at[e, c, d], ls.at[2]),
    ]
    for b in range(batches):
        local.append(pltpu.make_async_copy(tokens.at[b], column.at[b, me], ls.at[3 + b]))
    for copy in local:
        copy.start()

    def source_of(item):
        return output if item == 0 else tokens.at[item - 1]

    def place(item, level):
        return full_output.at[e, level, d] if item == 0 else column.at[item - 1, level * G + d]

    def to_sibling(source, item, level, arrival):
        return remote(
            source, place(item, level), ts.at[item, arrival], tr.at[item, arrival], sibling
        )

    def step(hop, source, item, level, up):
        to = (e, c + 1, d) if up else (e, c - 1, d)
        way = 0 if up else 1
        return remote(
            source, place(item, level), hs.at[way, item, hop], hr.at[way, item, hop], to
        )

    def relay(item, hop):
        for up in (True, False):
            level = c - hop if up else c + hop
            here = (c >= hop) if up else (c + hop < C)
            onward = (c < C - 1) if up else (c > 0)

            @pl.when(here)
            def _():
                landed = place(item, level)
                step(hop - 1, landed, item, level, up).wait_recv()
                if hop < C - 1:

                    @pl.when(onward)
                    def _():
                        step(hop, landed, item, level, up).start()

                if item == 0:
                    for i, _, device in planes:
                        output_copy(i, level, device).start()
                if G > 1:
                    to_sibling(landed, item, level, hop if up else C - 1 + hop).start()

    def output_copy(i, level, device):
        mine = full_output.at[e, level, d]
        return remote(mine, mine, fs.at[i, level], fr.at[i, level], device)

    def output_sibling(i, level):
        part = full_output.at[lax.rem(e + E - i, E), level, d]
        return remote(part, part, gs.at[i, level], gr.at[i, level], sibling)

    for item in range(batches + 1):

        @pl.when(c < C - 1)
        def _():
            step(0, source_of(item), item, c, True).start()

        @pl.when(c > 0)
        def _():
            step(0, source_of(item), item, c, False).start()

        if G > 1:
            to_sibling(source_of(item), item, c, 0).start()
    small = []
    for offset, _, device in peers:
        small.append(remote(ids, ids_out.at[me], ms.at[offset], mr.at[offset], device))
    for i, level, device in level_peers(C):
        small.append(remote(slots.at[level], slots_out.at[i], ps.at[i], pr.at[i], device))
    for copy in small:
        copy.start()
    ids_out[me] = ids[...]
    slots_out[0] = slots[c]
    for copy in weight_copies:
        copy.wait_recv()
    for copy in local[:3]:
        copy.wait()
    plane_copies = []
    for j, (_, target) in enumerate(kinds):
        for i, _, device in planes:
            copy = remote(target.at[e], target.at[e], bs.at[j, i], br.at[j, i], device)
            copy.start()
            plane_copies.append(copy)
    for i, _, device in planes:
        output_copy(i, c, device).start()
    for hop in range(1, C):
        for item in range(batches + 1):
            relay(item, hop)
    for level in range(C):
        for i, _, device in planes:
            output_copy(i, level, device).wait_recv()
            if G > 1:
                output_sibling(i, level).start()

    for item in range(batches + 1):
        if G > 1:
            to_sibling(source_of(item), item, c, 0).wait()
        for hop in range(C - 1):
            for up in (True, False):
                arrival = hop + 1 if up else C + hop
                origin = c - hop if up else c + hop
                if up:
                    sends = jnp.logical_and(origin >= 0, c < C - 1)
                    arrives = c >= hop + 1
                else:
                    sends = jnp.logical_and(origin < C, c > 0)
                    arrives = c + hop + 1 < C

                @pl.when(sends)
                def _():
                    step(hop, source_of(item), item, c, up).wait_send()

                if G > 1:

                    @pl.when(arrives)
                    def _():
                        to_sibling(source_of(item), item, c, arrival).wait()

    for level in range(C):
        for i, _, device in planes:
            output_copy(i, level, device).wait_send()
            if G > 1:
                output_sibling(i, level).wait()
    for copy in weight_copies:
        copy.wait_send()
    for copy in plane_copies + small + local[3:]:
        copy.wait()


def start(E, C, G, tokens, weights, small_weights, output, ids, slots):
    batches, run, width = tokens.shape
    count = C * G
    rows, columns = weights.shape[1:]
    items = batches + 1
    return call(
        functools.partial(start_kernel, E, C, G),
        (tokens, weights, small_weights, output, ids, slots),
        (
            jax.ShapeDtypeStruct((batches, count, run, width), tokens.dtype),
            jax.ShapeDtypeStruct((E, count, rows, columns), weights.dtype),
            jax.ShapeDtypeStruct((E, count) + small_weights.shape, weights.dtype),
            jax.ShapeDtypeStruct((E, C, G, rows, width), weights.dtype),
            jax.ShapeDtypeStruct((count,) + ids.shape, ids.dtype),
            jax.ShapeDtypeStruct(slots.shape, slots.dtype),
        ),
        [ANY, ANY, ANY, ANY, VMEM, VMEM],
        (ANY, ANY, ANY, ANY, VMEM, VMEM),
        [
            DMA((2, count)),
            DMA((2, count)),
            DMA((2, E)),
            DMA((2, E)),
            DMA((2, items, C)),
            DMA((2, items, C)),
            DMA((items, 2 * C)),
            DMA((items, 2 * C)),
            DMA((items + 2,)),
            DMA((count,)),
            DMA((count,)),
            DMA((C,)),
            DMA((C,)),
            DMA((E, C)),
            DMA((E, C)),
            DMA((E, C)),
            DMA((E, C)),
        ],
        1,
        "start",
        vmem=62,
    )


def choose(slots, count):
    cells = lax.broadcasted_iota(jnp.int32, (count, slots.shape[1]), 0).astype(f32)
    return jnp.concatenate(
        [(cells == slots[i : i + 1, :]).astype(bf16) for i in range(slots.shape[0])], axis=0
    )


class Flow:
    def __init__(self, E, C, rows, slots, landed, packed, target, own, zs, zr, xs, xr, stay):
        self.E, self.C, self.rows, self.slots = E, C, rows, slots
        self.landed, self.packed, self.target = landed, packed, target
        self.sems = own, zs, zr, xs, xr, stay
        self.e, self.c, self.d = position()
        self.batches = rows.shape[0]
        self.cap, self.width = target.shape[3:]
        self.kept = packed.shape[0]
        self.chunks = self.batches * C

    def level_entry(self, far):
        high = 2 * self.c // self.C
        return high * far + (1 - high) * lax.rem(self.C - far, self.C)

    def own(self, b):
        return pltpu.make_async_copy(self.rows.at[b], self.landed.at[0, b], self.sems[0].at[b])

    def hop(self, b, i, way):
        there = i + 1 if way == 0 else lax.rem(i + self.C - 1, self.C)
        level = lax.rem(self.c + (1 if way == 0 else self.C - 1), self.C)
        return remote(
            self.landed.at[i, b],
            self.landed.at[there, b],
            self.sems[1].at[way, i, b],
            self.sems[2].at[there, b],
            (self.e, level, self.d),
        )

    def arrival(self, b, i):
        entry = self.landed.at[i, b]
        return remote(
            entry,
            entry,
            self.sems[1].at[0, i, b],
            self.sems[2].at[i, b],
            (self.e, self.c, 1 - self.d),
        )

    def onward(self, i, way):
        if way == 0:
            return jnp.logical_and(i <= self.c, self.c < self.C - 1)
        return jnp.logical_and(lax.rem(self.C - i, self.C) + self.c < self.C, self.c > 0)

    def begin(self):
        for b in range(self.batches):
            self.own(b).start()
        for b in range(self.batches):
            self.own(b).wait()
            for way in range(2):

                @pl.when(self.onward(0, way))
                def _():
                    self.hop(b, 0, way).start()

    def relay(self, far, b):
        for way in range(2):
            i = far if way == 0 else self.C - far

            @pl.when((far <= self.c) if way == 0 else (far + self.c < self.C))
            def _():
                self.arrival(b, i).wait_recv()

                @pl.when(self.onward(i, way))
                def _():
                    self.hop(b, i, way).start()

    def hops_sent(self, b, i):
        for way in range(2):

            @pl.when(self.onward(i, way))
            def _():
                self.hop(b, i, way).wait_send()

    def across(self, n, b, i, k):
        plane = lax.rem(self.e + k, self.E)
        return remote(
            self.packed.at[lax.rem(n, self.kept), plane],
            self.target.at[i, b, k],
            self.sems[3].at[i, b, k],
            self.sems[4].at[i, b, k],
            (plane, self.c, self.d),
        )

    def stay(self, n, b, i):
        return pltpu.make_async_copy(
            self.packed.at[lax.rem(n, self.kept), self.e],
            self.target.at[i, b, 0],
            self.sems[5].at[i, b],
        )

    def compact(self, n, b, i):
        place = lax.rem(n, self.kept)
        picks = choose(self.slots[i, b], self.cap)
        for at in range(0, self.width, 512):
            part = jnp.dot(
                picks, self.landed[i, b, :, at : at + 512], preferred_element_type=f32
            ).astype(bf16)
            self.packed[place, :, :, at : at + 512] = part.reshape(self.E, self.cap, 512)
        for k in range(1, self.E):
            self.across(n, b, i, k).start()
        self.stay(n, b, i).start()

    def crossed(self, n, b, i):
        for k in range(1, self.E):
            self.across(n, b, i, k).wait_send()

    def arrived(self, n, b, i):
        for k in range(1, self.E):
            self.across(n, b, i, k).wait_recv()

    @staticmethod
    def scratch(E, C, batches, run, width, cap, kept):
        return [
            pltpu.VMEM((C, batches, run, width), bf16),
            pltpu.VMEM((kept, E, cap, width), bf16),
            DMA((batches,)),
            DMA((2, C, batches)),
            DMA((C, batches)),
            DMA((C, batches, E)),
            DMA((C, batches, E)),
            DMA((C, batches)),
        ]


class Return:
    def __init__(self, E, C, runs, rows, slots, out, returned, sums, ys, yr, bs, us, ur, ks):
        self.E, self.C, self.runs = E, C, runs
        self.rows, self.slots, self.out = rows, slots, out
        self.returned, self.sums = returned, sums
        self.sems = ys, yr, bs, us, ur, ks
        self.e, self.c, self.d = position()

    def back(self, n, k):
        b, i = self.runs[n]
        return remote(
            self.rows.at[i, b, k],
            self.returned.at[n, self.e],
            self.sems[0].at[n, k],
            self.sems[1].at[n, k],
            (lax.rem(self.e + self.E - k, self.E), self.c, self.d),
        )

    def own(self, n):
        b, i = self.runs[n]
        return pltpu.make_async_copy(
            self.rows.at[i, b, 0], self.returned.at[n, self.e], self.sems[2].at[n]
        )

    def along(self, n):
        i = self.runs[n][1]
        if i == 0:
            return pltpu.make_async_copy(self.sums.at[n], self.out.at[n], self.sems[5].at[n])
        to = (self.e, lax.rem(self.c + self.C - i, self.C), self.d)
        return remote(
            self.sums.at[n], self.out.at[n], self.sems[3].at[n], self.sems[4].at[n], to
        )

    def send(self, n):
        if n < len(self.runs):
            for k in range(1, self.E):
                self.back(n, k).start()
            self.own(n).start()

    def begin(self):
        self.send(0)
        self.send(1)

    def combine(self, n):
        b, i = self.runs[n]
        for k in range(1, self.E):
            self.back(n, k).wait_recv()
        self.own(n).wait()
        self.send(n + 2)
        cap, width = self.rows.shape[3:]
        picks = choose(self.slots[i, b], cap)
        for at in range(0, width, 512):
            part = self.returned[n, :, :, at : at + 512].reshape(self.E * cap, 512)
            self.sums[n, :, at : at + 512] = contract(picks, part, (0, 0)).astype(bf16)
        self.along(n).start()

    def end(self):
        for n in range(len(self.runs)):
            for k in range(1, self.E):
                self.back(n, k).wait_send()
            self.along(n).wait()

    @staticmethod
    def scratch(E, C, count, run, width, cap):
        return [
            pltpu.VMEM((count, E, cap, width), bf16),
            pltpu.VMEM((count, run, width), bf16),
            DMA((count, E)),
            DMA((count, E)),
            DMA((count,)),
            DMA((count,)),
            DMA((count,)),
            DMA((count,)),
        ]


def forward_kernel(
    E,
    C,
    G,
    column,
    gain,
    head_gains,
    w_qkv,
    row_ids,
    key_ids,
    slots,
    upstream,
    normed,
    queries,
    keys,
    values,
    query_hat,
    key_hat,
    log_total,
    factors,
    mixed,
    u_out,
    raw,
    low,
    squares,
    parts,
    heads,
    landed,
    packed,
    own,
    zs,
    zr,
    xs,
    xr,
    stay,
    raw_sem,
    low_sem,
    ss,
    sr,
    ms,
    mr,
    ml,
):
    me, peers = column_peers(E, C, G)
    planes = plane_peers(E)
    every, width = column.shape
    batches, length, size = heads.shape
    run = length // (C * G)
    block = raw.shape[1]
    blocks = every // block
    scale = HEAD**-0.5
    meet([device for _, _, device in peers] + [device for _, _, device in planes])
    flow = Flow(E, C, upstream, slots, landed, packed, u_out, own, zs, zr, xs, xr, stay)

    def load(j):
        at = pl.multiple_of(j * block, block)
        place = lax.rem(j, 2)
        return pltpu.make_async_copy(column.at[pl.ds(at, block)], raw.at[place], raw_sem.at[place])

    def store(j):
        at = pl.multiple_of(j * block, block)
        place = lax.rem(j, 2)
        return pltpu.make_async_copy(low.at[place], normed.at[pl.ds(at, block)], low_sem.at[place])

    def chunk_of(n):
        return n % batches, flow.level_entry(n // batches)

    chunk = iter(range(flow.chunks))

    def carry_on(count):
        for _ in range(count):
            n = next(chunk, None)
            if n is None:
                return
            if n >= flow.kept:
                before = n - flow.kept, *chunk_of(n - flow.kept)
                flow.crossed(*before)
                flow.stay(*before).wait()
            if n >= batches:
                flow.relay(n // batches, n % batches)
            flow.compact(n, *chunk_of(n))

    load(0).start()
    load(1).start()
    flow.begin()
    carry_on(batches)
    ones = jnp.ones((8, size), f32)

    def project(j, carry):
        place = lax.rem(j, 2)
        rows = pl.ds(pl.multiple_of(j * block, block), block)
        load(j).wait()

        @pl.when(j >= 2)
        def _():
            store(j - 2).wait()

        total = jnp.zeros((block, 1), f32)
        for at in range(0, width, 512):
            part = raw[place, :, at : at + 512].astype(f32)
            total += jnp.sum(part * part, axis=1, keepdims=True)
        factor = lax.rsqrt(total / width + EPSILON)
        for at in range(0, width, 512):
            part = raw[place, :, at : at + 512].astype(f32) * factor
            low[place, :, at : at + 512] = (part * gain[:, at : at + 512]).astype(bf16)
        store(j).start()

        @pl.when(j + 2 < blocks)
        def _():
            load(j + 2).start()

        for kind in range(3):
            part = jnp.dot(
                low[place],
                w_qkv[:, kind * size : (kind + 1) * size],
                preferred_element_type=f32,
            )
            if kind == 2:
                values[rows] = part.astype(bf16)
            else:
                (query_hat, key_hat)[kind][rows] = part
                sums = lax.dot_general(
                    ones,
                    part * part,
                    (((1,), (1,)), ((), ())),
                    precision=lax.Precision.HIGHEST,
                    preferred_element_type=f32,
                )
                squares[kind, :, rows] = sums[:1]
        return carry

    half = blocks // 2
    lax.fori_loop(0, half, project, 0)
    carry_on(1)
    lax.fori_loop(half, blocks, project, 0)
    shares = [
        remote(squares, parts.at[me], ss.at[offset], sr.at[offset], device)
        for offset, _, device in peers
    ]
    for copy in shares:
        copy.start()
    parts[me] = squares[...]
    carry_on(1)
    for copy in shares:
        copy.wait_recv()
    total = parts[0]
    for index in range(1, C * G):
        total = total + parts[index]
    factors[...] = lax.rsqrt(total / width + EPSILON)
    rows_at = lax.broadcasted_iota(jnp.int32, (block, block), 0)
    same = rows_at == lax.broadcasted_iota(jnp.int32, (block, block), 1)

    def scaled(j, carry):
        rows = pl.ds(pl.multiple_of(j * block, block), block)
        for kind, (hat, out) in enumerate(((query_hat, queries), (key_hat, keys))):
            factor = jnp.sum(jnp.where(same, factors[kind, :, rows], 0.0), axis=1, keepdims=True)
            part = hat[rows] * factor
            hat[rows] = part
            out[rows] = (part * head_gains[kind : kind + 1]).astype(bf16)
        return carry

    lax.fori_loop(0, blocks, scaled, 0)
    carry_on(1)

    def mixed_copy(b, offset, index, device):
        where = pl.ds(pl.multiple_of(me * size, size), size)
        part = heads.at[b, pl.ds(pl.multiple_of(index * run, run), run)]
        return remote(part, mixed.at[b, :, where], ms.at[b, offset], mr.at[b, offset], device)

    def mixed_own(b):
        where = pl.ds(pl.multiple_of(me * size, size), size)
        part = heads.at[b, pl.ds(pl.multiple_of(me * run, run), run)]
        return pltpu.make_async_copy(part, mixed.at[b, :, where], ml.at[b])

    for b in range(batches):

        def head(h, carry, b=b):
            lanes = pl.ds(pl.multiple_of(h * HEAD, HEAD), HEAD)
            for first, count, seen in query_blocks(length):
                rows = pl.ds(b * length + first, count)
                seen_rows = pl.ds(b * length, seen)
                scores = contract(queries[rows, lanes], keys[seen_rows, lanes], (1, 1)) * scale
                allowed = key_ids[b, :, :seen] <= row_ids[b, first : first + count]
                scores = jnp.where(allowed, scores, MASKED)
                peak = jnp.max(scores, axis=1, keepdims=True)
                grown = jnp.exp(scores - peak)
                total = jnp.sum(grown, axis=1, keepdims=True)
                probs = (grown * (1.0 / total)).astype(bf16)
                heads[b, first : first + count, lanes] = jnp.dot(
                    probs, values[seen_rows, lanes], preferred_element_type=f32
                ).astype(bf16)
                log_total[b, h, first : first + count] = peak + jnp.log(total)
            return carry

        lax.fori_loop(0, size // HEAD, head, 0)
        for offset, index, device in peers:
            mixed_copy(b, offset, index, device).start()
        mixed_own(b).start()
        carry_on(1)
    carry_on(flow.chunks)

    for copy in shares:
        copy.wait_send()
    for j in (blocks - 2, blocks - 1):
        store(j).wait()
    for b in range(batches):
        for offset, index, device in peers:
            mixed_copy(b, offset, index, device).wait()
        mixed_own(b).wait()

    for n in range(flow.chunks):
        b, i = chunk_of(n)
        flow.hops_sent(b, i)
        flow.arrived(n, b, i)
        if n >= flow.chunks - flow.kept:
            flow.crossed(n, b, i)
            flow.stay(n, b, i).wait()


def run_forward(E, C, G, column, gain, head_gains, w_qkv, ids, slots, upstream, cap, collective, name):
    every, width = column.shape
    batches, run = upstream.shape[:2]
    count = C * G
    length = count * run
    size = width // count
    block = min(256, every)
    low = jax.ShapeDtypeStruct((every, size), bf16)
    wide = jax.ShapeDtypeStruct((every, size), f32)
    return call(
        functools.partial(forward_kernel, E, C, G),
        (column, gain, head_gains, w_qkv, ids[:, :, None], ids[:, None, :], slots, upstream),
        (
            jax.ShapeDtypeStruct((every, width), bf16),
            low,
            low,
            low,
            wide,
            wide,
            jax.ShapeDtypeStruct((batches, size // HEAD, length, 1), f32),
            jax.ShapeDtypeStruct((2, 1, every), f32),
            jax.ShapeDtypeStruct(upstream.shape, bf16),
            jax.ShapeDtypeStruct((C, batches, E, cap, width), bf16),
        ),
        [ANY] + [VMEM] * 6 + [ANY],
        (ANY,) + (VMEM,) * 7 + (ANY, ANY),
        [
            pltpu.VMEM((2, block, width), bf16),
            pltpu.VMEM((2, block, width), bf16),
            pltpu.VMEM((2, 1, every), f32),
            pltpu.VMEM((count, 2, 1, every), f32),
            pltpu.VMEM((batches, length, size), bf16),
        ]
        + Flow.scratch(E, C, batches, run, width, cap, 3)
        + [
            DMA((2,)),
            DMA((2,)),
            DMA((count,)),
            DMA((count,)),
            DMA((batches, count)),
            DMA((batches, count)),
            DMA((batches,)),
        ],
        collective,
        name,
        vmem=56,
    )


def experts_kernel(
    E,
    C,
    rows_x,
    u_in,
    slots,
    gates,
    w_gate,
    w_up,
    w_down,
    out,
    x_out,
    y_out,
    pair_out,
    act_out,
    gate_back_out,
    up_back_out,
    scalars_out,
    table,
    scalars,
    landed,
    packed,
    own,
    zs,
    zr,
    xs,
    xr,
    stay,
    sums,
    returned,
    x,
    u,
    pair,
    act,
    gate_back,
    up_back,
    gated,
    sent,
    gs,
    gr,
    ss,
    sr,
    ys,
    yr,
    bs,
    us,
    ur,
    ks,
    loads,
    stores,
):
    e, c, d = position()
    batches, run, width = rows_x.shape
    cap = x_out.shape[3]
    units = w_gate.shape[1]
    chunks = batches * C
    total = E * cap
    kept = sent.shape[0]
    lead, lag = 1, 2
    everyone = [(k, i) for k in range(E) for i in range(C) if k + i > 0]
    ahead = [(k, i, (lax.rem(e + k, E), lax.rem(c + i, C), d)) for k, i in everyone]
    behind = [(k, i, (lax.rem(e + E - k, E), lax.rem(c + C - i, C), d)) for k, i in everyone]
    meet([device for _, _, device in ahead])
    flow = Flow(E, C, rows_x, slots, landed, packed, x_out, own, zs, zr, xs, xr, stay)

    def far_of(n):
        return lax.rem((n + batches - 1) // batches, C), lax.rem(n + batches - 1, batches)

    def chunk_of(n):
        far, b = far_of(n)
        return b, flow.level_entry(far)

    def back(n, b, i, k):
        return remote(
            sent.at[lax.rem(n, kept), k],
            returned.at[i, b, e],
            ys.at[i, b, k],
            yr.at[i, b, k],
            (lax.rem(e + E - k, E), c, d),
        )

    def back_own(n, b, i):
        return pltpu.make_async_copy(
            sent.at[lax.rem(n, kept), 0], returned.at[i, b, e], bs.at[i, b]
        )

    def up(b, i):
        return remote(
            sums.at[i, b],
            out.at[c, b],
            us.at[i, b],
            ur.at[i, b],
            (e, lax.rem(c + C - i, C), d),
        )

    def keep(b):
        return pltpu.make_async_copy(sums.at[0, b], out.at[c, b], ks.at[b])

    def load(a, b, i):
        source, target = ((x_out, x), (u_in, u))[a]
        return pltpu.make_async_copy(source.at[i, b], target, loads.at[a])

    def store(j, b, i):
        source = (pair, act, gate_back, up_back, gated)[j]
        target = (pair_out, act_out, gate_back_out, up_back_out, y_out)[j]
        return pltpu.make_async_copy(source, target.at[i, b], stores.at[j])

    flow.begin()
    small = [
        remote(gates.at[device[0], device[1]], table.at[k, i], gs.at[k, i], gr.at[k, i], device)
        for k, i, device in ahead
    ]
    for copy in small:
        copy.start()
    table[0, 0] = gates[e, c]

    def compact(n):
        @pl.when(n >= flow.kept)
        def _():
            flow.crossed(n - flow.kept, *chunk_of(n - flow.kept))

        flow.compact(n, *chunk_of(n))

    def expert(n):
        b, i = chunk_of(n)
        load(1, b, i).start()
        flow.arrived(n, b, i)
        flow.stay(n, b, i).wait()
        load(0, b, i).start()

        @pl.when(n > 0)
        def _():
            before = chunk_of(n - 1)
            for j in range(5):
                store(j, *before).wait()

        @pl.when(n >= kept)
        def _():
            before = chunk_of(n - kept)
            for k in range(1, E):
                back(n - kept, *before, k).wait_send()

        holds, gate = [], []
        cells = lax.broadcasted_iota(jnp.int32, (cap, run), 0).astype(f32)
        for k in range(E):
            hold = cells == table[k, i, b]
            holds.append(hold)
            gate.append(
                jnp.sum(jnp.where(hold, table[k, i, batches + b], 0.0), axis=1, keepdims=True)
            )
        gate = jnp.concatenate(gate, axis=0)
        for a in range(2):
            load(a, b, i).wait()
        for at in range(0, width, 512):
            part = u[:, :, at : at + 512].reshape(total, 512).astype(f32)
            pair[:, :, at : at + 512] = (gate * part).astype(bf16).reshape(E, cap, 512)
        store(0, b, i).start()
        inputs = x[...].reshape(total, width)
        grads = pair[...].reshape(total, width)
        for at in range(0, units, 256):
            gate_pre = jnp.dot(inputs, w_gate[:, at : at + 256], preferred_element_type=f32)
            up_pre = jnp.dot(inputs, w_up[:, at : at + 256], preferred_element_type=f32)
            act_grad = contract(grads, w_down[at : at + 256, :], (1, 1))
            sigmoid = jax.nn.sigmoid(gate_pre)
            silu = gate_pre * sigmoid
            act[:, at : at + 256] = (silu * up_pre).astype(bf16)
            gate_back[:, at : at + 256] = (
                act_grad * up_pre * sigmoid * (1.0 + gate_pre * (1.0 - sigmoid))
            ).astype(bf16)
            up_back[:, at : at + 256] = (act_grad * silu).astype(bf16)
        for j in range(1, 4):
            store(j, b, i).start()
        place = lax.rem(n, kept)
        gate_grad = jnp.zeros((total, 1), f32)
        for at in range(0, width, 512):
            out = jnp.dot(act[...], w_down[:, at : at + 512], preferred_element_type=f32)
            out = out.astype(bf16).astype(f32)
            gate_grad += jnp.sum(
                out * u[:, :, at : at + 512].reshape(total, 512).astype(f32), axis=1, keepdims=True
            )
            gated[:, :, at : at + 512] = (gate * out).astype(bf16).reshape(E, cap, 512)
            back_rows = contract(gate_back[...], w_gate[at : at + 512, :], (1, 1))
            back_rows += contract(up_back[...], w_up[at : at + 512, :], (1, 1))
            sent[place, :, :, at : at + 512] = back_rows.astype(bf16).reshape(E, cap, 512)
        for k in range(1, E):
            back(n, b, i, k).start()
        back_own(n, b, i).start()
        store(4, b, i).start()
        for k in range(E):
            scalars[k, i, b] = jnp.sum(
                jnp.where(holds[k], gate_grad[k * cap : (k + 1) * cap], 0.0), axis=0, keepdims=True
            )

    def combine(n):
        b, i = chunk_of(n)
        picks = choose(slots[i, b], cap)
        for k in range(1, E):
            back(n, b, i, k).wait_recv()
        back_own(n, b, i).wait()
        for at in range(0, width, 512):
            part = returned[i, b, :, :, at : at + 512].reshape(total, 512)
            sums[i, b, :, at : at + 512] = contract(picks, part, (0, 0)).astype(bf16)

        @pl.when(i > 0)
        def _():
            up(b, i).start()

        @pl.when(i == 0)
        def _():
            keep(b).start()

    def step(s, carry):
        @pl.when(jnp.logical_and(s > 0, s <= batches * (C - 1)))
        def _():
            flow.relay(*far_of(s))

        @pl.when(s < chunks)
        def _():
            compact(s)

        @pl.when(jnp.logical_and(s >= lead, s < chunks + lead))
        def _():
            expert(s - lead)

        @pl.when(s >= lag)
        def _():
            combine(s - lag)

        return carry

    for copy in small:
        copy.wait_recv()
    lax.fori_loop(0, chunks + lag, step, 0)
    scalars_out[e, c] = scalars[0, 0]
    last = [
        remote(scalars.at[k, i], scalars_out.at[e, c], ss.at[k, i], sr.at[k, i], device)
        for k, i, device in behind
    ]
    for copy in last:
        copy.start()
    for copy in small:
        copy.wait_send()
    for j in range(5):
        store(j, *chunk_of(chunks - 1)).wait()

    def finish(n, carry):
        b, i = chunk_of(n)
        flow.hops_sent(b, i)

        @pl.when(n >= chunks - flow.kept)
        def _():
            flow.crossed(n, b, i)

        @pl.when(n >= chunks - kept)
        def _():
            for k in range(1, E):
                back(n, b, i, k).wait_send()

        @pl.when(i > 0)
        def _():
            up(b, i).wait()

        @pl.when(i == 0)
        def _():
            keep(b).wait()

        return carry

    lax.fori_loop(0, chunks, finish, 0)
    for copy in last:
        copy.wait()


def run_experts(E, C, rows_x, u_in, slots, gates, w_gate, w_up, w_down, cap, collective, name):
    batches, run, width = rows_x.shape
    units = w_gate.shape[1]
    total = E * cap
    kept = 3
    by_slot = jax.ShapeDtypeStruct((C, batches, E, cap, width), bf16)
    by_token = jax.ShapeDtypeStruct((C, batches, run, width), bf16)
    hidden = jax.ShapeDtypeStruct((C, batches, total, units), bf16)
    return call(
        functools.partial(experts_kernel, E, C),
        (rows_x, u_in, slots, gates, w_gate, w_up, w_down),
        (
            by_token,
            by_slot,
            by_slot,
            by_slot,
            hidden,
            hidden,
            hidden,
            jax.ShapeDtypeStruct((E, C, batches, 1, run), f32),
        ),
        [ANY, ANY, VMEM, VMEM, VMEM, VMEM, VMEM],
        (ANY,) * 7 + (VMEM,),
        [
            pltpu.VMEM(gates.shape, f32),
            pltpu.VMEM((E, C, batches, 1, run), f32),
        ]
        + Flow.scratch(E, C, batches, run, width, cap, kept)
        + [
            pltpu.VMEM((C, batches, run, width), bf16),
            pltpu.VMEM((C, batches, E, cap, width), bf16),
            pltpu.VMEM((E, cap, width), bf16),
            pltpu.VMEM((E, cap, width), bf16),
            pltpu.VMEM((E, cap, width), bf16),
            pltpu.VMEM((total, units), bf16),
            pltpu.VMEM((total, units), bf16),
            pltpu.VMEM((total, units), bf16),
            pltpu.VMEM((E, cap, width), bf16),
            pltpu.VMEM((kept, E, cap, width), bf16),
            DMA((E, C)),
            DMA((E, C)),
            DMA((E, C)),
            DMA((E, C)),
            DMA((C, batches, E)),
            DMA((C, batches, E)),
            DMA((C, batches)),
            DMA((C, batches)),
            DMA((C, batches)),
            DMA((batches,)),
            DMA((2,)),
            DMA((5,)),
        ],
        collective,
        name,
        vmem=60,
    )


def middle_kernel(
    E,
    C,
    G,
    runs,
    parts,
    resid,
    factor,
    upstream,
    gain,
    logit_grad,
    router,
    w_output,
    mixed,
    x,
    pair,
    gate_back,
    up_back,
    act,
    y_rows,
    slots,
    resid_grad,
    gain_grad,
    heads,
    proj,
    own_gate,
    own_up,
    own_down,
    other_gate,
    other_up,
    other_down,
    out,
    attn_grad,
    stage,
    blocks,
    hidden,
    wide,
    kept,
    sent,
    swap,
    swapped,
    chip,
    plane_parts,
    level_part,
    hs,
    hr,
    hl,
    block_sem,
    cs,
    cr,
    ps,
    pr,
    zs,
    zr,
    rs,
    wide_sem,
    ks,
    xs,
    xr,
    *return_scratch,
):
    e, c, d = position()
    me, peers = column_peers(E, C, G)
    planes, levels = plane_peers(E), level_peers(C)
    batches, run = parts.shape[1:3]
    own, width = resid.shape
    size = blocks.shape[1]
    step = wide.shape[2]
    half = own_gate.shape[1]
    sibling = (e, c, 1 - d)
    meet([device for _, _, device in peers] + [device for _, _, device in planes])
    way_back = Return(E, C, runs, y_rows, slots, out, *return_scratch)
    way_back.begin()

    turns = [index for _, index, _ in peers] + [me]

    def block_copy(n):
        at = pl.ds(pl.multiple_of(turns[n] * size, size), size)
        return pltpu.make_async_copy(w_output.at[at], blocks.at[n % 2], block_sem.at[n % 2])

    block_copy(0).start()
    block_copy(1).start()
    hidden_copies = [
        pltpu.make_async_copy(source, hidden.at[j % 2], rs.at[j % 2])
        for j, source in enumerate((gate_back, up_back, act))
    ]
    hidden_copies[0].start()
    hidden_copies[1].start()
    count = width // step
    sources = [x] * count + [pair] * count

    def wide_copy(item):
        at = (item % count) * step
        return pltpu.make_async_copy(
            sources[item].at[:, pl.ds(at, step)], wide.at[item % 2], wide_sem.at[item % 2]
        )

    wide_copy(0).start()
    wide_copy(1).start()

    total = jnp.zeros((own, 1), f32)
    for at in range(0, width, 512):
        lanes = pl.ds(at, 512)
        grad = contract(logit_grad[...], router[lanes], (1, 1))
        for level in range(C):
            grad += parts[level, :, :, lanes].reshape(own, 512).astype(f32)
        hat = resid[:, lanes] * factor[...]
        gain_grad[:, lanes] = jnp.sum(grad * hat, axis=0, keepdims=True)
        grad = grad * gain[:, lanes]
        total += jnp.sum(grad * hat, axis=1, keepdims=True)
        resid_grad[:, lanes] = grad
    mean = total / width
    for at in range(0, width, 512):
        lanes = pl.ds(at, 512)
        hat = resid[:, lanes] * factor[...]
        grad = upstream[:, lanes].astype(f32) + factor[...] * (resid_grad[:, lanes] - hat * mean)
        resid_grad[:, lanes] = grad
        attn_grad[:, lanes] = grad.astype(bf16)

    head_copies = []
    for n in range(len(turns)):
        block_copy(n).wait()
        part = contract(attn_grad[...], blocks[n % 2], (1, 1))
        stage[n] = part.astype(bf16).reshape(batches, run, size)
        if n + 2 < len(turns):
            block_copy(n + 2).start()
        for b in range(batches):
            if n < len(peers):
                offset, _, device = peers[n]
                copy = remote(
                    stage.at[n, b], heads.at[b, me], hs.at[b, offset], hr.at[b, offset], device
                )
            else:
                copy = pltpu.make_async_copy(stage.at[n, b], heads.at[b, me], hl.at[b])
            copy.start()
            head_copies.append(copy)

    block = width // E

    def chip_copy(plane):
        return remote(swap.at[plane], swapped.at[plane], cs.at[plane], cr.at[plane], sibling)

    def plane_copy(i, level):
        plane = lax.rem(e + i, E)
        return remote(
            chip.at[plane, level],
            plane_parts.at[i, level],
            ps.at[i, level],
            pr.at[i, level],
            (plane, c, d),
        )

    def give(i, carry):
        plane = lax.rem(e + 1 + i, E)
        rows = pl.ds(pl.multiple_of(plane * block, block), block)
        left = mixed[:, rows]
        for at in range(0, width, 512):
            lanes = pl.ds(at, 512)
            part = contract(left, attn_grad[:, lanes], (0, 0)).astype(bf16)
            part = part.reshape(C, G, block // (C * G), 512)
            first, last = part[:, 0], part[:, G - 1]
            chip[plane, :, :, lanes] = jnp.where(d == 0, first, last)
            swap[plane, :, :, lanes] = jnp.where(d == 0, last, first)
        chip_copy(plane).start()
        return carry

    def take(i, carry):
        plane = lax.rem(e + 1 + i, E)
        chip_copy(plane).wait_recv()
        for at in range(0, width, 512):
            lanes = pl.ds(at, 512)
            part = chip[plane, :, :, lanes].astype(f32) + swapped[plane, :, :, lanes].astype(f32)
            chip[plane, :, :, lanes] = part.astype(bf16)
        return carry

    lax.fori_loop(0, E, give, 0)
    lax.fori_loop(0, E, take, 0)
    order = [lax.rem(c + i, C) for i in list(range(1, C)) + [0]]
    levels_left = iter(order)

    def level_send():
        level = next(levels_left, None)
        if level is not None:
            for i in range(1, E):
                plane_copy(i, level).start()

    level_send()

    def keep_copy(j, at, place):
        target = (own_gate, own_up, own_down)[j]
        where = target.at[:, pl.ds(at, step)] if j == 2 else target.at[pl.ds(at, step)]
        return pltpu.make_async_copy(kept.at[place], where, ks.at[place])

    def send_copy(j, at, place):
        target = (other_gate, other_up, other_down)[j]
        where = target.at[:, pl.ds(at, step)] if j == 2 else target.at[pl.ds(at, step)]
        return remote(sent.at[place % slots_sent], where, xs.at[place], xr.at[place], sibling)

    slots_sent = sent.shape[0]
    combine_at, combine_step, level_at = 0, 1, (2, 3, 4)
    kept_copies, sent_copies, after = [], [], {}
    for n in range(len(runs)):
        after.setdefault(combine_at + combine_step * n, []).append(n)
    hidden_copies[0].wait()
    hidden_copies[1].wait()
    for item in range(2 * count):
        if item == count:
            hidden_copies[2].start()
            hidden_copies[2].wait()
        wide_copy(item).wait()
        at = (item % count) * step
        left = wide[item % 2]
        for j in (0, 1) if item < count else (2,):
            place = len(sent_copies)

            def product(core):
                part = hidden[j % 2, :, pl.ds(pl.multiple_of(core * half, half), half)]
                return contract(part, left, (0, 0)) if j == 2 else contract(left, part, (0, 0))

            if place >= slots_sent:
                sent_copies[place - slots_sent].wait_send()
            sent[place % slots_sent] = product(1 - d).astype(bf16)
            copy = send_copy(j, at, place)
            copy.start()
            sent_copies.append(copy)
            if place >= 2:
                kept_copies[place - 2].wait()
            kept[place % 2] = product(d)
            copy = keep_copy(j, at, place % 2)
            copy.start()
            kept_copies.append(copy)
        if item + 2 < 2 * count:
            wide_copy(item + 2).start()
        for n in after.get(item, ()):
            way_back.combine(n)
        if item in level_at:
            level_send()
    for _ in range(C):
        level_send()

    def level_copy(i, level):
        return remote(level_part.at[level], proj.at[c], zs.at[i], zr.at[i], (e, level, d))

    for i, level in zip(list(range(1, C)) + [0], order):
        for k in range(1, E):
            plane_copy(k, level).wait_recv()
        total = chip[e, level].astype(f32)
        for k in range(1, E):
            total = total + plane_parts[k, level].astype(f32)
        level_part[level] = total.astype(bf16)
        if i > 0:
            level_copy(i, level).start()
        else:
            proj[c] = level_part[c]

    for copy in kept_copies[-2:]:
        copy.wait()
    for copy in sent_copies:
        copy.wait_recv()
    for copy in sent_copies[-slots_sent:]:
        copy.wait_send()
    for copy in head_copies:
        copy.wait()
    for i, level, _ in levels:
        level_copy(i, level).wait()
    way_back.end()
    for plane in range(E):
        chip_copy(plane).wait_send()
    for i in range(1, E):
        for level in range(C):
            plane_copy(i, level).wait_send()


def middle(
    E,
    C,
    G,
    runs,
    parts,
    resid,
    factor,
    upstream,
    gain,
    logit_grad,
    router,
    w_output,
    mixed,
    x,
    pair,
    gate_back,
    up_back,
    act,
    y_rows,
    slots,
    collective,
    name,
):
    batches, run, width = parts.shape[1:]
    own = resid.shape[0]
    count = C * G
    size = width // count
    block = width // E
    part = block // count
    total, units = act.shape
    half = units // G
    step = min(512, width)
    items = 3 * (width // step)
    tall = (width, half)
    flat = (half, width)
    by_plane = pltpu.VMEM((E, C, part, width), bf16)
    return call(
        functools.partial(middle_kernel, E, C, G, runs),
        (
            parts,
            resid,
            factor,
            upstream,
            gain,
            logit_grad,
            router,
            w_output,
            mixed,
            x,
            pair,
            gate_back,
            up_back,
            act,
            y_rows,
            slots,
        ),
        (
            jax.ShapeDtypeStruct((own, width), f32),
            jax.ShapeDtypeStruct((1, width), f32),
            jax.ShapeDtypeStruct((batches, count, run, size), bf16),
            jax.ShapeDtypeStruct((C, part, width), bf16),
            jax.ShapeDtypeStruct(tall, f32),
            jax.ShapeDtypeStruct(tall, f32),
            jax.ShapeDtypeStruct(flat, f32),
            jax.ShapeDtypeStruct(tall, bf16),
            jax.ShapeDtypeStruct(tall, bf16),
            jax.ShapeDtypeStruct(flat, bf16),
            jax.ShapeDtypeStruct((len(runs), run, width), bf16),
        ),
        [VMEM] * 7 + [ANY, VMEM] + [ANY] * 6 + [VMEM],
        (VMEM, VMEM, ANY, VMEM) + (ANY,) * 7,
        [
            pltpu.VMEM((own, width), bf16),
            pltpu.VMEM((count, batches, run, size), bf16),
            pltpu.VMEM((2, size, width), bf16),
            pltpu.VMEM((2, total, units), bf16),
            pltpu.VMEM((2, total, step), bf16),
            pltpu.VMEM((2, step, half), f32),
            pltpu.VMEM((4, step, half), bf16),
            by_plane,
            by_plane,
            by_plane,
            by_plane,
            pltpu.VMEM((C, part, width), bf16),
            DMA((batches, count)),
            DMA((batches, count)),
            DMA((batches,)),
            DMA((2,)),
            DMA((E,)),
            DMA((E,)),
            DMA((E, C)),
            DMA((E, C)),
            DMA((C,)),
            DMA((C,)),
            DMA((2,)),
            DMA((2,)),
            DMA((2,)),
            DMA((items,)),
            DMA((items,)),
        ]
        + Return.scratch(E, C, len(runs), run, width, y_rows.shape[3]),
        collective,
        name,
        vmem=62,
    )


def backward_kernel(
    E,
    C,
    G,
    runs,
    queries,
    keys,
    values,
    grads,
    row_ids,
    key_ids,
    log_total,
    query_hat,
    key_hat,
    factors,
    head_gains,
    y_rows,
    slots,
    w_qkv,
    normed,
    small,
    first,
    out_qkv,
    out_small,
    out_gains,
    out,
    raw,
    query_grad,
    key_grad,
    key_sum,
    value_sum,
    sums,
    sum_parts,
    gain_sum,
    gain_parts,
    small_parts,
    small_sum,
    swap,
    swapped,
    own,
    passed,
    tokens,
    parts,
    plane_parts,
    sum_qkv,
    cs,
    cr,
    zs,
    zr,
    ts,
    qs,
    qr,
    os,
    orr,
    ss,
    sr,
    fs,
    fr,
    ms,
    mr,
    hs,
    hr,
    gs,
    gr,
    *return_scratch,
):
    e, c, d = position()
    me, peers = column_peers(E, C, G)
    planes = plane_peers(E)
    count = C * G
    _, run, columns = raw.shape
    every, size = queries.shape
    batches, length = row_ids.shape[:2]
    scale = HEAD**-0.5
    width = w_qkv.shape[0]
    rows = batches * run
    sibling = (e, c, 1 - d)
    meet([device for _, _, device in peers] + [device for _, _, device in planes])
    half = tokens.shape[2]
    block = parts.shape[1]
    cuts = block // half

    def token_copy(part):
        at = lax.rem(e + 1 + part // cuts, E) * block + part % cuts * half
        return pltpu.make_async_copy(
            normed.at[:, pl.ds(pl.multiple_of(at, half), half)],
            tokens.at[part % 2],
            ts.at[part % 2],
        )

    token_copy(0).start()
    token_copy(1).start()
    small_copies = [
        remote(small.at[plane], small_parts.at[i], ss.at[i], sr.at[i], device)
        for i, plane, device in planes
    ]
    for copy in small_copies:
        copy.start()

    way_back = Return(E, C, runs, y_rows, slots, out, *return_scratch)
    way_back.begin()
    heads = size // HEAD

    def head_back(n, carry):
        b, h = n // heads, lax.rem(n, heads)
        lanes = pl.ds(pl.multiple_of(h * HEAD, HEAD), HEAD)
        start = pl.multiple_of(b * length, length)
        key_sum[...] = jnp.zeros_like(key_sum)
        value_sum[...] = jnp.zeros_like(value_sum)
        for at, many, seen in query_blocks(length):
            rows_here = pl.ds(pl.multiple_of(start + at, many), many)
            rows_seen = pl.ds(start, seen)
            query, grad = queries[rows_here, lanes], grads[rows_here, lanes]
            scores = contract(query, keys[rows_seen, lanes], (1, 1)) * scale
            allowed = key_ids[b, :, :seen] <= row_ids[b, at : at + many]
            scores = jnp.where(allowed, scores, MASKED)
            probs = jnp.exp(scores - log_total[b, h, at : at + many])
            prod = contract(grad, values[rows_seen, lanes], (1, 1))
            delta = jnp.sum(probs * prod, axis=1, keepdims=True)
            score_grad = (probs * (prod - delta)).astype(bf16)
            query_grad[rows_here, lanes] = (
                jnp.dot(score_grad, keys[rows_seen, lanes], preferred_element_type=f32) * scale
            )
            key_sum[:seen] += contract(score_grad, query, (0, 0)) * scale
            value_sum[:seen] += contract(probs.astype(bf16), grad, (0, 0))
        key_grad[pl.ds(start, length), lanes] = key_sum[...]
        value_lanes = pl.ds(pl.multiple_of(2 * size + h * HEAD, HEAD), HEAD)
        raw[pl.ds(b * count, count), :, value_lanes] = (
            value_sum[...].astype(bf16).reshape(count, run, HEAD)
        )
        for q in range(min(beside, len(runs))):

            @pl.when(n == batches * heads - beside + q)
            def _():
                way_back.combine(q)

        return carry

    beside = 2
    pending = iter(range(beside, len(runs)))

    def carry_on(many):
        for _ in range(many):
            n = next(pending, None)
            if n is not None:
                way_back.combine(n)

    lax.fori_loop(0, batches * heads, head_back, 0)

    chunk = min(2 * run, every)
    per_chunk = chunk // run
    ones = jnp.ones((8, size), f32)
    gain_sum[...] = jnp.zeros_like(gain_sum)
    pairs = ((query_grad, query_hat), (key_grad, key_hat))

    def dots(j, carry):
        rows_here = pl.ds(pl.multiple_of(j * chunk, chunk), chunk)
        for kind, (grad, hat) in enumerate(pairs):
            prod = grad[rows_here] * hat[rows_here]
            gain_sum[kind] += jnp.sum(prod, axis=0, keepdims=True)
            total = lax.dot_general(
                ones,
                prod * head_gains[kind : kind + 1],
                (((1,), (1,)), ((), ())),
                precision=lax.Precision.HIGHEST,
                preferred_element_type=f32,
            )
            sums[kind, :, rows_here] = total[:1]
        return carry

    lax.fori_loop(0, every // chunk, dots, 0)
    shares = [
        remote(sums, sum_parts.at[me], ms.at[offset], mr.at[offset], device)
        for offset, _, device in peers
    ]
    gain_copies = [
        remote(gain_sum, gain_parts.at[i], hs.at[i], hr.at[i], device) for i, _, device in planes
    ]
    for copy in shares + gain_copies:
        copy.start()
    sum_parts[me] = sums[...]
    carry_on(1)
    for copy in shares:
        copy.wait()
    total = sum_parts[0]
    for index in range(1, count):
        total = total + sum_parts[index]
    sums[...] = total / width
    rows_at = lax.broadcasted_iota(jnp.int32, (chunk, chunk), 0)
    same = rows_at == lax.broadcasted_iota(jnp.int32, (chunk, chunk), 1)

    def column_of(row):
        return jnp.sum(jnp.where(same, row, 0.0), axis=1, keepdims=True)

    def through_norm(j, carry):
        rows_here = pl.ds(pl.multiple_of(j * chunk, chunk), chunk)
        for kind, (grad, hat) in enumerate(pairs):
            part = grad[rows_here] * head_gains[kind : kind + 1]
            part = part - hat[rows_here] * column_of(sums[kind, :, rows_here])
            part = (column_of(factors[kind, :, rows_here]) * part).astype(bf16)
            raw[pl.ds(j * per_chunk, per_chunk), :, kind * size : (kind + 1) * size] = part.reshape(
                per_chunk, run, size
            )
        return carry

    lax.fori_loop(0, every // chunk, through_norm, 0)

    def gain_copy(offset, device):
        return remote(gain_sum, out_gains.at[me], gs.at[offset], gr.at[offset], device)

    for copy in gain_copies:
        copy.wait()
    total = gain_sum[...]
    for i in range(1, E):
        total = total + gain_parts[i]
    gain_sum[...] = total
    out_gains[me] = total
    for offset, _, device in peers:
        gain_copy(offset, device).start()

    def product(level, core, at, many):
        left = jnp.concatenate(
            [raw[b * count + level * G + core] for b in range(batches)], axis=0
        )
        return contract(left, w_qkv[at : at + many, :], (1, 1))

    def chip_copy(level):
        return remote(swap.at[level], swapped.at[level], cs.at[level], cr.at[level], sibling)

    def give(level):
        for at in range(0, width, 512):
            swap[level, :, at : at + 512] = product(level, 1 - d, at, 512).astype(bf16)
        chip_copy(level).start()

    def take(level):
        chip_copy(level).wait_recv()
        for at in range(0, width, 512):
            part = product(level, d, at, 512) + swapped[level, :, at : at + 512].astype(f32)
            own[level, :, at : at + 512] = part.astype(bf16)

    def hop(way, level, b):
        there = c + 1 if way == 0 else c - 1
        to = level if way == 0 else level + (C - level) * ((C - 1 - (there - level)) // (C - 1))
        return remote(
            own.at[level, pl.ds(b * run, run)],
            passed.at[to, pl.ds(b * run, run)],
            zs.at[way, level, b],
            zr.at[to, b],
            (e, there, d),
        )

    def arrival(entry, b):
        part = passed.at[entry, pl.ds(b * run, run)]
        return remote(part, part, zs.at[0, 0, b], zr.at[entry, b], sibling)

    def send(way, level, last):
        for b in range(batches):

            @pl.when(last)
            def _():
                arrival(level, b).wait_recv()
                piece = pl.ds(b * run, run)
                own[level, piece] = (
                    own[level, piece].astype(f32) + passed[level, piece].astype(f32)
                ).astype(bf16)

            hop(way, level, b).start()

    order = [C - 1, 0] + list(range(C - 2, 0, -1))
    for level in order:
        give(level)
    carry_on(1)

    def plane_copy(item):
        plane = lax.rem(e + 1 + item, E)
        return remote(
            parts.at[item],
            plane_parts.at[item],
            qs.at[item],
            qr.at[item],
            (plane, c, d),
        )

    def weights(item):
        for part in range(cuts * item, cuts * (item + 1)):
            token_copy(part).wait()
            for at in range(0, columns, 256):
                many = min(256, columns - at)
                piece = raw[:, :, at : at + many].reshape(every, many)
                rows_here = pl.ds(part % cuts * half, half)
                parts[item, rows_here, at : at + many] = contract(
                    tokens[part % 2], piece, (0, 0)
                ).astype(bf16)
            if part + 2 < cuts * E:
                token_copy(part + 2).start()
        if item < E - 1:
            plane_copy(item).start()

    mirror = C - 1 - c
    items = list(range(E))
    for level in order:
        take(level)
        if level == 0:
            @pl.when(c == 0)
            def _():
                send(0, C - 1, False)

            @pl.when(c == C - 1)
            def _():
                send(1, 0, False)

            weights(items.pop(0))
            carry_on(1)
    weights(items.pop(0))
    carry_on(len(runs))
    for turn in range(1, C - 1):

        @pl.when(c <= turn)
        def _():
            send(0, C - 1 - (turn - c), c > 0)

        @pl.when(mirror <= turn)
        def _():
            send(1, turn - mirror, mirror > 0)

        if items:
            weights(items.pop(0))
    while items:
        weights(items.pop(0))
    for item in range(E - 1):
        plane_copy(item).wait_recv()
    for at in range(0, block, 128):
        piece = pl.ds(at, min(128, block - at))
        total = parts[E - 1, piece].astype(f32)
        for item in range(E - 1):
            total = total + plane_parts[item, piece].astype(f32)
        sum_qkv[piece] = total.astype(bf16)
    share = block // (C * G)

    def row_copy(offset, index, device):
        return remote(
            sum_qkv.at[pl.ds(pl.multiple_of(index * share, share), share)],
            out_qkv.at[me],
            os.at[offset],
            orr.at[offset],
            device,
        )

    def small_copy(offset, index, device):
        return remote(
            small_sum.at[pl.ds(pl.multiple_of(index * share, share), share)],
            out_small.at[me],
            fs.at[offset],
            fr.at[offset],
            device,
        )

    for copy in small_copies:
        copy.wait_recv()
    total = small[e]
    for i in range(1, E):
        total = total + small_parts[i]
    small_sum[...] = total
    for offset, index, device in peers:
        small_copy(offset, index, device).start()
        row_copy(offset, index, device).start()
    out_small[me] = small_sum[pl.ds(pl.multiple_of(me * share, share), share)]
    out_qkv[me] = sum_qkv[pl.ds(pl.multiple_of(me * share, share), share)]

    def arrived(entry):
        for b in range(batches):
            arrival(entry, b).wait_recv()

    @pl.when(c > 0)
    def _():
        arrived(c)

    @pl.when(c < C - 1)
    def _():
        arrived(C)

    for at in range(0, width, 512):
        first[:, at : at + 512] = own[c, :, at : at + 512].astype(f32)

    @pl.when(c > 0)
    def _():
        for at in range(0, width, 512):
            first[:, at : at + 512] += passed[c, :, at : at + 512].astype(f32)

    @pl.when(c < C - 1)
    def _():
        for at in range(0, width, 512):
            first[:, at : at + 512] += passed[C, :, at : at + 512].astype(f32)

    for level in range(C):
        chip_copy(level).wait_send()
        for b in range(batches):

            @pl.when(level > c)
            def _():
                hop(0, level, b).wait_send()

            @pl.when(level < c)
            def _():
                hop(1, level, b).wait_send()

    for item in range(E - 1):
        plane_copy(item).wait_send()
    for copy in small_copies:
        copy.wait_send()
    for offset, _, device in peers:
        gain_copy(offset, device).wait()
    way_back.end()
    for offset, index, device in peers:
        row_copy(offset, index, device).wait()
        small_copy(offset, index, device).wait()


def run_backward(
    E,
    C,
    G,
    runs,
    queries,
    keys,
    values,
    grads,
    ids,
    log_total,
    query_hat,
    key_hat,
    factors,
    head_gains,
    y_rows,
    slots,
    w_qkv,
    normed,
    small,
    collective,
    name,
):
    every, size = queries.shape
    batches, length = ids.shape
    count = C * G
    run = length // count
    columns = 3 * size
    width = w_qkv.shape[0]
    rows = batches * run
    block = width // E
    share = block // count
    lanes = small.shape[2]
    by_level = pltpu.VMEM((C, rows, width), bf16)
    wide = pltpu.VMEM((every, size), f32)
    head = pltpu.VMEM((length, HEAD), f32)
    return call(
        functools.partial(backward_kernel, E, C, G, runs),
        (
            queries,
            keys,
            values,
            grads,
            ids[:, :, None],
            ids[:, None, :],
            log_total,
            query_hat,
            key_hat,
            factors,
            head_gains,
            y_rows,
            slots,
            w_qkv,
            normed,
            small,
        ),
        (
            jax.ShapeDtypeStruct((rows, width), f32),
            jax.ShapeDtypeStruct((count, share, columns), bf16),
            jax.ShapeDtypeStruct((count, share, lanes), f32),
            jax.ShapeDtypeStruct((count, 2, 1, size), f32),
            jax.ShapeDtypeStruct((len(runs), run, width), bf16),
        ),
        [VMEM] * 11 + [ANY, VMEM, VMEM, ANY, VMEM],
        (VMEM, VMEM, VMEM, VMEM, ANY),
        [
            pltpu.VMEM((batches * count, run, columns), bf16),
            wide,
            wide,
            head,
            head,
            pltpu.VMEM((2, 1, every), f32),
            pltpu.VMEM((count, 2, 1, every), f32),
            pltpu.VMEM((2, 1, size), f32),
            pltpu.VMEM((E, 2, 1, size), f32),
            pltpu.VMEM((E, block, lanes), f32),
            pltpu.VMEM((block, lanes), f32),
            by_level,
            by_level,
            by_level,
            pltpu.VMEM((C + 1, rows, width), bf16),
            pltpu.VMEM((2, every, min(block, 256)), bf16),
            pltpu.VMEM((E, block, columns), bf16),
            pltpu.VMEM((E, block, columns), bf16),
            pltpu.VMEM((block, columns), bf16),
            DMA((C,)),
            DMA((C,)),
            DMA((2, C, batches)),
            DMA((C + 1, batches)),
            DMA((2,)),
            DMA((E,)),
            DMA((E,)),
            DMA((count,)),
            DMA((count,)),
            DMA((E,)),
            DMA((E,)),
            DMA((count,)),
            DMA((count,)),
            DMA((count,)),
            DMA((count,)),
            DMA((E,)),
            DMA((E,)),
            DMA((count,)),
            DMA((count,)),
        ]
        + Return.scratch(E, C, len(runs), run, width, y_rows.shape[3]),
        collective,
        name,
        vmem=62,
    )


def contract(left, right, axes):
    return lax.dot_general(left, right, ((axes[:1], axes[1:]), ((), ())), preferred_element_type=f32)


def query_blocks(length):
    size = min(256, length)
    return [(i, size, min(length, i + 2 * size)) for i in range(0, length, size)]


def rms_factor(values):
    return lax.rsqrt(jnp.mean(values * values, axis=-1, keepdims=True) + EPSILON)


def norm_back(grad_hat, hatted, factor):
    return factor * (grad_hat - hatted * jnp.mean(grad_hat * hatted, axis=-1, keepdims=True))


def slot_table(routes, experts):
    batches, run, top = routes.shape
    hits = jnp.swapaxes(routes, 1, 2)[:, :, :, None] == jnp.arange(experts, dtype=jnp.int32)
    ones = hits.astype(bf16)
    tokens, ranks = jnp.arange(run), jnp.arange(top)
    before = (tokens[None, :] < tokens[:, None]).astype(bf16)
    above = (ranks[None, :] < ranks[:, None]).astype(bf16)
    within = jnp.einsum("ts,bksx->bktx", before, ones, preferred_element_type=f32)
    totals = jnp.sum(hits.astype(f32), axis=2)
    earlier = jnp.einsum(
        "kj,bjx->bkx", above, totals.astype(bf16), preferred_element_type=f32
    )
    places = jnp.sum(jnp.where(hits, within + earlier[:, :, None, :], 0.0), axis=1)
    places = jnp.where(jnp.any(hits, axis=1), places, UNUSED_SLOT)
    return jnp.swapaxes(places, 1, 2)


def body(
    tokens,
    block_ids,
    routes,
    norm_gains,
    w_query,
    w_key,
    w_value,
    w_output,
    router,
    expert_gate,
    expert_up,
    expert_down,
    cotangent,
):
    E, C, G = lax.axis_size("expert"), lax.axis_size("context"), lax.axis_size("dp")
    batches, run, width = tokens.shape
    top = routes.shape[2]
    experts = E * C * expert_gate.shape[0]
    capacity = max(2, run * top // experts)
    count = C * G
    size = width // count
    length = count * run
    every = batches * length
    own = batches * run
    me = lax.axis_index("context") * G + lax.axis_index("dp")

    rows = w_query.shape[0]
    small_width = -(-(norm_gains.shape[1] + experts) // 128) * 128
    small = jnp.concatenate([norm_gains, router], axis=1)
    small = jnp.pad(small, ((0, 0), (0, small_width - small.shape[1])))
    pieces = [w.reshape(rows, count, size) for w in (w_query, w_key, w_value)]
    weights = jnp.swapaxes(jnp.concatenate(pieces, axis=2), 0, 1)
    places = slot_table(routes, experts).reshape(batches, E, C, run)
    by_level = jnp.transpose(places, (2, 0, 1, 3))
    by_expert = jnp.transpose(places, (1, 2, 0, 3))
    column, w_qkv, small, full_output, ids, slots = start(
        E, C, G, tokens, weights, small, w_output, block_ids, by_level
    )
    ids = jnp.swapaxes(ids, 0, 1).reshape(batches, length)
    w_qkv = w_qkv.reshape(width, 3 * size)
    small = small.reshape(width, small_width)
    full_output = full_output.reshape(width, width)
    gains = small[:, :4].astype(f32)
    full_router = small[:, 4 : 4 + experts]
    head_gains = lax.dynamic_slice(gains, (me * size, 0), (size, 4))

    (
        normed,
        query_low,
        key_low,
        value_low,
        query_hat,
        key_hat,
        log_total,
        factors,
        mixed_low,
        upstream_rows,
    ) = run_forward(
        E,
        C,
        G,
        column.reshape(every, width),
        jnp.swapaxes(gains[:, :1], 0, 1),
        jnp.swapaxes(head_gains[:, 1:3], 0, 1),
        w_qkv,
        ids,
        slots,
        cotangent,
        capacity,
        2,
        "forward",
    )
    mixed_low = mixed_low.reshape(own, width)

    inputs = tokens.reshape(own, width).astype(f32)
    resid = inputs + jnp.dot(mixed_low, full_output, preferred_element_type=f32)
    second_factor = rms_factor(resid)
    second_hat = resid * second_factor
    second_low = (second_hat * gains[:, 3]).astype(bf16)
    logits = jnp.dot(second_low, full_router, preferred_element_type=f32)
    router_probs = jax.nn.softmax(logits, axis=-1)
    gate_table = jnp.transpose(router_probs.reshape(batches, run, E, C), (2, 3, 0, 1))
    table = jnp.concatenate([by_expert, gate_table], axis=2)[:, :, :, None, :]

    second_grad, x, y_rows, pair_grad, act, gate_pre_grad, up_pre_grad, gate_grad = run_experts(
        E,
        C,
        second_low.reshape(batches, run, width),
        upstream_rows,
        slots,
        table,
        expert_gate[0],
        expert_up[0],
        expert_down[0],
        capacity,
        4,
        "experts",
    )
    slot_count = E * C * batches * capacity
    x, pair_grad, act, gate_pre_grad, up_pre_grad = (
        rows.reshape(slot_count, -1) for rows in (x, pair_grad, act, gate_pre_grad, up_pre_grad)
    )
    prob_grad = jnp.transpose(gate_grad[:, :, :, 0, :], (2, 3, 0, 1)).reshape(own, experts)
    logit_grad = router_probs * (
        prob_grad - jnp.sum(router_probs * prob_grad, axis=-1, keepdims=True)
    )
    logit_grad = jnp.pad(logit_grad.astype(bf16), ((0, 0), (0, small_width - experts)))
    router_wide = jnp.pad(full_router, ((0, 0), (0, small_width - experts)))

    early = [(b, i) for b in range(batches // 2) for i in list(range(1, C)) + [0]]
    late = [(b, i) for b in range(batches // 2, batches) for i in list(range(1, C)) + [0]]
    resid_grad, gain_second, mixed_grad, grad_proj, *expert_grads, early_mixture = middle(
        E,
        C,
        G,
        early,
        second_grad,
        resid,
        second_factor,
        cotangent.reshape(own, width),
        jnp.swapaxes(gains[:, 3:4], 0, 1),
        logit_grad,
        router_wide,
        full_output,
        mixed_low,
        x,
        pair_grad,
        gate_pre_grad,
        up_pre_grad,
        act,
        y_rows,
        slots,
        6,
        "middle",
    )
    grad_gate, grad_up, grad_down = (
        (mine + other.astype(f32))[None] for mine, other in zip(expert_grads[:3], expert_grads[3:])
    )
    grad_proj = jnp.sum(grad_proj.astype(f32), axis=0)
    sums = contract(second_low, logit_grad, (0, 0))
    sums = jnp.where(jnp.arange(small_width) == experts, gain_second.reshape(width, 1), sums)
    first_grad, grad_qkv, sums, gain_heads, late_mixture = run_backward(
        E,
        C,
        G,
        late,
        query_low,
        key_low,
        value_low,
        mixed_grad.reshape(every, size),
        ids,
        log_total,
        query_hat,
        key_hat,
        factors,
        jnp.swapaxes(head_gains[:, 1:3], 0, 1),
        y_rows,
        slots,
        w_qkv,
        normed,
        sums.reshape(E, width // E, small_width),
        8,
        "backward",
    )
    gain_heads = jnp.swapaxes(gain_heads[:, :, 0], 0, 1).reshape(2, width)
    first_row = (lax.axis_index("expert") * count + me) * rows
    gain_heads = lax.dynamic_slice(gain_heads, (0, first_row), (2, rows))
    mixture = [0.0] * batches
    for runs, parts in ((early, early_mixture), (late, late_mixture)):
        for n, (b, _) in enumerate(runs):
            mixture[b] = mixture[b] + parts[n].astype(f32)
    mixture = jnp.stack(mixture)
    activations = (resid.reshape(tokens.shape) + mixture).astype(bf16)
    sums = jnp.sum(sums, axis=0)
    first_factor = rms_factor(inputs)
    first_hat = inputs * first_factor
    input_grad = resid_grad + norm_back(first_grad * gains[:, 0], first_hat, first_factor)

    grad_qkv = jnp.swapaxes(grad_qkv.astype(f32), 0, 1)
    grad_query, grad_key, grad_value = (
        grad_qkv[:, :, i * size : (i + 1) * size].reshape(rows, width) for i in range(3)
    )
    gain_first = sum(
        jnp.sum(w.astype(f32) * grad, axis=1)
        for w, grad in ((w_query, grad_query), (w_key, grad_key), (w_value, grad_value))
    )
    gain_first = gain_first / norm_gains[:, 0].astype(f32)
    grad_gains = jnp.stack([gain_first, gain_heads[0], gain_heads[1], sums[:, experts]], axis=1)
    return (
        activations,
        input_grad.reshape(tokens.shape),
        grad_gains,
        grad_query,
        grad_key,
        grad_value,
        grad_proj,
        sums[:, :experts],
        grad_gate,
        grad_up,
        grad_down,
    )


def solution(mesh):
    by_token = ("context", "dp")
    by_expert = P(("expert", "context"), None, None)
    by_row = P(ALL_AXES, None)
    rows = P("expert", by_token, None)
    return jax.shard_map(
        body,
        mesh=mesh,
        in_specs=(
            rows,
            P("expert", by_token),
            rows,
            by_row,
            by_row,
            by_row,
            by_row,
            by_row,
            by_row,
            by_expert,
            by_expert,
            by_expert,
            rows,
        ),
        out_specs=(
            rows,
            rows,
            by_row,
            by_row,
            by_row,
            by_row,
            by_row,
            by_row,
            P(("expert", "context"), None, "dp"),
            P(("expert", "context"), None, "dp"),
            P(("expert", "context"), "dp", None),
        ),
        check_vma=False,
    )
```

```python
import functools

import jax
import jax.numpy as jnp
from jax import lax
from jax.experimental import pallas as pl
from jax.experimental.pallas import tpu as pltpu
from jax.sharding import PartitionSpec as P

HEAD = 128
EPSILON = 1e-05
MASKED = -1e30
UNUSED_SLOT = 4096.0
ALL_AXES = ("expert", "context", "dp")
MESH = pl.DeviceIdType.MESH
ANY = pl.BlockSpec(memory_space=pl.ANY)
VMEM = pl.BlockSpec(memory_space=pltpu.VMEM)
DMA = pltpu.SemaphoreType.DMA
MIB = 1 << 20
f32 = jnp.float32
bf16 = jnp.bfloat16


def call(kernel, operands, out_shapes, in_specs, out_specs, scratch, collective, name, vmem=32):
    return pl.pallas_call(
        kernel,
        out_shape=out_shapes,
        in_specs=in_specs,
        out_specs=out_specs,
        scratch_shapes=scratch,
        compiler_params=pltpu.CompilerParams(
            collective_id=collective, has_side_effects=True, vmem_limit_bytes=vmem * MIB
        ),
        name=name,
    )(*operands)


def position():
    return lax.axis_index("expert"), lax.axis_index("context"), lax.axis_index("dp")


def meet(devices):
    barrier = pltpu.get_barrier_semaphore()
    for device in devices:
        pl.semaphore_signal(barrier, inc=1, device_id=device, device_id_type=MESH)
    pl.semaphore_wait(barrier, len(devices))


def remote(source, target, send_sem, recv_sem, device):
    return pltpu.make_async_remote_copy(
        src_ref=source,
        dst_ref=target,
        send_sem=send_sem,
        recv_sem=recv_sem,
        device_id=device,
        device_id_type=MESH,
    )


def column_peers(E, C, G):
    e, c, d = position()
    me = c * G + d
    peers = []
    for offset in range(1, C * G):
        index = lax.rem(me + offset, C * G)
        peers.append((offset, index, (e, index // G, lax.rem(index, G))))
    return me, peers


def plane_peers(E):
    e, c, d = position()
    return [(i, lax.rem(e + i, E), (lax.rem(e + i, E), c, d)) for i in range(1, E)]


def level_peers(C):
    e, c, d = position()
    return [(i, lax.rem(c + i, C), (e, lax.rem(c + i, C), d)) for i in range(1, C)]


def start_kernel(
    E,
    C,
    G,
    tokens,
    weights,
    small_weights,
    output,
    ids,
    slots,
    column,
    gathered,
    small_gathered,
    full_output,
    ids_out,
    slots_out,
    ws,
    wr,
    bs,
    br,
    hs,
    hr,
    ts,
    tr,
    ls,
    ms,
    mr,
    ps,
    pr,
    fs,
    fr,
    gs,
    gr,
):
    e, c, d = position()
    me, peers = column_peers(E, C, G)
    planes = plane_peers(E)
    batches = tokens.shape[0]
    sibling = (e, c, 1 - d)
    meet([device for _, _, device in peers] + [device for _, _, device in planes])
    kinds = ((weights, gathered), (small_weights, small_gathered))
    weight_copies = []
    for j, (source, target) in enumerate(kinds):
        for offset, index, device in peers:
            part = source.at[index] if j == 0 else source
            weight_copies.append(
                remote(part, target.at[e, me], ws.at[j, offset], wr.at[j, offset], device)
            )
    for copy in weight_copies:
        copy.start()
    local = [
        pltpu.make_async_copy(weights.at[me], gathered.at[e, me], ls.at[0]),
        pltpu.make_async_copy(small_weights, small_gathered.at[e, me], ls.at[1]),
        pltpu.make_async_copy(output, full_output.at[e, c, d], ls.at[2]),
    ]
    for b in range(batches):
        local.append(pltpu.make_async_copy(tokens.at[b], column.at[b, me], ls.at[3 + b]))
    for copy in local:
        copy.start()

    def source_of(item):
        return output if item == 0 else tokens.at[item - 1]

    def place(item, level):
        return full_output.at[e, level, d] if item == 0 else column.at[item - 1, level * G + d]

    def to_sibling(source, item, level, arrival):
        return remote(
            source, place(item, level), ts.at[item, arrival], tr.at[item, arrival], sibling
        )

    def step(hop, source, item, level, up):
        to = (e, c + 1, d) if up else (e, c - 1, d)
        way = 0 if up else 1
        return remote(
            source, place(item, level), hs.at[way, item, hop], hr.at[way, item, hop], to
        )

    def relay(item, hop):
        for up in (True, False):
            level = c - hop if up else c + hop
            here = (c >= hop) if up else (c + hop < C)
            onward = (c < C - 1) if up else (c > 0)

            @pl.when(here)
            def _():
                landed = place(item, level)
                step(hop - 1, landed, item, level, up).wait_recv()
                if hop < C - 1:

                    @pl.when(onward)
                    def _():
                        step(hop, landed, item, level, up).start()

                if item == 0:
                    for i, _, device in planes:
                        output_copy(i, level, device).start()
                if G > 1:
                    to_sibling(landed, item, level, hop if up else C - 1 + hop).start()

    def output_copy(i, level, device):
        mine = full_output.at[e, level, d]
        return remote(mine, mine, fs.at[i, level], fr.at[i, level], device)

    def output_sibling(i, level):
        part = full_output.at[lax.rem(e + E - i, E), level, d]
        return remote(part, part, gs.at[i, level], gr.at[i, level], sibling)

    for item in range(batches + 1):

        @pl.when(c < C - 1)
        def _():
            step(0, source_of(item), item, c, True).start()

        @pl.when(c > 0)
        def _():
            step(0, source_of(item), item, c, False).start()

        if G > 1:
            to_sibling(source_of(item), item, c, 0).start()
    small = []
    for offset, _, device in peers:
        small.append(remote(ids, ids_out.at[me], ms.at[offset], mr.at[offset], device))
    for i, level, device in level_peers(C):
        small.append(remote(slots.at[level], slots_out.at[i], ps.at[i], pr.at[i], device))
    for copy in small:
        copy.start()
    ids_out[me] = ids[...]
    slots_out[0] = slots[c]
    for copy in weight_copies:
        copy.wait_recv()
    for copy in local[:3]:
        copy.wait()
    plane_copies = []
    for j, (_, target) in enumerate(kinds):
        for i, _, device in planes:
            copy = remote(target.at[e], target.at[e], bs.at[j, i], br.at[j, i], device)
            copy.start()
            plane_copies.append(copy)
    for i, _, device in planes:
        output_copy(i, c, device).start()
    for hop in range(1, C):
        for item in range(batches + 1):
            relay(item, hop)
    for level in range(C):
        for i, _, device in planes:
            output_copy(i, level, device).wait_recv()
            if G > 1:
                output_sibling(i, level).start()

    for item in range(batches + 1):
        if G > 1:
            to_sibling(source_of(item), item, c, 0).wait()
        for hop in range(C - 1):
            for up in (True, False):
                arrival = hop + 1 if up else C + hop
                origin = c - hop if up else c + hop
                if up:
                    sends = jnp.logical_and(origin >= 0, c < C - 1)
                    arrives = c >= hop + 1
                else:
                    sends = jnp.logical_and(origin < C, c > 0)
                    arrives = c + hop + 1 < C

                @pl.when(sends)
                def _():
                    step(hop, source_of(item), item, c, up).wait_send()

                if G > 1:

                    @pl.when(arrives)
                    def _():
                        to_sibling(source_of(item), item, c, arrival).wait()

    for level in range(C):
        for i, _, device in planes:
            output_copy(i, level, device).wait_send()
            if G > 1:
                output_sibling(i, level).wait()
    for copy in weight_copies:
        copy.wait_send()
    for copy in plane_copies + small + local[3:]:
        copy.wait()


def start(E, C, G, tokens, weights, small_weights, output, ids, slots):
    batches, run, width = tokens.shape
    count = C * G
    rows, columns = weights.shape[1:]
    items = batches + 1
    return call(
        functools.partial(start_kernel, E, C, G),
        (tokens, weights, small_weights, output, ids, slots),
        (
            jax.ShapeDtypeStruct((batches, count, run, width), tokens.dtype),
            jax.ShapeDtypeStruct((E, count, rows, columns), weights.dtype),
            jax.ShapeDtypeStruct((E, count) + small_weights.shape, weights.dtype),
            jax.ShapeDtypeStruct((E, C, G, rows, width), weights.dtype),
            jax.ShapeDtypeStruct((count,) + ids.shape, ids.dtype),
            jax.ShapeDtypeStruct(slots.shape, slots.dtype),
        ),
        [ANY, ANY, ANY, ANY, VMEM, VMEM],
        (ANY, ANY, ANY, ANY, VMEM, VMEM),
        [
            DMA((2, count)),
            DMA((2, count)),
            DMA((2, E)),
            DMA((2, E)),
            DMA((2, items, C)),
            DMA((2, items, C)),
            DMA((items, 2 * C)),
            DMA((items, 2 * C)),
            DMA((items + 2,)),
            DMA((count,)),
            DMA((count,)),
            DMA((C,)),
            DMA((C,)),
            DMA((E, C)),
            DMA((E, C)),
            DMA((E, C)),
            DMA((E, C)),
        ],
        1,
        "start",
        vmem=62,
    )


def choose(slots, count):
    cells = lax.broadcasted_iota(jnp.int32, (count, slots.shape[1]), 0).astype(f32)
    return jnp.concatenate(
        [(cells == slots[i : i + 1, :]).astype(bf16) for i in range(slots.shape[0])], axis=0
    )


class Flow:
    def __init__(self, E, C, rows, slots, landed, packed, target, own, zs, zr, xs, xr, stay):
        self.E, self.C, self.rows, self.slots = E, C, rows, slots
        self.landed, self.packed, self.target = landed, packed, target
        self.sems = own, zs, zr, xs, xr, stay
        self.e, self.c, self.d = position()
        self.batches = rows.shape[0]
        self.cap, self.width = target.shape[3:]
        self.kept = packed.shape[0]
        self.chunks = self.batches * C

    def level_entry(self, far):
        high = 2 * self.c // self.C
        return high * far + (1 - high) * lax.rem(self.C - far, self.C)

    def own(self, b):
        return pltpu.make_async_copy(self.rows.at[b], self.landed.at[0, b], self.sems[0].at[b])

    def hop(self, b, i, way):
        there = i + 1 if way == 0 else lax.rem(i + self.C - 1, self.C)
        level = lax.rem(self.c + (1 if way == 0 else self.C - 1), self.C)
        return remote(
            self.landed.at[i, b],
            self.landed.at[there, b],
            self.sems[1].at[way, i, b],
            self.sems[2].at[there, b],
            (self.e, level, self.d),
        )

    def arrival(self, b, i):
        entry = self.landed.at[i, b]
        return remote(
            entry,
            entry,
            self.sems[1].at[0, i, b],
            self.sems[2].at[i, b],
            (self.e, self.c, 1 - self.d),
        )

    def onward(self, i, way):
        if way == 0:
            return jnp.logical_and(i <= self.c, self.c < self.C - 1)
        return jnp.logical_and(lax.rem(self.C - i, self.C) + self.c < self.C, self.c > 0)

    def pass_on(self, far, b):
        for way in range(2):
            i = far if way == 0 else lax.rem(self.C - far, self.C)
            here = (far <= self.c) if way == 0 else (far + self.c < self.C)

            @pl.when(jnp.logical_and(here, self.onward(i, way)))
            def _():
                self.hop(b, i, way).start()

    def begin(self, count):
        for b in range(self.batches):
            self.own(b).start()
        for b in range(self.batches):
            self.own(b).wait()
        for b in range(count):
            self.pass_on(0, b)

    def receive(self, far, b):
        for way in range(2):
            i = far if way == 0 else self.C - far

            @pl.when((far <= self.c) if way == 0 else (far + self.c < self.C))
            def _():
                self.arrival(b, i).wait_recv()

    def hops_sent(self, b, i):
        for way in range(2):

            @pl.when(self.onward(i, way))
            def _():
                self.hop(b, i, way).wait_send()

    def across(self, n, b, i, k):
        plane = lax.rem(self.e + k, self.E)
        return remote(
            self.packed.at[lax.rem(n, self.kept), plane],
            self.target.at[i, b, k],
            self.sems[3].at[i, b, k],
            self.sems[4].at[i, b, k],
            (plane, self.c, self.d),
        )

    def stay(self, n, b, i):
        return pltpu.make_async_copy(
            self.packed.at[lax.rem(n, self.kept), self.e],
            self.target.at[i, b, 0],
            self.sems[5].at[i, b],
        )

    def compact(self, n, b, i):
        place = lax.rem(n, self.kept)
        picks = choose(self.slots[i, b], self.cap)
        for at in range(0, self.width, 512):
            part = jnp.dot(
                picks, self.landed[i, b, :, at : at + 512], preferred_element_type=f32
            ).astype(bf16)
            self.packed[place, :, :, at : at + 512] = part.reshape(self.E, self.cap, 512)
        for k in range(1, self.E):
            self.across(n, b, i, k).start()
        self.stay(n, b, i).start()

    def crossed(self, n, b, i):
        for k in range(1, self.E):
            self.across(n, b, i, k).wait_send()

    def arrived(self, n, b, i):
        for k in range(1, self.E):
            self.across(n, b, i, k).wait_recv()

    @staticmethod
    def scratch(E, C, batches, run, width, cap, kept):
        return [
            pltpu.VMEM((C, batches, run, width), bf16),
            pltpu.VMEM((kept, E, cap, width), bf16),
            DMA((batches,)),
            DMA((2, C, batches)),
            DMA((C, batches)),
            DMA((C, batches, E)),
            DMA((C, batches, E)),
            DMA((C, batches)),
        ]


class Return:
    def __init__(self, E, C, runs, rows, slots, out, returned, sums, ys, yr, bs, us, ur, ks):
        self.E, self.C, self.runs = E, C, runs
        self.rows, self.slots, self.out = rows, slots, out
        self.returned, self.sums = returned, sums
        self.sems = ys, yr, bs, us, ur, ks
        self.e, self.c, self.d = position()

    def back(self, n, k):
        b, i = self.runs[n]
        return remote(
            self.rows.at[i, b, k],
            self.returned.at[n, self.e],
            self.sems[0].at[n, k],
            self.sems[1].at[n, k],
            (lax.rem(self.e + self.E - k, self.E), self.c, self.d),
        )

    def own(self, n):
        b, i = self.runs[n]
        return pltpu.make_async_copy(
            self.rows.at[i, b, 0], self.returned.at[n, self.e], self.sems[2].at[n]
        )

    def along(self, n):
        i = self.runs[n][1]
        if i == 0:
            return pltpu.make_async_copy(self.sums.at[n], self.out.at[n], self.sems[5].at[n])
        to = (self.e, lax.rem(self.c + self.C - i, self.C), self.d)
        return remote(
            self.sums.at[n], self.out.at[n], self.sems[3].at[n], self.sems[4].at[n], to
        )

    def send(self, n):
        if n < len(self.runs):
            for k in range(1, self.E):
                self.back(n, k).start()
            self.own(n).start()

    def begin(self):
        self.send(0)
        self.send(1)

    def combine(self, n):
        b, i = self.runs[n]
        for k in range(1, self.E):
            self.back(n, k).wait_recv()
        self.own(n).wait()
        self.send(n + 2)
        cap, width = self.rows.shape[3:]
        picks = choose(self.slots[i, b], cap)
        for at in range(0, width, 512):
            part = self.returned[n, :, :, at : at + 512].reshape(self.E * cap, 512)
            self.sums[n, :, at : at + 512] = contract(picks, part, (0, 0)).astype(bf16)
        self.along(n).start()

    def end(self):
        for n in range(len(self.runs)):
            for k in range(1, self.E):
                self.back(n, k).wait_send()
            self.along(n).wait()

    @staticmethod
    def scratch(E, C, count, run, width, cap):
        return [
            pltpu.VMEM((count, E, cap, width), bf16),
            pltpu.VMEM((count, run, width), bf16),
            DMA((count, E)),
            DMA((count, E)),
            DMA((count,)),
            DMA((count,)),
            DMA((count,)),
            DMA((count,)),
        ]


def forward_kernel(
    E,
    C,
    G,
    column,
    gain,
    head_gains,
    w_qkv,
    row_ids,
    key_ids,
    slots,
    upstream,
    normed,
    queries,
    keys,
    values,
    query_hat,
    key_hat,
    log_total,
    factors,
    mixed,
    u_out,
    raw,
    low,
    squares,
    parts,
    heads,
    landed,
    packed,
    own,
    zs,
    zr,
    xs,
    xr,
    stay,
    raw_sem,
    low_sem,
    ss,
    sr,
    ms,
    mr,
    ml,
):
    me, peers = column_peers(E, C, G)
    planes = plane_peers(E)
    every, width = column.shape
    batches, length, size = heads.shape
    run = length // (C * G)
    block = raw.shape[1]
    blocks = every // block
    scale = HEAD**-0.5
    meet([device for _, _, device in peers] + [device for _, _, device in planes])
    flow = Flow(E, C, upstream, slots, landed, packed, u_out, own, zs, zr, xs, xr, stay)

    def load(j):
        at = pl.multiple_of(j * block, block)
        place = lax.rem(j, 2)
        return pltpu.make_async_copy(column.at[pl.ds(at, block)], raw.at[place], raw_sem.at[place])

    def store(j):
        at = pl.multiple_of(j * block, block)
        place = lax.rem(j, 2)
        return pltpu.make_async_copy(low.at[place], normed.at[pl.ds(at, block)], low_sem.at[place])

    def chunk_of(n):
        return n % batches, flow.level_entry(n // batches)

    chunk = iter(range(flow.chunks))

    def carry_on(count):
        for _ in range(count):
            n = next(chunk, None)
            if n is None:
                return
            if n >= flow.kept:
                before = n - flow.kept, *chunk_of(n - flow.kept)
                flow.crossed(*before)
                flow.stay(*before).wait()
            if n >= batches:
                flow.receive(n // batches, n % batches)
                flow.pass_on(n // batches, n % batches)
            flow.compact(n, *chunk_of(n))

    load(0).start()
    load(1).start()
    flow.begin(batches)
    carry_on(batches)
    ones = jnp.ones((8, size), f32)

    def project(j, carry):
        place = lax.rem(j, 2)
        rows = pl.ds(pl.multiple_of(j * block, block), block)
        load(j).wait()

        @pl.when(j >= 2)
        def _():
            store(j - 2).wait()

        total = jnp.zeros((block, 1), f32)
        for at in range(0, width, 512):
            part = raw[place, :, at : at + 512].astype(f32)
            total += jnp.sum(part * part, axis=1, keepdims=True)
        factor = lax.rsqrt(total / width + EPSILON)
        for at in range(0, width, 512):
            part = raw[place, :, at : at + 512].astype(f32) * factor
            low[place, :, at : at + 512] = (part * gain[:, at : at + 512]).astype(bf16)
        store(j).start()

        @pl.when(j + 2 < blocks)
        def _():
            load(j + 2).start()

        for kind in range(3):
            part = jnp.dot(
                low[place],
                w_qkv[:, kind * size : (kind + 1) * size],
                preferred_element_type=f32,
            )
            if kind == 2:
                values[rows] = part.astype(bf16)
            else:
                (query_hat, key_hat)[kind][rows] = part
                sums = lax.dot_general(
                    ones,
                    part * part,
                    (((1,), (1,)), ((), ())),
                    precision=lax.Precision.HIGHEST,
                    preferred_element_type=f32,
                )
                squares[kind, :, rows] = sums[:1]
        return carry

    half = blocks // 2
    lax.fori_loop(0, half, project, 0)
    carry_on(1)
    lax.fori_loop(half, blocks, project, 0)
    shares = [
        remote(squares, parts.at[me], ss.at[offset], sr.at[offset], device)
        for offset, _, device in peers
    ]
    for copy in shares:
        copy.start()
    parts[me] = squares[...]
    carry_on(1)
    for copy in shares:
        copy.wait_recv()
    total = parts[0]
    for index in range(1, C * G):
        total = total + parts[index]
    factors[...] = lax.rsqrt(total / width + EPSILON)
    rows_at = lax.broadcasted_iota(jnp.int32, (block, block), 0)
    same = rows_at == lax.broadcasted_iota(jnp.int32, (block, block), 1)

    def scaled(j, carry):
        rows = pl.ds(pl.multiple_of(j * block, block), block)
        for kind, (hat, out) in enumerate(((query_hat, queries), (key_hat, keys))):
            factor = jnp.sum(jnp.where(same, factors[kind, :, rows], 0.0), axis=1, keepdims=True)
            part = hat[rows] * factor
            hat[rows] = part
            out[rows] = (part * head_gains[kind : kind + 1]).astype(bf16)
        return carry

    lax.fori_loop(0, blocks, scaled, 0)
    carry_on(1)

    def mixed_copy(b, offset, index, device):
        where = pl.ds(pl.multiple_of(me * size, size), size)
        part = heads.at[b, pl.ds(pl.multiple_of(index * run, run), run)]
        return remote(part, mixed.at[b, :, where], ms.at[b, offset], mr.at[b, offset], device)

    def mixed_own(b):
        where = pl.ds(pl.multiple_of(me * size, size), size)
        part = heads.at[b, pl.ds(pl.multiple_of(me * run, run), run)]
        return pltpu.make_async_copy(part, mixed.at[b, :, where], ml.at[b])

    for b in range(batches):

        def head(h, carry, b=b):
            lanes = pl.ds(pl.multiple_of(h * HEAD, HEAD), HEAD)
            for first, count, seen in query_blocks(length):
                rows = pl.ds(b * length + first, count)
                seen_rows = pl.ds(b * length, seen)
                scores = contract(queries[rows, lanes], keys[seen_rows, lanes], (1, 1)) * scale
                allowed = key_ids[b, :, :seen] <= row_ids[b, first : first + count]
                scores = jnp.where(allowed, scores, MASKED)
                peak = jnp.max(scores, axis=1, keepdims=True)
                grown = jnp.exp(scores - peak)
                total = jnp.sum(grown, axis=1, keepdims=True)
                probs = (grown * (1.0 / total)).astype(bf16)
                heads[b, first : first + count, lanes] = jnp.dot(
                    probs, values[seen_rows, lanes], preferred_element_type=f32
                ).astype(bf16)
                log_total[b, h, first : first + count] = peak + jnp.log(total)
            return carry

        lax.fori_loop(0, size // HEAD, head, 0)
        for offset, index, device in peers:
            mixed_copy(b, offset, index, device).start()
        mixed_own(b).start()
        carry_on(1)
    carry_on(flow.chunks)

    for copy in shares:
        copy.wait_send()
    for j in (blocks - 2, blocks - 1):
        store(j).wait()
    for b in range(batches):
        for offset, index, device in peers:
            mixed_copy(b, offset, index, device).wait()
        mixed_own(b).wait()

    for n in range(flow.chunks):
        b, i = chunk_of(n)
        flow.hops_sent(b, i)
        flow.arrived(n, b, i)
        if n >= flow.chunks - flow.kept:
            flow.crossed(n, b, i)
            flow.stay(n, b, i).wait()


def run_forward(E, C, G, column, gain, head_gains, w_qkv, ids, slots, upstream, cap, collective, name):
    every, width = column.shape
    batches, run = upstream.shape[:2]
    count = C * G
    length = count * run
    size = width // count
    block = min(256, every)
    low = jax.ShapeDtypeStruct((every, size), bf16)
    wide = jax.ShapeDtypeStruct((every, size), f32)
    return call(
        functools.partial(forward_kernel, E, C, G),
        (column, gain, head_gains, w_qkv, ids[:, :, None], ids[:, None, :], slots, upstream),
        (
            jax.ShapeDtypeStruct((every, width), bf16),
            low,
            low,
            low,
            wide,
            wide,
            jax.ShapeDtypeStruct((batches, size // HEAD, length, 1), f32),
            jax.ShapeDtypeStruct((2, 1, every), f32),
            jax.ShapeDtypeStruct(upstream.shape, bf16),
            jax.ShapeDtypeStruct((C, batches, E, cap, width), bf16),
        ),
        [ANY] + [VMEM] * 6 + [ANY],
        (ANY,) + (VMEM,) * 7 + (ANY, ANY),
        [
            pltpu.VMEM((2, block, width), bf16),
            pltpu.VMEM((2, block, width), bf16),
            pltpu.VMEM((2, 1, every), f32),
            pltpu.VMEM((count, 2, 1, every), f32),
            pltpu.VMEM((batches, length, size), bf16),
        ]
        + Flow.scratch(E, C, batches, run, width, cap, 3)
        + [
            DMA((2,)),
            DMA((2,)),
            DMA((count,)),
            DMA((count,)),
            DMA((batches, count)),
            DMA((batches, count)),
            DMA((batches,)),
        ],
        collective,
        name,
        vmem=46,
    )


def experts_kernel(
    E,
    C,
    rows_x,
    u_in,
    slots,
    gates,
    gate_in,
    up_in,
    down_in,
    out,
    x_out,
    y_out,
    pair_out,
    act_out,
    gate_back_out,
    up_back_out,
    scalars_out,
    w_gate,
    w_up,
    w_down,
    table,
    scalars,
    landed,
    packed,
    own,
    zs,
    zr,
    xs,
    xr,
    stay,
    sums,
    returned,
    x,
    u,
    pair,
    act,
    gate_back,
    up_back,
    gated,
    sent,
    gs,
    gr,
    ss,
    sr,
    ys,
    yr,
    bs,
    us,
    ur,
    ks,
    loads,
    stores,
    weight_sem,
):
    e, c, d = position()
    batches, run, width = rows_x.shape
    cap = x_out.shape[3]
    units = w_gate.shape[1]
    chunks = batches * C
    total = E * cap
    kept = sent.shape[0]
    lead, lag = 1, 2
    everyone = [(k, i) for k in range(E) for i in range(C) if k + i > 0]
    ahead = [(k, i, (lax.rem(e + k, E), lax.rem(c + i, C), d)) for k, i in everyone]
    behind = [(k, i, (lax.rem(e + E - k, E), lax.rem(c + C - i, C), d)) for k, i in everyone]
    meet([device for _, _, device in ahead])
    flow = Flow(E, C, rows_x, slots, landed, packed, x_out, own, zs, zr, xs, xr, stay)

    def far_of(n):
        return lax.rem((n + batches - 1) // batches, C), lax.rem(n + batches - 1, batches)

    def chunk_of(n):
        far, b = far_of(n)
        return b, flow.level_entry(far)

    def back(n, b, i, k):
        return remote(
            sent.at[lax.rem(n, kept), k],
            returned.at[i, b, e],
            ys.at[i, b, k],
            yr.at[i, b, k],
            (lax.rem(e + E - k, E), c, d),
        )

    def back_own(n, b, i):
        return pltpu.make_async_copy(
            sent.at[lax.rem(n, kept), 0], returned.at[i, b, e], bs.at[i, b]
        )

    def up(b, i):
        return remote(
            sums.at[i, b],
            out.at[c, b],
            us.at[i, b],
            ur.at[i, b],
            (e, lax.rem(c + C - i, C), d),
        )

    def keep(b):
        return pltpu.make_async_copy(sums.at[0, b], out.at[c, b], ks.at[b])

    def load(a, b, i):
        source, target = ((x_out, x), (u_in, u))[a]
        return pltpu.make_async_copy(source.at[i, b], target, loads.at[a])

    def store(j, b, i):
        source = (pair, act, gate_back, up_back, gated)[j]
        target = (pair_out, act_out, gate_back_out, up_back_out, y_out)[j]
        return pltpu.make_async_copy(source, target.at[i, b], stores.at[j])

    weight_copies = [
        pltpu.make_async_copy(source, target, weight_sem.at[j])
        for j, (source, target) in enumerate(
            ((gate_in, w_gate), (up_in, w_up), (down_in, w_down))
        )
    ]
    for copy in weight_copies:
        copy.start()

    flow.begin(1)
    small = [
        remote(gates.at[device[0], device[1]], table.at[k, i], gs.at[k, i], gr.at[k, i], device)
        for k, i, device in ahead
    ]
    for copy in small:
        copy.start()
    table[0, 0] = gates[e, c]

    def compact(n):
        @pl.when(n >= flow.kept)
        def _():
            flow.crossed(n - flow.kept, *chunk_of(n - flow.kept))

        flow.compact(n, *chunk_of(n))

    def expert(n):
        b, i = chunk_of(n)
        load(1, b, i).start()
        flow.arrived(n, b, i)
        flow.stay(n, b, i).wait()
        load(0, b, i).start()

        @pl.when(n == 0)
        def _():
            for copy in weight_copies:
                copy.wait()

        @pl.when(n > 0)
        def _():
            before = chunk_of(n - 1)
            for j in range(5):
                store(j, *before).wait()

        @pl.when(n >= kept)
        def _():
            before = chunk_of(n - kept)
            for k in range(1, E):
                back(n - kept, *before, k).wait_send()

        holds, gate = [], []
        cells = lax.broadcasted_iota(jnp.int32, (cap, run), 0).astype(f32)
        for k in range(E):
            hold = cells == table[k, i, b]
            holds.append(hold)
            gate.append(
                jnp.sum(jnp.where(hold, table[k, i, batches + b], 0.0), axis=1, keepdims=True)
            )
        gate = jnp.concatenate(gate, axis=0)
        for a in range(2):
            load(a, b, i).wait()
        for at in range(0, width, 512):
            part = u[:, :, at : at + 512].reshape(total, 512).astype(f32)
            pair[:, :, at : at + 512] = (gate * part).astype(bf16).reshape(E, cap, 512)
        store(0, b, i).start()
        inputs = x[...].reshape(total, width)
        grads = pair[...].reshape(total, width)
        for at in range(0, units, 256):
            gate_pre = jnp.dot(inputs, w_gate[:, at : at + 256], preferred_element_type=f32)
            up_pre = jnp.dot(inputs, w_up[:, at : at + 256], preferred_element_type=f32)
            act_grad = contract(grads, w_down[at : at + 256, :], (1, 1))
            sigmoid = jax.nn.sigmoid(gate_pre)
            silu = gate_pre * sigmoid
            act[:, at : at + 256] = (silu * up_pre).astype(bf16)
            gate_back[:, at : at + 256] = (
                act_grad * up_pre * sigmoid * (1.0 + gate_pre * (1.0 - sigmoid))
            ).astype(bf16)
            up_back[:, at : at + 256] = (act_grad * silu).astype(bf16)
        for j in range(1, 4):
            store(j, b, i).start()
        place = lax.rem(n, kept)
        gate_grad = jnp.zeros((total, 1), f32)
        for at in range(0, width, 512):
            out = jnp.dot(act[...], w_down[:, at : at + 512], preferred_element_type=f32)
            out = out.astype(bf16).astype(f32)
            gate_grad += jnp.sum(
                out * u[:, :, at : at + 512].reshape(total, 512).astype(f32), axis=1, keepdims=True
            )
            gated[:, :, at : at + 512] = (gate * out).astype(bf16).reshape(E, cap, 512)
            back_rows = contract(gate_back[...], w_gate[at : at + 512, :], (1, 1))
            back_rows += contract(up_back[...], w_up[at : at + 512, :], (1, 1))
            sent[place, :, :, at : at + 512] = back_rows.astype(bf16).reshape(E, cap, 512)
        for k in range(1, E):
            back(n, b, i, k).start()
        back_own(n, b, i).start()
        store(4, b, i).start()
        for k in range(E):
            scalars[k, i, b] = jnp.sum(
                jnp.where(holds[k], gate_grad[k * cap : (k + 1) * cap], 0.0), axis=0, keepdims=True
            )

    def combine(n):
        b, i = chunk_of(n)
        picks = choose(slots[i, b], cap)
        for k in range(1, E):
            back(n, b, i, k).wait_recv()
        back_own(n, b, i).wait()
        for at in range(0, width, 512):
            part = returned[i, b, :, :, at : at + 512].reshape(total, 512)
            sums[i, b, :, at : at + 512] = contract(picks, part, (0, 0)).astype(bf16)

        @pl.when(i > 0)
        def _():
            up(b, i).start()

        @pl.when(i == 0)
        def _():
            keep(b).start()

    def step(s, carry):
        @pl.when(jnp.logical_and(s > 0, s <= batches * (C - 1)))
        def _():
            flow.receive(*far_of(s))
            flow.pass_on(s // batches, lax.rem(s, batches))

        @pl.when(s < chunks)
        def _():
            compact(s)

        @pl.when(jnp.logical_and(s >= lead, s < chunks + lead))
        def _():
            expert(s - lead)

        @pl.when(s >= lag)
        def _():
            combine(s - lag)

        return carry

    for copy in small:
        copy.wait_recv()
    lax.fori_loop(0, chunks + lag, step, 0)
    scalars_out[e, c] = scalars[0, 0]
    last = [
        remote(scalars.at[k, i], scalars_out.at[e, c], ss.at[k, i], sr.at[k, i], device)
        for k, i, device in behind
    ]
    for copy in last:
        copy.start()
    for copy in small:
        copy.wait_send()
    for j in range(5):
        store(j, *chunk_of(chunks - 1)).wait()

    def finish(n, carry):
        b, i = chunk_of(n)
        flow.hops_sent(b, i)

        @pl.when(n >= chunks - flow.kept)
        def _():
            flow.crossed(n, b, i)

        @pl.when(n >= chunks - kept)
        def _():
            for k in range(1, E):
                back(n, b, i, k).wait_send()

        @pl.when(i > 0)
        def _():
            up(b, i).wait()

        @pl.when(i == 0)
        def _():
            keep(b).wait()

        return carry

    lax.fori_loop(0, chunks, finish, 0)
    for copy in last:
        copy.wait()


def run_experts(E, C, rows_x, u_in, slots, gates, w_gate, w_up, w_down, cap, collective, name):
    batches, run, width = rows_x.shape
    units = w_gate.shape[1]
    total = E * cap
    kept = 3
    by_slot = jax.ShapeDtypeStruct((C, batches, E, cap, width), bf16)
    by_token = jax.ShapeDtypeStruct((C, batches, run, width), bf16)
    hidden = jax.ShapeDtypeStruct((C, batches, total, units), bf16)
    return call(
        functools.partial(experts_kernel, E, C),
        (rows_x, u_in, slots, gates, w_gate, w_up, w_down),
        (
            by_token,
            by_slot,
            by_slot,
            by_slot,
            hidden,
            hidden,
            hidden,
            jax.ShapeDtypeStruct((E, C, batches, 1, run), f32),
        ),
        [ANY, ANY, VMEM, VMEM, ANY, ANY, ANY],
        (ANY,) * 7 + (VMEM,),
        [
            pltpu.VMEM(w_gate.shape, bf16),
            pltpu.VMEM(w_up.shape, bf16),
            pltpu.VMEM(w_down.shape, bf16),
            pltpu.VMEM(gates.shape, f32),
            pltpu.VMEM((E, C, batches, 1, run), f32),
        ]
        + Flow.scratch(E, C, batches, run, width, cap, kept)
        + [
            pltpu.VMEM((C, batches, run, width), bf16),
            pltpu.VMEM((C, batches, E, cap, width), bf16),
            pltpu.VMEM((E, cap, width), bf16),
            pltpu.VMEM((E, cap, width), bf16),
            pltpu.VMEM((E, cap, width), bf16),
            pltpu.VMEM((total, units), bf16),
            pltpu.VMEM((total, units), bf16),
            pltpu.VMEM((total, units), bf16),
            pltpu.VMEM((E, cap, width), bf16),
            pltpu.VMEM((kept, E, cap, width), bf16),
            DMA((E, C)),
            DMA((E, C)),
            DMA((E, C)),
            DMA((E, C)),
            DMA((C, batches, E)),
            DMA((C, batches, E)),
            DMA((C, batches)),
            DMA((C, batches)),
            DMA((C, batches)),
            DMA((batches,)),
            DMA((2,)),
            DMA((5,)),
            DMA((3,)),
        ],
        collective,
        name,
        vmem=60,
    )


def middle_kernel(
    E,
    C,
    G,
    runs,
    parts,
    resid,
    factor,
    upstream,
    gain,
    logit_grad,
    router,
    w_output,
    mixed,
    x,
    pair,
    gate_back,
    up_back,
    act,
    y_rows,
    slots,
    resid_grad,
    gain_grad,
    heads,
    proj,
    own_gate,
    own_up,
    own_down,
    other_gate,
    other_up,
    other_down,
    out,
    attn_grad,
    stage,
    blocks,
    hidden,
    wide,
    kept,
    sent,
    swap,
    swapped,
    chip,
    plane_parts,
    level_part,
    hs,
    hr,
    hl,
    block_sem,
    cs,
    cr,
    ps,
    pr,
    zs,
    zr,
    rs,
    wide_sem,
    ks,
    xs,
    xr,
    *return_scratch,
):
    e, c, d = position()
    me, peers = column_peers(E, C, G)
    planes, levels = plane_peers(E), level_peers(C)
    batches, run = parts.shape[1:3]
    own, width = resid.shape
    size = blocks.shape[1]
    step = wide.shape[2]
    half = own_gate.shape[1]
    sibling = (e, c, 1 - d)
    meet([device for _, _, device in peers] + [device for _, _, device in planes])
    way_back = Return(E, C, runs, y_rows, slots, out, *return_scratch)
    way_back.begin()

    turns = [index for _, index, _ in peers] + [me]

    def block_copy(n):
        at = pl.ds(pl.multiple_of(turns[n] * size, size), size)
        return pltpu.make_async_copy(w_output.at[at], blocks.at[n % 2], block_sem.at[n % 2])

    block_copy(0).start()
    block_copy(1).start()
    hidden_copies = [
        pltpu.make_async_copy(source, hidden.at[j % 2], rs.at[j % 2])
        for j, source in enumerate((gate_back, up_back, act))
    ]
    hidden_copies[0].start()
    hidden_copies[1].start()
    count = width // step
    sources = [x] * count + [pair] * count

    def wide_copy(item):
        at = (item % count) * step
        return pltpu.make_async_copy(
            sources[item].at[:, pl.ds(at, step)], wide.at[item % 2], wide_sem.at[item % 2]
        )

    wide_copy(0).start()
    wide_copy(1).start()

    total = jnp.zeros((own, 1), f32)
    for at in range(0, width, 512):
        lanes = pl.ds(at, 512)
        grad = contract(logit_grad[...], router[lanes], (1, 1))
        for level in range(C):
            grad += parts[level, :, :, lanes].reshape(own, 512).astype(f32)
        hat = resid[:, lanes] * factor[...]
        gain_grad[:, lanes] = jnp.sum(grad * hat, axis=0, keepdims=True)
        grad = grad * gain[:, lanes]
        total += jnp.sum(grad * hat, axis=1, keepdims=True)
        resid_grad[:, lanes] = grad
    mean = total / width
    for at in range(0, width, 512):
        lanes = pl.ds(at, 512)
        hat = resid[:, lanes] * factor[...]
        grad = upstream[:, lanes].astype(f32) + factor[...] * (resid_grad[:, lanes] - hat * mean)
        resid_grad[:, lanes] = grad
        attn_grad[:, lanes] = grad.astype(bf16)

    head_copies = []
    for n in range(len(turns)):
        block_copy(n).wait()
        part = contract(attn_grad[...], blocks[n % 2], (1, 1))
        stage[n] = part.astype(bf16).reshape(batches, run, size)
        if n + 2 < len(turns):
            block_copy(n + 2).start()
        for b in range(batches):
            if n < len(peers):
                offset, _, device = peers[n]
                copy = remote(
                    stage.at[n, b], heads.at[b, me], hs.at[b, offset], hr.at[b, offset], device
                )
            else:
                copy = pltpu.make_async_copy(stage.at[n, b], heads.at[b, me], hl.at[b])
            copy.start()
            head_copies.append(copy)

    block = width // E

    def chip_copy(plane):
        return remote(swap.at[plane], swapped.at[plane], cs.at[plane], cr.at[plane], sibling)

    def plane_copy(i, level):
        plane = lax.rem(e + i, E)
        return remote(
            chip.at[plane, level],
            plane_parts.at[i, level],
            ps.at[i, level],
            pr.at[i, level],
            (plane, c, d),
        )

    def give(i, carry):
        plane = lax.rem(e + 1 + i, E)
        rows = pl.ds(pl.multiple_of(plane * block, block), block)
        left = mixed[:, rows]
        for at in range(0, width, 512):
            lanes = pl.ds(at, 512)
            part = contract(left, attn_grad[:, lanes], (0, 0)).astype(bf16)
            part = part.reshape(C, G, block // (C * G), 512)
            first, last = part[:, 0], part[:, G - 1]
            chip[plane, :, :, lanes] = jnp.where(d == 0, first, last)
            swap[plane, :, :, lanes] = jnp.where(d == 0, last, first)
        chip_copy(plane).start()
        return carry

    def take(i, carry):
        plane = lax.rem(e + 1 + i, E)
        chip_copy(plane).wait_recv()
        for at in range(0, width, 512):
            lanes = pl.ds(at, 512)
            part = chip[plane, :, :, lanes].astype(f32) + swapped[plane, :, :, lanes].astype(f32)
            chip[plane, :, :, lanes] = part.astype(bf16)
        return carry

    lax.fori_loop(0, E, give, 0)
    lax.fori_loop(0, E, take, 0)
    order = [lax.rem(c + i, C) for i in list(range(1, C)) + [0]]
    levels_left = iter(order)

    def level_send():
        level = next(levels_left, None)
        if level is not None:
            for i in range(1, E):
                plane_copy(i, level).start()

    level_send()

    def keep_copy(j, at, place):
        target = (own_gate, own_up, own_down)[j]
        where = target.at[:, pl.ds(at, step)] if j == 2 else target.at[pl.ds(at, step)]
        return pltpu.make_async_copy(kept.at[place], where, ks.at[place])

    def send_copy(j, at, place):
        target = (other_gate, other_up, other_down)[j]
        where = target.at[:, pl.ds(at, step)] if j == 2 else target.at[pl.ds(at, step)]
        return remote(sent.at[place % slots_sent], where, xs.at[place], xr.at[place], sibling)

    slots_sent = sent.shape[0]
    combine_at, combine_step, level_at = 0, 1, (2, 3, 4)
    kept_copies, sent_copies, after = [], [], {}
    for n in range(len(runs)):
        after.setdefault(combine_at + combine_step * n, []).append(n)
    hidden_copies[0].wait()
    hidden_copies[1].wait()
    for item in range(2 * count):
        if item == count:
            hidden_copies[2].start()
            hidden_copies[2].wait()
        wide_copy(item).wait()
        at = (item % count) * step
        left = wide[item % 2]
        for j in (0, 1) if item < count else (2,):
            place = len(sent_copies)

            def product(core):
                part = hidden[j % 2, :, pl.ds(pl.multiple_of(core * half, half), half)]
                return contract(part, left, (0, 0)) if j == 2 else contract(left, part, (0, 0))

            if place >= slots_sent:
                sent_copies[place - slots_sent].wait_send()
            sent[place % slots_sent] = product(1 - d).astype(bf16)
            copy = send_copy(j, at, place)
            copy.start()
            sent_copies.append(copy)
            if place >= 2:
                kept_copies[place - 2].wait()
            kept[place % 2] = product(d)
            copy = keep_copy(j, at, place % 2)
            copy.start()
            kept_copies.append(copy)
        if item + 2 < 2 * count:
            wide_copy(item + 2).start()
        for n in after.get(item, ()):
            way_back.combine(n)
        if item in level_at:
            level_send()
    for _ in range(C):
        level_send()

    def level_copy(i, level):
        return remote(level_part.at[level], proj.at[c], zs.at[i], zr.at[i], (e, level, d))

    for i, level in zip(list(range(1, C)) + [0], order):
        for k in range(1, E):
            plane_copy(k, level).wait_recv()
        total = chip[e, level].astype(f32)
        for k in range(1, E):
            total = total + plane_parts[k, level].astype(f32)
        level_part[level] = total.astype(bf16)
        if i > 0:
            level_copy(i, level).start()
        else:
            proj[c] = level_part[c]

    for copy in kept_copies[-2:]:
        copy.wait()
    for copy in sent_copies:
        copy.wait_recv()
    for copy in sent_copies[-slots_sent:]:
        copy.wait_send()
    for copy in head_copies:
        copy.wait()
    for i, level, _ in levels:
        level_copy(i, level).wait()
    way_back.end()
    for plane in range(E):
        chip_copy(plane).wait_send()
    for i in range(1, E):
        for level in range(C):
            plane_copy(i, level).wait_send()


def middle(
    E,
    C,
    G,
    runs,
    parts,
    resid,
    factor,
    upstream,
    gain,
    logit_grad,
    router,
    w_output,
    mixed,
    x,
    pair,
    gate_back,
    up_back,
    act,
    y_rows,
    slots,
    collective,
    name,
):
    batches, run, width = parts.shape[1:]
    own = resid.shape[0]
    count = C * G
    size = width // count
    block = width // E
    part = block // count
    total, units = act.shape
    half = units // G
    step = min(512, width)
    items = 3 * (width // step)
    tall = (width, half)
    flat = (half, width)
    by_plane = pltpu.VMEM((E, C, part, width), bf16)
    return call(
        functools.partial(middle_kernel, E, C, G, runs),
        (
            parts,
            resid,
            factor,
            upstream,
            gain,
            logit_grad,
            router,
            w_output,
            mixed,
            x,
            pair,
            gate_back,
            up_back,
            act,
            y_rows,
            slots,
        ),
        (
            jax.ShapeDtypeStruct((own, width), f32),
            jax.ShapeDtypeStruct((1, width), f32),
            jax.ShapeDtypeStruct((batches, count, run, size), bf16),
            jax.ShapeDtypeStruct((C, part, width), bf16),
            jax.ShapeDtypeStruct(tall, f32),
            jax.ShapeDtypeStruct(tall, f32),
            jax.ShapeDtypeStruct(flat, f32),
            jax.ShapeDtypeStruct(tall, bf16),
            jax.ShapeDtypeStruct(tall, bf16),
            jax.ShapeDtypeStruct(flat, bf16),
            jax.ShapeDtypeStruct((len(runs), run, width), bf16),
        ),
        [VMEM] * 7 + [ANY, VMEM] + [ANY] * 6 + [VMEM],
        (VMEM, VMEM, ANY, VMEM) + (ANY,) * 7,
        [
            pltpu.VMEM((own, width), bf16),
            pltpu.VMEM((count, batches, run, size), bf16),
            pltpu.VMEM((2, size, width), bf16),
            pltpu.VMEM((2, total, units), bf16),
            pltpu.VMEM((2, total, step), bf16),
            pltpu.VMEM((2, step, half), f32),
            pltpu.VMEM((4, step, half), bf16),
            by_plane,
            by_plane,
            by_plane,
            by_plane,
            pltpu.VMEM((C, part, width), bf16),
            DMA((batches, count)),
            DMA((batches, count)),
            DMA((batches,)),
            DMA((2,)),
            DMA((E,)),
            DMA((E,)),
            DMA((E, C)),
            DMA((E, C)),
            DMA((C,)),
            DMA((C,)),
            DMA((2,)),
            DMA((2,)),
            DMA((2,)),
            DMA((items,)),
            DMA((items,)),
        ]
        + Return.scratch(E, C, len(runs), run, width, y_rows.shape[3]),
        collective,
        name,
        vmem=62,
    )


def backward_kernel(
    E,
    C,
    G,
    runs,
    queries,
    keys,
    values,
    grads,
    row_ids,
    key_ids,
    log_total,
    query_hat,
    key_hat,
    factors,
    head_gains,
    y_rows,
    slots,
    w_qkv,
    normed,
    small,
    first,
    out_qkv,
    out_small,
    out_gains,
    out,
    raw,
    query_grad,
    key_grad,
    key_sum,
    value_sum,
    sums,
    sum_parts,
    gain_sum,
    gain_parts,
    small_parts,
    small_sum,
    swap,
    swapped,
    own,
    passed,
    tokens,
    parts,
    plane_parts,
    sum_qkv,
    cs,
    cr,
    zs,
    zr,
    ts,
    qs,
    qr,
    os,
    orr,
    ss,
    sr,
    fs,
    fr,
    ms,
    mr,
    hs,
    hr,
    gs,
    gr,
    *return_scratch,
):
    e, c, d = position()
    me, peers = column_peers(E, C, G)
    planes = plane_peers(E)
    count = C * G
    _, run, columns = raw.shape
    every, size = queries.shape
    batches, length = row_ids.shape[:2]
    scale = HEAD**-0.5
    width = w_qkv.shape[0]
    rows = batches * run
    sibling = (e, c, 1 - d)
    meet([device for _, _, device in peers] + [device for _, _, device in planes])
    half = tokens.shape[2]
    block = parts.shape[1]
    cuts = block // half

    def token_copy(part):
        at = lax.rem(e + 1 + part // cuts, E) * block + part % cuts * half
        return pltpu.make_async_copy(
            normed.at[:, pl.ds(pl.multiple_of(at, half), half)],
            tokens.at[part % 2],
            ts.at[part % 2],
        )

    token_copy(0).start()
    token_copy(1).start()
    small_copies = [
        remote(small.at[plane], small_parts.at[i], ss.at[i], sr.at[i], device)
        for i, plane, device in planes
    ]
    for copy in small_copies:
        copy.start()

    way_back = Return(E, C, runs, y_rows, slots, out, *return_scratch)
    way_back.begin()
    heads = size // HEAD

    def head_back(n, carry):
        b, h = n // heads, lax.rem(n, heads)
        lanes = pl.ds(pl.multiple_of(h * HEAD, HEAD), HEAD)
        start = pl.multiple_of(b * length, length)
        key_sum[...] = jnp.zeros_like(key_sum)
        value_sum[...] = jnp.zeros_like(value_sum)
        for at, many, seen in query_blocks(length):
            rows_here = pl.ds(pl.multiple_of(start + at, many), many)
            rows_seen = pl.ds(start, seen)
            query, grad = queries[rows_here, lanes], grads[rows_here, lanes]
            scores = contract(query, keys[rows_seen, lanes], (1, 1)) * scale
            allowed = key_ids[b, :, :seen] <= row_ids[b, at : at + many]
            scores = jnp.where(allowed, scores, MASKED)
            probs = jnp.exp(scores - log_total[b, h, at : at + many])
            prod = contract(grad, values[rows_seen, lanes], (1, 1))
            delta = jnp.sum(probs * prod, axis=1, keepdims=True)
            score_grad = (probs * (prod - delta)).astype(bf16)
            query_grad[rows_here, lanes] = (
                jnp.dot(score_grad, keys[rows_seen, lanes], preferred_element_type=f32) * scale
            )
            key_sum[:seen] += contract(score_grad, query, (0, 0)) * scale
            value_sum[:seen] += contract(probs.astype(bf16), grad, (0, 0))
        key_grad[pl.ds(start, length), lanes] = key_sum[...]
        value_lanes = pl.ds(pl.multiple_of(2 * size + h * HEAD, HEAD), HEAD)
        raw[pl.ds(b * count, count), :, value_lanes] = (
            value_sum[...].astype(bf16).reshape(count, run, HEAD)
        )
        for q in range(min(beside, len(runs))):

            @pl.when(n == batches * heads - beside + q)
            def _():
                way_back.combine(q)

        return carry

    beside = 2
    pending = iter(range(beside, len(runs)))

    def carry_on(many):
        for _ in range(many):
            n = next(pending, None)
            if n is not None:
                way_back.combine(n)

    lax.fori_loop(0, batches * heads, head_back, 0)

    chunk = min(2 * run, every)
    per_chunk = chunk // run
    ones = jnp.ones((8, size), f32)
    gain_sum[...] = jnp.zeros_like(gain_sum)
    pairs = ((query_grad, query_hat), (key_grad, key_hat))

    def dots(j, carry):
        rows_here = pl.ds(pl.multiple_of(j * chunk, chunk), chunk)
        for kind, (grad, hat) in enumerate(pairs):
            prod = grad[rows_here] * hat[rows_here]
            gain_sum[kind] += jnp.sum(prod, axis=0, keepdims=True)
            total = lax.dot_general(
                ones,
                prod * head_gains[kind : kind + 1],
                (((1,), (1,)), ((), ())),
                precision=lax.Precision.HIGHEST,
                preferred_element_type=f32,
            )
            sums[kind, :, rows_here] = total[:1]
        return carry

    lax.fori_loop(0, every // chunk, dots, 0)
    shares = [
        remote(sums, sum_parts.at[me], ms.at[offset], mr.at[offset], device)
        for offset, _, device in peers
    ]
    gain_copies = [
        remote(gain_sum, gain_parts.at[i], hs.at[i], hr.at[i], device) for i, _, device in planes
    ]
    for copy in shares + gain_copies:
        copy.start()
    sum_parts[me] = sums[...]
    carry_on(1)
    for copy in shares:
        copy.wait()
    total = sum_parts[0]
    for index in range(1, count):
        total = total + sum_parts[index]
    sums[...] = total / width
    rows_at = lax.broadcasted_iota(jnp.int32, (chunk, chunk), 0)
    same = rows_at == lax.broadcasted_iota(jnp.int32, (chunk, chunk), 1)

    def column_of(row):
        return jnp.sum(jnp.where(same, row, 0.0), axis=1, keepdims=True)

    def through_norm(j, carry):
        rows_here = pl.ds(pl.multiple_of(j * chunk, chunk), chunk)
        for kind, (grad, hat) in enumerate(pairs):
            part = grad[rows_here] * head_gains[kind : kind + 1]
            part = part - hat[rows_here] * column_of(sums[kind, :, rows_here])
            part = (column_of(factors[kind, :, rows_here]) * part).astype(bf16)
            raw[pl.ds(j * per_chunk, per_chunk), :, kind * size : (kind + 1) * size] = part.reshape(
                per_chunk, run, size
            )
        return carry

    lax.fori_loop(0, every // chunk, through_norm, 0)

    def gain_copy(offset, device):
        return remote(gain_sum, out_gains.at[me], gs.at[offset], gr.at[offset], device)

    for copy in gain_copies:
        copy.wait()
    total = gain_sum[...]
    for i in range(1, E):
        total = total + gain_parts[i]
    gain_sum[...] = total
    out_gains[me] = total
    for offset, _, device in peers:
        gain_copy(offset, device).start()

    def product(level, core, at, many):
        left = jnp.concatenate(
            [raw[b * count + level * G + core] for b in range(batches)], axis=0
        )
        return contract(left, w_qkv[at : at + many, :], (1, 1))

    def chip_copy(level):
        return remote(swap.at[level], swapped.at[level], cs.at[level], cr.at[level], sibling)

    def give(level):
        for at in range(0, width, 512):
            swap[level, :, at : at + 512] = product(level, 1 - d, at, 512).astype(bf16)
        chip_copy(level).start()

    def take(level):
        chip_copy(level).wait_recv()
        for at in range(0, width, 512):
            part = product(level, d, at, 512) + swapped[level, :, at : at + 512].astype(f32)
            own[level, :, at : at + 512] = part.astype(bf16)

    def hop(way, level, b):
        there = c + 1 if way == 0 else c - 1
        to = level if way == 0 else level + (C - level) * ((C - 1 - (there - level)) // (C - 1))
        return remote(
            own.at[level, pl.ds(b * run, run)],
            passed.at[to, pl.ds(b * run, run)],
            zs.at[way, level, b],
            zr.at[to, b],
            (e, there, d),
        )

    def arrival(entry, b):
        part = passed.at[entry, pl.ds(b * run, run)]
        return remote(part, part, zs.at[0, 0, b], zr.at[entry, b], sibling)

    def send(way, level, last):
        for b in range(batches):

            @pl.when(last)
            def _():
                arrival(level, b).wait_recv()
                piece = pl.ds(b * run, run)
                own[level, piece] = (
                    own[level, piece].astype(f32) + passed[level, piece].astype(f32)
                ).astype(bf16)

            hop(way, level, b).start()

    order = [C - 1, 0] + list(range(C - 2, 0, -1))
    for level in order:
        give(level)
    carry_on(1)

    def plane_copy(item):
        plane = lax.rem(e + 1 + item, E)
        return remote(
            parts.at[item],
            plane_parts.at[item],
            qs.at[item],
            qr.at[item],
            (plane, c, d),
        )

    def weights(item):
        for part in range(cuts * item, cuts * (item + 1)):
            token_copy(part).wait()
            for at in range(0, columns, 256):
                many = min(256, columns - at)
                piece = raw[:, :, at : at + many].reshape(every, many)
                rows_here = pl.ds(part % cuts * half, half)
                parts[item, rows_here, at : at + many] = contract(
                    tokens[part % 2], piece, (0, 0)
                ).astype(bf16)
            if part + 2 < cuts * E:
                token_copy(part + 2).start()
        if item < E - 1:
            plane_copy(item).start()

    mirror = C - 1 - c
    items = list(range(E))
    for level in order:
        take(level)
        if level == 0:
            @pl.when(c == 0)
            def _():
                send(0, C - 1, False)

            @pl.when(c == C - 1)
            def _():
                send(1, 0, False)

            weights(items.pop(0))
            carry_on(1)
    weights(items.pop(0))
    carry_on(len(runs))
    for turn in range(1, C - 1):

        @pl.when(c <= turn)
        def _():
            send(0, C - 1 - (turn - c), c > 0)

        @pl.when(mirror <= turn)
        def _():
            send(1, turn - mirror, mirror > 0)

        if items:
            weights(items.pop(0))
    while items:
        weights(items.pop(0))
    for item in range(E - 1):
        plane_copy(item).wait_recv()
    for at in range(0, block, 128):
        piece = pl.ds(at, min(128, block - at))
        total = parts[E - 1, piece].astype(f32)
        for item in range(E - 1):
            total = total + plane_parts[item, piece].astype(f32)
        sum_qkv[piece] = total.astype(bf16)
    share = block // (C * G)

    def row_copy(offset, index, device):
        return remote(
            sum_qkv.at[pl.ds(pl.multiple_of(index * share, share), share)],
            out_qkv.at[me],
            os.at[offset],
            orr.at[offset],
            device,
        )

    def small_copy(offset, index, device):
        return remote(
            small_sum.at[pl.ds(pl.multiple_of(index * share, share), share)],
            out_small.at[me],
            fs.at[offset],
            fr.at[offset],
            device,
        )

    for copy in small_copies:
        copy.wait_recv()
    total = small[e].astype(f32)
    for i in range(1, E):
        total = total + small_parts[i].astype(f32)
    small_sum[...] = total.astype(bf16)
    for offset, index, device in peers:
        small_copy(offset, index, device).start()
        row_copy(offset, index, device).start()
    out_small[me] = small_sum[pl.ds(pl.multiple_of(me * share, share), share)]
    out_qkv[me] = sum_qkv[pl.ds(pl.multiple_of(me * share, share), share)]

    def arrived(entry):
        for b in range(batches):
            arrival(entry, b).wait_recv()

    @pl.when(c > 0)
    def _():
        arrived(c)

    @pl.when(c < C - 1)
    def _():
        arrived(C)

    for at in range(0, width, 512):
        first[:, at : at + 512] = own[c, :, at : at + 512].astype(f32)

    @pl.when(c > 0)
    def _():
        for at in range(0, width, 512):
            first[:, at : at + 512] += passed[c, :, at : at + 512].astype(f32)

    @pl.when(c < C - 1)
    def _():
        for at in range(0, width, 512):
            first[:, at : at + 512] += passed[C, :, at : at + 512].astype(f32)

    for level in range(C):
        chip_copy(level).wait_send()
        for b in range(batches):

            @pl.when(level > c)
            def _():
                hop(0, level, b).wait_send()

            @pl.when(level < c)
            def _():
                hop(1, level, b).wait_send()

    for item in range(E - 1):
        plane_copy(item).wait_send()
    for copy in small_copies:
        copy.wait_send()
    for offset, _, device in peers:
        gain_copy(offset, device).wait()
    way_back.end()
    for offset, index, device in peers:
        row_copy(offset, index, device).wait()
        small_copy(offset, index, device).wait()


def run_backward(
    E,
    C,
    G,
    runs,
    queries,
    keys,
    values,
    grads,
    ids,
    log_total,
    query_hat,
    key_hat,
    factors,
    head_gains,
    y_rows,
    slots,
    w_qkv,
    normed,
    small,
    collective,
    name,
):
    every, size = queries.shape
    batches, length = ids.shape
    count = C * G
    run = length // count
    columns = 3 * size
    width = w_qkv.shape[0]
    rows = batches * run
    block = width // E
    share = block // count
    lanes = small.shape[2]
    by_level = pltpu.VMEM((C, rows, width), bf16)
    wide = pltpu.VMEM((every, size), f32)
    head = pltpu.VMEM((length, HEAD), f32)
    return call(
        functools.partial(backward_kernel, E, C, G, runs),
        (
            queries,
            keys,
            values,
            grads,
            ids[:, :, None],
            ids[:, None, :],
            log_total,
            query_hat,
            key_hat,
            factors,
            head_gains,
            y_rows,
            slots,
            w_qkv,
            normed,
            small,
        ),
        (
            jax.ShapeDtypeStruct((rows, width), f32),
            jax.ShapeDtypeStruct((count, share, columns), bf16),
            jax.ShapeDtypeStruct((count, share, lanes), bf16),
            jax.ShapeDtypeStruct((count, 2, 1, size), f32),
            jax.ShapeDtypeStruct((len(runs), run, width), bf16),
        ),
        [VMEM] * 11 + [ANY, VMEM, VMEM, ANY, VMEM],
        (VMEM, VMEM, VMEM, VMEM, ANY),
        [
            pltpu.VMEM((batches * count, run, columns), bf16),
            wide,
            wide,
            head,
            head,
            pltpu.VMEM((2, 1, every), f32),
            pltpu.VMEM((count, 2, 1, every), f32),
            pltpu.VMEM((2, 1, size), f32),
            pltpu.VMEM((E, 2, 1, size), f32),
            pltpu.VMEM((E, block, lanes), bf16),
            pltpu.VMEM((block, lanes), bf16),
            by_level,
            by_level,
            by_level,
            pltpu.VMEM((C + 1, rows, width), bf16),
            pltpu.VMEM((2, every, min(block, 256)), bf16),
            pltpu.VMEM((E, block, columns), bf16),
            pltpu.VMEM((E, block, columns), bf16),
            pltpu.VMEM((block, columns), bf16),
            DMA((C,)),
            DMA((C,)),
            DMA((2, C, batches)),
            DMA((C + 1, batches)),
            DMA((2,)),
            DMA((E,)),
            DMA((E,)),
            DMA((count,)),
            DMA((count,)),
            DMA((E,)),
            DMA((E,)),
            DMA((count,)),
            DMA((count,)),
            DMA((count,)),
            DMA((count,)),
            DMA((E,)),
            DMA((E,)),
            DMA((count,)),
            DMA((count,)),
        ]
        + Return.scratch(E, C, len(runs), run, width, y_rows.shape[3]),
        collective,
        name,
        vmem=62,
    )


def contract(left, right, axes):
    return lax.dot_general(left, right, ((axes[:1], axes[1:]), ((), ())), preferred_element_type=f32)


def query_blocks(length):
    size = min(256, length)
    return [(i, size, min(length, i + 2 * size)) for i in range(0, length, size)]


def rms_factor(values):
    return lax.rsqrt(jnp.mean(values * values, axis=-1, keepdims=True) + EPSILON)


def norm_back(grad_hat, hatted, factor):
    return factor * (grad_hat - hatted * jnp.mean(grad_hat * hatted, axis=-1, keepdims=True))


def slot_table(routes, experts):
    batches, run, top = routes.shape
    hits = jnp.swapaxes(routes, 1, 2)[:, :, :, None] == jnp.arange(experts, dtype=jnp.int32)
    ones = hits.astype(bf16)
    tokens, ranks = jnp.arange(run), jnp.arange(top)
    before = (tokens[None, :] < tokens[:, None]).astype(bf16)
    above = (ranks[None, :] < ranks[:, None]).astype(bf16)
    within = jnp.einsum("ts,bksx->bktx", before, ones, preferred_element_type=f32)
    totals = jnp.sum(hits.astype(f32), axis=2)
    earlier = jnp.einsum(
        "kj,bjx->bkx", above, totals.astype(bf16), preferred_element_type=f32
    )
    places = jnp.sum(jnp.where(hits, within + earlier[:, :, None, :], 0.0), axis=1)
    places = jnp.where(jnp.any(hits, axis=1), places, UNUSED_SLOT)
    return jnp.swapaxes(places, 1, 2)


def body(
    tokens,
    block_ids,
    routes,
    norm_gains,
    w_query,
    w_key,
    w_value,
    w_output,
    router,
    expert_gate,
    expert_up,
    expert_down,
    cotangent,
):
    E, C, G = lax.axis_size("expert"), lax.axis_size("context"), lax.axis_size("dp")
    batches, run, width = tokens.shape
    top = routes.shape[2]
    experts = E * C * expert_gate.shape[0]
    capacity = max(2, run * top // experts)
    count = C * G
    size = width // count
    length = count * run
    every = batches * length
    own = batches * run
    me = lax.axis_index("context") * G + lax.axis_index("dp")

    rows = w_query.shape[0]
    small_width = -(-(norm_gains.shape[1] + experts) // 128) * 128
    small = jnp.concatenate([norm_gains, router], axis=1)
    small = jnp.pad(small, ((0, 0), (0, small_width - small.shape[1])))
    pieces = [w.reshape(rows, count, size) for w in (w_query, w_key, w_value)]
    weights = jnp.swapaxes(jnp.concatenate(pieces, axis=2), 0, 1)
    places = slot_table(routes, experts).reshape(batches, E, C, run)
    by_level = jnp.transpose(places, (2, 0, 1, 3))
    by_expert = jnp.transpose(places, (1, 2, 0, 3))
    column, w_qkv, small, full_output, ids, slots = start(
        E, C, G, tokens, weights, small, w_output, block_ids, by_level
    )
    ids = jnp.swapaxes(ids, 0, 1).reshape(batches, length)
    w_qkv = w_qkv.reshape(width, 3 * size)
    small = small.reshape(width, small_width)
    full_output = full_output.reshape(width, width)
    gains = small[:, :4].astype(f32)
    full_router = small[:, 4 : 4 + experts]
    head_gains = lax.dynamic_slice(gains, (me * size, 0), (size, 4))

    (
        normed,
        query_low,
        key_low,
        value_low,
        query_hat,
        key_hat,
        log_total,
        factors,
        mixed_low,
        upstream_rows,
    ) = run_forward(
        E,
        C,
        G,
        column.reshape(every, width),
        jnp.swapaxes(gains[:, :1], 0, 1),
        jnp.swapaxes(head_gains[:, 1:3], 0, 1),
        w_qkv,
        ids,
        slots,
        cotangent,
        capacity,
        2,
        "forward",
    )
    mixed_low = mixed_low.reshape(own, width)

    inputs = tokens.reshape(own, width).astype(f32)
    resid = inputs + jnp.dot(mixed_low, full_output, preferred_element_type=f32)
    second_factor = rms_factor(resid)
    second_hat = resid * second_factor
    second_low = (second_hat * gains[:, 3]).astype(bf16)
    logits = jnp.dot(second_low, full_router, preferred_element_type=f32)
    router_probs = jax.nn.softmax(logits, axis=-1)
    gate_table = jnp.transpose(router_probs.reshape(batches, run, E, C), (2, 3, 0, 1))
    table = jnp.concatenate([by_expert, gate_table], axis=2)[:, :, :, None, :]

    second_grad, x, y_rows, pair_grad, act, gate_pre_grad, up_pre_grad, gate_grad = run_experts(
        E,
        C,
        second_low.reshape(batches, run, width),
        upstream_rows,
        slots,
        table,
        expert_gate[0],
        expert_up[0],
        expert_down[0],
        capacity,
        4,
        "experts",
    )
    slot_count = E * C * batches * capacity
    x, pair_grad, act, gate_pre_grad, up_pre_grad = (
        rows.reshape(slot_count, -1) for rows in (x, pair_grad, act, gate_pre_grad, up_pre_grad)
    )
    prob_grad = jnp.transpose(gate_grad[:, :, :, 0, :], (2, 3, 0, 1)).reshape(own, experts)
    logit_grad = router_probs * (
        prob_grad - jnp.sum(router_probs * prob_grad, axis=-1, keepdims=True)
    )
    logit_grad = jnp.pad(logit_grad.astype(bf16), ((0, 0), (0, small_width - experts)))
    router_wide = jnp.pad(full_router, ((0, 0), (0, small_width - experts)))

    early = [(b, i) for b in range(batches // 2) for i in list(range(1, C)) + [0]]
    late = [(b, i) for b in range(batches // 2, batches) for i in list(range(1, C)) + [0]]
    resid_grad, gain_second, mixed_grad, grad_proj, *expert_grads, early_mixture = middle(
        E,
        C,
        G,
        early,
        second_grad,
        resid,
        second_factor,
        cotangent.reshape(own, width),
        jnp.swapaxes(gains[:, 3:4], 0, 1),
        logit_grad,
        router_wide,
        full_output,
        mixed_low,
        x,
        pair_grad,
        gate_pre_grad,
        up_pre_grad,
        act,
        y_rows,
        slots,
        6,
        "middle",
    )
    grad_gate, grad_up, grad_down = (
        (mine + other.astype(f32))[None] for mine, other in zip(expert_grads[:3], expert_grads[3:])
    )
    grad_proj = jnp.sum(grad_proj.astype(f32), axis=0)
    sums = contract(second_low, logit_grad, (0, 0))
    sums = jnp.where(jnp.arange(small_width) == experts, gain_second.reshape(width, 1), sums)
    sums = sums.astype(bf16)
    first_grad, grad_qkv, sums, gain_heads, late_mixture = run_backward(
        E,
        C,
        G,
        late,
        query_low,
        key_low,
        value_low,
        mixed_grad.reshape(every, size),
        ids,
        log_total,
        query_hat,
        key_hat,
        factors,
        jnp.swapaxes(head_gains[:, 1:3], 0, 1),
        y_rows,
        slots,
        w_qkv,
        normed,
        sums.reshape(E, width // E, small_width),
        8,
        "backward",
    )
    gain_heads = jnp.swapaxes(gain_heads[:, :, 0], 0, 1).reshape(2, width)
    first_row = (lax.axis_index("expert") * count + me) * rows
    gain_heads = lax.dynamic_slice(gain_heads, (0, first_row), (2, rows))
    mixture = [0.0] * batches
    for runs, parts in ((early, early_mixture), (late, late_mixture)):
        for n, (b, _) in enumerate(runs):
            mixture[b] = mixture[b] + parts[n].astype(f32)
    mixture = jnp.stack(mixture)
    activations = (resid.reshape(tokens.shape) + mixture).astype(bf16)
    sums = jnp.sum(sums.astype(f32), axis=0)
    first_factor = rms_factor(inputs)
    first_hat = inputs * first_factor
    input_grad = resid_grad + norm_back(first_grad * gains[:, 0], first_hat, first_factor)

    grad_qkv = jnp.swapaxes(grad_qkv.astype(f32), 0, 1)
    grad_query, grad_key, grad_value = (
        grad_qkv[:, :, i * size : (i + 1) * size].reshape(rows, width) for i in range(3)
    )
    gain_first = sum(
        jnp.sum(w.astype(f32) * grad, axis=1)
        for w, grad in ((w_query, grad_query), (w_key, grad_key), (w_value, grad_value))
    )
    gain_first = gain_first / norm_gains[:, 0].astype(f32)
    grad_gains = jnp.stack([gain_first, gain_heads[0], gain_heads[1], sums[:, experts]], axis=1)
    return (
        activations,
        input_grad.reshape(tokens.shape),
        grad_gains,
        grad_query,
        grad_key,
        grad_value,
        grad_proj,
        sums[:, :experts],
        grad_gate,
        grad_up,
        grad_down,
    )


def solution(mesh):
    by_token = ("context", "dp")
    by_expert = P(("expert", "context"), None, None)
    by_row = P(ALL_AXES, None)
    rows = P("expert", by_token, None)
    return jax.shard_map(
        body,
        mesh=mesh,
        in_specs=(
            rows,
            P("expert", by_token),
            rows,
            by_row,
            by_row,
            by_row,
            by_row,
            by_row,
            by_row,
            by_expert,
            by_expert,
            by_expert,
            rows,
        ),
        out_specs=(
            rows,
            rows,
            by_row,
            by_row,
            by_row,
            by_row,
            by_row,
            by_row,
            P(("expert", "context"), None, "dp"),
            P(("expert", "context"), None, "dp"),
            P(("expert", "context"), "dp", None),
        ),
        check_vma=False,
    )
```

```python
import functools

import jax
import jax.numpy as jnp
from jax import lax
from jax.experimental import pallas as pl
from jax.experimental.pallas import tpu as pltpu
from jax.sharding import PartitionSpec as P

HEAD = 128
EPSILON = 1e-05
MASKED = -1e30
UNUSED_SLOT = 4096.0
ALL_AXES = ("expert", "context", "dp")
MESH = pl.DeviceIdType.MESH
ANY = pl.BlockSpec(memory_space=pl.ANY)
VMEM = pl.BlockSpec(memory_space=pltpu.VMEM)
DMA = pltpu.SemaphoreType.DMA
MIB = 1 << 20
f32 = jnp.float32
bf16 = jnp.bfloat16


def call(kernel, operands, out_shapes, in_specs, out_specs, scratch, collective, name, vmem=32):
    return pl.pallas_call(
        kernel,
        out_shape=out_shapes,
        in_specs=in_specs,
        out_specs=out_specs,
        scratch_shapes=scratch,
        compiler_params=pltpu.CompilerParams(
            collective_id=collective, has_side_effects=True, vmem_limit_bytes=vmem * MIB
        ),
        name=name,
    )(*operands)


def position():
    return lax.axis_index("expert"), lax.axis_index("context"), lax.axis_index("dp")


def meet(devices):
    barrier = pltpu.get_barrier_semaphore()
    for device in devices:
        pl.semaphore_signal(barrier, inc=1, device_id=device, device_id_type=MESH)
    pl.semaphore_wait(barrier, len(devices))


def remote(source, target, send_sem, recv_sem, device):
    return pltpu.make_async_remote_copy(
        src_ref=source,
        dst_ref=target,
        send_sem=send_sem,
        recv_sem=recv_sem,
        device_id=device,
        device_id_type=MESH,
    )


def column_peers(E, C, G):
    e, c, d = position()
    me = c * G + d
    peers = []
    for offset in range(1, C * G):
        index = lax.rem(me + offset, C * G)
        peers.append((offset, index, (e, index // G, lax.rem(index, G))))
    return me, peers


def plane_peers(E):
    e, c, d = position()
    return [(i, lax.rem(e + i, E), (lax.rem(e + i, E), c, d)) for i in range(1, E)]


def level_peers(C):
    e, c, d = position()
    return [(i, lax.rem(c + i, C), (e, lax.rem(c + i, C), d)) for i in range(1, C)]


def start_kernel(
    E,
    C,
    G,
    tokens,
    weights,
    small_weights,
    output,
    ids,
    slots,
    column,
    gathered,
    small_gathered,
    full_output,
    ids_out,
    slots_out,
    ws,
    wr,
    bs,
    br,
    hs,
    hr,
    ts,
    tr,
    ls,
    ms,
    mr,
    ps,
    pr,
    fs,
    fr,
    gs,
    gr,
):
    e, c, d = position()
    me, peers = column_peers(E, C, G)
    planes = plane_peers(E)
    batches = tokens.shape[0]
    sibling = (e, c, 1 - d)
    meet([device for _, _, device in peers] + [device for _, _, device in planes])
    kinds = ((weights, gathered), (small_weights, small_gathered))
    weight_copies = []
    for j, (source, target) in enumerate(kinds):
        for offset, index, device in peers:
            part = source.at[index] if j == 0 else source
            weight_copies.append(
                remote(part, target.at[e, me], ws.at[j, offset], wr.at[j, offset], device)
            )
    for copy in weight_copies:
        copy.start()
    local = [
        pltpu.make_async_copy(weights.at[me], gathered.at[e, me], ls.at[0]),
        pltpu.make_async_copy(small_weights, small_gathered.at[e, me], ls.at[1]),
        pltpu.make_async_copy(output, full_output.at[e, c, d], ls.at[2]),
    ]
    for b in range(batches):
        local.append(pltpu.make_async_copy(tokens.at[b], column.at[b, me], ls.at[3 + b]))
    for copy in local:
        copy.start()

    def source_of(item):
        return output if item == 0 else tokens.at[item - 1]

    def place(item, level):
        return full_output.at[e, level, d] if item == 0 else column.at[item - 1, level * G + d]

    def to_sibling(source, item, level, arrival):
        return remote(
            source, place(item, level), ts.at[item, arrival], tr.at[item, arrival], sibling
        )

    def step(hop, source, item, level, up):
        to = (e, c + 1, d) if up else (e, c - 1, d)
        way = 0 if up else 1
        return remote(
            source, place(item, level), hs.at[way, item, hop], hr.at[way, item, hop], to
        )

    def relay(item, hop):
        for up in (True, False):
            level = c - hop if up else c + hop
            here = (c >= hop) if up else (c + hop < C)
            onward = (c < C - 1) if up else (c > 0)

            @pl.when(here)
            def _():
                landed = place(item, level)
                step(hop - 1, landed, item, level, up).wait_recv()
                if hop < C - 1:

                    @pl.when(onward)
                    def _():
                        step(hop, landed, item, level, up).start()

                if item == 0:
                    for i, _, device in planes:
                        output_copy(i, level, device).start()
                if G > 1:
                    to_sibling(landed, item, level, hop if up else C - 1 + hop).start()

    def output_copy(i, level, device):
        mine = full_output.at[e, level, d]
        return remote(mine, mine, fs.at[i, level], fr.at[i, level], device)

    def output_sibling(i, level):
        part = full_output.at[lax.rem(e + E - i, E), level, d]
        return remote(part, part, gs.at[i, level], gr.at[i, level], sibling)

    for item in range(batches + 1):

        @pl.when(c < C - 1)
        def _():
            step(0, source_of(item), item, c, True).start()

        @pl.when(c > 0)
        def _():
            step(0, source_of(item), item, c, False).start()

        if G > 1:
            to_sibling(source_of(item), item, c, 0).start()
    small = []
    for offset, _, device in peers:
        small.append(remote(ids, ids_out.at[me], ms.at[offset], mr.at[offset], device))
    for i, level, device in level_peers(C):
        small.append(remote(slots.at[level], slots_out.at[i], ps.at[i], pr.at[i], device))
    for copy in small:
        copy.start()
    ids_out[me] = ids[...]
    slots_out[0] = slots[c]
    for copy in weight_copies:
        copy.wait_recv()
    for copy in local[:3]:
        copy.wait()
    plane_copies = []
    for j, (_, target) in enumerate(kinds):
        for i, _, device in planes:
            copy = remote(target.at[e], target.at[e], bs.at[j, i], br.at[j, i], device)
            copy.start()
            plane_copies.append(copy)
    for i, _, device in planes:
        output_copy(i, c, device).start()
    for hop in range(1, C):
        for item in range(batches + 1):
            relay(item, hop)
    for level in range(C):
        for i, _, device in planes:
            output_copy(i, level, device).wait_recv()
            if G > 1:
                output_sibling(i, level).start()

    for item in range(batches + 1):
        if G > 1:
            to_sibling(source_of(item), item, c, 0).wait()
        for hop in range(C - 1):
            for up in (True, False):
                arrival = hop + 1 if up else C + hop
                origin = c - hop if up else c + hop
                if up:
                    sends = jnp.logical_and(origin >= 0, c < C - 1)
                    arrives = c >= hop + 1
                else:
                    sends = jnp.logical_and(origin < C, c > 0)
                    arrives = c + hop + 1 < C

                @pl.when(sends)
                def _():
                    step(hop, source_of(item), item, c, up).wait_send()

                if G > 1:

                    @pl.when(arrives)
                    def _():
                        to_sibling(source_of(item), item, c, arrival).wait()

    for level in range(C):
        for i, _, device in planes:
            output_copy(i, level, device).wait_send()
            if G > 1:
                output_sibling(i, level).wait()
    for copy in weight_copies:
        copy.wait_send()
    for copy in plane_copies + small + local[3:]:
        copy.wait()


def start(E, C, G, tokens, weights, small_weights, output, ids, slots):
    batches, run, width = tokens.shape
    count = C * G
    rows, columns = weights.shape[1:]
    items = batches + 1
    return call(
        functools.partial(start_kernel, E, C, G),
        (tokens, weights, small_weights, output, ids, slots),
        (
            jax.ShapeDtypeStruct((batches, count, run, width), tokens.dtype),
            jax.ShapeDtypeStruct((E, count, rows, columns), weights.dtype),
            jax.ShapeDtypeStruct((E, count) + small_weights.shape, weights.dtype),
            jax.ShapeDtypeStruct((E, C, G, rows, width), weights.dtype),
            jax.ShapeDtypeStruct((count,) + ids.shape, ids.dtype),
            jax.ShapeDtypeStruct(slots.shape, slots.dtype),
        ),
        [ANY, ANY, ANY, ANY, VMEM, VMEM],
        (ANY, ANY, ANY, ANY, VMEM, VMEM),
        [
            DMA((2, count)),
            DMA((2, count)),
            DMA((2, E)),
            DMA((2, E)),
            DMA((2, items, C)),
            DMA((2, items, C)),
            DMA((items, 2 * C)),
            DMA((items, 2 * C)),
            DMA((items + 2,)),
            DMA((count,)),
            DMA((count,)),
            DMA((C,)),
            DMA((C,)),
            DMA((E, C)),
            DMA((E, C)),
            DMA((E, C)),
            DMA((E, C)),
        ],
        1,
        "start",
        vmem=62,
    )


def choose(slots, count):
    cells = lax.broadcasted_iota(jnp.int32, (count, slots.shape[1]), 0).astype(f32)
    return jnp.concatenate(
        [(cells == slots[i : i + 1, :]).astype(bf16) for i in range(slots.shape[0])], axis=0
    )


class Flow:
    def __init__(self, E, C, rows, slots, landed, packed, target, own, zs, zr, xs, xr, stay):
        self.E, self.C, self.rows, self.slots = E, C, rows, slots
        self.landed, self.packed, self.target = landed, packed, target
        self.sems = own, zs, zr, xs, xr, stay
        self.e, self.c, self.d = position()
        self.batches = rows.shape[0]
        self.cap, self.width = target.shape[3:]
        self.kept = packed.shape[0]
        self.chunks = self.batches * C

    def level_entry(self, far):
        high = 2 * self.c // self.C
        return high * far + (1 - high) * lax.rem(self.C - far, self.C)

    def own(self, b):
        return pltpu.make_async_copy(self.rows.at[b], self.landed.at[0, b], self.sems[0].at[b])

    def hop(self, b, i, way):
        there = i + 1 if way == 0 else lax.rem(i + self.C - 1, self.C)
        level = lax.rem(self.c + (1 if way == 0 else self.C - 1), self.C)
        return remote(
            self.landed.at[i, b],
            self.landed.at[there, b],
            self.sems[1].at[way, i, b],
            self.sems[2].at[there, b],
            (self.e, level, self.d),
        )

    def arrival(self, b, i):
        entry = self.landed.at[i, b]
        return remote(
            entry,
            entry,
            self.sems[1].at[0, i, b],
            self.sems[2].at[i, b],
            (self.e, self.c, 1 - self.d),
        )

    def onward(self, i, way):
        if way == 0:
            return jnp.logical_and(i <= self.c, self.c < self.C - 1)
        return jnp.logical_and(lax.rem(self.C - i, self.C) + self.c < self.C, self.c > 0)

    def pass_on(self, far, b):
        for way in range(2):
            i = far if way == 0 else lax.rem(self.C - far, self.C)
            here = (far <= self.c) if way == 0 else (far + self.c < self.C)

            @pl.when(jnp.logical_and(here, self.onward(i, way)))
            def _():
                self.hop(b, i, way).start()

    def begin(self, count):
        for b in range(self.batches):
            self.own(b).start()
        for b in range(self.batches):
            self.own(b).wait()
        for b in range(count):
            self.pass_on(0, b)

    def receive(self, far, b):
        for way in range(2):
            i = far if way == 0 else self.C - far

            @pl.when((far <= self.c) if way == 0 else (far + self.c < self.C))
            def _():
                self.arrival(b, i).wait_recv()

    def hops_sent(self, b, i):
        for way in range(2):

            @pl.when(self.onward(i, way))
            def _():
                self.hop(b, i, way).wait_send()

    def across(self, n, b, i, k):
        plane = lax.rem(self.e + k, self.E)
        return remote(
            self.packed.at[lax.rem(n, self.kept), plane],
            self.target.at[i, b, k],
            self.sems[3].at[i, b, k],
            self.sems[4].at[i, b, k],
            (plane, self.c, self.d),
        )

    def stay(self, n, b, i):
        return pltpu.make_async_copy(
            self.packed.at[lax.rem(n, self.kept), self.e],
            self.target.at[i, b, 0],
            self.sems[5].at[i, b],
        )

    def compact(self, n, b, i):
        place = lax.rem(n, self.kept)
        picks = choose(self.slots[i, b], self.cap)
        for at in range(0, self.width, 512):
            part = jnp.dot(
                picks, self.landed[i, b, :, at : at + 512], preferred_element_type=f32
            ).astype(bf16)
            self.packed[place, :, :, at : at + 512] = part.reshape(self.E, self.cap, 512)
        for k in range(1, self.E):
            self.across(n, b, i, k).start()
        self.stay(n, b, i).start()

    def crossed(self, n, b, i):
        for k in range(1, self.E):
            self.across(n, b, i, k).wait_send()

    def arrived(self, n, b, i):
        for k in range(1, self.E):
            self.across(n, b, i, k).wait_recv()

    @staticmethod
    def scratch(E, C, batches, run, width, cap, kept):
        return [
            pltpu.VMEM((C, batches, run, width), bf16),
            pltpu.VMEM((kept, E, cap, width), bf16),
            DMA((batches,)),
            DMA((2, C, batches)),
            DMA((C, batches)),
            DMA((C, batches, E)),
            DMA((C, batches, E)),
            DMA((C, batches)),
        ]


class Return:
    def __init__(self, E, C, runs, rows, slots, out, returned, sums, ys, yr, bs, us, ur, ks):
        self.E, self.C, self.runs = E, C, runs
        self.rows, self.slots, self.out = rows, slots, out
        self.returned, self.sums = returned, sums
        self.sems = ys, yr, bs, us, ur, ks
        self.e, self.c, self.d = position()

    def back(self, n, k):
        b, i = self.runs[n]
        return remote(
            self.rows.at[i, b, k],
            self.returned.at[n, self.e],
            self.sems[0].at[n, k],
            self.sems[1].at[n, k],
            (lax.rem(self.e + self.E - k, self.E), self.c, self.d),
        )

    def own(self, n):
        b, i = self.runs[n]
        return pltpu.make_async_copy(
            self.rows.at[i, b, 0], self.returned.at[n, self.e], self.sems[2].at[n]
        )

    def along(self, n):
        i = self.runs[n][1]
        if i == 0:
            return pltpu.make_async_copy(self.sums.at[n], self.out.at[n], self.sems[5].at[n])
        to = (self.e, lax.rem(self.c + self.C - i, self.C), self.d)
        return remote(
            self.sums.at[n], self.out.at[n], self.sems[3].at[n], self.sems[4].at[n], to
        )

    def send(self, n):
        if n < len(self.runs):
            for k in range(1, self.E):
                self.back(n, k).start()
            self.own(n).start()

    def combine(self, n):
        b, i = self.runs[n]
        for k in range(1, self.E):
            self.back(n, k).wait_recv()
        self.own(n).wait()
        self.send(n + 2)
        cap, width = self.rows.shape[3:]
        picks = choose(self.slots[i, b], cap)
        for at in range(0, width, 512):
            part = self.returned[n, :, :, at : at + 512].reshape(self.E * cap, 512)
            self.sums[n, :, at : at + 512] = contract(picks, part, (0, 0)).astype(bf16)
        self.along(n).start()

    def end(self):
        for n in range(len(self.runs)):
            for k in range(1, self.E):
                self.back(n, k).wait_send()
            self.along(n).wait()

    @staticmethod
    def scratch(E, C, count, run, width, cap):
        return [
            pltpu.VMEM((count, E, cap, width), bf16),
            pltpu.VMEM((count, run, width), bf16),
            DMA((count, E)),
            DMA((count, E)),
            DMA((count,)),
            DMA((count,)),
            DMA((count,)),
            DMA((count,)),
        ]


def forward_kernel(
    E,
    C,
    G,
    column,
    gain,
    head_gains,
    w_qkv,
    row_ids,
    key_ids,
    slots,
    upstream,
    normed,
    queries_out,
    keys_out,
    values_out,
    query_hat_out,
    key_hat_out,
    log_total,
    factors,
    mixed,
    u_out,
    queries,
    keys,
    values,
    query_hat,
    key_hat,
    raw,
    low,
    squares,
    parts,
    heads,
    landed,
    packed,
    own,
    zs,
    zr,
    xs,
    xr,
    stay,
    raw_sem,
    low_sem,
    ss,
    sr,
    ms,
    mr,
    ml,
    out_sem,
):
    me, peers = column_peers(E, C, G)
    planes = plane_peers(E)
    every, width = column.shape
    batches, length, size = heads.shape
    run = length // (C * G)
    block = raw.shape[1]
    blocks = every // block
    scale = HEAD**-0.5
    meet([device for _, _, device in peers] + [device for _, _, device in planes])
    flow = Flow(E, C, upstream, slots, landed, packed, u_out, own, zs, zr, xs, xr, stay)

    def load(j):
        at = pl.multiple_of(j * block, block)
        place = lax.rem(j, 2)
        return pltpu.make_async_copy(column.at[pl.ds(at, block)], raw.at[place], raw_sem.at[place])

    def store(j):
        at = pl.multiple_of(j * block, block)
        place = lax.rem(j, 2)
        return pltpu.make_async_copy(low.at[place], normed.at[pl.ds(at, block)], low_sem.at[place])

    def chunk_of(n):
        return n % batches, flow.level_entry(n // batches)

    chunk = iter(range(flow.chunks))

    def carry_on(count):
        for _ in range(count):
            n = next(chunk, None)
            if n is None:
                return
            if n >= flow.kept:
                before = n - flow.kept, *chunk_of(n - flow.kept)
                flow.crossed(*before)
                flow.stay(*before).wait()
            if n >= batches:
                flow.receive(n // batches, n % batches)
                flow.pass_on(n // batches, n % batches)
            flow.compact(n, *chunk_of(n))

    load(0).start()
    load(1).start()
    flow.begin(batches)
    carry_on(batches)
    ones = jnp.ones((8, size), f32)

    def project(j, carry):
        place = lax.rem(j, 2)
        rows = pl.ds(pl.multiple_of(j * block, block), block)
        load(j).wait()

        @pl.when(j >= 2)
        def _():
            store(j - 2).wait()

        total = jnp.zeros((block, 1), f32)
        for at in range(0, width, 512):
            part = raw[place, :, at : at + 512].astype(f32)
            total += jnp.sum(part * part, axis=1, keepdims=True)
        factor = lax.rsqrt(total / width + EPSILON)
        for at in range(0, width, 512):
            part = raw[place, :, at : at + 512].astype(f32) * factor
            low[place, :, at : at + 512] = (part * gain[:, at : at + 512]).astype(bf16)
        store(j).start()

        @pl.when(j + 2 < blocks)
        def _():
            load(j + 2).start()

        for kind in range(3):
            part = jnp.dot(
                low[place],
                w_qkv[:, kind * size : (kind + 1) * size],
                preferred_element_type=f32,
            )
            if kind == 2:
                values[rows] = part.astype(bf16)
            else:
                (query_hat, key_hat)[kind][rows] = part
                sums = lax.dot_general(
                    ones,
                    part * part,
                    (((1,), (1,)), ((), ())),
                    precision=lax.Precision.HIGHEST,
                    preferred_element_type=f32,
                )
                squares[kind, :, rows] = sums[:1]
        return carry

    half = blocks // 2
    lax.fori_loop(0, half, project, 0)
    carry_on(1)
    lax.fori_loop(half, blocks, project, 0)
    shares = [
        remote(squares, parts.at[me], ss.at[offset], sr.at[offset], device)
        for offset, _, device in peers
    ]
    for copy in shares:
        copy.start()
    parts[me] = squares[...]
    carry_on(1)
    for copy in shares:
        copy.wait_recv()
    total = parts[0]
    for index in range(1, C * G):
        total = total + parts[index]
    factors[...] = lax.rsqrt(total / width + EPSILON)
    rows_at = lax.broadcasted_iota(jnp.int32, (block, block), 0)
    same = rows_at == lax.broadcasted_iota(jnp.int32, (block, block), 1)

    def scaled(j, carry):
        rows = pl.ds(pl.multiple_of(j * block, block), block)
        for kind, (hat, out) in enumerate(((query_hat, queries), (key_hat, keys))):
            factor = jnp.sum(jnp.where(same, factors[kind, :, rows], 0.0), axis=1, keepdims=True)
            part = hat[rows] * factor
            hat[rows] = part
            out[rows] = (part * head_gains[kind : kind + 1]).astype(bf16)
        return carry

    lax.fori_loop(0, blocks, scaled, 0)
    out_copies = [
        pltpu.make_async_copy(source, target, out_sem.at[j])
        for j, (source, target) in enumerate(
            (
                (queries, queries_out),
                (keys, keys_out),
                (values, values_out),
                (query_hat, query_hat_out),
                (key_hat, key_hat_out),
            )
        )
    ]
    for copy in out_copies:
        copy.start()
    carry_on(1)

    def mixed_copy(b, offset, index, device):
        where = pl.ds(pl.multiple_of(me * size, size), size)
        part = heads.at[b, pl.ds(pl.multiple_of(index * run, run), run)]
        return remote(part, mixed.at[b, :, where], ms.at[b, offset], mr.at[b, offset], device)

    def mixed_own(b):
        where = pl.ds(pl.multiple_of(me * size, size), size)
        part = heads.at[b, pl.ds(pl.multiple_of(me * run, run), run)]
        return pltpu.make_async_copy(part, mixed.at[b, :, where], ml.at[b])

    for b in range(batches):

        def head(h, carry, b=b):
            lanes = pl.ds(pl.multiple_of(h * HEAD, HEAD), HEAD)
            for first, count, seen in query_blocks(length):
                rows = pl.ds(b * length + first, count)
                seen_rows = pl.ds(b * length, seen)
                scores = contract(queries[rows, lanes], keys[seen_rows, lanes], (1, 1)) * scale
                allowed = key_ids[b, :, :seen] <= row_ids[b, first : first + count]
                scores = jnp.where(allowed, scores, MASKED)
                peak = jnp.max(scores, axis=1, keepdims=True)
                grown = jnp.exp(scores - peak)
                total = jnp.sum(grown, axis=1, keepdims=True)
                probs = (grown * (1.0 / total)).astype(bf16)
                heads[b, first : first + count, lanes] = jnp.dot(
                    probs, values[seen_rows, lanes], preferred_element_type=f32
                ).astype(bf16)
                log_total[b, h, first : first + count] = peak + jnp.log(total)
            return carry

        lax.fori_loop(0, size // HEAD, head, 0)
        for offset, index, device in peers:
            mixed_copy(b, offset, index, device).start()
        mixed_own(b).start()
        carry_on(1)
    carry_on(flow.chunks)

    for copy in out_copies:
        copy.wait()
    for copy in shares:
        copy.wait_send()
    for j in (blocks - 2, blocks - 1):
        store(j).wait()
    for b in range(batches):
        for offset, index, device in peers:
            mixed_copy(b, offset, index, device).wait()
        mixed_own(b).wait()

    for n in range(flow.chunks):
        b, i = chunk_of(n)
        flow.hops_sent(b, i)
        flow.arrived(n, b, i)
        if n >= flow.chunks - flow.kept:
            flow.crossed(n, b, i)
            flow.stay(n, b, i).wait()


def run_forward(E, C, G, column, gain, head_gains, w_qkv, ids, slots, upstream, cap, collective, name):
    every, width = column.shape
    batches, run = upstream.shape[:2]
    count = C * G
    length = count * run
    size = width // count
    block = min(256, every)
    low = jax.ShapeDtypeStruct((every, size), bf16)
    wide = jax.ShapeDtypeStruct((every, size), f32)
    return call(
        functools.partial(forward_kernel, E, C, G),
        (column, gain, head_gains, w_qkv, ids[:, :, None], ids[:, None, :], slots, upstream),
        (
            jax.ShapeDtypeStruct((every, width), bf16),
            low,
            low,
            low,
            wide,
            wide,
            jax.ShapeDtypeStruct((batches, size // HEAD, length, 1), f32),
            jax.ShapeDtypeStruct((2, 1, every), f32),
            jax.ShapeDtypeStruct(upstream.shape, bf16),
            jax.ShapeDtypeStruct((C, batches, E, cap, width), bf16),
        ),
        [ANY] + [VMEM] * 6 + [ANY],
        (ANY,) * 6 + (VMEM,) * 2 + (ANY, ANY),
        [
            pltpu.VMEM(low.shape, bf16),
            pltpu.VMEM(low.shape, bf16),
            pltpu.VMEM(low.shape, bf16),
            pltpu.VMEM(wide.shape, f32),
            pltpu.VMEM(wide.shape, f32),
            pltpu.VMEM((2, block, width), bf16),
            pltpu.VMEM((2, block, width), bf16),
            pltpu.VMEM((2, 1, every), f32),
            pltpu.VMEM((count, 2, 1, every), f32),
            pltpu.VMEM((batches, length, size), bf16),
        ]
        + Flow.scratch(E, C, batches, run, width, cap, 3)
        + [
            DMA((2,)),
            DMA((2,)),
            DMA((count,)),
            DMA((count,)),
            DMA((batches, count)),
            DMA((batches, count)),
            DMA((batches,)),
            DMA((5,)),
        ],
        collective,
        name,
        vmem=46,
    )


def experts_kernel(
    E,
    C,
    rows_x,
    u_in,
    slots,
    gates,
    gate_in,
    up_in,
    down_in,
    out,
    x_out,
    y_out,
    pair_out,
    act_out,
    gate_back_out,
    up_back_out,
    scalars_out,
    w_gate,
    w_up,
    w_down,
    table,
    scalars,
    landed,
    packed,
    own,
    zs,
    zr,
    xs,
    xr,
    stay,
    sums,
    returned,
    x,
    u,
    pair,
    act,
    gate_back,
    up_back,
    gated,
    sent,
    gs,
    gr,
    ss,
    sr,
    ys,
    yr,
    bs,
    us,
    ur,
    ks,
    loads,
    stores,
    weight_sem,
):
    e, c, d = position()
    batches, run, width = rows_x.shape
    cap = x_out.shape[3]
    units = w_gate.shape[1]
    chunks = batches * C
    total = E * cap
    kept = sent.shape[0]
    lead, lag = 1, 2
    everyone = [(k, i) for k in range(E) for i in range(C) if k + i > 0]
    ahead = [(k, i, (lax.rem(e + k, E), lax.rem(c + i, C), d)) for k, i in everyone]
    behind = [(k, i, (lax.rem(e + E - k, E), lax.rem(c + C - i, C), d)) for k, i in everyone]
    meet([device for _, _, device in ahead])
    flow = Flow(E, C, rows_x, slots, landed, packed, x_out, own, zs, zr, xs, xr, stay)

    def far_of(n):
        return lax.rem((n + batches - 1) // batches, C), lax.rem(n + batches - 1, batches)

    def chunk_of(n):
        far, b = far_of(n)
        return b, flow.level_entry(far)

    def back(n, b, i, k):
        return remote(
            sent.at[lax.rem(n, kept), k],
            returned.at[i, b, e],
            ys.at[i, b, k],
            yr.at[i, b, k],
            (lax.rem(e + E - k, E), c, d),
        )

    def back_own(n, b, i):
        return pltpu.make_async_copy(
            sent.at[lax.rem(n, kept), 0], returned.at[i, b, e], bs.at[i, b]
        )

    def up(b, i):
        return remote(
            sums.at[i, b],
            out.at[c, b],
            us.at[i, b],
            ur.at[i, b],
            (e, lax.rem(c + C - i, C), d),
        )

    def keep(b):
        return pltpu.make_async_copy(sums.at[0, b], out.at[c, b], ks.at[b])

    def load(a, b, i):
        source, target = ((x_out, x), (u_in, u))[a]
        return pltpu.make_async_copy(source.at[i, b], target, loads.at[a])

    def store(j, b, i):
        source = (pair, act, gate_back, up_back, gated)[j]
        target = (pair_out, act_out, gate_back_out, up_back_out, y_out)[j]
        return pltpu.make_async_copy(source, target.at[i, b], stores.at[j])

    weight_copies = [
        pltpu.make_async_copy(source, target, weight_sem.at[j])
        for j, (source, target) in enumerate(
            ((gate_in, w_gate), (up_in, w_up), (down_in, w_down))
        )
    ]
    for copy in weight_copies:
        copy.start()

    flow.begin(1)
    small = [
        remote(gates.at[device[0], device[1]], table.at[k, i], gs.at[k, i], gr.at[k, i], device)
        for k, i, device in ahead
    ]
    for copy in small:
        copy.start()
    table[0, 0] = gates[e, c]

    def compact(n):
        @pl.when(n >= flow.kept)
        def _():
            flow.crossed(n - flow.kept, *chunk_of(n - flow.kept))

        flow.compact(n, *chunk_of(n))

    def expert(n):
        b, i = chunk_of(n)
        load(1, b, i).start()
        flow.arrived(n, b, i)
        flow.stay(n, b, i).wait()
        load(0, b, i).start()

        @pl.when(n == 0)
        def _():
            for copy in weight_copies:
                copy.wait()

        @pl.when(n > 0)
        def _():
            before = chunk_of(n - 1)
            for j in range(5):
                store(j, *before).wait()

        @pl.when(n >= kept)
        def _():
            before = chunk_of(n - kept)
            for k in range(1, E):
                back(n - kept, *before, k).wait_send()

        holds, gate = [], []
        cells = lax.broadcasted_iota(jnp.int32, (cap, run), 0).astype(f32)
        for k in range(E):
            hold = cells == table[k, i, b]
            holds.append(hold)
            gate.append(
                jnp.sum(jnp.where(hold, table[k, i, batches + b], 0.0), axis=1, keepdims=True)
            )
        gate = jnp.concatenate(gate, axis=0)
        for a in range(2):
            load(a, b, i).wait()
        for at in range(0, width, 512):
            part = u[:, :, at : at + 512].reshape(total, 512).astype(f32)
            pair[:, :, at : at + 512] = (gate * part).astype(bf16).reshape(E, cap, 512)
        store(0, b, i).start()
        inputs = x[...].reshape(total, width)
        grads = pair[...].reshape(total, width)
        for at in range(0, units, 256):
            gate_pre = jnp.dot(inputs, w_gate[:, at : at + 256], preferred_element_type=f32)
            up_pre = jnp.dot(inputs, w_up[:, at : at + 256], preferred_element_type=f32)
            act_grad = contract(grads, w_down[at : at + 256, :], (1, 1))
            sigmoid = jax.nn.sigmoid(gate_pre)
            silu = gate_pre * sigmoid
            act[:, at : at + 256] = (silu * up_pre).astype(bf16)
            gate_back[:, at : at + 256] = (
                act_grad * up_pre * sigmoid * (1.0 + gate_pre * (1.0 - sigmoid))
            ).astype(bf16)
            up_back[:, at : at + 256] = (act_grad * silu).astype(bf16)
        for j in range(1, 4):
            store(j, b, i).start()
        place = lax.rem(n, kept)
        gate_grad = jnp.zeros((total, 1), f32)
        for at in range(0, width, 512):
            out = jnp.dot(act[...], w_down[:, at : at + 512], preferred_element_type=f32)
            out = out.astype(bf16).astype(f32)
            gate_grad += jnp.sum(
                out * u[:, :, at : at + 512].reshape(total, 512).astype(f32), axis=1, keepdims=True
            )
            gated[:, :, at : at + 512] = (gate * out).astype(bf16).reshape(E, cap, 512)
            back_rows = contract(gate_back[...], w_gate[at : at + 512, :], (1, 1))
            back_rows += contract(up_back[...], w_up[at : at + 512, :], (1, 1))
            sent[place, :, :, at : at + 512] = back_rows.astype(bf16).reshape(E, cap, 512)
        for k in range(1, E):
            back(n, b, i, k).start()
        back_own(n, b, i).start()
        store(4, b, i).start()
        for k in range(E):
            scalars[k, i, b] = jnp.sum(
                jnp.where(holds[k], gate_grad[k * cap : (k + 1) * cap], 0.0), axis=0, keepdims=True
            )

    def combine(n):
        b, i = chunk_of(n)
        picks = choose(slots[i, b], cap)
        for k in range(1, E):
            back(n, b, i, k).wait_recv()
        back_own(n, b, i).wait()
        for at in range(0, width, 512):
            part = returned[i, b, :, :, at : at + 512].reshape(total, 512)
            sums[i, b, :, at : at + 512] = contract(picks, part, (0, 0)).astype(bf16)

        @pl.when(i > 0)
        def _():
            up(b, i).start()

        @pl.when(i == 0)
        def _():
            keep(b).start()

    def step(s, carry):
        @pl.when(jnp.logical_and(s > 0, s <= batches * (C - 1)))
        def _():
            flow.receive(*far_of(s))
            flow.pass_on(s // batches, lax.rem(s, batches))

        @pl.when(s < chunks)
        def _():
            compact(s)

        @pl.when(jnp.logical_and(s >= lead, s < chunks + lead))
        def _():
            expert(s - lead)

        @pl.when(s >= lag)
        def _():
            combine(s - lag)

        return carry

    for copy in small:
        copy.wait_recv()
    lax.fori_loop(0, chunks + lag, step, 0)
    scalars_out[e, c] = scalars[0, 0]
    last = [
        remote(scalars.at[k, i], scalars_out.at[e, c], ss.at[k, i], sr.at[k, i], device)
        for k, i, device in behind
    ]
    for copy in last:
        copy.start()
    for copy in small:
        copy.wait_send()
    for j in range(5):
        store(j, *chunk_of(chunks - 1)).wait()

    def finish(n, carry):
        b, i = chunk_of(n)
        flow.hops_sent(b, i)

        @pl.when(n >= chunks - flow.kept)
        def _():
            flow.crossed(n, b, i)

        @pl.when(n >= chunks - kept)
        def _():
            for k in range(1, E):
                back(n, b, i, k).wait_send()

        @pl.when(i > 0)
        def _():
            up(b, i).wait()

        @pl.when(i == 0)
        def _():
            keep(b).wait()

        return carry

    lax.fori_loop(0, chunks, finish, 0)
    for copy in last:
        copy.wait()


def run_experts(E, C, rows_x, u_in, slots, gates, w_gate, w_up, w_down, cap, collective, name):
    batches, run, width = rows_x.shape
    units = w_gate.shape[1]
    total = E * cap
    kept = 3
    by_slot = jax.ShapeDtypeStruct((C, batches, E, cap, width), bf16)
    by_token = jax.ShapeDtypeStruct((C, batches, run, width), bf16)
    hidden = jax.ShapeDtypeStruct((C, batches, total, units), bf16)
    return call(
        functools.partial(experts_kernel, E, C),
        (rows_x, u_in, slots, gates, w_gate, w_up, w_down),
        (
            by_token,
            by_slot,
            by_slot,
            by_slot,
            hidden,
            hidden,
            hidden,
            jax.ShapeDtypeStruct((E, C, batches, 1, run), f32),
        ),
        [ANY, ANY, VMEM, VMEM, ANY, ANY, ANY],
        (ANY,) * 7 + (VMEM,),
        [
            pltpu.VMEM(w_gate.shape, bf16),
            pltpu.VMEM(w_up.shape, bf16),
            pltpu.VMEM(w_down.shape, bf16),
            pltpu.VMEM(gates.shape, f32),
            pltpu.VMEM((E, C, batches, 1, run), f32),
        ]
        + Flow.scratch(E, C, batches, run, width, cap, kept)
        + [
            pltpu.VMEM((C, batches, run, width), bf16),
            pltpu.VMEM((C, batches, E, cap, width), bf16),
            pltpu.VMEM((E, cap, width), bf16),
            pltpu.VMEM((E, cap, width), bf16),
            pltpu.VMEM((E, cap, width), bf16),
            pltpu.VMEM((total, units), bf16),
            pltpu.VMEM((total, units), bf16),
            pltpu.VMEM((total, units), bf16),
            pltpu.VMEM((E, cap, width), bf16),
            pltpu.VMEM((kept, E, cap, width), bf16),
            DMA((E, C)),
            DMA((E, C)),
            DMA((E, C)),
            DMA((E, C)),
            DMA((C, batches, E)),
            DMA((C, batches, E)),
            DMA((C, batches)),
            DMA((C, batches)),
            DMA((C, batches)),
            DMA((batches,)),
            DMA((2,)),
            DMA((5,)),
            DMA((3,)),
        ],
        collective,
        name,
        vmem=60,
    )


def middle_kernel(
    E,
    C,
    G,
    runs,
    parts,
    resid,
    factor,
    upstream,
    gain,
    logit_grad,
    router,
    w_output,
    mixed,
    x,
    pair,
    gate_back,
    up_back,
    act,
    y_rows,
    slots,
    resid_grad,
    gain_grad,
    heads,
    proj,
    own_gate,
    own_up,
    own_down,
    other_gate,
    other_up,
    other_down,
    out,
    attn_grad,
    stage,
    blocks,
    hidden,
    wide,
    kept,
    sent,
    swap,
    swapped,
    chip,
    plane_parts,
    level_part,
    hs,
    hr,
    hl,
    block_sem,
    cs,
    cr,
    ps,
    pr,
    zs,
    zr,
    rs,
    wide_sem,
    ks,
    xs,
    xr,
    *return_scratch,
):
    e, c, d = position()
    me, peers = column_peers(E, C, G)
    planes, levels = plane_peers(E), level_peers(C)
    batches, run = parts.shape[1:3]
    own, width = resid.shape
    size = blocks.shape[1]
    step = wide.shape[2]
    half = own_gate.shape[1]
    sibling = (e, c, 1 - d)
    meet([device for _, _, device in peers] + [device for _, _, device in planes])
    way_back = Return(E, C, runs, y_rows, slots, out, *return_scratch)
    way_back.send(0)

    turns = [index for _, index, _ in peers] + [me]

    def block_copy(n):
        at = pl.ds(pl.multiple_of(turns[n] * size, size), size)
        return pltpu.make_async_copy(w_output.at[at], blocks.at[n % 2], block_sem.at[n % 2])

    block_copy(0).start()
    block_copy(1).start()
    hidden_copies = [
        pltpu.make_async_copy(source, hidden.at[j % 2], rs.at[j % 2])
        for j, source in enumerate((gate_back, up_back, act))
    ]
    hidden_copies[0].start()
    hidden_copies[1].start()
    count = width // step
    sources = [x] * count + [pair] * count

    def wide_copy(item):
        at = (item % count) * step
        return pltpu.make_async_copy(
            sources[item].at[:, pl.ds(at, step)], wide.at[item % 2], wide_sem.at[item % 2]
        )

    wide_copy(0).start()
    wide_copy(1).start()

    total = jnp.zeros((own, 1), f32)
    for at in range(0, width, 512):
        lanes = pl.ds(at, 512)
        grad = contract(logit_grad[...], router[lanes], (1, 1))
        for level in range(C):
            grad += parts[level, :, :, lanes].reshape(own, 512).astype(f32)
        hat = resid[:, lanes] * factor[...]
        gain_grad[:, lanes] = jnp.sum(grad * hat, axis=0, keepdims=True)
        grad = grad * gain[:, lanes]
        total += jnp.sum(grad * hat, axis=1, keepdims=True)
        resid_grad[:, lanes] = grad
    mean = total / width
    for at in range(0, width, 512):
        lanes = pl.ds(at, 512)
        hat = resid[:, lanes] * factor[...]
        grad = upstream[:, lanes].astype(f32) + factor[...] * (resid_grad[:, lanes] - hat * mean)
        resid_grad[:, lanes] = grad
        attn_grad[:, lanes] = grad.astype(bf16)

    way_back.send(1)

    head_copies = []
    for n in range(len(turns)):
        block_copy(n).wait()
        part = contract(attn_grad[...], blocks[n % 2], (1, 1))
        stage[n] = part.astype(bf16).reshape(batches, run, size)
        if n + 2 < len(turns):
            block_copy(n + 2).start()
        for b in range(batches):
            if n < len(peers):
                offset, _, device = peers[n]
                copy = remote(
                    stage.at[n, b], heads.at[b, me], hs.at[b, offset], hr.at[b, offset], device
                )
            else:
                copy = pltpu.make_async_copy(stage.at[n, b], heads.at[b, me], hl.at[b])
            copy.start()
            head_copies.append(copy)

    block = width // E

    def chip_copy(plane):
        return remote(swap.at[plane], swapped.at[plane], cs.at[plane], cr.at[plane], sibling)

    def plane_copy(i, level):
        plane = lax.rem(e + i, E)
        return remote(
            chip.at[plane, level],
            plane_parts.at[i, level],
            ps.at[i, level],
            pr.at[i, level],
            (plane, c, d),
        )

    def give(i, carry):
        plane = lax.rem(e + 1 + i, E)
        rows = pl.ds(pl.multiple_of(plane * block, block), block)
        left = mixed[:, rows]
        for at in range(0, width, 512):
            lanes = pl.ds(at, 512)
            part = contract(left, attn_grad[:, lanes], (0, 0)).astype(bf16)
            part = part.reshape(C, G, block // (C * G), 512)
            first, last = part[:, 0], part[:, G - 1]
            chip[plane, :, :, lanes] = jnp.where(d == 0, first, last)
            swap[plane, :, :, lanes] = jnp.where(d == 0, last, first)
        chip_copy(plane).start()
        return carry

    def take(i, carry):
        plane = lax.rem(e + 1 + i, E)
        chip_copy(plane).wait_recv()
        for at in range(0, width, 512):
            lanes = pl.ds(at, 512)
            part = chip[plane, :, :, lanes].astype(f32) + swapped[plane, :, :, lanes].astype(f32)
            chip[plane, :, :, lanes] = part.astype(bf16)
        return carry

    lax.fori_loop(0, E, give, 0)
    lax.fori_loop(0, E, take, 0)
    order = [lax.rem(c + i, C) for i in list(range(1, C)) + [0]]
    levels_left = iter(order)

    def level_send():
        level = next(levels_left, None)
        if level is not None:
            for i in range(1, E):
                plane_copy(i, level).start()

    level_send()

    def keep_copy(j, at, place):
        target = (own_gate, own_up, own_down)[j]
        where = target.at[:, pl.ds(at, step)] if j == 2 else target.at[pl.ds(at, step)]
        return pltpu.make_async_copy(kept.at[place], where, ks.at[place])

    def send_copy(j, at, place):
        target = (other_gate, other_up, other_down)[j]
        where = target.at[:, pl.ds(at, step)] if j == 2 else target.at[pl.ds(at, step)]
        return remote(sent.at[place % slots_sent], where, xs.at[place], xr.at[place], sibling)

    slots_sent = sent.shape[0]
    combine_at, combine_step, level_at = 0, 1, (2, 3, 4)
    kept_copies, sent_copies, after = [], [], {}
    for n in range(len(runs)):
        after.setdefault(combine_at + combine_step * n, []).append(n)
    hidden_copies[0].wait()
    hidden_copies[1].wait()
    for item in range(2 * count):
        if item == count:
            hidden_copies[2].start()
            hidden_copies[2].wait()
        wide_copy(item).wait()
        at = (item % count) * step
        left = wide[item % 2]
        for j in (0, 1) if item < count else (2,):
            place = len(sent_copies)

            def product(core):
                part = hidden[j % 2, :, pl.ds(pl.multiple_of(core * half, half), half)]
                return contract(part, left, (0, 0)) if j == 2 else contract(left, part, (0, 0))

            if place >= slots_sent:
                sent_copies[place - slots_sent].wait_send()
            sent[place % slots_sent] = product(1 - d).astype(bf16)
            copy = send_copy(j, at, place)
            copy.start()
            sent_copies.append(copy)
            if place >= 2:
                kept_copies[place - 2].wait()
            kept[place % 2] = product(d)
            copy = keep_copy(j, at, place % 2)
            copy.start()
            kept_copies.append(copy)
        if item + 2 < 2 * count:
            wide_copy(item + 2).start()
        for n in after.get(item, ()):
            way_back.combine(n)
        if item in level_at:
            level_send()
    for _ in range(C):
        level_send()

    def level_copy(i, level):
        return remote(level_part.at[level], proj.at[c], zs.at[i], zr.at[i], (e, level, d))

    for i, level in zip(list(range(1, C)) + [0], order):
        for k in range(1, E):
            plane_copy(k, level).wait_recv()
        total = chip[e, level].astype(f32)
        for k in range(1, E):
            total = total + plane_parts[k, level].astype(f32)
        level_part[level] = total.astype(bf16)
        if i > 0:
            level_copy(i, level).start()
        else:
            proj[c] = level_part[c]

    for copy in kept_copies[-2:]:
        copy.wait()
    for copy in sent_copies:
        copy.wait_recv()
    for copy in sent_copies[-slots_sent:]:
        copy.wait_send()
    for copy in head_copies:
        copy.wait()
    for i, level, _ in levels:
        level_copy(i, level).wait()
    way_back.end()
    for plane in range(E):
        chip_copy(plane).wait_send()
    for i in range(1, E):
        for level in range(C):
            plane_copy(i, level).wait_send()


def middle(
    E,
    C,
    G,
    runs,
    parts,
    resid,
    factor,
    upstream,
    gain,
    logit_grad,
    router,
    w_output,
    mixed,
    x,
    pair,
    gate_back,
    up_back,
    act,
    y_rows,
    slots,
    collective,
    name,
):
    batches, run, width = parts.shape[1:]
    own = resid.shape[0]
    count = C * G
    size = width // count
    block = width // E
    part = block // count
    total, units = act.shape
    half = units // G
    step = min(512, width)
    items = 3 * (width // step)
    tall = (width, half)
    flat = (half, width)
    by_plane = pltpu.VMEM((E, C, part, width), bf16)
    return call(
        functools.partial(middle_kernel, E, C, G, runs),
        (
            parts,
            resid,
            factor,
            upstream,
            gain,
            logit_grad,
            router,
            w_output,
            mixed,
            x,
            pair,
            gate_back,
            up_back,
            act,
            y_rows,
            slots,
        ),
        (
            jax.ShapeDtypeStruct((own, width), f32),
            jax.ShapeDtypeStruct((1, width), f32),
            jax.ShapeDtypeStruct((batches, count, run, size), bf16),
            jax.ShapeDtypeStruct((C, part, width), bf16),
            jax.ShapeDtypeStruct(tall, f32),
            jax.ShapeDtypeStruct(tall, f32),
            jax.ShapeDtypeStruct(flat, f32),
            jax.ShapeDtypeStruct(tall, bf16),
            jax.ShapeDtypeStruct(tall, bf16),
            jax.ShapeDtypeStruct(flat, bf16),
            jax.ShapeDtypeStruct((len(runs), run, width), bf16),
        ),
        [VMEM] * 7 + [ANY, VMEM] + [ANY] * 6 + [VMEM],
        (VMEM, VMEM, ANY, VMEM) + (ANY,) * 7,
        [
            pltpu.VMEM((own, width), bf16),
            pltpu.VMEM((count, batches, run, size), bf16),
            pltpu.VMEM((2, size, width), bf16),
            pltpu.VMEM((2, total, units), bf16),
            pltpu.VMEM((2, total, step), bf16),
            pltpu.VMEM((2, step, half), f32),
            pltpu.VMEM((4, step, half), bf16),
            by_plane,
            by_plane,
            by_plane,
            by_plane,
            pltpu.VMEM((C, part, width), bf16),
            DMA((batches, count)),
            DMA((batches, count)),
            DMA((batches,)),
            DMA((2,)),
            DMA((E,)),
            DMA((E,)),
            DMA((E, C)),
            DMA((E, C)),
            DMA((C,)),
            DMA((C,)),
            DMA((2,)),
            DMA((2,)),
            DMA((2,)),
            DMA((items,)),
            DMA((items,)),
        ]
        + Return.scratch(E, C, len(runs), run, width, y_rows.shape[3]),
        collective,
        name,
        vmem=62,
    )


def backward_kernel(
    E,
    C,
    G,
    runs,
    queries,
    keys,
    values,
    grads,
    row_ids,
    key_ids,
    log_total,
    query_hat_in,
    key_hat_in,
    factors,
    head_gains,
    y_rows,
    slots,
    w_qkv_in,
    normed,
    small,
    first,
    out_qkv,
    out_small,
    out_gains,
    out,
    query_hat,
    key_hat,
    w_qkv,
    raw,
    query_grad,
    key_grad,
    key_sum,
    value_sum,
    sums,
    sum_parts,
    gain_sum,
    gain_parts,
    small_parts,
    small_sum,
    swap,
    swapped,
    own,
    passed,
    tokens,
    parts,
    plane_parts,
    sum_qkv,
    cs,
    cr,
    zs,
    zr,
    ts,
    qs,
    qr,
    os,
    orr,
    ss,
    sr,
    fs,
    fr,
    ms,
    mr,
    hs,
    hr,
    gs,
    gr,
    in_sem,
    *return_scratch,
):
    e, c, d = position()
    me, peers = column_peers(E, C, G)
    planes = plane_peers(E)
    count = C * G
    _, run, columns = raw.shape
    every, size = queries.shape
    batches, length = row_ids.shape[:2]
    scale = HEAD**-0.5
    width = w_qkv.shape[0]
    rows = batches * run
    sibling = (e, c, 1 - d)
    meet([device for _, _, device in peers] + [device for _, _, device in planes])
    half = tokens.shape[2]
    block = parts.shape[1]
    cuts = block // half

    def token_copy(part):
        at = lax.rem(e + 1 + part // cuts, E) * block + part % cuts * half
        return pltpu.make_async_copy(
            normed.at[:, pl.ds(pl.multiple_of(at, half), half)],
            tokens.at[part % 2],
            ts.at[part % 2],
        )

    token_copy(0).start()
    token_copy(1).start()
    small_copies = [
        remote(small.at[plane], small_parts.at[i], ss.at[i], sr.at[i], device)
        for i, plane, device in planes
    ]
    for copy in small_copies:
        copy.start()

    way_back = Return(E, C, runs, y_rows, slots, out, *return_scratch)
    way_back.send(0)
    in_copies = [
        pltpu.make_async_copy(source, target, in_sem.at[j])
        for j, (source, target) in enumerate(
            ((query_hat_in, query_hat), (key_hat_in, key_hat), (w_qkv_in, w_qkv))
        )
    ]
    for copy in in_copies:
        copy.start()
    heads = size // HEAD

    def head_back(n, carry):
        b, h = n // heads, lax.rem(n, heads)
        lanes = pl.ds(pl.multiple_of(h * HEAD, HEAD), HEAD)
        start = pl.multiple_of(b * length, length)
        key_sum[...] = jnp.zeros_like(key_sum)
        value_sum[...] = jnp.zeros_like(value_sum)
        for at, many, seen in query_blocks(length):
            rows_here = pl.ds(pl.multiple_of(start + at, many), many)
            rows_seen = pl.ds(start, seen)
            query, grad = queries[rows_here, lanes], grads[rows_here, lanes]
            scores = contract(query, keys[rows_seen, lanes], (1, 1)) * scale
            allowed = key_ids[b, :, :seen] <= row_ids[b, at : at + many]
            scores = jnp.where(allowed, scores, MASKED)
            probs = jnp.exp(scores - log_total[b, h, at : at + many])
            prod = contract(grad, values[rows_seen, lanes], (1, 1))
            delta = jnp.sum(probs * prod, axis=1, keepdims=True)
            score_grad = (probs * (prod - delta)).astype(bf16)
            query_grad[rows_here, lanes] = (
                jnp.dot(score_grad, keys[rows_seen, lanes], preferred_element_type=f32) * scale
            )
            key_sum[:seen] += contract(score_grad, query, (0, 0)) * scale
            value_sum[:seen] += contract(probs.astype(bf16), grad, (0, 0))
        key_grad[pl.ds(start, length), lanes] = key_sum[...]
        value_lanes = pl.ds(pl.multiple_of(2 * size + h * HEAD, HEAD), HEAD)
        raw[pl.ds(b * count, count), :, value_lanes] = (
            value_sum[...].astype(bf16).reshape(count, run, HEAD)
        )
        @pl.when(n == 0)
        def _():
            way_back.send(1)

        for q, turn in enumerate(beside):

            @pl.when(n == turn)
            def _():
                way_back.combine(q)

        return carry

    beside = (1, 3)[: len(runs)]
    pending = iter(range(len(beside), len(runs)))

    def carry_on(many):
        for _ in range(many):
            n = next(pending, None)
            if n is not None:
                way_back.combine(n)

    lax.fori_loop(0, batches * heads, head_back, 0)
    for copy in in_copies:
        copy.wait()

    chunk = min(2 * run, every)
    per_chunk = chunk // run
    ones = jnp.ones((8, size), f32)
    gain_sum[...] = jnp.zeros_like(gain_sum)
    pairs = ((query_grad, query_hat), (key_grad, key_hat))

    def dots(j, carry):
        rows_here = pl.ds(pl.multiple_of(j * chunk, chunk), chunk)
        for kind, (grad, hat) in enumerate(pairs):
            prod = grad[rows_here] * hat[rows_here]
            gain_sum[kind] += jnp.sum(prod, axis=0, keepdims=True)
            total = lax.dot_general(
                ones,
                prod * head_gains[kind : kind + 1],
                (((1,), (1,)), ((), ())),
                precision=lax.Precision.HIGHEST,
                preferred_element_type=f32,
            )
            sums[kind, :, rows_here] = total[:1]
        return carry

    lax.fori_loop(0, every // chunk, dots, 0)
    shares = [
        remote(sums, sum_parts.at[me], ms.at[offset], mr.at[offset], device)
        for offset, _, device in peers
    ]
    gain_copies = [
        remote(gain_sum, gain_parts.at[i], hs.at[i], hr.at[i], device) for i, _, device in planes
    ]
    for copy in shares + gain_copies:
        copy.start()
    sum_parts[me] = sums[...]
    carry_on(1)
    for copy in shares:
        copy.wait()
    total = sum_parts[0]
    for index in range(1, count):
        total = total + sum_parts[index]
    sums[...] = total / width
    rows_at = lax.broadcasted_iota(jnp.int32, (chunk, chunk), 0)
    same = rows_at == lax.broadcasted_iota(jnp.int32, (chunk, chunk), 1)

    def column_of(row):
        return jnp.sum(jnp.where(same, row, 0.0), axis=1, keepdims=True)

    def through_norm(j, carry):
        rows_here = pl.ds(pl.multiple_of(j * chunk, chunk), chunk)
        for kind, (grad, hat) in enumerate(pairs):
            part = grad[rows_here] * head_gains[kind : kind + 1]
            part = part - hat[rows_here] * column_of(sums[kind, :, rows_here])
            part = (column_of(factors[kind, :, rows_here]) * part).astype(bf16)
            raw[pl.ds(j * per_chunk, per_chunk), :, kind * size : (kind + 1) * size] = part.reshape(
                per_chunk, run, size
            )
        return carry

    lax.fori_loop(0, every // chunk, through_norm, 0)

    def gain_copy(offset, device):
        return remote(gain_sum, out_gains.at[me], gs.at[offset], gr.at[offset], device)

    for copy in gain_copies:
        copy.wait()
    total = gain_sum[...]
    for i in range(1, E):
        total = total + gain_parts[i]
    gain_sum[...] = total
    out_gains[me] = total
    for offset, _, device in peers:
        gain_copy(offset, device).start()

    def product(level, core, at, many):
        left = jnp.concatenate(
            [raw[b * count + level * G + core] for b in range(batches)], axis=0
        )
        return contract(left, w_qkv[at : at + many, :], (1, 1))

    def chip_copy(level):
        return remote(swap.at[level], swapped.at[level], cs.at[level], cr.at[level], sibling)

    def give(level):
        for at in range(0, width, 512):
            swap[level, :, at : at + 512] = product(level, 1 - d, at, 512).astype(bf16)
        chip_copy(level).start()

    def take(level):
        chip_copy(level).wait_recv()
        for at in range(0, width, 512):
            part = product(level, d, at, 512) + swapped[level, :, at : at + 512].astype(f32)
            own[level, :, at : at + 512] = part.astype(bf16)

    def hop(way, level, b):
        there = c + 1 if way == 0 else c - 1
        to = level if way == 0 else level + (C - level) * ((C - 1 - (there - level)) // (C - 1))
        return remote(
            own.at[level, pl.ds(b * run, run)],
            passed.at[to, pl.ds(b * run, run)],
            zs.at[way, level, b],
            zr.at[to, b],
            (e, there, d),
        )

    def arrival(entry, b):
        part = passed.at[entry, pl.ds(b * run, run)]
        return remote(part, part, zs.at[0, 0, b], zr.at[entry, b], sibling)

    def send(way, level, last):
        for b in range(batches):

            @pl.when(last)
            def _():
                arrival(level, b).wait_recv()
                piece = pl.ds(b * run, run)
                own[level, piece] = (
                    own[level, piece].astype(f32) + passed[level, piece].astype(f32)
                ).astype(bf16)

            hop(way, level, b).start()

    order = [C - 1, 0] + list(range(C - 2, 0, -1))
    for level in order:
        give(level)
    carry_on(1)

    def plane_copy(item):
        plane = lax.rem(e + 1 + item, E)
        return remote(
            parts.at[item],
            plane_parts.at[item],
            qs.at[item],
            qr.at[item],
            (plane, c, d),
        )

    def weights(item):
        for part in range(cuts * item, cuts * (item + 1)):
            token_copy(part).wait()
            for at in range(0, columns, 256):
                many = min(256, columns - at)
                piece = raw[:, :, at : at + many].reshape(every, many)
                rows_here = pl.ds(part % cuts * half, half)
                parts[item, rows_here, at : at + many] = contract(
                    tokens[part % 2], piece, (0, 0)
                ).astype(bf16)
            if part + 2 < cuts * E:
                token_copy(part + 2).start()
        if item < E - 1:
            plane_copy(item).start()

    mirror = C - 1 - c
    items = list(range(E))
    for level in order:
        take(level)
        if level == 0:
            @pl.when(c == 0)
            def _():
                send(0, C - 1, False)

            @pl.when(c == C - 1)
            def _():
                send(1, 0, False)

            weights(items.pop(0))
            carry_on(1)
    weights(items.pop(0))
    carry_on(len(runs))
    for turn in range(1, C - 1):

        @pl.when(c <= turn)
        def _():
            send(0, C - 1 - (turn - c), c > 0)

        @pl.when(mirror <= turn)
        def _():
            send(1, turn - mirror, mirror > 0)

        if items:
            weights(items.pop(0))
    while items:
        weights(items.pop(0))
    for item in range(E - 1):
        plane_copy(item).wait_recv()
    for at in range(0, block, 128):
        piece = pl.ds(at, min(128, block - at))
        total = parts[E - 1, piece].astype(f32)
        for item in range(E - 1):
            total = total + plane_parts[item, piece].astype(f32)
        sum_qkv[piece] = total.astype(bf16)
    share = block // (C * G)

    def row_copy(offset, index, device):
        return remote(
            sum_qkv.at[pl.ds(pl.multiple_of(index * share, share), share)],
            out_qkv.at[me],
            os.at[offset],
            orr.at[offset],
            device,
        )

    def small_copy(offset, index, device):
        return remote(
            small_sum.at[pl.ds(pl.multiple_of(index * share, share), share)],
            out_small.at[me],
            fs.at[offset],
            fr.at[offset],
            device,
        )

    for copy in small_copies:
        copy.wait_recv()
    total = small[e].astype(f32)
    for i in range(1, E):
        total = total + small_parts[i].astype(f32)
    small_sum[...] = total.astype(bf16)
    for offset, index, device in peers:
        small_copy(offset, index, device).start()
        row_copy(offset, index, device).start()
    out_small[me] = small_sum[pl.ds(pl.multiple_of(me * share, share), share)]
    out_qkv[me] = sum_qkv[pl.ds(pl.multiple_of(me * share, share), share)]

    def arrived(entry):
        for b in range(batches):
            arrival(entry, b).wait_recv()

    @pl.when(c > 0)
    def _():
        arrived(c)

    @pl.when(c < C - 1)
    def _():
        arrived(C)

    for at in range(0, width, 512):
        first[:, at : at + 512] = own[c, :, at : at + 512].astype(f32)

    @pl.when(c > 0)
    def _():
        for at in range(0, width, 512):
            first[:, at : at + 512] += passed[c, :, at : at + 512].astype(f32)

    @pl.when(c < C - 1)
    def _():
        for at in range(0, width, 512):
            first[:, at : at + 512] += passed[C, :, at : at + 512].astype(f32)

    for level in range(C):
        chip_copy(level).wait_send()
        for b in range(batches):

            @pl.when(level > c)
            def _():
                hop(0, level, b).wait_send()

            @pl.when(level < c)
            def _():
                hop(1, level, b).wait_send()

    for item in range(E - 1):
        plane_copy(item).wait_send()
    for copy in small_copies:
        copy.wait_send()
    for offset, _, device in peers:
        gain_copy(offset, device).wait()
    way_back.end()
    for offset, index, device in peers:
        row_copy(offset, index, device).wait()
        small_copy(offset, index, device).wait()


def run_backward(
    E,
    C,
    G,
    runs,
    queries,
    keys,
    values,
    grads,
    ids,
    log_total,
    query_hat,
    key_hat,
    factors,
    head_gains,
    y_rows,
    slots,
    w_qkv,
    normed,
    small,
    collective,
    name,
):
    every, size = queries.shape
    batches, length = ids.shape
    count = C * G
    run = length // count
    columns = 3 * size
    width = w_qkv.shape[0]
    rows = batches * run
    block = width // E
    share = block // count
    lanes = small.shape[2]
    by_level = pltpu.VMEM((C, rows, width), bf16)
    wide = pltpu.VMEM((every, size), f32)
    head = pltpu.VMEM((length, HEAD), f32)
    return call(
        functools.partial(backward_kernel, E, C, G, runs),
        (
            queries,
            keys,
            values,
            grads,
            ids[:, :, None],
            ids[:, None, :],
            log_total,
            query_hat,
            key_hat,
            factors,
            head_gains,
            y_rows,
            slots,
            w_qkv,
            normed,
            small,
        ),
        (
            jax.ShapeDtypeStruct((rows, width), f32),
            jax.ShapeDtypeStruct((count, share, columns), bf16),
            jax.ShapeDtypeStruct((count, share, lanes), bf16),
            jax.ShapeDtypeStruct((count, 2, 1, size), f32),
            jax.ShapeDtypeStruct((len(runs), run, width), bf16),
        ),
        [VMEM] * 7 + [ANY, ANY, VMEM, VMEM, ANY, VMEM, ANY, ANY, VMEM],
        (VMEM, VMEM, VMEM, VMEM, ANY),
        [
            wide,
            wide,
            pltpu.VMEM(w_qkv.shape, bf16),
            pltpu.VMEM((batches * count, run, columns), bf16),
            wide,
            wide,
            head,
            head,
            pltpu.VMEM((2, 1, every), f32),
            pltpu.VMEM((count, 2, 1, every), f32),
            pltpu.VMEM((2, 1, size), f32),
            pltpu.VMEM((E, 2, 1, size), f32),
            pltpu.VMEM((E, block, lanes), bf16),
            pltpu.VMEM((block, lanes), bf16),
            by_level,
            by_level,
            by_level,
            pltpu.VMEM((C + 1, rows, width), bf16),
            pltpu.VMEM((2, every, min(block, 256)), bf16),
            pltpu.VMEM((E, block, columns), bf16),
            pltpu.VMEM((E, block, columns), bf16),
            pltpu.VMEM((block, columns), bf16),
            DMA((C,)),
            DMA((C,)),
            DMA((2, C, batches)),
            DMA((C + 1, batches)),
            DMA((2,)),
            DMA((E,)),
            DMA((E,)),
            DMA((count,)),
            DMA((count,)),
            DMA((E,)),
            DMA((E,)),
            DMA((count,)),
            DMA((count,)),
            DMA((count,)),
            DMA((count,)),
            DMA((E,)),
            DMA((E,)),
            DMA((count,)),
            DMA((count,)),
            DMA((3,)),
        ]
        + Return.scratch(E, C, len(runs), run, width, y_rows.shape[3]),
        collective,
        name,
        vmem=62,
    )


def contract(left, right, axes):
    return lax.dot_general(left, right, ((axes[:1], axes[1:]), ((), ())), preferred_element_type=f32)


def query_blocks(length):
    size = min(256, length)
    return [(i, size, min(length, i + 2 * size)) for i in range(0, length, size)]


def rms_factor(values):
    return lax.rsqrt(jnp.mean(values * values, axis=-1, keepdims=True) + EPSILON)


def norm_back(grad_hat, hatted, factor):
    return factor * (grad_hat - hatted * jnp.mean(grad_hat * hatted, axis=-1, keepdims=True))


def slot_table(routes, experts):
    batches, run, top = routes.shape
    hits = jnp.swapaxes(routes, 1, 2)[:, :, :, None] == jnp.arange(experts, dtype=jnp.int32)
    ones = hits.astype(bf16)
    tokens, ranks = jnp.arange(run), jnp.arange(top)
    before = (tokens[None, :] < tokens[:, None]).astype(bf16)
    above = (ranks[None, :] < ranks[:, None]).astype(bf16)
    within = jnp.einsum("ts,bksx->bktx", before, ones, preferred_element_type=f32)
    totals = jnp.sum(hits.astype(f32), axis=2)
    earlier = jnp.einsum(
        "kj,bjx->bkx", above, totals.astype(bf16), preferred_element_type=f32
    )
    places = jnp.sum(jnp.where(hits, within + earlier[:, :, None, :], 0.0), axis=1)
    places = jnp.where(jnp.any(hits, axis=1), places, UNUSED_SLOT)
    return jnp.swapaxes(places, 1, 2)


def body(
    tokens,
    block_ids,
    routes,
    norm_gains,
    w_query,
    w_key,
    w_value,
    w_output,
    router,
    expert_gate,
    expert_up,
    expert_down,
    cotangent,
):
    E, C, G = lax.axis_size("expert"), lax.axis_size("context"), lax.axis_size("dp")
    batches, run, width = tokens.shape
    top = routes.shape[2]
    experts = E * C * expert_gate.shape[0]
    capacity = max(2, run * top // experts)
    count = C * G
    size = width // count
    length = count * run
    every = batches * length
    own = batches * run
    me = lax.axis_index("context") * G + lax.axis_index("dp")

    rows = w_query.shape[0]
    small_width = -(-(norm_gains.shape[1] + experts) // 128) * 128
    small = jnp.concatenate([norm_gains, router], axis=1)
    small = jnp.pad(small, ((0, 0), (0, small_width - small.shape[1])))
    pieces = [w.reshape(rows, count, size) for w in (w_query, w_key, w_value)]
    weights = jnp.swapaxes(jnp.concatenate(pieces, axis=2), 0, 1)
    places = slot_table(routes, experts).reshape(batches, E, C, run)
    by_level = jnp.transpose(places, (2, 0, 1, 3))
    by_expert = jnp.transpose(places, (1, 2, 0, 3))
    column, w_qkv, small, full_output, ids, slots = start(
        E, C, G, tokens, weights, small, w_output, block_ids, by_level
    )
    ids = jnp.swapaxes(ids, 0, 1).reshape(batches, length)
    w_qkv = w_qkv.reshape(width, 3 * size)
    small = small.reshape(width, small_width)
    full_output = full_output.reshape(width, width)
    gains = small[:, :4].astype(f32)
    full_router = small[:, 4 : 4 + experts]
    head_gains = lax.dynamic_slice(gains, (me * size, 0), (size, 4))

    (
        normed,
        query_low,
        key_low,
        value_low,
        query_hat,
        key_hat,
        log_total,
        factors,
        mixed_low,
        upstream_rows,
    ) = run_forward(
        E,
        C,
        G,
        column.reshape(every, width),
        jnp.swapaxes(gains[:, :1], 0, 1),
        jnp.swapaxes(head_gains[:, 1:3], 0, 1),
        w_qkv,
        ids,
        slots,
        cotangent,
        capacity,
        2,
        "forward",
    )
    mixed_low = mixed_low.reshape(own, width)

    inputs = tokens.reshape(own, width).astype(f32)
    resid = inputs + jnp.dot(mixed_low, full_output, preferred_element_type=f32)
    second_factor = rms_factor(resid)
    second_hat = resid * second_factor
    second_low = (second_hat * gains[:, 3]).astype(bf16)
    logits = jnp.dot(second_low, full_router, preferred_element_type=f32)
    router_probs = jax.nn.softmax(logits, axis=-1)
    gate_table = jnp.transpose(router_probs.reshape(batches, run, E, C), (2, 3, 0, 1))
    table = jnp.concatenate([by_expert, gate_table], axis=2)[:, :, :, None, :]

    second_grad, x, y_rows, pair_grad, act, gate_pre_grad, up_pre_grad, gate_grad = run_experts(
        E,
        C,
        second_low.reshape(batches, run, width),
        upstream_rows,
        slots,
        table,
        expert_gate[0],
        expert_up[0],
        expert_down[0],
        capacity,
        4,
        "experts",
    )
    slot_count = E * C * batches * capacity
    x, pair_grad, act, gate_pre_grad, up_pre_grad = (
        rows.reshape(slot_count, -1) for rows in (x, pair_grad, act, gate_pre_grad, up_pre_grad)
    )
    prob_grad = jnp.transpose(gate_grad[:, :, :, 0, :], (2, 3, 0, 1)).reshape(own, experts)
    logit_grad = router_probs * (
        prob_grad - jnp.sum(router_probs * prob_grad, axis=-1, keepdims=True)
    )
    logit_grad = jnp.pad(logit_grad.astype(bf16), ((0, 0), (0, small_width - experts)))
    router_wide = jnp.pad(full_router, ((0, 0), (0, small_width - experts)))

    early = [(b, i) for b in range(batches // 2) for i in list(range(1, C)) + [0]]
    late = [(b, i) for b in range(batches // 2, batches) for i in list(range(1, C)) + [0]]
    resid_grad, gain_second, mixed_grad, grad_proj, *expert_grads, early_mixture = middle(
        E,
        C,
        G,
        early,
        second_grad,
        resid,
        second_factor,
        cotangent.reshape(own, width),
        jnp.swapaxes(gains[:, 3:4], 0, 1),
        logit_grad,
        router_wide,
        full_output,
        mixed_low,
        x,
        pair_grad,
        gate_pre_grad,
        up_pre_grad,
        act,
        y_rows,
        slots,
        6,
        "middle",
    )
    grad_gate, grad_up, grad_down = (
        (mine + other.astype(f32))[None] for mine, other in zip(expert_grads[:3], expert_grads[3:])
    )
    grad_proj = jnp.sum(grad_proj.astype(f32), axis=0)
    sums = contract(second_low, logit_grad, (0, 0))
    sums = jnp.where(jnp.arange(small_width) == experts, gain_second.reshape(width, 1), sums)
    sums = sums.astype(bf16)
    first_grad, grad_qkv, sums, gain_heads, late_mixture = run_backward(
        E,
        C,
        G,
        late,
        query_low,
        key_low,
        value_low,
        mixed_grad.reshape(every, size),
        ids,
        log_total,
        query_hat,
        key_hat,
        factors,
        jnp.swapaxes(head_gains[:, 1:3], 0, 1),
        y_rows,
        slots,
        w_qkv,
        normed,
        sums.reshape(E, width // E, small_width),
        8,
        "backward",
    )
    gain_heads = jnp.swapaxes(gain_heads[:, :, 0], 0, 1).reshape(2, width)
    first_row = (lax.axis_index("expert") * count + me) * rows
    gain_heads = lax.dynamic_slice(gain_heads, (0, first_row), (2, rows))
    mixture = [0.0] * batches
    for runs, parts in ((early, early_mixture), (late, late_mixture)):
        for n, (b, _) in enumerate(runs):
            mixture[b] = mixture[b] + parts[n].astype(f32)
    mixture = jnp.stack(mixture)
    activations = (resid.reshape(tokens.shape) + mixture).astype(bf16)
    sums = jnp.sum(sums.astype(f32), axis=0)
    first_factor = rms_factor(inputs)
    first_hat = inputs * first_factor
    input_grad = resid_grad + norm_back(first_grad * gains[:, 0], first_hat, first_factor)

    grad_qkv = jnp.swapaxes(grad_qkv.astype(f32), 0, 1)
    grad_query, grad_key, grad_value = (
        grad_qkv[:, :, i * size : (i + 1) * size].reshape(rows, width) for i in range(3)
    )
    gain_first = sum(
        jnp.sum(w.astype(f32) * grad, axis=1)
        for w, grad in ((w_query, grad_query), (w_key, grad_key), (w_value, grad_value))
    )
    gain_first = gain_first / norm_gains[:, 0].astype(f32)
    grad_gains = jnp.stack([gain_first, gain_heads[0], gain_heads[1], sums[:, experts]], axis=1)
    return (
        activations,
        input_grad.reshape(tokens.shape),
        grad_gains,
        grad_query,
        grad_key,
        grad_value,
        grad_proj,
        sums[:, :experts],
        grad_gate,
        grad_up,
        grad_down,
    )


def solution(mesh):
    by_token = ("context", "dp")
    by_expert = P(("expert", "context"), None, None)
    by_row = P(ALL_AXES, None)
    rows = P("expert", by_token, None)
    return jax.shard_map(
        body,
        mesh=mesh,
        in_specs=(
            rows,
            P("expert", by_token),
            rows,
            by_row,
            by_row,
            by_row,
            by_row,
            by_row,
            by_row,
            by_expert,
            by_expert,
            by_expert,
            rows,
        ),
        out_specs=(
            rows,
            rows,
            by_row,
            by_row,
            by_row,
            by_row,
            by_row,
            by_row,
            P(("expert", "context"), None, "dp"),
            P(("expert", "context"), None, "dp"),
            P(("expert", "context"), "dp", None),
        ),
        check_vma=False,
    )
```

```python
import functools

import jax
import jax.numpy as jnp
from jax import lax
from jax.experimental import pallas as pl
from jax.experimental.pallas import tpu as pltpu
from jax.sharding import PartitionSpec as P

HEAD = 128
EPSILON = 1e-05
MASKED = -1e30
UNUSED_SLOT = 4096.0
ALL_AXES = ("expert", "context", "dp")
MESH = pl.DeviceIdType.MESH
ANY = pl.BlockSpec(memory_space=pl.ANY)
VMEM = pl.BlockSpec(memory_space=pltpu.VMEM)
DMA = pltpu.SemaphoreType.DMA
MIB = 1 << 20
f32 = jnp.float32
bf16 = jnp.bfloat16


def call(kernel, operands, out_shapes, in_specs, out_specs, scratch, collective, name, vmem=32):
    return pl.pallas_call(
        kernel,
        out_shape=out_shapes,
        in_specs=in_specs,
        out_specs=out_specs,
        scratch_shapes=scratch,
        compiler_params=pltpu.CompilerParams(
            collective_id=collective, has_side_effects=True, vmem_limit_bytes=vmem * MIB
        ),
        name=name,
    )(*operands)


def position():
    return lax.axis_index("expert"), lax.axis_index("context"), lax.axis_index("dp")


def meet(devices):
    barrier = pltpu.get_barrier_semaphore()
    for device in devices:
        pl.semaphore_signal(barrier, inc=1, device_id=device, device_id_type=MESH)
    pl.semaphore_wait(barrier, len(devices))


def remote(source, target, send_sem, recv_sem, device):
    return pltpu.make_async_remote_copy(
        src_ref=source,
        dst_ref=target,
        send_sem=send_sem,
        recv_sem=recv_sem,
        device_id=device,
        device_id_type=MESH,
    )


def column_peers(E, C, G):
    e, c, d = position()
    me = c * G + d
    peers = []
    for offset in range(1, C * G):
        index = lax.rem(me + offset, C * G)
        peers.append((offset, index, (e, index // G, lax.rem(index, G))))
    return me, peers


def plane_peers(E):
    e, c, d = position()
    return [(i, lax.rem(e + i, E), (lax.rem(e + i, E), c, d)) for i in range(1, E)]


def level_peers(C):
    e, c, d = position()
    return [(i, lax.rem(c + i, C), (e, lax.rem(c + i, C), d)) for i in range(1, C)]


def start_kernel(
    E,
    C,
    G,
    tokens,
    weights,
    small_weights,
    output,
    ids,
    slots,
    column,
    gathered,
    small_gathered,
    full_output,
    ids_out,
    slots_out,
    ws,
    wr,
    bs,
    br,
    hs,
    hr,
    ts,
    tr,
    ls,
    ms,
    mr,
    ps,
    pr,
    fs,
    fr,
    gs,
    gr,
):
    e, c, d = position()
    me, peers = column_peers(E, C, G)
    planes = plane_peers(E)
    batches = tokens.shape[0]
    sibling = (e, c, 1 - d)
    meet([device for _, _, device in peers] + [device for _, _, device in planes])
    kinds = ((weights, gathered), (small_weights, small_gathered))
    weight_copies = []
    for j, (source, target) in enumerate(kinds):
        for offset, index, device in peers:
            part = source.at[index] if j == 0 else source
            weight_copies.append(
                remote(part, target.at[e, me], ws.at[j, offset], wr.at[j, offset], device)
            )
    for copy in weight_copies:
        copy.start()
    local = [
        pltpu.make_async_copy(weights.at[me], gathered.at[e, me], ls.at[0]),
        pltpu.make_async_copy(small_weights, small_gathered.at[e, me], ls.at[1]),
        pltpu.make_async_copy(output, full_output.at[e, c, d], ls.at[2]),
    ]
    for b in range(batches):
        local.append(pltpu.make_async_copy(tokens.at[b], column.at[b, me], ls.at[3 + b]))
    for copy in local:
        copy.start()

    def source_of(item):
        return output if item == 0 else tokens.at[item - 1]

    def place(item, level):
        return full_output.at[e, level, d] if item == 0 else column.at[item - 1, level * G + d]

    def to_sibling(source, item, level, arrival):
        return remote(
            source, place(item, level), ts.at[item, arrival], tr.at[item, arrival], sibling
        )

    def step(hop, source, item, level, up):
        to = (e, c + 1, d) if up else (e, c - 1, d)
        way = 0 if up else 1
        return remote(
            source, place(item, level), hs.at[way, item, hop], hr.at[way, item, hop], to
        )

    def relay(item, hop):
        for up in (True, False):
            level = c - hop if up else c + hop
            here = (c >= hop) if up else (c + hop < C)
            onward = (c < C - 1) if up else (c > 0)

            @pl.when(here)
            def _():
                landed = place(item, level)
                step(hop - 1, landed, item, level, up).wait_recv()
                if hop < C - 1:

                    @pl.when(onward)
                    def _():
                        step(hop, landed, item, level, up).start()

                if item == 0:
                    for i, _, device in planes:
                        output_copy(i, level, device).start()
                if G > 1:
                    to_sibling(landed, item, level, hop if up else C - 1 + hop).start()

    def output_copy(i, level, device):
        mine = full_output.at[e, level, d]
        return remote(mine, mine, fs.at[i, level], fr.at[i, level], device)

    def output_sibling(i, level):
        part = full_output.at[lax.rem(e + E - i, E), level, d]
        return remote(part, part, gs.at[i, level], gr.at[i, level], sibling)

    for item in range(batches + 1):

        @pl.when(c < C - 1)
        def _():
            step(0, source_of(item), item, c, True).start()

        @pl.when(c > 0)
        def _():
            step(0, source_of(item), item, c, False).start()

        if G > 1:
            to_sibling(source_of(item), item, c, 0).start()
    small = []
    for offset, _, device in peers:
        small.append(remote(ids, ids_out.at[me], ms.at[offset], mr.at[offset], device))
    for i, level, device in level_peers(C):
        small.append(remote(slots.at[level], slots_out.at[i], ps.at[i], pr.at[i], device))
    for copy in small:
        copy.start()
    ids_out[me] = ids[...]
    slots_out[0] = slots[c]
    for copy in weight_copies:
        copy.wait_recv()
    for copy in local[:3]:
        copy.wait()
    plane_copies = []
    for j, (_, target) in enumerate(kinds):
        for i, _, device in planes:
            copy = remote(target.at[e], target.at[e], bs.at[j, i], br.at[j, i], device)
            copy.start()
            plane_copies.append(copy)
    for i, _, device in planes:
        output_copy(i, c, device).start()
    for hop in range(1, C):
        for item in range(batches + 1):
            relay(item, hop)
    for level in range(C):
        for i, _, device in planes:
            output_copy(i, level, device).wait_recv()
            if G > 1:
                output_sibling(i, level).start()

    for item in range(batches + 1):
        if G > 1:
            to_sibling(source_of(item), item, c, 0).wait()
        for hop in range(C - 1):
            for up in (True, False):
                arrival = hop + 1 if up else C + hop
                origin = c - hop if up else c + hop
                if up:
                    sends = jnp.logical_and(origin >= 0, c < C - 1)
                    arrives = c >= hop + 1
                else:
                    sends = jnp.logical_and(origin < C, c > 0)
                    arrives = c + hop + 1 < C

                @pl.when(sends)
                def _():
                    step(hop, source_of(item), item, c, up).wait_send()

                if G > 1:

                    @pl.when(arrives)
                    def _():
                        to_sibling(source_of(item), item, c, arrival).wait()

    for level in range(C):
        for i, _, device in planes:
            output_copy(i, level, device).wait_send()
            if G > 1:
                output_sibling(i, level).wait()
    for copy in weight_copies:
        copy.wait_send()
    for copy in plane_copies + small + local[3:]:
        copy.wait()


def start(E, C, G, tokens, weights, small_weights, output, ids, slots):
    batches, run, width = tokens.shape
    count = C * G
    rows, columns = weights.shape[1:]
    items = batches + 1
    return call(
        functools.partial(start_kernel, E, C, G),
        (tokens, weights, small_weights, output, ids, slots),
        (
            jax.ShapeDtypeStruct((batches, count, run, width), tokens.dtype),
            jax.ShapeDtypeStruct((E, count, rows, columns), weights.dtype),
            jax.ShapeDtypeStruct((E, count) + small_weights.shape, weights.dtype),
            jax.ShapeDtypeStruct((E, C, G, rows, width), weights.dtype),
            jax.ShapeDtypeStruct((count,) + ids.shape, ids.dtype),
            jax.ShapeDtypeStruct(slots.shape, slots.dtype),
        ),
        [ANY, ANY, ANY, ANY, VMEM, VMEM],
        (ANY, ANY, ANY, ANY, VMEM, VMEM),
        [
            DMA((2, count)),
            DMA((2, count)),
            DMA((2, E)),
            DMA((2, E)),
            DMA((2, items, C)),
            DMA((2, items, C)),
            DMA((items, 2 * C)),
            DMA((items, 2 * C)),
            DMA((items + 2,)),
            DMA((count,)),
            DMA((count,)),
            DMA((C,)),
            DMA((C,)),
            DMA((E, C)),
            DMA((E, C)),
            DMA((E, C)),
            DMA((E, C)),
        ],
        1,
        "start",
        vmem=62,
    )


def choose(slots, count):
    cells = lax.broadcasted_iota(jnp.int32, (count, slots.shape[1]), 0).astype(f32)
    return jnp.concatenate(
        [(cells == slots[i : i + 1, :]).astype(bf16) for i in range(slots.shape[0])], axis=0
    )


class Flow:
    def __init__(self, E, C, rows, slots, landed, packed, target, own, zs, zr, xs, xr, stay):
        self.E, self.C, self.rows, self.slots = E, C, rows, slots
        self.landed, self.packed, self.target = landed, packed, target
        self.sems = own, zs, zr, xs, xr, stay
        self.e, self.c, self.d = position()
        self.batches = rows.shape[0]
        self.cap, self.width = target.shape[3:]
        self.kept = packed.shape[0]
        self.chunks = self.batches * C

    def level_entry(self, far):
        high = 2 * self.c // self.C
        return high * far + (1 - high) * lax.rem(self.C - far, self.C)

    def own(self, b):
        return pltpu.make_async_copy(self.rows.at[b], self.landed.at[0, b], self.sems[0].at[b])

    def hop(self, b, i, way):
        there = i + 1 if way == 0 else lax.rem(i + self.C - 1, self.C)
        level = lax.rem(self.c + (1 if way == 0 else self.C - 1), self.C)
        return remote(
            self.landed.at[i, b],
            self.landed.at[there, b],
            self.sems[1].at[way, i, b],
            self.sems[2].at[there, b],
            (self.e, level, self.d),
        )

    def arrival(self, b, i):
        entry = self.landed.at[i, b]
        return remote(
            entry,
            entry,
            self.sems[1].at[0, i, b],
            self.sems[2].at[i, b],
            (self.e, self.c, 1 - self.d),
        )

    def onward(self, i, way):
        if way == 0:
            return jnp.logical_and(i <= self.c, self.c < self.C - 1)
        return jnp.logical_and(lax.rem(self.C - i, self.C) + self.c < self.C, self.c > 0)

    def pass_on(self, far, b):
        for way in range(2):
            i = far if way == 0 else lax.rem(self.C - far, self.C)
            here = (far <= self.c) if way == 0 else (far + self.c < self.C)

            @pl.when(jnp.logical_and(here, self.onward(i, way)))
            def _():
                self.hop(b, i, way).start()

    def begin(self, count):
        for b in range(self.batches):
            self.own(b).start()
        for b in range(self.batches):
            self.own(b).wait()
        for b in range(count):
            self.pass_on(0, b)

    def receive(self, far, b):
        for way in range(2):
            i = far if way == 0 else self.C - far

            @pl.when((far <= self.c) if way == 0 else (far + self.c < self.C))
            def _():
                self.arrival(b, i).wait_recv()

    def hops_sent(self, b, i):
        for way in range(2):

            @pl.when(self.onward(i, way))
            def _():
                self.hop(b, i, way).wait_send()

    def across(self, n, b, i, k):
        plane = lax.rem(self.e + k, self.E)
        return remote(
            self.packed.at[lax.rem(n, self.kept), plane],
            self.target.at[i, b, k],
            self.sems[3].at[i, b, k],
            self.sems[4].at[i, b, k],
            (plane, self.c, self.d),
        )

    def stay(self, n, b, i):
        return pltpu.make_async_copy(
            self.packed.at[lax.rem(n, self.kept), self.e],
            self.target.at[i, b, 0],
            self.sems[5].at[i, b],
        )

    def compact(self, n, b, i):
        place = lax.rem(n, self.kept)
        picks = choose(self.slots[i, b], self.cap)
        for at in range(0, self.width, 512):
            part = jnp.dot(
                picks, self.landed[i, b, :, at : at + 512], preferred_element_type=f32
            ).astype(bf16)
            self.packed[place, :, :, at : at + 512] = part.reshape(self.E, self.cap, 512)
        for k in range(1, self.E):
            self.across(n, b, i, k).start()
        self.stay(n, b, i).start()

    def crossed(self, n, b, i):
        for k in range(1, self.E):
            self.across(n, b, i, k).wait_send()

    def arrived(self, n, b, i):
        for k in range(1, self.E):
            self.across(n, b, i, k).wait_recv()

    @staticmethod
    def scratch(E, C, batches, run, width, cap, kept):
        return [
            pltpu.VMEM((C, batches, run, width), bf16),
            pltpu.VMEM((kept, E, cap, width), bf16),
            DMA((batches,)),
            DMA((2, C, batches)),
            DMA((C, batches)),
            DMA((C, batches, E)),
            DMA((C, batches, E)),
            DMA((C, batches)),
        ]


class Return:
    def __init__(self, E, C, runs, rows, slots, out, returned, sums, ys, yr, bs, us, ur, ks):
        self.E, self.C, self.runs = E, C, runs
        self.rows, self.slots, self.out = rows, slots, out
        self.returned, self.sums = returned, sums
        self.sems = ys, yr, bs, us, ur, ks
        self.e, self.c, self.d = position()

    def back(self, n, k):
        b, i = self.runs[n]
        return remote(
            self.rows.at[i, b, k],
            self.returned.at[n, self.e],
            self.sems[0].at[n, k],
            self.sems[1].at[n, k],
            (lax.rem(self.e + self.E - k, self.E), self.c, self.d),
        )

    def own(self, n):
        b, i = self.runs[n]
        return pltpu.make_async_copy(
            self.rows.at[i, b, 0], self.returned.at[n, self.e], self.sems[2].at[n]
        )

    def along(self, n):
        i = self.runs[n][1]
        if i == 0:
            return pltpu.make_async_copy(self.sums.at[n], self.out.at[n], self.sems[5].at[n])
        to = (self.e, lax.rem(self.c + self.C - i, self.C), self.d)
        return remote(
            self.sums.at[n], self.out.at[n], self.sems[3].at[n], self.sems[4].at[n], to
        )

    def send(self, n):
        if n < len(self.runs):
            for k in range(1, self.E):
                self.back(n, k).start()
            self.own(n).start()

    def combine(self, n):
        b, i = self.runs[n]
        for k in range(1, self.E):
            self.back(n, k).wait_recv()
        self.own(n).wait()
        self.send(n + 2)
        cap, width = self.rows.shape[3:]
        picks = choose(self.slots[i, b], cap)
        for at in range(0, width, 512):
            part = self.returned[n, :, :, at : at + 512].reshape(self.E * cap, 512)
            self.sums[n, :, at : at + 512] = contract(picks, part, (0, 0)).astype(bf16)
        self.along(n).start()

    def end(self):
        for n in range(len(self.runs)):
            for k in range(1, self.E):
                self.back(n, k).wait_send()
            self.along(n).wait()

    @staticmethod
    def scratch(E, C, count, run, width, cap):
        return [
            pltpu.VMEM((count, E, cap, width), bf16),
            pltpu.VMEM((count, run, width), bf16),
            DMA((count, E)),
            DMA((count, E)),
            DMA((count,)),
            DMA((count,)),
            DMA((count,)),
            DMA((count,)),
        ]


def forward_kernel(
    E,
    C,
    G,
    column,
    gain,
    head_gains,
    w_qkv,
    row_ids,
    key_ids,
    slots,
    upstream,
    normed,
    queries_out,
    keys_out,
    values_out,
    query_hat_out,
    key_hat_out,
    log_total,
    factors,
    mixed,
    u_out,
    queries,
    keys,
    values,
    query_hat,
    key_hat,
    raw,
    low,
    squares,
    parts,
    heads,
    landed,
    packed,
    own,
    zs,
    zr,
    xs,
    xr,
    stay,
    raw_sem,
    low_sem,
    ss,
    sr,
    ms,
    mr,
    ml,
    out_sem,
):
    me, peers = column_peers(E, C, G)
    planes = plane_peers(E)
    every, width = column.shape
    batches, length, size = heads.shape
    run = length // (C * G)
    block = raw.shape[1]
    blocks = every // block
    scale = HEAD**-0.5
    meet([device for _, _, device in peers] + [device for _, _, device in planes])
    flow = Flow(E, C, upstream, slots, landed, packed, u_out, own, zs, zr, xs, xr, stay)

    def load(j):
        at = pl.multiple_of(j * block, block)
        place = lax.rem(j, 2)
        return pltpu.make_async_copy(column.at[pl.ds(at, block)], raw.at[place], raw_sem.at[place])

    def store(j):
        at = pl.multiple_of(j * block, block)
        place = lax.rem(j, 2)
        return pltpu.make_async_copy(low.at[place], normed.at[pl.ds(at, block)], low_sem.at[place])

    def chunk_of(n):
        return n % batches, flow.level_entry(n // batches)

    chunk = iter(range(flow.chunks))

    def carry_on(count):
        for _ in range(count):
            n = next(chunk, None)
            if n is None:
                return
            if n >= flow.kept:
                before = n - flow.kept, *chunk_of(n - flow.kept)
                flow.crossed(*before)
                flow.stay(*before).wait()
            if n >= batches:
                flow.receive(n // batches, n % batches)
                flow.pass_on(n // batches, n % batches)
            flow.compact(n, *chunk_of(n))

    load(0).start()
    load(1).start()
    flow.begin(batches)
    carry_on(batches)
    ones = jnp.ones((8, size), f32)

    def project(j, carry):
        place = lax.rem(j, 2)
        rows = pl.ds(pl.multiple_of(j * block, block), block)
        load(j).wait()

        @pl.when(j >= 2)
        def _():
            store(j - 2).wait()

        total = jnp.zeros((block, 1), f32)
        for at in range(0, width, 512):
            part = raw[place, :, at : at + 512].astype(f32)
            total += jnp.sum(part * part, axis=1, keepdims=True)
        factor = lax.rsqrt(total / width + EPSILON)
        for at in range(0, width, 512):
            part = raw[place, :, at : at + 512].astype(f32) * factor
            low[place, :, at : at + 512] = (part * gain[:, at : at + 512]).astype(bf16)
        store(j).start()

        @pl.when(j + 2 < blocks)
        def _():
            load(j + 2).start()

        for kind in range(3):
            part = jnp.dot(
                low[place],
                w_qkv[:, kind * size : (kind + 1) * size],
                preferred_element_type=f32,
            )
            if kind == 2:
                values[rows] = part.astype(bf16)
            else:
                (query_hat, key_hat)[kind][rows] = part
                sums = lax.dot_general(
                    ones,
                    part * part,
                    (((1,), (1,)), ((), ())),
                    precision=lax.Precision.HIGHEST,
                    preferred_element_type=f32,
                )
                squares[kind, :, rows] = sums[:1]
        return carry

    half = blocks // 2
    lax.fori_loop(0, half, project, 0)
    carry_on(1)
    lax.fori_loop(half, blocks, project, 0)
    shares = [
        remote(squares, parts.at[me], ss.at[offset], sr.at[offset], device)
        for offset, _, device in peers
    ]
    for copy in shares:
        copy.start()
    parts[me] = squares[...]
    carry_on(1)
    for copy in shares:
        copy.wait_recv()
    total = parts[0]
    for index in range(1, C * G):
        total = total + parts[index]
    factors[...] = lax.rsqrt(total / width + EPSILON)
    rows_at = lax.broadcasted_iota(jnp.int32, (block, block), 0)
    same = rows_at == lax.broadcasted_iota(jnp.int32, (block, block), 1)

    def scaled(j, carry):
        rows = pl.ds(pl.multiple_of(j * block, block), block)
        for kind, (hat, out) in enumerate(((query_hat, queries), (key_hat, keys))):
            factor = jnp.sum(jnp.where(same, factors[kind, :, rows], 0.0), axis=1, keepdims=True)
            part = hat[rows] * factor
            hat[rows] = part
            out[rows] = (part * head_gains[kind : kind + 1]).astype(bf16)
        return carry

    lax.fori_loop(0, blocks, scaled, 0)
    out_copies = [
        pltpu.make_async_copy(source, target, out_sem.at[j])
        for j, (source, target) in enumerate(
            (
                (queries, queries_out),
                (keys, keys_out),
                (values, values_out),
                (query_hat, query_hat_out),
                (key_hat, key_hat_out),
            )
        )
    ]
    for copy in out_copies:
        copy.start()
    carry_on(1)

    def mixed_copy(b, offset, index, device):
        where = pl.ds(pl.multiple_of(me * size, size), size)
        part = heads.at[b, pl.ds(pl.multiple_of(index * run, run), run)]
        return remote(part, mixed.at[b, :, where], ms.at[b, offset], mr.at[b, offset], device)

    def mixed_own(b):
        where = pl.ds(pl.multiple_of(me * size, size), size)
        part = heads.at[b, pl.ds(pl.multiple_of(me * run, run), run)]
        return pltpu.make_async_copy(part, mixed.at[b, :, where], ml.at[b])

    for b in range(batches):

        def head(h, carry, b=b):
            lanes = pl.ds(pl.multiple_of(h * HEAD, HEAD), HEAD)
            for first, count, seen in query_blocks(length):
                rows = pl.ds(b * length + first, count)
                seen_rows = pl.ds(b * length, seen)
                scores = contract(queries[rows, lanes], keys[seen_rows, lanes], (1, 1)) * scale
                allowed = key_ids[b, :, :seen] <= row_ids[b, first : first + count]
                scores = jnp.where(allowed, scores, MASKED)
                peak = jnp.max(scores, axis=1, keepdims=True)
                grown = jnp.exp(scores - peak)
                total = jnp.sum(grown, axis=1, keepdims=True)
                probs = (grown * (1.0 / total)).astype(bf16)
                heads[b, first : first + count, lanes] = jnp.dot(
                    probs, values[seen_rows, lanes], preferred_element_type=f32
                ).astype(bf16)
                log_total[b, h, first : first + count] = peak + jnp.log(total)
            return carry

        lax.fori_loop(0, size // HEAD, head, 0)
        for offset, index, device in peers:
            mixed_copy(b, offset, index, device).start()
        mixed_own(b).start()
        carry_on(1)
    carry_on(flow.chunks)

    for copy in out_copies:
        copy.wait()
    for copy in shares:
        copy.wait_send()
    for j in (blocks - 2, blocks - 1):
        store(j).wait()
    for b in range(batches):
        for offset, index, device in peers:
            mixed_copy(b, offset, index, device).wait()
        mixed_own(b).wait()

    for n in range(flow.chunks):
        b, i = chunk_of(n)
        flow.hops_sent(b, i)
        flow.arrived(n, b, i)
        if n >= flow.chunks - flow.kept:
            flow.crossed(n, b, i)
            flow.stay(n, b, i).wait()


def run_forward(E, C, G, column, gain, head_gains, w_qkv, ids, slots, upstream, cap, collective, name):
    every, width = column.shape
    batches, run = upstream.shape[:2]
    count = C * G
    length = count * run
    size = width // count
    block = min(256, every)
    low = jax.ShapeDtypeStruct((every, size), bf16)
    wide = jax.ShapeDtypeStruct((every, size), f32)
    return call(
        functools.partial(forward_kernel, E, C, G),
        (column, gain, head_gains, w_qkv, ids[:, :, None], ids[:, None, :], slots, upstream),
        (
            jax.ShapeDtypeStruct((every, width), bf16),
            low,
            low,
            low,
            wide,
            wide,
            jax.ShapeDtypeStruct((batches, size // HEAD, length, 1), f32),
            jax.ShapeDtypeStruct((2, 1, every), f32),
            jax.ShapeDtypeStruct(upstream.shape, bf16),
            jax.ShapeDtypeStruct((C, batches, E, cap, width), bf16),
        ),
        [ANY] + [VMEM] * 6 + [ANY],
        (ANY,) * 6 + (VMEM,) * 2 + (ANY, ANY),
        [
            pltpu.VMEM(low.shape, bf16),
            pltpu.VMEM(low.shape, bf16),
            pltpu.VMEM(low.shape, bf16),
            pltpu.VMEM(wide.shape, f32),
            pltpu.VMEM(wide.shape, f32),
            pltpu.VMEM((2, block, width), bf16),
            pltpu.VMEM((2, block, width), bf16),
            pltpu.VMEM((2, 1, every), f32),
            pltpu.VMEM((count, 2, 1, every), f32),
            pltpu.VMEM((batches, length, size), bf16),
        ]
        + Flow.scratch(E, C, batches, run, width, cap, 3)
        + [
            DMA((2,)),
            DMA((2,)),
            DMA((count,)),
            DMA((count,)),
            DMA((batches, count)),
            DMA((batches, count)),
            DMA((batches,)),
            DMA((5,)),
        ],
        collective,
        name,
        vmem=46,
    )


def experts_kernel(
    E,
    C,
    rows_x,
    u_in,
    slots,
    gates,
    gate_in,
    up_in,
    down_in,
    out,
    x_out,
    y_out,
    pair_out,
    act_out,
    gate_back_out,
    up_back_out,
    scalars_out,
    w_gate,
    w_up,
    w_down,
    table,
    scalars,
    landed,
    packed,
    own,
    zs,
    zr,
    xs,
    xr,
    stay,
    sums,
    returned,
    x,
    u,
    pair,
    act,
    gate_back,
    up_back,
    gated,
    sent,
    gs,
    gr,
    ss,
    sr,
    ys,
    yr,
    bs,
    us,
    ur,
    ks,
    loads,
    stores,
    weight_sem,
):
    e, c, d = position()
    batches, run, width = rows_x.shape
    cap = x_out.shape[3]
    units = w_gate.shape[1]
    chunks = batches * C
    total = E * cap
    kept = sent.shape[0]
    lead, lag = 1, 2
    everyone = [(k, i) for k in range(E) for i in range(C) if k + i > 0]
    ahead = [(k, i, (lax.rem(e + k, E), lax.rem(c + i, C), d)) for k, i in everyone]
    behind = [(k, i, (lax.rem(e + E - k, E), lax.rem(c + C - i, C), d)) for k, i in everyone]
    meet([device for _, _, device in ahead])
    flow = Flow(E, C, rows_x, slots, landed, packed, x_out, own, zs, zr, xs, xr, stay)

    def far_of(n):
        return lax.rem((n + batches - 1) // batches, C), lax.rem(n + batches - 1, batches)

    def chunk_of(n):
        far, b = far_of(n)
        return b, flow.level_entry(far)

    def back(n, b, i, k):
        return remote(
            sent.at[lax.rem(n, kept), k],
            returned.at[i, b, e],
            ys.at[i, b, k],
            yr.at[i, b, k],
            (lax.rem(e + E - k, E), c, d),
        )

    def back_own(n, b, i):
        return pltpu.make_async_copy(
            sent.at[lax.rem(n, kept), 0], returned.at[i, b, e], bs.at[i, b]
        )

    def up(b, i):
        return remote(
            sums.at[i, b],
            out.at[c, b],
            us.at[i, b],
            ur.at[i, b],
            (e, lax.rem(c + C - i, C), d),
        )

    def keep(b):
        return pltpu.make_async_copy(sums.at[0, b], out.at[c, b], ks.at[b])

    def load(a, b, i):
        source, target = ((x_out, x), (u_in, u))[a]
        return pltpu.make_async_copy(source.at[i, b], target, loads.at[a])

    def store(j, b, i):
        source = (pair, act, gate_back, up_back, gated)[j]
        target = (pair_out, act_out, gate_back_out, up_back_out, y_out)[j]
        return pltpu.make_async_copy(source, target.at[i, b], stores.at[j])

    weight_copies = [
        pltpu.make_async_copy(source, target, weight_sem.at[j])
        for j, (source, target) in enumerate(
            ((gate_in, w_gate), (up_in, w_up), (down_in, w_down))
        )
    ]
    for copy in weight_copies:
        copy.start()

    flow.begin(1)
    small = [
        remote(gates.at[device[0], device[1]], table.at[k, i], gs.at[k, i], gr.at[k, i], device)
        for k, i, device in ahead
    ]
    for copy in small:
        copy.start()
    table[0, 0] = gates[e, c]

    def compact(n):
        @pl.when(n >= flow.kept)
        def _():
            flow.crossed(n - flow.kept, *chunk_of(n - flow.kept))

        flow.compact(n, *chunk_of(n))

    def expert(n):
        b, i = chunk_of(n)
        load(1, b, i).start()
        flow.arrived(n, b, i)
        flow.stay(n, b, i).wait()
        load(0, b, i).start()

        @pl.when(n == 0)
        def _():
            for copy in weight_copies:
                copy.wait()

        @pl.when(n > 0)
        def _():
            before = chunk_of(n - 1)
            for j in range(5):
                store(j, *before).wait()

        @pl.when(n >= kept)
        def _():
            before = chunk_of(n - kept)
            for k in range(1, E):
                back(n - kept, *before, k).wait_send()

        holds, gate = [], []
        cells = lax.broadcasted_iota(jnp.int32, (cap, run), 0).astype(f32)
        for k in range(E):
            hold = cells == table[k, i, b]
            holds.append(hold)
            gate.append(
                jnp.sum(jnp.where(hold, table[k, i, batches + b], 0.0), axis=1, keepdims=True)
            )
        gate = jnp.concatenate(gate, axis=0)
        for a in range(2):
            load(a, b, i).wait()
        for at in range(0, width, 512):
            part = u[:, :, at : at + 512].reshape(total, 512).astype(f32)
            pair[:, :, at : at + 512] = (gate * part).astype(bf16).reshape(E, cap, 512)
        store(0, b, i).start()
        inputs = x[...].reshape(total, width)
        grads = pair[...].reshape(total, width)
        for at in range(0, units, 256):
            gate_pre = jnp.dot(inputs, w_gate[:, at : at + 256], preferred_element_type=f32)
            up_pre = jnp.dot(inputs, w_up[:, at : at + 256], preferred_element_type=f32)
            act_grad = contract(grads, w_down[at : at + 256, :], (1, 1))
            sigmoid = jax.nn.sigmoid(gate_pre)
            silu = gate_pre * sigmoid
            act[:, at : at + 256] = (silu * up_pre).astype(bf16)
            gate_back[:, at : at + 256] = (
                act_grad * up_pre * sigmoid * (1.0 + gate_pre * (1.0 - sigmoid))
            ).astype(bf16)
            up_back[:, at : at + 256] = (act_grad * silu).astype(bf16)
        for j in range(1, 4):
            store(j, b, i).start()
        place = lax.rem(n, kept)
        gate_grad = jnp.zeros((total, 1), f32)
        for at in range(0, width, 512):
            out = jnp.dot(act[...], w_down[:, at : at + 512], preferred_element_type=f32)
            out = out.astype(bf16).astype(f32)
            gate_grad += jnp.sum(
                out * u[:, :, at : at + 512].reshape(total, 512).astype(f32), axis=1, keepdims=True
            )
            gated[:, :, at : at + 512] = (gate * out).astype(bf16).reshape(E, cap, 512)
            back_rows = contract(gate_back[...], w_gate[at : at + 512, :], (1, 1))
            back_rows += contract(up_back[...], w_up[at : at + 512, :], (1, 1))
            sent[place, :, :, at : at + 512] = back_rows.astype(bf16).reshape(E, cap, 512)
        for k in range(1, E):
            back(n, b, i, k).start()
        back_own(n, b, i).start()
        store(4, b, i).start()
        for k in range(E):
            scalars[k, i, b] = jnp.sum(
                jnp.where(holds[k], gate_grad[k * cap : (k + 1) * cap], 0.0), axis=0, keepdims=True
            )

    def combine(n):
        b, i = chunk_of(n)
        picks = choose(slots[i, b], cap)
        for k in range(1, E):
            back(n, b, i, k).wait_recv()
        back_own(n, b, i).wait()
        for at in range(0, width, 512):
            part = returned[i, b, :, :, at : at + 512].reshape(total, 512)
            sums[i, b, :, at : at + 512] = contract(picks, part, (0, 0)).astype(bf16)

        @pl.when(i > 0)
        def _():
            up(b, i).start()

        @pl.when(i == 0)
        def _():
            keep(b).start()

    def step(s, carry):
        @pl.when(jnp.logical_and(s > 0, s <= batches * (C - 1)))
        def _():
            flow.receive(*far_of(s))
            flow.pass_on(s // batches, lax.rem(s, batches))

        @pl.when(s < chunks)
        def _():
            compact(s)

        @pl.when(jnp.logical_and(s >= lead, s < chunks + lead))
        def _():
            expert(s - lead)

        @pl.when(s >= lag)
        def _():
            combine(s - lag)

        return carry

    for copy in small:
        copy.wait_recv()
    lax.fori_loop(0, chunks + lag, step, 0)
    scalars_out[e, c] = scalars[0, 0]
    last = [
        remote(scalars.at[k, i], scalars_out.at[e, c], ss.at[k, i], sr.at[k, i], device)
        for k, i, device in behind
    ]
    for copy in last:
        copy.start()
    for copy in small:
        copy.wait_send()
    for j in range(5):
        store(j, *chunk_of(chunks - 1)).wait()

    def finish(n, carry):
        b, i = chunk_of(n)
        flow.hops_sent(b, i)

        @pl.when(n >= chunks - flow.kept)
        def _():
            flow.crossed(n, b, i)

        @pl.when(n >= chunks - kept)
        def _():
            for k in range(1, E):
                back(n, b, i, k).wait_send()

        @pl.when(i > 0)
        def _():
            up(b, i).wait()

        @pl.when(i == 0)
        def _():
            keep(b).wait()

        return carry

    lax.fori_loop(0, chunks, finish, 0)
    for copy in last:
        copy.wait()


def run_experts(E, C, rows_x, u_in, slots, gates, w_gate, w_up, w_down, cap, collective, name):
    batches, run, width = rows_x.shape
    units = w_gate.shape[1]
    total = E * cap
    kept = 3
    by_slot = jax.ShapeDtypeStruct((C, batches, E, cap, width), bf16)
    by_token = jax.ShapeDtypeStruct((C, batches, run, width), bf16)
    hidden = jax.ShapeDtypeStruct((C, batches, total, units), bf16)
    return call(
        functools.partial(experts_kernel, E, C),
        (rows_x, u_in, slots, gates, w_gate, w_up, w_down),
        (
            by_token,
            by_slot,
            by_slot,
            by_slot,
            hidden,
            hidden,
            hidden,
            jax.ShapeDtypeStruct((E, C, batches, 1, run), f32),
        ),
        [ANY, ANY, VMEM, VMEM, ANY, ANY, ANY],
        (ANY,) * 7 + (VMEM,),
        [
            pltpu.VMEM(w_gate.shape, bf16),
            pltpu.VMEM(w_up.shape, bf16),
            pltpu.VMEM(w_down.shape, bf16),
            pltpu.VMEM(gates.shape, f32),
            pltpu.VMEM((E, C, batches, 1, run), f32),
        ]
        + Flow.scratch(E, C, batches, run, width, cap, kept)
        + [
            pltpu.VMEM((C, batches, run, width), bf16),
            pltpu.VMEM((C, batches, E, cap, width), bf16),
            pltpu.VMEM((E, cap, width), bf16),
            pltpu.VMEM((E, cap, width), bf16),
            pltpu.VMEM((E, cap, width), bf16),
            pltpu.VMEM((total, units), bf16),
            pltpu.VMEM((total, units), bf16),
            pltpu.VMEM((total, units), bf16),
            pltpu.VMEM((E, cap, width), bf16),
            pltpu.VMEM((kept, E, cap, width), bf16),
            DMA((E, C)),
            DMA((E, C)),
            DMA((E, C)),
            DMA((E, C)),
            DMA((C, batches, E)),
            DMA((C, batches, E)),
            DMA((C, batches)),
            DMA((C, batches)),
            DMA((C, batches)),
            DMA((batches,)),
            DMA((2,)),
            DMA((5,)),
            DMA((3,)),
        ],
        collective,
        name,
        vmem=60,
    )


def middle_kernel(
    E,
    C,
    G,
    runs,
    parts,
    resid,
    factor,
    upstream,
    gain,
    logit_grad,
    router,
    w_output,
    mixed,
    x,
    pair,
    gate_back,
    up_back,
    act,
    y_rows,
    slots,
    resid_grad,
    gain_grad,
    heads,
    proj,
    own_gate,
    own_up,
    own_down,
    other_gate,
    other_up,
    other_down,
    out,
    attn_grad,
    stage,
    blocks,
    hidden,
    wide,
    kept,
    sent,
    swap,
    swapped,
    chip,
    plane_parts,
    level_part,
    hs,
    hr,
    hl,
    block_sem,
    cs,
    cr,
    ps,
    pr,
    zs,
    zr,
    rs,
    wide_sem,
    ks,
    xs,
    xr,
    *return_scratch,
):
    e, c, d = position()
    me, peers = column_peers(E, C, G)
    planes, levels = plane_peers(E), level_peers(C)
    batches, run = parts.shape[1:3]
    own, width = resid.shape
    size = blocks.shape[1]
    step = wide.shape[2]
    half = own_gate.shape[1]
    sibling = (e, c, 1 - d)
    meet([device for _, _, device in peers] + [device for _, _, device in planes])
    way_back = Return(E, C, runs, y_rows, slots, out, *return_scratch)
    way_back.send(0)

    turns = [index for _, index, _ in peers] + [me]

    def block_copy(n):
        at = pl.ds(pl.multiple_of(turns[n] * size, size), size)
        return pltpu.make_async_copy(w_output.at[at], blocks.at[n % 2], block_sem.at[n % 2])

    block_copy(0).start()
    block_copy(1).start()
    hidden_copies = [
        pltpu.make_async_copy(source, hidden.at[j % 2], rs.at[j % 2])
        for j, source in enumerate((gate_back, up_back, act))
    ]
    hidden_copies[0].start()
    hidden_copies[1].start()
    count = width // step
    sources = [x] * count + [pair] * count

    def wide_copy(item):
        at = (item % count) * step
        return pltpu.make_async_copy(
            sources[item].at[:, pl.ds(at, step)], wide.at[item % 2], wide_sem.at[item % 2]
        )

    wide_copy(0).start()
    wide_copy(1).start()

    total = jnp.zeros((own, 1), f32)
    for at in range(0, width, 512):
        lanes = pl.ds(at, 512)
        grad = contract(logit_grad[...], router[lanes], (1, 1))
        for level in range(C):
            grad += parts[level, :, :, lanes].reshape(own, 512).astype(f32)
        hat = resid[:, lanes] * factor[...]
        gain_grad[:, lanes] = jnp.sum(grad * hat, axis=0, keepdims=True)
        grad = grad * gain[:, lanes]
        total += jnp.sum(grad * hat, axis=1, keepdims=True)
        resid_grad[:, lanes] = grad
    mean = total / width
    for at in range(0, width, 512):
        lanes = pl.ds(at, 512)
        hat = resid[:, lanes] * factor[...]
        grad = upstream[:, lanes].astype(f32) + factor[...] * (resid_grad[:, lanes] - hat * mean)
        resid_grad[:, lanes] = grad
        attn_grad[:, lanes] = grad.astype(bf16)

    way_back.send(1)

    head_copies = []
    for n in range(len(turns)):
        block_copy(n).wait()
        part = contract(attn_grad[...], blocks[n % 2], (1, 1))
        stage[n] = part.astype(bf16).reshape(batches, run, size)
        if n + 2 < len(turns):
            block_copy(n + 2).start()
        for b in range(batches):
            if n < len(peers):
                offset, _, device = peers[n]
                copy = remote(
                    stage.at[n, b], heads.at[b, me], hs.at[b, offset], hr.at[b, offset], device
                )
            else:
                copy = pltpu.make_async_copy(stage.at[n, b], heads.at[b, me], hl.at[b])
            copy.start()
            head_copies.append(copy)

    block = width // E

    def chip_copy(plane):
        return remote(swap.at[plane], swapped.at[plane], cs.at[plane], cr.at[plane], sibling)

    def plane_copy(i, level):
        plane = lax.rem(e + i, E)
        return remote(
            chip.at[plane, level],
            plane_parts.at[i, level],
            ps.at[i, level],
            pr.at[i, level],
            (plane, c, d),
        )

    def give(i, carry):
        plane = lax.rem(e + 1 + i, E)
        rows = pl.ds(pl.multiple_of(plane * block, block), block)
        left = mixed[:, rows]
        for at in range(0, width, 512):
            lanes = pl.ds(at, 512)
            part = contract(left, attn_grad[:, lanes], (0, 0)).astype(bf16)
            part = part.reshape(C, G, block // (C * G), 512)
            first, last = part[:, 0], part[:, G - 1]
            chip[plane, :, :, lanes] = jnp.where(d == 0, first, last)
            swap[plane, :, :, lanes] = jnp.where(d == 0, last, first)
        chip_copy(plane).start()
        return carry

    def take(i, carry):
        plane = lax.rem(e + 1 + i, E)
        chip_copy(plane).wait_recv()
        for at in range(0, width, 512):
            lanes = pl.ds(at, 512)
            part = chip[plane, :, :, lanes].astype(f32) + swapped[plane, :, :, lanes].astype(f32)
            chip[plane, :, :, lanes] = part.astype(bf16)
        return carry

    lax.fori_loop(0, E, give, 0)
    lax.fori_loop(0, E, take, 0)
    order = [lax.rem(c + i, C) for i in list(range(1, C)) + [0]]
    levels_left = iter(order)

    def level_send():
        level = next(levels_left, None)
        if level is not None:
            for i in range(1, E):
                plane_copy(i, level).start()

    level_send()

    def keep_copy(j, at, place):
        target = (own_gate, own_up, own_down)[j]
        where = target.at[:, pl.ds(at, step)] if j == 2 else target.at[pl.ds(at, step)]
        return pltpu.make_async_copy(kept.at[place], where, ks.at[place])

    def send_copy(j, at, place):
        target = (other_gate, other_up, other_down)[j]
        where = target.at[:, pl.ds(at, step)] if j == 2 else target.at[pl.ds(at, step)]
        return remote(sent.at[place % slots_sent], where, xs.at[place], xr.at[place], sibling)

    slots_sent = sent.shape[0]
    combine_at, combine_step, level_at = 0, 1, (2, 3, 4)
    kept_copies, sent_copies, after = [], [], {}
    for n in range(len(runs)):
        after.setdefault(combine_at + combine_step * n, []).append(n)
    hidden_copies[0].wait()
    hidden_copies[1].wait()
    for item in range(2 * count):
        if item == count:
            hidden_copies[2].start()
            hidden_copies[2].wait()
        wide_copy(item).wait()
        at = (item % count) * step
        left = wide[item % 2]
        for j in (0, 1) if item < count else (2,):
            place = len(sent_copies)

            def product(core):
                part = hidden[j % 2, :, pl.ds(pl.multiple_of(core * half, half), half)]
                return contract(part, left, (0, 0)) if j == 2 else contract(left, part, (0, 0))

            if place >= slots_sent:
                sent_copies[place - slots_sent].wait_send()
            sent[place % slots_sent] = product(1 - d).astype(bf16)
            copy = send_copy(j, at, place)
            copy.start()
            sent_copies.append(copy)
            if place >= 2:
                kept_copies[place - 2].wait()
            kept[place % 2] = product(d).astype(bf16)
            copy = keep_copy(j, at, place % 2)
            copy.start()
            kept_copies.append(copy)
        if item + 2 < 2 * count:
            wide_copy(item + 2).start()
        for n in after.get(item, ()):
            way_back.combine(n)
        if item in level_at:
            level_send()
    for _ in range(C):
        level_send()

    def level_copy(i, level):
        return remote(level_part.at[level], proj.at[c], zs.at[i], zr.at[i], (e, level, d))

    for i, level in zip(list(range(1, C)) + [0], order):
        for k in range(1, E):
            plane_copy(k, level).wait_recv()
        total = chip[e, level].astype(f32)
        for k in range(1, E):
            total = total + plane_parts[k, level].astype(f32)
        level_part[level] = total.astype(bf16)
        if i > 0:
            level_copy(i, level).start()
        else:
            proj[c] = level_part[c]

    for copy in kept_copies[-2:]:
        copy.wait()
    for copy in sent_copies:
        copy.wait_recv()
    for copy in sent_copies[-slots_sent:]:
        copy.wait_send()
    for copy in head_copies:
        copy.wait()
    for i, level, _ in levels:
        level_copy(i, level).wait()
    way_back.end()
    for plane in range(E):
        chip_copy(plane).wait_send()
    for i in range(1, E):
        for level in range(C):
            plane_copy(i, level).wait_send()


def middle(
    E,
    C,
    G,
    runs,
    parts,
    resid,
    factor,
    upstream,
    gain,
    logit_grad,
    router,
    w_output,
    mixed,
    x,
    pair,
    gate_back,
    up_back,
    act,
    y_rows,
    slots,
    collective,
    name,
):
    batches, run, width = parts.shape[1:]
    own = resid.shape[0]
    count = C * G
    size = width // count
    block = width // E
    part = block // count
    total, units = act.shape
    half = units // G
    step = min(512, width)
    items = 3 * (width // step)
    tall = (width, half)
    flat = (half, width)
    by_plane = pltpu.VMEM((E, C, part, width), bf16)
    return call(
        functools.partial(middle_kernel, E, C, G, runs),
        (
            parts,
            resid,
            factor,
            upstream,
            gain,
            logit_grad,
            router,
            w_output,
            mixed,
            x,
            pair,
            gate_back,
            up_back,
            act,
            y_rows,
            slots,
        ),
        (
            jax.ShapeDtypeStruct((own, width), f32),
            jax.ShapeDtypeStruct((1, width), f32),
            jax.ShapeDtypeStruct((batches, count, run, size), bf16),
            jax.ShapeDtypeStruct((C, part, width), bf16),
            jax.ShapeDtypeStruct(tall, bf16),
            jax.ShapeDtypeStruct(tall, bf16),
            jax.ShapeDtypeStruct(flat, bf16),
            jax.ShapeDtypeStruct(tall, bf16),
            jax.ShapeDtypeStruct(tall, bf16),
            jax.ShapeDtypeStruct(flat, bf16),
            jax.ShapeDtypeStruct((len(runs), run, width), bf16),
        ),
        [VMEM] * 7 + [ANY, VMEM] + [ANY] * 6 + [VMEM],
        (VMEM, VMEM, ANY, VMEM) + (ANY,) * 7,
        [
            pltpu.VMEM((own, width), bf16),
            pltpu.VMEM((count, batches, run, size), bf16),
            pltpu.VMEM((2, size, width), bf16),
            pltpu.VMEM((2, total, units), bf16),
            pltpu.VMEM((2, total, step), bf16),
            pltpu.VMEM((2, step, half), bf16),
            pltpu.VMEM((4, step, half), bf16),
            by_plane,
            by_plane,
            by_plane,
            by_plane,
            pltpu.VMEM((C, part, width), bf16),
            DMA((batches, count)),
            DMA((batches, count)),
            DMA((batches,)),
            DMA((2,)),
            DMA((E,)),
            DMA((E,)),
            DMA((E, C)),
            DMA((E, C)),
            DMA((C,)),
            DMA((C,)),
            DMA((2,)),
            DMA((2,)),
            DMA((2,)),
            DMA((items,)),
            DMA((items,)),
        ]
        + Return.scratch(E, C, len(runs), run, width, y_rows.shape[3]),
        collective,
        name,
        vmem=62,
    )


def backward_kernel(
    E,
    C,
    G,
    runs,
    queries,
    keys,
    values,
    grads,
    row_ids,
    key_ids,
    log_total,
    query_hat_in,
    key_hat_in,
    factors,
    head_gains,
    y_rows,
    slots,
    w_qkv_in,
    normed,
    small,
    first,
    out_qkv,
    out_small,
    out_gains,
    out,
    query_hat,
    key_hat,
    w_qkv,
    raw,
    query_grad,
    key_grad,
    key_sum,
    value_sum,
    sums,
    sum_parts,
    gain_sum,
    gain_parts,
    small_parts,
    small_sum,
    swap,
    swapped,
    own,
    passed,
    tokens,
    parts,
    plane_parts,
    sum_qkv,
    cs,
    cr,
    zs,
    zr,
    ts,
    qs,
    qr,
    os,
    orr,
    ss,
    sr,
    fs,
    fr,
    ms,
    mr,
    hs,
    hr,
    gs,
    gr,
    in_sem,
    *return_scratch,
):
    e, c, d = position()
    me, peers = column_peers(E, C, G)
    planes = plane_peers(E)
    count = C * G
    _, run, columns = raw.shape
    every, size = queries.shape
    batches, length = row_ids.shape[:2]
    scale = HEAD**-0.5
    width = w_qkv.shape[0]
    rows = batches * run
    sibling = (e, c, 1 - d)
    meet([device for _, _, device in peers] + [device for _, _, device in planes])
    half = tokens.shape[2]
    block = parts.shape[1]
    cuts = block // half

    def token_copy(part):
        at = lax.rem(e + 1 + part // cuts, E) * block + part % cuts * half
        return pltpu.make_async_copy(
            normed.at[:, pl.ds(pl.multiple_of(at, half), half)],
            tokens.at[part % 2],
            ts.at[part % 2],
        )

    token_copy(0).start()
    token_copy(1).start()
    small_copies = [
        remote(small.at[plane], small_parts.at[i], ss.at[i], sr.at[i], device)
        for i, plane, device in planes
    ]
    for copy in small_copies:
        copy.start()

    way_back = Return(E, C, runs, y_rows, slots, out, *return_scratch)
    way_back.send(0)
    in_copies = [
        pltpu.make_async_copy(source, target, in_sem.at[j])
        for j, (source, target) in enumerate(
            ((query_hat_in, query_hat), (key_hat_in, key_hat), (w_qkv_in, w_qkv))
        )
    ]
    for copy in in_copies:
        copy.start()
    heads = size // HEAD

    def head_back(n, carry):
        b, h = n // heads, lax.rem(n, heads)
        lanes = pl.ds(pl.multiple_of(h * HEAD, HEAD), HEAD)
        start = pl.multiple_of(b * length, length)
        key_sum[...] = jnp.zeros_like(key_sum)
        value_sum[...] = jnp.zeros_like(value_sum)
        for at, many, seen in query_blocks(length):
            rows_here = pl.ds(pl.multiple_of(start + at, many), many)
            rows_seen = pl.ds(start, seen)
            query, grad = queries[rows_here, lanes], grads[rows_here, lanes]
            scores = contract(query, keys[rows_seen, lanes], (1, 1)) * scale
            allowed = key_ids[b, :, :seen] <= row_ids[b, at : at + many]
            scores = jnp.where(allowed, scores, MASKED)
            probs = jnp.exp(scores - log_total[b, h, at : at + many])
            prod = contract(grad, values[rows_seen, lanes], (1, 1))
            delta = jnp.sum(probs * prod, axis=1, keepdims=True)
            score_grad = (probs * (prod - delta)).astype(bf16)
            query_grad[rows_here, lanes] = (
                jnp.dot(score_grad, keys[rows_seen, lanes], preferred_element_type=f32) * scale
            )
            key_sum[:seen] += contract(score_grad, query, (0, 0)) * scale
            value_sum[:seen] += contract(probs.astype(bf16), grad, (0, 0))
        key_grad[pl.ds(start, length), lanes] = key_sum[...]
        value_lanes = pl.ds(pl.multiple_of(2 * size + h * HEAD, HEAD), HEAD)
        raw[pl.ds(b * count, count), :, value_lanes] = (
            value_sum[...].astype(bf16).reshape(count, run, HEAD)
        )
        @pl.when(n == 0)
        def _():
            way_back.send(1)

        for q, turn in enumerate(beside):

            @pl.when(n == turn)
            def _():
                way_back.combine(q)

        return carry

    beside = (1, 3)[: len(runs)]
    pending = iter(range(len(beside), len(runs)))

    def carry_on(many):
        for _ in range(many):
            n = next(pending, None)
            if n is not None:
                way_back.combine(n)

    lax.fori_loop(0, batches * heads, head_back, 0)
    for copy in in_copies:
        copy.wait()

    chunk = min(2 * run, every)
    per_chunk = chunk // run
    ones = jnp.ones((8, size), f32)
    gain_sum[...] = jnp.zeros_like(gain_sum)
    pairs = ((query_grad, query_hat), (key_grad, key_hat))

    def dots(j, carry):
        rows_here = pl.ds(pl.multiple_of(j * chunk, chunk), chunk)
        for kind, (grad, hat) in enumerate(pairs):
            prod = grad[rows_here] * hat[rows_here]
            gain_sum[kind] += jnp.sum(prod, axis=0, keepdims=True)
            total = lax.dot_general(
                ones,
                prod * head_gains[kind : kind + 1],
                (((1,), (1,)), ((), ())),
                precision=lax.Precision.HIGHEST,
                preferred_element_type=f32,
            )
            sums[kind, :, rows_here] = total[:1]
        return carry

    lax.fori_loop(0, every // chunk, dots, 0)
    shares = [
        remote(sums, sum_parts.at[me], ms.at[offset], mr.at[offset], device)
        for offset, _, device in peers
    ]
    gain_copies = [
        remote(gain_sum, gain_parts.at[i], hs.at[i], hr.at[i], device) for i, _, device in planes
    ]
    for copy in shares + gain_copies:
        copy.start()
    sum_parts[me] = sums[...]
    carry_on(1)
    for copy in shares:
        copy.wait()
    total = sum_parts[0]
    for index in range(1, count):
        total = total + sum_parts[index]
    sums[...] = total / width
    rows_at = lax.broadcasted_iota(jnp.int32, (chunk, chunk), 0)
    same = rows_at == lax.broadcasted_iota(jnp.int32, (chunk, chunk), 1)

    def column_of(row):
        return jnp.sum(jnp.where(same, row, 0.0), axis=1, keepdims=True)

    def through_norm(j, carry):
        rows_here = pl.ds(pl.multiple_of(j * chunk, chunk), chunk)
        for kind, (grad, hat) in enumerate(pairs):
            part = grad[rows_here] * head_gains[kind : kind + 1]
            part = part - hat[rows_here] * column_of(sums[kind, :, rows_here])
            part = (column_of(factors[kind, :, rows_here]) * part).astype(bf16)
            raw[pl.ds(j * per_chunk, per_chunk), :, kind * size : (kind + 1) * size] = part.reshape(
                per_chunk, run, size
            )
        return carry

    lax.fori_loop(0, every // chunk, through_norm, 0)

    def gain_copy(offset, device):
        return remote(gain_sum, out_gains.at[me], gs.at[offset], gr.at[offset], device)

    for copy in gain_copies:
        copy.wait()
    total = gain_sum[...]
    for i in range(1, E):
        total = total + gain_parts[i]
    gain_sum[...] = total
    out_gains[me] = total
    for offset, _, device in peers:
        gain_copy(offset, device).start()

    def product(level, core, at, many):
        left = jnp.concatenate(
            [raw[b * count + level * G + core] for b in range(batches)], axis=0
        )
        return contract(left, w_qkv[at : at + many, :], (1, 1))

    def chip_copy(level):
        return remote(swap.at[level], swapped.at[level], cs.at[level], cr.at[level], sibling)

    def give(level):
        for at in range(0, width, 512):
            swap[level, :, at : at + 512] = product(level, 1 - d, at, 512).astype(bf16)
        chip_copy(level).start()

    def take(level):
        chip_copy(level).wait_recv()
        for at in range(0, width, 512):
            part = product(level, d, at, 512) + swapped[level, :, at : at + 512].astype(f32)
            own[level, :, at : at + 512] = part.astype(bf16)

    def hop(way, level, b):
        there = c + 1 if way == 0 else c - 1
        to = level if way == 0 else level + (C - level) * ((C - 1 - (there - level)) // (C - 1))
        return remote(
            own.at[level, pl.ds(b * run, run)],
            passed.at[to, pl.ds(b * run, run)],
            zs.at[way, level, b],
            zr.at[to, b],
            (e, there, d),
        )

    def arrival(entry, b):
        part = passed.at[entry, pl.ds(b * run, run)]
        return remote(part, part, zs.at[0, 0, b], zr.at[entry, b], sibling)

    def send(way, level, last):
        for b in range(batches):

            @pl.when(last)
            def _():
                arrival(level, b).wait_recv()
                piece = pl.ds(b * run, run)
                own[level, piece] = (
                    own[level, piece].astype(f32) + passed[level, piece].astype(f32)
                ).astype(bf16)

            hop(way, level, b).start()

    order = [C - 1, 0] + list(range(C - 2, 0, -1))
    for level in order:
        give(level)
    carry_on(1)

    def plane_copy(item):
        plane = lax.rem(e + 1 + item, E)
        return remote(
            parts.at[item],
            plane_parts.at[item],
            qs.at[item],
            qr.at[item],
            (plane, c, d),
        )

    def weights(item):
        for part in range(cuts * item, cuts * (item + 1)):
            token_copy(part).wait()
            for at in range(0, columns, 256):
                many = min(256, columns - at)
                piece = raw[:, :, at : at + many].reshape(every, many)
                rows_here = pl.ds(part % cuts * half, half)
                parts[item, rows_here, at : at + many] = contract(
                    tokens[part % 2], piece, (0, 0)
                ).astype(bf16)
            if part + 2 < cuts * E:
                token_copy(part + 2).start()
        if item < E - 1:
            plane_copy(item).start()

    mirror = C - 1 - c
    items = list(range(E))
    for level in order:
        take(level)
        if level == 0:
            @pl.when(c == 0)
            def _():
                send(0, C - 1, False)

            @pl.when(c == C - 1)
            def _():
                send(1, 0, False)

            weights(items.pop(0))
            carry_on(1)
    weights(items.pop(0))
    carry_on(len(runs))
    for turn in range(1, C - 1):

        @pl.when(c <= turn)
        def _():
            send(0, C - 1 - (turn - c), c > 0)

        @pl.when(mirror <= turn)
        def _():
            send(1, turn - mirror, mirror > 0)

        if items:
            weights(items.pop(0))
    while items:
        weights(items.pop(0))
    for item in range(E - 1):
        plane_copy(item).wait_recv()
    for at in range(0, block, 128):
        piece = pl.ds(at, min(128, block - at))
        total = parts[E - 1, piece].astype(f32)
        for item in range(E - 1):
            total = total + plane_parts[item, piece].astype(f32)
        sum_qkv[piece] = total.astype(bf16)
    share = block // (C * G)

    def row_copy(offset, index, device):
        return remote(
            sum_qkv.at[pl.ds(pl.multiple_of(index * share, share), share)],
            out_qkv.at[me],
            os.at[offset],
            orr.at[offset],
            device,
        )

    def small_copy(offset, index, device):
        return remote(
            small_sum.at[pl.ds(pl.multiple_of(index * share, share), share)],
            out_small.at[me],
            fs.at[offset],
            fr.at[offset],
            device,
        )

    for copy in small_copies:
        copy.wait_recv()
    total = small[e].astype(f32)
    for i in range(1, E):
        total = total + small_parts[i].astype(f32)
    small_sum[...] = total.astype(bf16)
    for offset, index, device in peers:
        small_copy(offset, index, device).start()
        row_copy(offset, index, device).start()
    out_small[me] = small_sum[pl.ds(pl.multiple_of(me * share, share), share)]
    out_qkv[me] = sum_qkv[pl.ds(pl.multiple_of(me * share, share), share)]

    def arrived(entry):
        for b in range(batches):
            arrival(entry, b).wait_recv()

    @pl.when(c > 0)
    def _():
        arrived(c)

    @pl.when(c < C - 1)
    def _():
        arrived(C)

    for at in range(0, width, 512):
        first[:, at : at + 512] = own[c, :, at : at + 512].astype(f32)

    @pl.when(c > 0)
    def _():
        for at in range(0, width, 512):
            first[:, at : at + 512] += passed[c, :, at : at + 512].astype(f32)

    @pl.when(c < C - 1)
    def _():
        for at in range(0, width, 512):
            first[:, at : at + 512] += passed[C, :, at : at + 512].astype(f32)

    for level in range(C):
        chip_copy(level).wait_send()
        for b in range(batches):

            @pl.when(level > c)
            def _():
                hop(0, level, b).wait_send()

            @pl.when(level < c)
            def _():
                hop(1, level, b).wait_send()

    for item in range(E - 1):
        plane_copy(item).wait_send()
    for copy in small_copies:
        copy.wait_send()
    for offset, _, device in peers:
        gain_copy(offset, device).wait()
    way_back.end()
    for offset, index, device in peers:
        row_copy(offset, index, device).wait()
        small_copy(offset, index, device).wait()


def run_backward(
    E,
    C,
    G,
    runs,
    queries,
    keys,
    values,
    grads,
    ids,
    log_total,
    query_hat,
    key_hat,
    factors,
    head_gains,
    y_rows,
    slots,
    w_qkv,
    normed,
    small,
    collective,
    name,
):
    every, size = queries.shape
    batches, length = ids.shape
    count = C * G
    run = length // count
    columns = 3 * size
    width = w_qkv.shape[0]
    rows = batches * run
    block = width // E
    share = block // count
    lanes = small.shape[2]
    by_level = pltpu.VMEM((C, rows, width), bf16)
    wide = pltpu.VMEM((every, size), f32)
    head = pltpu.VMEM((length, HEAD), f32)
    return call(
        functools.partial(backward_kernel, E, C, G, runs),
        (
            queries,
            keys,
            values,
            grads,
            ids[:, :, None],
            ids[:, None, :],
            log_total,
            query_hat,
            key_hat,
            factors,
            head_gains,
            y_rows,
            slots,
            w_qkv,
            normed,
            small,
        ),
        (
            jax.ShapeDtypeStruct((rows, width), f32),
            jax.ShapeDtypeStruct((count, share, columns), bf16),
            jax.ShapeDtypeStruct((count, share, lanes), bf16),
            jax.ShapeDtypeStruct((count, 2, 1, size), f32),
            jax.ShapeDtypeStruct((len(runs), run, width), bf16),
        ),
        [VMEM] * 7 + [ANY, ANY, VMEM, VMEM, ANY, VMEM, ANY, ANY, VMEM],
        (VMEM, VMEM, VMEM, VMEM, ANY),
        [
            wide,
            wide,
            pltpu.VMEM(w_qkv.shape, bf16),
            pltpu.VMEM((batches * count, run, columns), bf16),
            wide,
            wide,
            head,
            head,
            pltpu.VMEM((2, 1, every), f32),
            pltpu.VMEM((count, 2, 1, every), f32),
            pltpu.VMEM((2, 1, size), f32),
            pltpu.VMEM((E, 2, 1, size), f32),
            pltpu.VMEM((E, block, lanes), bf16),
            pltpu.VMEM((block, lanes), bf16),
            by_level,
            by_level,
            by_level,
            pltpu.VMEM((C + 1, rows, width), bf16),
            pltpu.VMEM((2, every, min(block, 256)), bf16),
            pltpu.VMEM((E, block, columns), bf16),
            pltpu.VMEM((E, block, columns), bf16),
            pltpu.VMEM((block, columns), bf16),
            DMA((C,)),
            DMA((C,)),
            DMA((2, C, batches)),
            DMA((C + 1, batches)),
            DMA((2,)),
            DMA((E,)),
            DMA((E,)),
            DMA((count,)),
            DMA((count,)),
            DMA((E,)),
            DMA((E,)),
            DMA((count,)),
            DMA((count,)),
            DMA((count,)),
            DMA((count,)),
            DMA((E,)),
            DMA((E,)),
            DMA((count,)),
            DMA((count,)),
            DMA((3,)),
        ]
        + Return.scratch(E, C, len(runs), run, width, y_rows.shape[3]),
        collective,
        name,
        vmem=62,
    )


def contract(left, right, axes):
    return lax.dot_general(left, right, ((axes[:1], axes[1:]), ((), ())), preferred_element_type=f32)


def query_blocks(length):
    size = min(256, length)
    return [(i, size, min(length, i + 2 * size)) for i in range(0, length, size)]


def rms_factor(values):
    return lax.rsqrt(jnp.mean(values * values, axis=-1, keepdims=True) + EPSILON)


def norm_back(grad_hat, hatted, factor):
    return factor * (grad_hat - hatted * jnp.mean(grad_hat * hatted, axis=-1, keepdims=True))


def slot_table(routes, experts):
    batches, run, top = routes.shape
    hits = jnp.swapaxes(routes, 1, 2)[:, :, :, None] == jnp.arange(experts, dtype=jnp.int32)
    ones = hits.astype(bf16)
    tokens, ranks = jnp.arange(run), jnp.arange(top)
    before = (tokens[None, :] < tokens[:, None]).astype(bf16)
    above = (ranks[None, :] < ranks[:, None]).astype(bf16)
    within = jnp.einsum("ts,bksx->bktx", before, ones, preferred_element_type=f32)
    totals = jnp.sum(hits.astype(f32), axis=2)
    earlier = jnp.einsum(
        "kj,bjx->bkx", above, totals.astype(bf16), preferred_element_type=f32
    )
    places = jnp.sum(jnp.where(hits, within + earlier[:, :, None, :], 0.0), axis=1)
    places = jnp.where(jnp.any(hits, axis=1), places, UNUSED_SLOT)
    return jnp.swapaxes(places, 1, 2)


def body(
    tokens,
    block_ids,
    routes,
    norm_gains,
    w_query,
    w_key,
    w_value,
    w_output,
    router,
    expert_gate,
    expert_up,
    expert_down,
    cotangent,
):
    E, C, G = lax.axis_size("expert"), lax.axis_size("context"), lax.axis_size("dp")
    batches, run, width = tokens.shape
    top = routes.shape[2]
    experts = E * C * expert_gate.shape[0]
    capacity = max(2, run * top // experts)
    count = C * G
    size = width // count
    length = count * run
    every = batches * length
    own = batches * run
    me = lax.axis_index("context") * G + lax.axis_index("dp")

    rows = w_query.shape[0]
    small_width = -(-(norm_gains.shape[1] + experts) // 128) * 128
    small = jnp.concatenate([norm_gains, router], axis=1)
    small = jnp.pad(small, ((0, 0), (0, small_width - small.shape[1])))
    pieces = [w.reshape(rows, count, size) for w in (w_query, w_key, w_value)]
    weights = jnp.swapaxes(jnp.concatenate(pieces, axis=2), 0, 1)
    places = slot_table(routes, experts).reshape(batches, E, C, run)
    by_level = jnp.transpose(places, (2, 0, 1, 3))
    by_expert = jnp.transpose(places, (1, 2, 0, 3))
    column, w_qkv, small, full_output, ids, slots = start(
        E, C, G, tokens, weights, small, w_output, block_ids, by_level
    )
    ids = jnp.swapaxes(ids, 0, 1).reshape(batches, length)
    w_qkv = w_qkv.reshape(width, 3 * size)
    small = small.reshape(width, small_width)
    full_output = full_output.reshape(width, width)
    gains = small[:, :4].astype(f32)
    full_router = small[:, 4 : 4 + experts]
    head_gains = lax.dynamic_slice(gains, (me * size, 0), (size, 4))

    (
        normed,
        query_low,
        key_low,
        value_low,
        query_hat,
        key_hat,
        log_total,
        factors,
        mixed_low,
        upstream_rows,
    ) = run_forward(
        E,
        C,
        G,
        column.reshape(every, width),
        jnp.swapaxes(gains[:, :1], 0, 1),
        jnp.swapaxes(head_gains[:, 1:3], 0, 1),
        w_qkv,
        ids,
        slots,
        cotangent,
        capacity,
        2,
        "forward",
    )
    mixed_low = mixed_low.reshape(own, width)

    inputs = tokens.reshape(own, width).astype(f32)
    resid = inputs + jnp.dot(mixed_low, full_output, preferred_element_type=f32)
    second_factor = rms_factor(resid)
    second_hat = resid * second_factor
    second_low = (second_hat * gains[:, 3]).astype(bf16)
    logits = jnp.dot(second_low, full_router, preferred_element_type=f32)
    router_probs = jax.nn.softmax(logits, axis=-1)
    gate_table = jnp.transpose(router_probs.reshape(batches, run, E, C), (2, 3, 0, 1))
    table = jnp.concatenate([by_expert, gate_table], axis=2)[:, :, :, None, :]

    second_grad, x, y_rows, pair_grad, act, gate_pre_grad, up_pre_grad, gate_grad = run_experts(
        E,
        C,
        second_low.reshape(batches, run, width),
        upstream_rows,
        slots,
        table,
        expert_gate[0],
        expert_up[0],
        expert_down[0],
        capacity,
        4,
        "experts",
    )
    slot_count = E * C * batches * capacity
    x, pair_grad, act, gate_pre_grad, up_pre_grad = (
        rows.reshape(slot_count, -1) for rows in (x, pair_grad, act, gate_pre_grad, up_pre_grad)
    )
    prob_grad = jnp.transpose(gate_grad[:, :, :, 0, :], (2, 3, 0, 1)).reshape(own, experts)
    logit_grad = router_probs * (
        prob_grad - jnp.sum(router_probs * prob_grad, axis=-1, keepdims=True)
    )
    logit_grad = jnp.pad(logit_grad.astype(bf16), ((0, 0), (0, small_width - experts)))
    router_wide = jnp.pad(full_router, ((0, 0), (0, small_width - experts)))

    early = [(b, i) for b in range(batches // 2) for i in list(range(1, C)) + [0]]
    late = [(b, i) for b in range(batches // 2, batches) for i in list(range(1, C)) + [0]]
    resid_grad, gain_second, mixed_grad, grad_proj, *expert_grads, early_mixture = middle(
        E,
        C,
        G,
        early,
        second_grad,
        resid,
        second_factor,
        cotangent.reshape(own, width),
        jnp.swapaxes(gains[:, 3:4], 0, 1),
        logit_grad,
        router_wide,
        full_output,
        mixed_low,
        x,
        pair_grad,
        gate_pre_grad,
        up_pre_grad,
        act,
        y_rows,
        slots,
        6,
        "middle",
    )
    grad_gate, grad_up, grad_down = (
        (mine.astype(f32) + other.astype(f32))[None] for mine, other in zip(expert_grads[:3], expert_grads[3:])
    )
    grad_proj = jnp.sum(grad_proj.astype(f32), axis=0)
    sums = contract(second_low, logit_grad, (0, 0))
    sums = jnp.where(jnp.arange(small_width) == experts, gain_second.reshape(width, 1), sums)
    sums = sums.astype(bf16)
    first_grad, grad_qkv, sums, gain_heads, late_mixture = run_backward(
        E,
        C,
        G,
        late,
        query_low,
        key_low,
        value_low,
        mixed_grad.reshape(every, size),
        ids,
        log_total,
        query_hat,
        key_hat,
        factors,
        jnp.swapaxes(head_gains[:, 1:3], 0, 1),
        y_rows,
        slots,
        w_qkv,
        normed,
        sums.reshape(E, width // E, small_width),
        8,
        "backward",
    )
    gain_heads = jnp.swapaxes(gain_heads[:, :, 0], 0, 1).reshape(2, width)
    first_row = (lax.axis_index("expert") * count + me) * rows
    gain_heads = lax.dynamic_slice(gain_heads, (0, first_row), (2, rows))
    mixture = [0.0] * batches
    for runs, parts in ((early, early_mixture), (late, late_mixture)):
        for n, (b, _) in enumerate(runs):
            mixture[b] = mixture[b] + parts[n].astype(f32)
    mixture = jnp.stack(mixture)
    activations = (resid.reshape(tokens.shape) + mixture).astype(bf16)
    sums = jnp.sum(sums.astype(f32), axis=0)
    first_factor = rms_factor(inputs)
    first_hat = inputs * first_factor
    input_grad = resid_grad + norm_back(first_grad * gains[:, 0], first_hat, first_factor)

    grad_qkv = jnp.swapaxes(grad_qkv.astype(f32), 0, 1)
    grad_query, grad_key, grad_value = (
        grad_qkv[:, :, i * size : (i + 1) * size].reshape(rows, width) for i in range(3)
    )
    gain_first = sum(
        jnp.sum(w.astype(f32) * grad, axis=1)
        for w, grad in ((w_query, grad_query), (w_key, grad_key), (w_value, grad_value))
    )
    gain_first = gain_first / norm_gains[:, 0].astype(f32)
    grad_gains = jnp.stack([gain_first, gain_heads[0], gain_heads[1], sums[:, experts]], axis=1)
    return (
        activations,
        input_grad.reshape(tokens.shape),
        grad_gains,
        grad_query,
        grad_key,
        grad_value,
        grad_proj,
        sums[:, :experts],
        grad_gate,
        grad_up,
        grad_down,
    )


def solution(mesh):
    by_token = ("context", "dp")
    by_expert = P(("expert", "context"), None, None)
    by_row = P(ALL_AXES, None)
    rows = P("expert", by_token, None)
    return jax.shard_map(
        body,
        mesh=mesh,
        in_specs=(
            rows,
            P("expert", by_token),
            rows,
            by_row,
            by_row,
            by_row,
            by_row,
            by_row,
            by_row,
            by_expert,
            by_expert,
            by_expert,
            rows,
        ),
        out_specs=(
            rows,
            rows,
            by_row,
            by_row,
            by_row,
            by_row,
            by_row,
            by_row,
            P(("expert", "context"), None, "dp"),
            P(("expert", "context"), None, "dp"),
            P(("expert", "context"), "dp", None),
        ),
        check_vma=False,
    )
```
